128 devices in a mesh: row: 16 (over x_lo, y, core), col: 8 (over z, x_hi).
Axes of the slice: x: 4 (x_hi: 2, x_lo: 2; x = x_hi * 2 + x_lo), y: 4, z: 4, core: 2. Of those that a mesh axis runs over, the one named last changes fastest.
Arguments:
- pair_map: bfloat16 [8, 48, 128, 1024], P(None, None, 'row', 'col'), may hold values from -6 to 6
- cotangent: bfloat16 [8, 48, 128, 1024], P(None, None, 'row', 'col'), may hold values from -6 to 6
- conv_weight: bfloat16 [24, 48, 3, 3], replicated, may hold values from -0.3125 to 0.3125
- conv_gain: float32 [24], replicated, may hold values from 0.1 to 1.9
- conv_bias: float32 [24], replicated, may hold values from -2 to 2
- mix_weight: bfloat16 [48, 24], replicated, may hold values from -1.25 to 1.25
- mix_gain: float32 [48], replicated, may hold values from 0.1 to 1.9
- mix_bias: float32 [48], replicated, may hold values from -2 to 2
Outputs:
- symmetric: bfloat16 [8, 48, 128, 1024], P(None, None, 'row', 'col')
- grad_input: bfloat16 [8, 48, 128, 1024], P(None, None, 'row', 'col')
- grad_conv: float32 [24, 48, 3, 3], replicated
- grad_mix: float32 [48, 24], replicated
The draws below stay inside these ranges and needn't reach their ends.
All inputs are finite; a program needn't handle non-finite values.
Results may differ from the reference program's by a relative error of at most 0.0065.
Values may be sent and summed in bfloat16 or wider, within the bound.
No kernel may reach another device: no remote copies, remote signals or barrier semaphores. Data moves between devices by JAX's collectives and lax.ppermute only.
A program may use at most 64 MiB of HBM per device.

```python
import jax
import jax.numpy as jnp
from jax import lax

CH = 48
MID = 24
DILATION = 4
GROUPS = 8
HEIGHT = 128
BINS = 1024


def shard_levels(key, shape, split, least, largest):
    factor_of, own = 1.0, jax.random.fold_in(key, 6)
    for dim, parts in split:
        draws = jnp.exp(jax.random.uniform(jax.random.fold_in(own, dim), (parts,), jnp.float32, least / len(split), largest / len(split)))
        factor_of = factor_of * jnp.repeat(draws, shape[dim] // parts).reshape([-1 if axis == dim else 1 for axis in range(len(shape))])
    return factor_of


def noise(own_key, shape, scale, limit, shards=(), held_as=jnp.bfloat16):
    drawn = jax.random.normal(own_key, shape, jnp.float32) * scale
    if len(shards) > 0:
        drawn = shard_levels(own_key, shape, shards, -0.22, 0.18) * drawn
    return jnp.clip(drawn, min=-limit, max=limit).astype(held_as)


def setup_inputs(seed: int = 0) -> dict:
    streams_of = jax.random.split(jax.random.key(seed), 9)
    pair_map = noise(streams_of[0], (GROUPS, CH, HEIGHT, BINS), 1.0, 6.0, ((2, 16), (3, 8)))
    cotangent = noise(streams_of[1], (GROUPS, CH, HEIGHT, BINS), 1.0, 6.0, ((2, 16), (3, 8)))
    conv_weight = noise(streams_of[2], (MID, CH, 3, 3), (9 * CH) ** -0.5, 0.3125)
    conv_gain = jnp.clip(1.0 + 0.18 * jax.random.normal(streams_of[3], (MID,), jnp.float32), 0.1, 1.9)
    conv_bias = noise(streams_of[4], (MID,), 0.5, 2.0, (), jnp.float32)
    mix_weight = noise(streams_of[5], (CH, MID), MID ** -0.5, 1.25)
    mix_gain = jnp.clip(1.0 + 0.18 * jax.random.normal(streams_of[6], (CH,), jnp.float32), 0.1, 1.9)
    mix_bias = noise(streams_of[7], (CH,), 0.5, 2.0, (), jnp.float32)
    return {"pair_map": pair_map, "cotangent": cotangent, "conv_weight": conv_weight, "conv_gain": conv_gain, "conv_bias": conv_bias, "mix_weight": mix_weight, "mix_gain": mix_gain, "mix_bias": mix_bias}


def smooth(values):
    return jax.nn.gelu(values, approximate=True)

def smooth_back(values, grads):
    return jax.vjp(smooth, values)[1](grads)[0]

def dilated(values, kernel):
    return lax.conv_general_dilated(values, kernel, (1, 1), ((DILATION, DILATION), (DILATION, DILATION)), rhs_dilation=(DILATION, DILATION), dimension_numbers=('NCHW', 'OIHW', 'NCHW'), precision=lax.Precision.HIGHEST)

def to_map(array):
    groups, channels, height, bins = array.shape
    return jnp.transpose(array, (1, 0, 2, 3)).reshape(channels, groups * height, bins)[None]

def from_map(field, groups):
    channels, bins = (field.shape[1], field.shape[2])
    return jnp.transpose(field[0].reshape(channels, groups, bins // groups, bins), (1, 0, 2, 3))

def bounce(values):
    return lax.optimization_barrier(values.astype(jnp.bfloat16)).astype(jnp.float32)

def reference(pair_map, cotangent, conv_weight, conv_gain, conv_bias, mix_weight, mix_gain, mix_bias):
    groups = pair_map.shape[0]
    source = to_map(pair_map).astype(jnp.float32)
    act = bounce(smooth(source))
    kernel = conv_weight.astype(jnp.float32)
    mixer = mix_weight.astype(jnp.float32)
    c_gain = conv_gain[None, :, None, None]
    m_gain = mix_gain[None, :, None, None]
    inner = dilated(act, kernel)
    pre = inner * c_gain + conv_bias[None, :, None, None]
    hidden = bounce(smooth(pre))
    mixed = jnp.einsum('om,nmhw->nohw', mixer, hidden, precision=lax.Precision.HIGHEST)
    block = bounce(source + mixed * m_gain + mix_bias[None, :, None, None])
    symmetric = (0.5 * (block + jnp.swapaxes(block, 2, 3))).astype(jnp.bfloat16)
    grad_out = to_map(cotangent).astype(jnp.float32)
    grad_block = 0.5 * (grad_out + jnp.swapaxes(grad_out, 2, 3))
    grad_mix_in = bounce(grad_block * m_gain)
    grad_hidden = jnp.einsum('om,nohw->nmhw', mixer, grad_mix_in, precision=lax.Precision.HIGHEST)
    grad_inner = bounce(smooth_back(pre, grad_hidden) * c_gain)
    pullback = jax.vjp(dilated, act, kernel)[1]
    grad_act, grad_kernel = pullback(grad_inner)
    grad_input = (grad_block + smooth_back(source, grad_act)).astype(jnp.bfloat16)
    all_bins = source.shape[2]
    grad_conv = grad_kernel / all_bins
    grad_mix = jnp.einsum('nohw,nmhw->om', grad_mix_in, hidden, precision=lax.Precision.HIGHEST) / all_bins
    return (from_map(symmetric, groups), from_map(grad_input, groups), grad_conv, grad_mix)
```

```python
import functools

import jax
import jax.numpy as jnp
from jax import lax
from jax.experimental import pallas as pl
from jax.experimental.pallas import tpu as pltpu
from jax.sharding import PartitionSpec as P

BF = jnp.bfloat16
F32 = jnp.float32
CH, MID, GROUPS, H, LANES, ROWS, COLS = 48, 24, 8, 8, 128, 16, 8
POS = GROUPS * LANES
CR, MR = CH * H, MID * H
TANH_SCALE = 0.7978845608028654
CUBIC = 0.044715
NN = (((1,), (0,)), ((), ()))
NT = (((1,), (1,)), ((), ()))
TN = (((0,), (0,)), ((), ()))


def smooth(v):
    t = jnp.tanh(TANH_SCALE * (v + CUBIC * (v * v * v)))
    return 0.5 * v * (1.0 + t)


def smooth_slope(v):
    s = v * v
    t = jnp.tanh(TANH_SCALE * (v + CUBIC * (v * s)))
    return 0.5 * (1.0 + t) + (0.5 * v) * (1.0 - t * t) * (TANH_SCALE * (1.0 + (3.0 * CUBIC) * s))


def dot(a, b, dims=NN):
    return lax.dot_general(a, b, dims, preferred_element_type=F32)


def iota(shape, dim):
    return lax.broadcasted_iota(jnp.int32, shape, dim)


def identity(n):
    return jnp.where(iota((n, n), 0) == iota((n, n), 1), 1.0, 0.0).astype(BF)


def lanes_of(rows):
    return iota((rows, LANES), 1)


def call(kernel, outs, args, name, smem=(), flops=4_000_000_000, scratch=()):
    specs = [
        pl.BlockSpec(memory_space=pltpu.SMEM if i in smem else pltpu.VMEM) for i in range(len(args))
    ]
    return pl.pallas_call(
        kernel,
        name=name,
        out_shape=[jax.ShapeDtypeStruct(s, t) for s, t in outs],
        in_specs=specs,
        out_specs=[pl.BlockSpec(memory_space=pltpu.VMEM) for _ in outs],
        scratch_shapes=list(scratch),
        compiler_params=pltpu.CompilerParams(vmem_limit_bytes=48 * 1024 * 1024),
        cost_estimate=pl.CostEstimate(flops=flops, bytes_accessed=1_000_000, transcendentals=0),
    )(*args)


def pack_rows(field, count):
    pairs = field.reshape(count // 2, 2, H, LANES)
    even, odd = pairs[:, 0], pairs[:, 1]
    low = iota(even.shape, 1) < 4
    last = jnp.where(low, pltpu.roll(even, 4, 1), odd)
    first = jnp.where(low, even, pltpu.roll(odd, 4, 1))
    return last, first


def send_rows(source, down, up, count):
    at_end = (lax.axis_index("row") == ROWS - 1).astype(jnp.int32)
    at_start = (lax.axis_index("row") == 0).astype(jnp.int32)
    for g in range(GROUPS):
        before = g - at_end
        last, _ = pack_rows(source[jnp.maximum(before, 0)].astype(F32), count)
        down[g] = jnp.where(before >= 0, last, 0.0).astype(BF)
        after = g + at_start
        _, first = pack_rows(source[jnp.minimum(after, GROUPS - 1)].astype(F32), count)
        up[g] = jnp.where(after < GROUPS, first, 0.0).astype(BF)


def rows_kernel(x, down, up):
    send_rows(x, down, up, CH)


def turn_out(value, eye, pieces, g, first_tile):
    turned = dot(eye, value, NT)
    for k in range(3):
        part = turned[:, k * LANES : (k + 1) * LANES].reshape(ROWS, H, LANES)
        pieces[:, g, first_tile + k] = part.astype(BF)


def turn_in(pieces, g, first_tile, buffer):
    parts = [
        pieces[r, g, first_tile : first_tile + 3].astype(F32).reshape(3 * H, LANES)
        for r in range(ROWS)
    ]
    lane = lanes_of(3 * H)
    for k in range(4):
        m = 1 << k
        high = (lane // (8 * m)) % 2 == 1
        for i in range(ROWS):
            if i & m:
                continue
            a, b = parts[i], parts[i | m]
            parts[i] = jnp.where(high, pltpu.roll(b, 8 * m, 1), a)
            parts[i | m] = jnp.where(high, b, pltpu.roll(a, LANES - 8 * m, 1))
    for i in range(ROWS):
        buffer[:, i] = parts[i].reshape(3, H, LANES)
    return buffer[...].reshape(CR, LANES)


def mirror_kernel(d, pieces):
    eye = identity(LANES)
    for g in range(GROUPS):
        turn_out(d[g].astype(F32).reshape(CR, LANES).astype(BF), eye, pieces, g, 0)


def weights_kernel(w, mix, cg, cb, mg, mb, a_out, b_out, mf_out, mb_out, cgf, cbf, mgf, mbf):
    for o in range(MID):
        cgf[o] = jnp.full((H, LANES), cg[o], F32)
        cbf[o] = jnp.full((H, LANES), cb[o], F32)
    for o in range(CH):
        mgf[o] = jnp.full((H, LANES), mg[o], F32)
        mbf[o] = jnp.full((H, LANES), mb[o], F32)

    def spread(n, own, width):
        col = iota((n, width), 1)
        half = (width - own) // 2
        rim = jnp.where(col < own + half, col - own, col - own - half) // 4
        return jnp.where(jnp.where(col < own, col // 8, rim) == iota((n, width), 0), 1.0, 0.0).astype(BF)

    def place(own, width):
        col, h = iota((H, width), 1), iota((H, width), 0)
        half = (width - own) // 2
        rim = jnp.where(col < own + half, (col - own) % 4 - 4, (col - own - half) % 4 + 8)
        return jnp.where(col < own, col % 8, rim) - h

    sf, st = spread(CH, CR, 2 * CR), spread(MID, MR, 2 * MR)
    pf, pt = place(CR, 2 * CR), place(MR, 2 * MR)
    for b in range(3):
        total_a = jnp.zeros((MID, H, 2 * CR), F32)
        total_b = jnp.zeros((CH, H, 2 * MR), F32)
        for a in range(3):
            tap = w[3 * a + b]
            mask = jnp.where(pf == 4 * (a - 1), 1.0, 0.0)
            total_a += dot(tap, sf)[:, None, :] * mask[None]
            mask = jnp.where(pt == -4 * (a - 1), 1.0, 0.0)
            total_b += dot(tap, st, TN)[:, None, :] * mask[None]
        a_out[b * MR : (b + 1) * MR] = total_a.reshape(MR, 2 * CR).astype(BF)
        b_out[b * CR : (b + 1) * CR] = total_b.reshape(CR, 2 * MR).astype(BF)
    mask = jnp.where(pf[:, :CR] == 0, 1.0, 0.0)
    mb_out[...] = (dot(mix[...], sf[:, :CR])[:, None, :] * mask[None]).reshape(MR, CR).astype(BF)
    mask = jnp.where(pt[:, :MR] == 0, 1.0, 0.0)
    mf_out[...] = (dot(mix[...], st[:, :MR], TN)[:, None, :] * mask[None]).reshape(CR, MR).astype(BF)


def act_kernel(x, above, below, act, edge):
    lane = lanes_of(CR)
    packed = jnp.zeros((CR, LANES), F32)
    for g in range(GROUPS):
        own = smooth(x[g].astype(F32).reshape(CR, LANES))
        high = smooth(above[g].astype(F32).reshape(CR // 2, LANES))
        low = smooth(below[g].astype(F32).reshape(CR // 2, LANES))
        rim = jnp.concatenate([high, low], axis=0)
        at = slice(g * LANES, (g + 1) * LANES)
        act[0:CR, at] = own.astype(BF)
        act[CR : 2 * CR, at] = rim.astype(BF)
        packed = jnp.where(lane // 8 == g, pltpu.roll(own, (8 * g - 124) % LANES, 1), packed)
        packed = jnp.where(lane // 8 == 8 + g, pltpu.roll(rim, (8 * g - 60) % LANES, 1), packed)
    edge[...] = packed.astype(BF)


def merge_edges(from_left, from_right):
    lane = lanes_of(from_left.shape[0])
    col = lax.axis_index("col")
    has_left = jnp.where(col > 0, 1.0, 0.0)
    has_right = jnp.where(col < COLS - 1, 1.0, 0.0)
    return jnp.where(
        lane % 8 < 4,
        pltpu.roll(from_right, LANES - 4, 1) * has_right,
        pltpu.roll(from_left, 4, 1) * has_left,
    )


def forward_kernel(
    x, act, from_left, from_right, weights, mixer, cg, cb, mg, mb,
    pre_out, hidden_out, rim_out, block_out, pieces,
):
    eye = identity(LANES)
    rim = merge_edges(from_left[...].astype(F32), from_right[...].astype(F32)).astype(BF)
    rim_out[...] = rim
    outer = dot(weights[:, 0:CR], rim) + pltpu.roll(dot(weights[:, CR : 2 * CR], rim), 64, 1)
    lane = lanes_of(MR)
    outer = jnp.where(lane % 8 < 4, outer[2 * MR : 3 * MR], outer[0:MR])
    gain, shift = cg[...].reshape(MR, LANES), cb[...].reshape(MR, LANES)
    for pair in range(GROUPS // 2):
        two = slice(pair * 2 * LANES, (pair + 1) * 2 * LANES)
        product = dot(weights[...], act[:, two])
        for half in range(2):
            g = 2 * pair + half
            p = product[:, half * LANES : (half + 1) * LANES]
            q = pltpu.roll(outer, (124 - 8 * g) % LANES, 1)
            inner = (
                p[MR : 2 * MR]
                + jnp.where(lane < 4, q, pltpu.roll(p[0:MR], 4, 1))
                + jnp.where(lane >= 124, q, pltpu.roll(p[2 * MR : 3 * MR], LANES - 4, 1))
            )
            pre = inner * gain + shift
            at = slice(g * LANES, (g + 1) * LANES)
            pre_out[:, at] = pre
            hidden_out[:, at] = smooth(pre).astype(BF)
        mixed = dot(mixer[...], hidden_out[:, two])
        for half in range(2):
            g = 2 * pair + half
            m = mixed[:, half * LANES : (half + 1) * LANES]
            value = x[g].astype(F32).reshape(CR, LANES) + m * mg[...].reshape(CR, LANES)
            value = (value + mb[...].reshape(CR, LANES)).astype(BF)
            block_out[g] = value.astype(F32).reshape(CH, H, LANES).astype(BF)
            turn_out(value, eye, pieces, g, 0)


def split(value):
    high = value.astype(BF)
    return high, (value - high.astype(F32)).astype(BF)


def exact_dot(value, onehot):
    high, low = split(value)
    return dot(high, onehot) + dot(low, onehot)


def backward_kernel(
    d, arrived, pre_in, hidden, act, rim, turned, mixer, cg, mg,
    grad_inner, down, up, half_sum, pieces,
    buffer, gmi, shifted, edge_rows, wide, mixwide,
):
    lane = lanes_of(MR)
    gain = cg[...].reshape(MR, LANES)
    packed = jnp.zeros((MR, LANES), F32)
    for pair in range(GROUPS // 2):
        two = slice(pair * 2 * LANES, (pair + 1) * 2 * LANES)
        for half in range(2):
            g = 2 * pair + half
            both = 0.5 * (d[g].astype(F32).reshape(CR, LANES) + turn_in(arrived, g, 0, buffer))
            half_sum[g] = both.reshape(CH, H, LANES)
            gmi[:, g * LANES : (g + 1) * LANES] = (both * mg[...].reshape(CR, LANES)).astype(BF)
        into = dot(mixer[...], gmi[:, two])
        for half in range(2):
            g = 2 * pair + half
            at = slice(g * LANES, (g + 1) * LANES)
            value = into[:, half * LANES : (half + 1) * LANES] * smooth_slope(pre_in[:, at]) * gain
            grad_inner[g] = value.reshape(MID, H, LANES).astype(BF)
            shifted[0:MR, at] = jnp.where(lane < 124, pltpu.roll(value, LANES - 4, 1), 0.0).astype(BF)
            shifted[MR : 2 * MR, at] = value.astype(BF)
            shifted[2 * MR : 3 * MR, at] = jnp.where(lane >= 4, pltpu.roll(value, 4, 1), 0.0).astype(BF)
            packed = jnp.where(lane // 8 == g, pltpu.roll(value, (8 * g - 124) % LANES, 1), packed)
    send_rows(grad_inner, down, up, MID)

    packed = packed + pltpu.roll(packed, 64, 1)
    edge_rows[0:MR] = jnp.where(lane % 8 >= 4, packed, 0.0).astype(BF)
    edge_rows[MR : 2 * MR] = jnp.zeros((MR, LANES), BF)
    edge_rows[2 * MR : 3 * MR] = jnp.where(lane % 8 < 4, packed, 0.0).astype(BF)
    lane_c = lanes_of(CR)
    rim_value = rim[...].astype(F32)
    rim_own = jnp.where(lane_c < 64, rim_value, 0.0).astype(BF)
    rim_far = jnp.where(lane_c >= 64, rim_value, 0.0).astype(BF)
    for k in range(2):
        rows = slice(k * CR, (k + 1) * CR)
        wide[:, rows] = dot(shifted[...], act[rows], NT) + dot(edge_rows[...], (rim_own, rim_far)[k], NT)
    mixwide[...] = dot(hidden[...], gmi[...], NT)

    h, col = iota((H, CR), 0), iota((H, CR), 1)
    same = jnp.where(col % 8 == h, 1.0, 0.0)[None]
    other = jnp.where(col % 8 == (h + 4) % 8, 1.0, 0.0)[None]
    far = jnp.where((col - jnp.where(col < CR // 2, 0, CR // 2)) % 4 == jnp.where(col < CR // 2, h, h - 4), 1.0, 0.0)[None]
    col, lane_s = iota((CR, LANES), 0), iota((CR, LANES), 1)

    def gather(keep, channel, side):
        return jnp.where(jnp.logical_and(keep, channel + 64 * side == lane_s), 1.0, 0.0).astype(BF)

    blocks = []
    sums = []
    for b in range(3):
        block = wide[b * MR : (b + 1) * MR]
        own = block[:, 0:CR].reshape(MID, H, CR)
        rest = block[:, CR : 2 * CR].reshape(MID, H, CR)
        sums.append([jnp.sum(own * same, axis=1), jnp.sum(own * other, axis=1), jnp.sum(rest * far, axis=1)])
    mixed = jnp.sum(mixwide[...].reshape(MID, H, CR) * same, axis=1)
    always = col >= 0
    own_low = col % 8 < 4
    rest_low = col < CR // 2
    rest_channel = jnp.where(rest_low, col, col - CR // 2) // 4
    for index in range(10):
        side = index % 2
        if index == 9:
            value = exact_dot(mixed, gather(always, col // 8, side))
        else:
            a, b = index // 3, index % 3
            if a == 1:
                value = exact_dot(sums[b][0], gather(always, col // 8, side))
            else:
                low = a == 0
                keep_own = own_low if low else jnp.logical_not(own_low)
                keep_rest = rest_low if low else jnp.logical_not(rest_low)
                value = exact_dot(sums[b][1], gather(keep_own, col // 8, side))
                value += exact_dot(sums[b][2], gather(keep_rest, rest_channel, side))
        blocks.append(value)
    for p in range(5):
        value = blocks[2 * p] + blocks[2 * p + 1]
        high = value.astype(BF).astype(F32)
        low = value - high
        for k in range(3):
            r = 3 * p + k
            rows = slice(k * H, (k + 1) * H)
            pieces[r, :, 0] = jnp.broadcast_to(high[rows][None], (COLS, H, LANES)).astype(BF)
            pieces[r, :, 1] = jnp.broadcast_to(low[rows][None], (COLS, H, LANES)).astype(BF)
    pieces[ROWS - 1, :, 0:2] = jnp.zeros((COLS, 2, H, LANES), BF)
    for r in range(ROWS):
        pieces[r, :, 2:5] = turned[r]


def spread_kernel(grad_inner, above, below, weights, main, edge, rhs):
    lane = lanes_of(CR)
    packed = jnp.zeros((CR, LANES), F32)
    for pair in range(GROUPS // 2):
        for half in range(2):
            g = 2 * pair + half
            at = slice(half * LANES, (half + 1) * LANES)
            rhs[0:MR, at] = grad_inner[g].astype(F32).reshape(MR, LANES).astype(BF)
            rhs[MR : MR + MR // 2, at] = above[g].astype(F32).reshape(MR // 2, LANES).astype(BF)
            rhs[MR + MR // 2 : 2 * MR, at] = below[g].astype(F32).reshape(MR // 2, LANES).astype(BF)
        product = dot(weights[...], rhs[...])
        for half in range(2):
            g = 2 * pair + half
            p = product[:, half * LANES : (half + 1) * LANES]
            left, mid, right = p[0:CR], p[CR : 2 * CR], p[2 * CR : 3 * CR]
            main[:, g * LANES : (g + 1) * LANES] = (
                mid
                + jnp.where(lane < 124, pltpu.roll(left, LANES - 4, 1), 0.0)
                + jnp.where(lane >= 4, pltpu.roll(right, 4, 1), 0.0)
            )
            out = jnp.where(lane >= 124, right, left)
            packed = jnp.where(lane // 8 == g, pltpu.roll(out, (8 * g - 124) % LANES, 1), packed)
    edge[...] = packed[0 : CR // 2] + pltpu.roll(packed[CR // 2 : CR], 64, 1)


def input_kernel(x, half_sum, main, from_left, from_right, grad_input):
    lane = lanes_of(CR)
    rim = merge_edges(from_left[...], from_right[...])
    rim = jnp.concatenate([rim, pltpu.roll(rim, 64, 1)], axis=0)
    for g in range(GROUPS):
        q = pltpu.roll(rim, (124 - 8 * g) % LANES, 1)
        total = main[:, g * LANES : (g + 1) * LANES]
        total = total + jnp.where(jnp.logical_or(lane < 4, lane >= 124), q, 0.0)
        slope = smooth_slope(x[g].astype(F32).reshape(CR, LANES))
        value = half_sum[g].reshape(CR, LANES) + total * slope
        grad_input[g] = value.reshape(CH, H, LANES).astype(BF)


def total_kernel(arrived, out):
    total = jnp.zeros((H, LANES), F32)
    for g in range(GROUPS):
        part = arrived[:, g].astype(F32)
        total += jnp.sum(part[:, 0] + part[:, 1], axis=0)
    out[...] = jnp.broadcast_to((total * (1.0 / (ROWS * H * COLS)))[None], (ROWS, H, LANES))


def symmetric_kernel(block, arrived, out, buffer):
    for g in range(GROUPS):
        value = 0.5 * (block[g].astype(F32).reshape(CR, LANES) + turn_in(arrived, g, 2, buffer))
        out[g] = value.reshape(CH, H, LANES).astype(BF)


def unpack_kernel(tiles, conv, mix):
    for p in range(5):
        value = tiles[3 * p : 3 * p + 3].reshape(3 * H, LANES)
        conv[2 * p] = value[:, 0:CH]
        if p < 4:
            conv[2 * p + 1] = value[:, 64 : 64 + CH]
        else:
            mix[...] = value[:, 64 : 64 + CH]


def both_ways(first, second, axis):
    count = lax.axis_size(axis)
    onward = [(i, (i + 1) % count) for i in range(count)]
    back = [(t, s) for s, t in onward]
    return lax.ppermute(first, axis, onward), lax.ppermute(second, axis, back)


def local(pair_map, cotangent, conv_weight, conv_gain, conv_bias, mix_weight, mix_gain, mix_bias):
    tile = (GROUPS, CH, H, LANES)
    everyone = ("row", "col")
    down, up = call(rows_kernel, [((GROUPS, CH // 2, H, LANES), BF)] * 2, (pair_map,), "rows")
    above, below = both_ways(down, up, "row")
    (d_pieces,) = call(mirror_kernel, [((ROWS, COLS, 3, H, LANES), BF)], (cotangent,), "turn_d")
    d_pieces = d_pieces.reshape(ROWS * COLS, 3, H, LANES)
    d_arrived = lax.all_to_all(d_pieces, everyone, 0, 0, tiled=True)
    d_arrived = d_arrived.reshape(ROWS, COLS, 3, H, LANES)

    taps = jnp.transpose(conv_weight, (2, 3, 0, 1)).reshape(9, MID, CH)
    wf, wb, mf, mbk, cg, cb, mg, mb = call(
        weights_kernel,
        [((3 * MR, 2 * CR), BF), ((3 * CR, 2 * MR), BF), ((CR, MR), BF), ((MR, CR), BF)]
        + [((MID, H, LANES), F32)] * 2
        + [((CH, H, LANES), F32)] * 2,
        (taps, mix_weight.T, conv_gain, conv_bias, mix_gain, mix_bias),
        "weights",
        smem=(2, 3, 4, 5),
    )
    act, edge = call(
        act_kernel, [((2 * CR, POS), BF), ((CR, LANES), BF)], (pair_map, above, below), "act"
    )
    from_left, from_right = both_ways(edge, edge, "col")
    pre, hidden, rim, block, b_turned = call(
        forward_kernel,
        [((MR, POS), F32), ((MR, POS), BF), ((CR, LANES), BF), (tile, BF), ((ROWS, COLS, 3, H, LANES), BF)],
        (pair_map, act, from_left, from_right, wf, mf, cg, cb, mg, mb),
        "forward",
    )
    grad_inner, g_down, g_up, half_sum, pieces = call(
        backward_kernel,
        [
            ((GROUPS, MID, H, LANES), BF),
            ((GROUPS, MID // 2, H, LANES), BF),
            ((GROUPS, MID // 2, H, LANES), BF),
            (tile, F32),
            ((ROWS, COLS, 5, H, LANES), BF),
        ],
        (cotangent, d_arrived, pre, hidden, act, rim, b_turned, mbk, cg, mg),
        "backward",
        scratch=[
            pltpu.VMEM((3, ROWS, H, LANES), F32),
            pltpu.VMEM((CR, POS), BF),
            pltpu.VMEM((3 * MR, POS), BF),
            pltpu.VMEM((3 * MR, LANES), BF),
            pltpu.VMEM((3 * MR, 2 * CR), F32),
            pltpu.VMEM((MR, CR), F32),
        ],
    )
    arrived = lax.all_to_all(pieces.reshape(ROWS * COLS, 5, H, LANES), everyone, 0, 0, tiled=True)
    arrived = arrived.reshape(ROWS, COLS, 5, H, LANES)
    g_above, g_below = both_ways(g_down, g_up, "row")
    main, g_edge = call(
        spread_kernel,
        [((CR, POS), F32), ((CR // 2, LANES), F32)],
        (grad_inner, g_above, g_below, wb),
        "spread",
        scratch=[pltpu.VMEM((2 * MR, 2 * LANES), BF)],
    )
    g_left, g_right = both_ways(g_edge, g_edge, "col")
    (grad_input,) = call(input_kernel, [(tile, BF)], (pair_map, half_sum, main, g_left, g_right), "grad_input")
    (sums,) = pl.pallas_call(
        total_kernel,
        name="total",
        grid=(1,),
        out_shape=[jax.ShapeDtypeStruct((ROWS, H, LANES), F32)],
        in_specs=[pl.BlockSpec((ROWS, COLS, 2, H, LANES), lambda i: (0, 0, 0, 0, 0))],
        out_specs=[pl.BlockSpec((ROWS, H, LANES), lambda i: (0, 0, 0))],
        cost_estimate=pl.CostEstimate(flops=500_000_000, bytes_accessed=600_000, transcendentals=0),
    )(arrived)
    sums = lax.all_to_all(sums, "row", 0, 0, tiled=True)
    (symmetric,) = call(
        symmetric_kernel, [(tile, BF)], (block, arrived), "symmetric",
        scratch=[pltpu.VMEM((3, ROWS, H, LANES), F32)],
    )
    conv, mix = call(
        unpack_kernel, [((9, MID, CH), F32), ((MID, CH), F32)], (sums,), "unpack", flops=100_000_000
    )
    grad_conv = jnp.transpose(conv.reshape(3, 3, MID, CH), (2, 3, 0, 1))
    return symmetric, grad_input, grad_conv, mix.T


def solution(mesh):
    field = P(None, None, "row", "col")
    return jax.shard_map(
        local,
        mesh=mesh,
        in_specs=(field, field, P(), P(), P(), P(), P(), P()),
        out_specs=(field, field, P(), P()),
        check_vma=False,
    )
```

```python
import functools

import jax
import jax.numpy as jnp
from jax import lax
from jax.experimental import pallas as pl
from jax.experimental.pallas import tpu as pltpu
from jax.sharding import PartitionSpec as P

BF = jnp.bfloat16
F32 = jnp.float32
CH, MID, GROUPS, H, LANES, ROWS, COLS = 48, 24, 8, 8, 128, 16, 8
POS = GROUPS * LANES
CR, MR = CH * H, MID * H
TANH_SCALE = 0.7978845608028654
CUBIC = 0.044715
NN = (((1,), (0,)), ((), ()))
NT = (((1,), (1,)), ((), ()))
TN = (((0,), (0,)), ((), ()))


def smooth(v):
    t = jnp.tanh(TANH_SCALE * (v + CUBIC * (v * v * v)))
    return 0.5 * v * (1.0 + t)


def smooth_slope(v):
    s = v * v
    t = jnp.tanh(TANH_SCALE * (v + CUBIC * (v * s)))
    return 0.5 * (1.0 + t) + (0.5 * v) * (1.0 - t * t) * (TANH_SCALE * (1.0 + (3.0 * CUBIC) * s))


def dot(a, b, dims=NN):
    return lax.dot_general(a, b, dims, preferred_element_type=F32)


def iota(shape, dim):
    return lax.broadcasted_iota(jnp.int32, shape, dim)


def identity(n):
    return jnp.where(iota((n, n), 0) == iota((n, n), 1), 1.0, 0.0).astype(BF)


def lanes_of(rows):
    return iota((rows, LANES), 1)


class Far:
    def __init__(self, sems):
        self.sems, self.used, self.open = sems, 0, []

    def start(self, source, target):
        copy = pltpu.make_async_copy(source, target, self.sems.at[self.used])
        self.used += 1
        copy.start()
        return copy

    def send(self, source, target):
        self.open.append(self.start(source, target))

    def finish(self):
        for copy in self.open:
            copy.wait()


def call(kernel, outs, args, name, smem=(), far=(), far_out=(), flops=4_000_000_000, scratch=(), copies=0, limit=16):
    specs = [
        pl.BlockSpec(memory_space=pltpu.SMEM if i in smem else pltpu.HBM if i in far else pltpu.VMEM)
        for i in range(len(args))
    ]
    scratch = list(scratch)
    if copies:
        scratch.append(pltpu.SemaphoreType.DMA((copies,)))
    return pl.pallas_call(
        kernel,
        name=name,
        out_shape=[
            pltpu.HBM(s, t) if i in far_out else jax.ShapeDtypeStruct(s, t)
            for i, (s, t) in enumerate(outs)
        ],
        in_specs=specs,
        out_specs=[
            pl.BlockSpec(memory_space=pltpu.HBM if i in far_out else pltpu.VMEM)
            for i in range(len(outs))
        ],
        scratch_shapes=scratch,
        compiler_params=pltpu.CompilerParams(vmem_limit_bytes=limit * 1024 * 1024),
        cost_estimate=pl.CostEstimate(flops=flops, bytes_accessed=1_000_000, transcendentals=0),
    )(
        *(
            pltpu.with_memory_space_constraint(v, pltpu.HBM) if i in far else v
            for i, v in enumerate(args)
        )
    )


def splat(values, count):
    return jnp.concatenate([jnp.full((H, LANES), values[o], F32) for o in range(count)], axis=0)


def pack_rows(field, count):
    pairs = field.reshape(count // 2, 2, H, LANES)
    even, odd = pairs[:, 0], pairs[:, 1]
    low = iota(even.shape, 1) < 4
    last = jnp.where(low, pltpu.roll(even, 4, 1), odd)
    first = jnp.where(low, even, pltpu.roll(odd, 4, 1))
    return last, first


def send_rows(source, down, up, count):
    at_end = (lax.axis_index("row") == ROWS - 1).astype(jnp.int32)
    at_start = (lax.axis_index("row") == 0).astype(jnp.int32)
    for g in range(GROUPS):
        before = g - at_end
        last, _ = pack_rows(source[jnp.maximum(before, 0)].astype(F32), count)
        down[g] = jnp.where(before >= 0, last, 0.0).astype(BF)
        after = g + at_start
        _, first = pack_rows(source[jnp.minimum(after, GROUPS - 1)].astype(F32), count)
        up[g] = jnp.where(after < GROUPS, first, 0.0).astype(BF)


def rows_kernel(x, down, up, held, sems):
    far = Far(sems)
    loads = [far.start(x.at[g], held.at[g]) for g in range(GROUPS)]
    for load in loads:
        load.wait()
    send_rows(held, down, up, CH)


def turn_out(value, eye, pieces, g, first_tile):
    turned = dot(eye, value, NT)
    for k in range(3):
        part = turned[:, k * LANES : (k + 1) * LANES].reshape(ROWS, H, LANES)
        pieces[:, g, first_tile + k] = part.astype(BF)


def turn_in(pieces, g, first_tile, buffer):
    parts = [
        pieces[r, g, first_tile : first_tile + 3].astype(F32).reshape(3 * H, LANES)
        for r in range(ROWS)
    ]
    lane = lanes_of(3 * H)
    for k in range(4):
        m = 1 << k
        high = (lane // (8 * m)) % 2 == 1
        for i in range(ROWS):
            if i & m:
                continue
            a, b = parts[i], parts[i | m]
            parts[i] = jnp.where(high, pltpu.roll(b, 8 * m, 1), a)
            parts[i | m] = jnp.where(high, b, pltpu.roll(a, LANES - 8 * m, 1))
    for i in range(ROWS):
        buffer[:, i] = parts[i].reshape(3, H, LANES)
    return buffer[...].reshape(CR, LANES)


def mirror_kernel(d, pieces, held, turned, sems):
    far = Far(sems)
    loads = [far.start(d.at[g], held.at[g]) for g in range(GROUPS)]
    eye = identity(LANES)
    for g in range(GROUPS):
        loads[g].wait()
        turn_out(held[g].astype(F32).reshape(CR, LANES).astype(BF), eye, turned, g, 0)
        far.send(turned.at[:, g], pieces.at[:, g])
    far.finish()


def weights_kernel(w, mix, a_out, b_far, mf_out, mb_far, b_out, mb_out, sems):
    far = Far(sems)

    def spread(n, own, width):
        col = iota((n, width), 1)
        half = (width - own) // 2
        rim = jnp.where(col < own + half, col - own, col - own - half) // 4
        return jnp.where(jnp.where(col < own, col // 8, rim) == iota((n, width), 0), 1.0, 0.0).astype(BF)

    def place(own, width):
        col, h = iota((H, width), 1), iota((H, width), 0)
        half = (width - own) // 2
        rim = jnp.where(col < own + half, (col - own) % 4 - 4, (col - own - half) % 4 + 8)
        return jnp.where(col < own, col % 8, rim) - h

    sf, st = spread(CH, CR, 2 * CR), spread(MID, MR, 2 * MR)
    pf, pt = place(CR, 2 * CR), place(MR, 2 * MR)
    for b in range(3):
        total_a = jnp.zeros((MID, H, 2 * CR), F32)
        total_b = jnp.zeros((CH, H, 2 * MR), F32)
        for a in range(3):
            tap = w[3 * a + b]
            mask = jnp.where(pf == 4 * (a - 1), 1.0, 0.0)
            total_a += dot(tap, sf)[:, None, :] * mask[None]
            mask = jnp.where(pt == -4 * (a - 1), 1.0, 0.0)
            total_b += dot(tap, st, TN)[:, None, :] * mask[None]
        a_out[b * MR : (b + 1) * MR] = total_a.reshape(MR, 2 * CR).astype(BF)
        b_out[b * CR : (b + 1) * CR] = total_b.reshape(CR, 2 * MR).astype(BF)
    mask = jnp.where(pf[:, :CR] == 0, 1.0, 0.0)
    mb_out[...] = (dot(mix[...], sf[:, :CR])[:, None, :] * mask[None]).reshape(MR, CR).astype(BF)
    mask = jnp.where(pt[:, :MR] == 0, 1.0, 0.0)
    mf_out[...] = (dot(mix[...], st[:, :MR], TN)[:, None, :] * mask[None]).reshape(CR, MR).astype(BF)
    far.send(b_out, b_far)
    far.send(mb_out, mb_far)
    far.finish()


def act_kernel(x, above, below, act, edge, act_far, held, sems):
    far = Far(sems)
    loads = [far.start(x.at[g], held.at[g]) for g in range(GROUPS)]
    lane = lanes_of(CR)
    packed = jnp.zeros((CR, LANES), F32)
    for g in range(GROUPS):
        loads[g].wait()
        own = smooth(held[g].astype(F32).reshape(CR, LANES))
        high = smooth(above[g].astype(F32).reshape(CR // 2, LANES))
        low = smooth(below[g].astype(F32).reshape(CR // 2, LANES))
        rim = jnp.concatenate([high, low], axis=0)
        at = slice(g * LANES, (g + 1) * LANES)
        act[0:CR, at] = own.astype(BF)
        act[CR : 2 * CR, at] = rim.astype(BF)
        packed = jnp.where(lane // 8 == g, pltpu.roll(own, (8 * g - 124) % LANES, 1), packed)
        packed = jnp.where(lane // 8 == 8 + g, pltpu.roll(rim, (8 * g - 60) % LANES, 1), packed)
    edge[...] = packed.astype(BF)
    far.send(act, act_far)
    far.finish()


def merge_edges(from_left, from_right):
    lane = lanes_of(from_left.shape[0])
    col = lax.axis_index("col")
    has_left = jnp.where(col > 0, 1.0, 0.0)
    has_right = jnp.where(col < COLS - 1, 1.0, 0.0)
    return jnp.where(
        lane % 8 < 4,
        pltpu.roll(from_right, LANES - 4, 1) * has_right,
        pltpu.roll(from_left, 4, 1) * has_left,
    )


def forward_kernel(
    x_far, act, from_left, from_right, weights, mixer, cg, cb, mg, mb,
    pre_far, hidden_far, rim_far, block_far, pieces_far,
    x, pre_out, hidden_out, rim_out, block_out, pieces, sems,
):
    far = Far(sems)
    load = far.start(x_far, x)
    eye = identity(LANES)
    rim = merge_edges(from_left[...].astype(F32), from_right[...].astype(F32)).astype(BF)
    rim_out[...] = rim
    far.send(rim_out, rim_far)
    outer = dot(weights[:, 0:CR], rim) + pltpu.roll(dot(weights[:, CR : 2 * CR], rim), 64, 1)
    lane = lanes_of(MR)
    outer = jnp.where(lane % 8 < 4, outer[2 * MR : 3 * MR], outer[0:MR])
    gain, shift = splat(cg, MID), splat(cb, MID)
    gain_out, shift_out = splat(mg, CH), splat(mb, CH)
    load.wait()
    for pair in range(GROUPS // 2):
        two = slice(pair * 2 * LANES, (pair + 1) * 2 * LANES)
        product = dot(weights[...], act[:, two])
        for half in range(2):
            g = 2 * pair + half
            p = product[:, half * LANES : (half + 1) * LANES]
            q = pltpu.roll(outer, (124 - 8 * g) % LANES, 1)
            inner = (
                p[MR : 2 * MR]
                + jnp.where(lane < 4, q, pltpu.roll(p[0:MR], 4, 1))
                + jnp.where(lane >= 124, q, pltpu.roll(p[2 * MR : 3 * MR], LANES - 4, 1))
            )
            pre = inner * gain + shift
            at = slice(g * LANES, (g + 1) * LANES)
            pre_out[:, at] = pre
            hidden_out[:, at] = smooth(pre).astype(BF)
        mixed = dot(mixer[...], hidden_out[:, two])
        for half in range(2):
            g = 2 * pair + half
            m = mixed[:, half * LANES : (half + 1) * LANES]
            value = x[g].astype(F32).reshape(CR, LANES) + m * gain_out
            value = (value + shift_out).astype(BF)
            block_out[g] = value.astype(F32).reshape(CH, H, LANES).astype(BF)
            turn_out(value, eye, pieces, g, 0)
            far.send(block_out.at[g], block_far.at[g])
            far.send(pieces.at[:, g], pieces_far.at[:, g])
    far.send(pre_out, pre_far)
    far.send(hidden_out, hidden_far)
    far.finish()


def split(value):
    high = value.astype(BF)
    return high, (value - high.astype(F32)).astype(BF)


def exact_dot(value, onehot):
    high, low = split(value)
    return dot(high, onehot) + dot(low, onehot)


def backward_kernel(
    d_far, arrived, pre_far, hidden_far, act_far, rim_far, turned_far, mixer_far, cg, mg,
    grad_inner_far, down_far, up_far, half_sum_far, pieces_far,
    d, pre_in, hidden, act, rim, turned, mixer, grad_inner, down, up, half_sum, pieces,
    buffer, gmi, shifted, edge_rows, wide, mixwide, sems,
):
    far = Far(sems)
    loads = [far.start(d_far, d), far.start(mixer_far, mixer), far.start(pre_far, pre_in)]
    late = [far.start(act_far, act), far.start(rim_far, rim), far.start(hidden_far, hidden), far.start(turned_far, turned)]
    lane = lanes_of(MR)
    gain, gain_out = splat(cg, MID), splat(mg, CH)
    for load in loads:
        load.wait()
    packed = jnp.zeros((MR, LANES), F32)
    for pair in range(GROUPS // 2):
        two = slice(pair * 2 * LANES, (pair + 1) * 2 * LANES)
        for half in range(2):
            g = 2 * pair + half
            both = 0.5 * (d[g].astype(F32).reshape(CR, LANES) + turn_in(arrived, g, 0, buffer))
            half_sum[g] = both.reshape(CH, H, LANES)
            gmi[:, g * LANES : (g + 1) * LANES] = (both * gain_out).astype(BF)
        into = dot(mixer[...], gmi[:, two])
        for half in range(2):
            g = 2 * pair + half
            at = slice(g * LANES, (g + 1) * LANES)
            value = into[:, half * LANES : (half + 1) * LANES] * smooth_slope(pre_in[:, at]) * gain
            grad_inner[g] = value.reshape(MID, H, LANES).astype(BF)
            shifted[0:MR, at] = jnp.where(lane < 124, pltpu.roll(value, LANES - 4, 1), 0.0).astype(BF)
            shifted[MR : 2 * MR, at] = value.astype(BF)
            shifted[2 * MR : 3 * MR, at] = jnp.where(lane >= 4, pltpu.roll(value, 4, 1), 0.0).astype(BF)
            packed = jnp.where(lane // 8 == g, pltpu.roll(value, (8 * g - 124) % LANES, 1), packed)
    send_rows(grad_inner, down, up, MID)
    far.send(down, down_far)
    far.send(up, up_far)
    far.send(grad_inner, grad_inner_far)
    far.send(half_sum, half_sum_far)
    for load in late:
        load.wait()

    packed = packed + pltpu.roll(packed, 64, 1)
    edge_rows[0:MR] = jnp.where(lane % 8 >= 4, packed, 0.0).astype(BF)
    edge_rows[MR : 2 * MR] = jnp.zeros((MR, LANES), BF)
    edge_rows[2 * MR : 3 * MR] = jnp.where(lane % 8 < 4, packed, 0.0).astype(BF)
    lane_c = lanes_of(CR)
    rim_value = rim[...].astype(F32)
    rim_own = jnp.where(lane_c < 64, rim_value, 0.0).astype(BF)
    rim_rest = jnp.where(lane_c >= 64, rim_value, 0.0).astype(BF)
    for k in range(2):
        rows = slice(k * CR, (k + 1) * CR)
        wide[:, rows] = dot(shifted[...], act[rows], NT) + dot(edge_rows[...], (rim_own, rim_rest)[k], NT)
    mixwide[...] = dot(hidden[...], gmi[...], NT)

    h, col = iota((H, CR), 0), iota((H, CR), 1)
    same = jnp.where(col % 8 == h, 1.0, 0.0)[None]
    other = jnp.where(col % 8 == (h + 4) % 8, 1.0, 0.0)[None]
    across = jnp.where((col - jnp.where(col < CR // 2, 0, CR // 2)) % 4 == jnp.where(col < CR // 2, h, h - 4), 1.0, 0.0)[None]
    col, lane_s = iota((CR, LANES), 0), iota((CR, LANES), 1)

    def gather(keep, channel, side):
        return jnp.where(jnp.logical_and(keep, channel + 64 * side == lane_s), 1.0, 0.0).astype(BF)

    blocks = []
    sums = []
    for b in range(3):
        block = wide[b * MR : (b + 1) * MR]
        own = block[:, 0:CR].reshape(MID, H, CR)
        rest = block[:, CR : 2 * CR].reshape(MID, H, CR)
        sums.append([jnp.sum(own * same, axis=1), jnp.sum(own * other, axis=1), jnp.sum(rest * across, axis=1)])
    mixed = jnp.sum(mixwide[...].reshape(MID, H, CR) * same, axis=1)
    always = col >= 0
    own_low = col % 8 < 4
    rest_low = col < CR // 2
    rest_channel = jnp.where(rest_low, col, col - CR // 2) // 4
    for index in range(10):
        side = index % 2
        if index == 9:
            value = exact_dot(mixed, gather(always, col // 8, side))
        else:
            a, b = index // 3, index % 3
            if a == 1:
                value = exact_dot(sums[b][0], gather(always, col // 8, side))
            else:
                low = a == 0
                keep_own = own_low if low else jnp.logical_not(own_low)
                keep_rest = rest_low if low else jnp.logical_not(rest_low)
                value = exact_dot(sums[b][1], gather(keep_own, col // 8, side))
                value += exact_dot(sums[b][2], gather(keep_rest, rest_channel, side))
        blocks.append(value)
    for p in range(5):
        value = blocks[2 * p] + blocks[2 * p + 1]
        high = value.astype(BF).astype(F32)
        low = value - high
        for k in range(3):
            r = 3 * p + k
            rows = slice(k * H, (k + 1) * H)
            pieces[r, :, 0] = jnp.broadcast_to(high[rows][None], (COLS, H, LANES)).astype(BF)
            pieces[r, :, 1] = jnp.broadcast_to(low[rows][None], (COLS, H, LANES)).astype(BF)
    pieces[ROWS - 1, :, 0:2] = jnp.zeros((COLS, 2, H, LANES), BF)
    for r in range(ROWS):
        pieces[r, :, 2:5] = turned[r]
    far.send(pieces, pieces_far)
    far.finish()


def spread_kernel(grad_inner_far, above, below, weights_far, after, main, edge, rhs, grad_inner, weights, sems):
    far = Far(sems)
    loads = [far.start(grad_inner_far, grad_inner), far.start(weights_far, weights)]
    for load in loads:
        load.wait()
    lane = lanes_of(CR)
    packed = jnp.zeros((CR, LANES), F32)
    for pair in range(GROUPS // 2):
        for half in range(2):
            g = 2 * pair + half
            at = slice(half * LANES, (half + 1) * LANES)
            rhs[0:MR, at] = grad_inner[g].astype(F32).reshape(MR, LANES).astype(BF)
            rhs[MR : MR + MR // 2, at] = above[g].astype(F32).reshape(MR // 2, LANES).astype(BF)
            rhs[MR + MR // 2 : 2 * MR, at] = below[g].astype(F32).reshape(MR // 2, LANES).astype(BF)
        product = dot(weights[...], rhs[...])
        for half in range(2):
            g = 2 * pair + half
            p = product[:, half * LANES : (half + 1) * LANES]
            left, mid, right = p[0:CR], p[CR : 2 * CR], p[2 * CR : 3 * CR]
            main[:, g * LANES : (g + 1) * LANES] = (
                mid
                + jnp.where(lane < 124, pltpu.roll(left, LANES - 4, 1), 0.0)
                + jnp.where(lane >= 4, pltpu.roll(right, 4, 1), 0.0)
            )
            out = jnp.where(lane >= 124, right, left)
            packed = jnp.where(lane // 8 == g, pltpu.roll(out, (8 * g - 124) % LANES, 1), packed)
    edge[...] = packed[0 : CR // 2] + pltpu.roll(packed[CR // 2 : CR], 64, 1)


def input_kernel(x_far, half_far, main, from_left, from_right, out_far, x, half_sum, grad_input, sems):
    far = Far(sems)
    loads = [(far.start(x_far.at[g], x.at[g]), far.start(half_far.at[g], half_sum.at[g])) for g in range(GROUPS)]
    lane = lanes_of(CR)
    rim = merge_edges(from_left[...], from_right[...])
    rim = jnp.concatenate([rim, pltpu.roll(rim, 64, 1)], axis=0)
    for g in range(GROUPS):
        for load in loads[g]:
            load.wait()
        q = pltpu.roll(rim, (124 - 8 * g) % LANES, 1)
        total = main[:, g * LANES : (g + 1) * LANES]
        total = total + jnp.where(jnp.logical_or(lane < 4, lane >= 124), q, 0.0)
        slope = smooth_slope(x[g].astype(F32).reshape(CR, LANES))
        value = half_sum[g].reshape(CR, LANES) + total * slope
        grad_input[g] = value.reshape(CH, H, LANES).astype(BF)
        far.send(grad_input.at[g], out_far.at[g])
    far.finish()


def total_kernel(arrived, out):
    total = jnp.zeros((H, LANES), F32)
    for g in range(COLS):
        part = arrived[:, g, 0:2].astype(F32)
        total += jnp.sum(part[:, 0] + part[:, 1], axis=0)
    out[...] = jnp.broadcast_to((total * (1.0 / (ROWS * H * COLS)))[None], (ROWS, H, LANES))


def symmetric_kernel(block_far, arrived_far, out_far, block, arrived, out, buffer, sems):
    far = Far(sems)
    loads = [
        (far.start(block_far.at[g], block.at[g]), far.start(arrived_far.at[:, g, 2:5], arrived.at[:, g]))
        for g in range(GROUPS)
    ]
    for g in range(GROUPS):
        for load in loads[g]:
            load.wait()
        value = 0.5 * (block[g].astype(F32).reshape(CR, LANES) + turn_in(arrived, g, 0, buffer))
        out[g] = value.reshape(CH, H, LANES).astype(BF)
        far.send(out.at[g], out_far.at[g])
    far.finish()


def unpack_kernel(tiles, conv, mix):
    for p in range(5):
        value = tiles[3 * p : 3 * p + 3].reshape(3 * H, LANES)
        conv[2 * p] = value[:, 0:CH]
        if p < 4:
            conv[2 * p + 1] = value[:, 64 : 64 + CH]
        else:
            mix[...] = value[:, 64 : 64 + CH]


def both_ways(first, second, axis):
    count = lax.axis_size(axis)
    onward = [(i, (i + 1) % count) for i in range(count)]
    back = [(t, s) for s, t in onward]
    return lax.ppermute(first, axis, onward), lax.ppermute(second, axis, back)


def local(pair_map, cotangent, conv_weight, conv_gain, conv_bias, mix_weight, mix_gain, mix_bias):
    tile = (GROUPS, CH, H, LANES)
    cut = (ROWS, COLS, 3, H, LANES)
    everyone = ("row", "col")
    vmem = pltpu.VMEM
    down, up = call(
        rows_kernel, [((GROUPS, CH // 2, H, LANES), BF)] * 2, (pair_map,), "rows",
        far=(0,), scratch=[vmem(tile, BF)], copies=GROUPS,
    )
    above, below = both_ways(down, up, "row")
    (d_pieces,) = call(
        mirror_kernel, [(cut, BF)], (cotangent,), "turn_d",
        far=(0,), far_out=(0,), scratch=[vmem(tile, BF), vmem(cut, BF)], copies=2 * GROUPS,
    )
    d_arrived = lax.all_to_all(d_pieces.reshape(ROWS * COLS, 3, H, LANES), everyone, 0, 0, tiled=True)
    d_arrived = d_arrived.reshape(cut)

    taps = jnp.transpose(conv_weight, (2, 3, 0, 1)).reshape(9, MID, CH)
    wf, wb, mf, mbk = call(
        weights_kernel,
        [((3 * MR, 2 * CR), BF), ((3 * CR, 2 * MR), BF), ((CR, MR), BF), ((MR, CR), BF)],
        (taps, mix_weight.T), "weights", far_out=(1, 3),
        scratch=[vmem((3 * CR, 2 * MR), BF), vmem((MR, CR), BF)], copies=2,
    )
    act, edge, act_far = call(
        act_kernel,
        [((2 * CR, POS), BF), ((CR, LANES), BF), ((2 * CR, POS), BF)],
        (pair_map, above, below), "act", far=(0,), far_out=(2,),
        scratch=[vmem(tile, BF)], copies=GROUPS + 1,
    )
    from_left, from_right = both_ways(edge, edge, "col")
    forward_outs = [((MR, POS), F32), ((MR, POS), BF), ((CR, LANES), BF), (tile, BF), (cut, BF)]
    pre, hidden, rim, block, b_turned = call(
        forward_kernel,
        forward_outs,
        (pair_map, act, from_left, from_right, wf, mf, conv_gain, conv_bias, mix_gain, mix_bias),
        "forward", smem=(6, 7, 8, 9), far=(0,), far_out=(0, 1, 2, 3, 4),
        scratch=[vmem(tile, BF)] + [vmem(s, t) for s, t in forward_outs], copies=2 * GROUPS + 4,
    )
    backward_outs = [
        ((GROUPS, MID, H, LANES), BF),
        ((GROUPS, MID // 2, H, LANES), BF),
        ((GROUPS, MID // 2, H, LANES), BF),
        (tile, F32),
        ((ROWS, COLS, 5, H, LANES), BF),
    ]
    grad_inner, g_down, g_up, half_sum, pieces = call(
        backward_kernel,
        backward_outs,
        (cotangent, d_arrived, pre, hidden, act_far, rim, b_turned, mbk, conv_gain, mix_gain),
        "backward", smem=(8, 9), far=(0, 2, 3, 4, 5, 6, 7), far_out=(0, 1, 2, 3, 4),
        scratch=[
            vmem(tile, BF), vmem((MR, POS), F32), vmem((MR, POS), BF), vmem((2 * CR, POS), BF),
            vmem((CR, LANES), BF), vmem(cut, BF), vmem((MR, CR), BF),
        ]
        + [vmem(s, t) for s, t in backward_outs]
        + [
            vmem((3, ROWS, H, LANES), F32),
            vmem((CR, POS), BF),
            vmem((3 * MR, POS), BF),
            vmem((3 * MR, LANES), BF),
            vmem((3 * MR, 2 * CR), F32),
            vmem((MR, CR), F32),
        ],
        copies=12, limit=32,
    )
    arrived = lax.all_to_all(pieces.reshape(ROWS * COLS, 5, H, LANES), everyone, 0, 0, tiled=True)
    arrived = arrived.reshape(ROWS, COLS, 5, H, LANES)
    g_above, g_below = both_ways(g_down, g_up, "row")
    (sums,) = call(
        total_kernel, [((ROWS, H, LANES), F32)], (arrived,), "total", flops=500_000_000
    )
    spread_sums = lax.all_to_all(sums, "row", 0, 0, tiled=True)
    main, g_edge = call(
        spread_kernel,
        [((CR, POS), F32), ((CR // 2, LANES), F32)],
        (grad_inner, g_above, g_below, wb, sums),
        "spread", far=(0, 3), copies=2,
        scratch=[vmem((2 * MR, 2 * LANES), BF), vmem((GROUPS, MID, H, LANES), BF), vmem((3 * CR, 2 * MR), BF)],
    )
    g_left, g_right = both_ways(g_edge, g_edge, "col")
    (grad_input,) = call(
        input_kernel, [(tile, BF)], (pair_map, half_sum, main, g_left, g_right), "grad_input",
        far=(0, 1), far_out=(0,), scratch=[vmem(tile, BF), vmem(tile, F32), vmem(tile, BF)], copies=3 * GROUPS,
    )
    (symmetric,) = call(
        symmetric_kernel, [(tile, BF)], (block, arrived), "symmetric", far=(0, 1), far_out=(0,),
        scratch=[vmem(tile, BF), vmem(cut, BF), vmem(tile, BF), vmem((3, ROWS, H, LANES), F32)], copies=3 * GROUPS,
    )
    conv, mix = call(
        unpack_kernel, [((9, MID, CH), F32), ((MID, CH), F32)], (spread_sums,), "unpack", flops=100_000_000
    )
    grad_conv = jnp.transpose(conv.reshape(3, 3, MID, CH), (2, 3, 0, 1))
    return symmetric, grad_input, grad_conv, mix.T


def solution(mesh):
    field = P(None, None, "row", "col")
    return jax.shard_map(
        local,
        mesh=mesh,
        in_specs=(field, field, P(), P(), P(), P(), P(), P()),
        out_specs=(field, field, P(), P()),
        check_vma=False,
    )
```

```python
import functools

import jax
import jax.numpy as jnp
from jax import lax
from jax.experimental import pallas as pl
from jax.experimental.pallas import tpu as pltpu
from jax.sharding import PartitionSpec as P

BF = jnp.bfloat16
F32 = jnp.float32
CH, MID, GROUPS, H, LANES, ROWS, COLS = 48, 24, 8, 8, 128, 16, 8
POS = GROUPS * LANES
CR, MR = CH * H, MID * H
TANH_SCALE = 0.7978845608028654
CUBIC = 0.044715
NN = (((1,), (0,)), ((), ()))
NT = (((1,), (1,)), ((), ()))
TN = (((0,), (0,)), ((), ()))


def smooth(v):
    t = jnp.tanh(TANH_SCALE * (v + CUBIC * (v * v * v)))
    return 0.5 * v * (1.0 + t)


def smooth_slope(v):
    s = v * v
    t = jnp.tanh(TANH_SCALE * (v + CUBIC * (v * s)))
    return 0.5 * (1.0 + t) + (0.5 * v) * (1.0 - t * t) * (TANH_SCALE * (1.0 + (3.0 * CUBIC) * s))


def dot(a, b, dims=NN):
    return lax.dot_general(a, b, dims, preferred_element_type=F32)


def iota(shape, dim):
    return lax.broadcasted_iota(jnp.int32, shape, dim)


def identity(n):
    return jnp.where(iota((n, n), 0) == iota((n, n), 1), 1.0, 0.0).astype(BF)


def lanes_of(rows):
    return iota((rows, LANES), 1)


class Far:
    def __init__(self, sems):
        self.sems, self.used, self.open = sems, 0, []

    def start(self, source, target):
        copy = pltpu.make_async_copy(source, target, self.sems.at[self.used])
        self.used += 1
        copy.start()
        return copy

    def send(self, source, target):
        self.open.append(self.start(source, target))

    def finish(self):
        for copy in self.open:
            copy.wait()


def call(kernel, outs, args, name, smem=(), far=(), far_out=(), flops=4_000_000_000, scratch=(), copies=0, limit=16, alias=None):
    specs = [
        pl.BlockSpec(memory_space=pltpu.SMEM if i in smem else pltpu.HBM if i in far else pltpu.VMEM)
        for i in range(len(args))
    ]
    scratch = list(scratch)
    if copies:
        scratch.append(pltpu.SemaphoreType.DMA((copies,)))
    return pl.pallas_call(
        kernel,
        name=name,
        out_shape=[
            pltpu.HBM(s, t) if i in far_out else jax.ShapeDtypeStruct(s, t)
            for i, (s, t) in enumerate(outs)
        ],
        in_specs=specs,
        out_specs=[
            pl.BlockSpec(memory_space=pltpu.HBM if i in far_out else pltpu.VMEM)
            for i in range(len(outs))
        ],
        scratch_shapes=scratch,
        input_output_aliases=alias or {},
        compiler_params=pltpu.CompilerParams(vmem_limit_bytes=limit * 1024 * 1024),
        cost_estimate=pl.CostEstimate(flops=flops, bytes_accessed=1_000_000, transcendentals=0),
    )(
        *(
            pltpu.with_memory_space_constraint(v, pltpu.HBM) if i in far else v
            for i, v in enumerate(args)
        )
    )


def splat(values, count):
    return jnp.concatenate([jnp.full((H, LANES), values[o], F32) for o in range(count)], axis=0)


def pack_rows(field, count):
    pairs = field.reshape(count // 2, 2, H, LANES)
    even, odd = pairs[:, 0], pairs[:, 1]
    low = iota(even.shape, 1) < 4
    last = jnp.where(low, pltpu.roll(even, 4, 1), odd)
    first = jnp.where(low, even, pltpu.roll(odd, 4, 1))
    return last, first


def send_rows(source, down, up, count):
    at_end = (lax.axis_index("row") == ROWS - 1).astype(jnp.int32)
    at_start = (lax.axis_index("row") == 0).astype(jnp.int32)
    for g in range(GROUPS):
        before = g - at_end
        last, _ = pack_rows(source[jnp.maximum(before, 0)].astype(F32), count)
        down[g] = jnp.where(before >= 0, last, 0.0).astype(BF)
        after = g + at_start
        _, first = pack_rows(source[jnp.minimum(after, GROUPS - 1)].astype(F32), count)
        up[g] = jnp.where(after < GROUPS, first, 0.0).astype(BF)


def rows_kernel(x, down, up, held, sems):
    far = Far(sems)
    loads = [far.start(x.at[g], held.at[g]) for g in range(GROUPS)]
    for load in loads:
        load.wait()
    send_rows(held, down, up, CH)


def turn_out(value, eye, pieces, g, first_tile):
    turned = dot(eye, value, NT)
    for k in range(3):
        part = turned[:, k * LANES : (k + 1) * LANES].reshape(ROWS, H, LANES)
        pieces[:, g, first_tile + k] = part.astype(BF)


def turn_in(pieces, g, first_tile, buffer):
    parts = [
        pieces[r, g, first_tile : first_tile + 3].astype(F32).reshape(3 * H, LANES)
        for r in range(ROWS)
    ]
    lane = lanes_of(3 * H)
    for k in range(4):
        m = 1 << k
        high = (lane // (8 * m)) % 2 == 1
        for i in range(ROWS):
            if i & m:
                continue
            a, b = parts[i], parts[i | m]
            parts[i] = jnp.where(high, pltpu.roll(b, 8 * m, 1), a)
            parts[i | m] = jnp.where(high, b, pltpu.roll(a, LANES - 8 * m, 1))
    for i in range(ROWS):
        buffer[:, i] = parts[i].reshape(3, H, LANES)
    return buffer[...].reshape(CR, LANES)


def mirror_kernel(d, pieces, turned, sems):
    far = Far(sems)
    eye = identity(LANES)
    for g in range(GROUPS):
        turn_out(d[g].astype(F32).reshape(CR, LANES).astype(BF), eye, turned, g, 0)
        far.send(turned.at[:, g], pieces.at[:, g])
    far.finish()


def weights_kernel(w, mix, a_out, b_far, mf_out, mb_far, a_far, mf_far, b_out, mb_out, sems):
    far = Far(sems)

    def spread(n, own, width):
        col = iota((n, width), 1)
        half = (width - own) // 2
        rim = jnp.where(col < own + half, col - own, col - own - half) // 4
        return jnp.where(jnp.where(col < own, col // 8, rim) == iota((n, width), 0), 1.0, 0.0).astype(BF)

    def place(own, width):
        col, h = iota((H, width), 1), iota((H, width), 0)
        half = (width - own) // 2
        rim = jnp.where(col < own + half, (col - own) % 4 - 4, (col - own - half) % 4 + 8)
        return jnp.where(col < own, col % 8, rim) - h

    sf, st = spread(CH, CR, 2 * CR), spread(MID, MR, 2 * MR)
    pf, pt = place(CR, 2 * CR), place(MR, 2 * MR)
    for b in range(3):
        total_a = jnp.zeros((MID, H, 2 * CR), F32)
        total_b = jnp.zeros((CH, H, 2 * MR), F32)
        for a in range(3):
            tap = w[3 * a + b]
            mask = jnp.where(pf == 4 * (a - 1), 1.0, 0.0)
            total_a += dot(tap, sf)[:, None, :] * mask[None]
            mask = jnp.where(pt == -4 * (a - 1), 1.0, 0.0)
            total_b += dot(tap, st, TN)[:, None, :] * mask[None]
        a_out[b * MR : (b + 1) * MR] = total_a.reshape(MR, 2 * CR).astype(BF)
        b_out[b * CR : (b + 1) * CR] = total_b.reshape(CR, 2 * MR).astype(BF)
    mask = jnp.where(pf[:, :CR] == 0, 1.0, 0.0)
    mb_out[...] = (dot(mix[...], sf[:, :CR])[:, None, :] * mask[None]).reshape(MR, CR).astype(BF)
    mask = jnp.where(pt[:, :MR] == 0, 1.0, 0.0)
    mf_out[...] = (dot(mix[...], st[:, :MR], TN)[:, None, :] * mask[None]).reshape(CR, MR).astype(BF)
    far.send(b_out, b_far)
    far.send(mb_out, mb_far)
    far.send(a_out, a_far)
    far.send(mf_out, mf_far)
    far.finish()


def act_kernel(x, above, below, act, edge, act_far, held, sems):
    far = Far(sems)
    loads = [far.start(x.at[g], held.at[g]) for g in range(GROUPS)]
    lane = lanes_of(CR)
    packed = jnp.zeros((CR, LANES), F32)
    for g in range(GROUPS):
        loads[g].wait()
        own = smooth(held[g].astype(F32).reshape(CR, LANES))
        high = smooth(above[g].astype(F32).reshape(CR // 2, LANES))
        low = smooth(below[g].astype(F32).reshape(CR // 2, LANES))
        rim = jnp.concatenate([high, low], axis=0)
        at = slice(g * LANES, (g + 1) * LANES)
        act[0:CR, at] = own.astype(BF)
        act[CR : 2 * CR, at] = rim.astype(BF)
        packed = jnp.where(lane // 8 == g, pltpu.roll(own, (8 * g - 124) % LANES, 1), packed)
        packed = jnp.where(lane // 8 == 8 + g, pltpu.roll(rim, (8 * g - 60) % LANES, 1), packed)
    edge[...] = packed.astype(BF)
    far.send(act, act_far)
    far.finish()


def merge_edges(from_left, from_right):
    lane = lanes_of(from_left.shape[0])
    col = lax.axis_index("col")
    has_left = jnp.where(col > 0, 1.0, 0.0)
    has_right = jnp.where(col < COLS - 1, 1.0, 0.0)
    return jnp.where(
        lane % 8 < 4,
        pltpu.roll(from_right, LANES - 4, 1) * has_right,
        pltpu.roll(from_left, 4, 1) * has_left,
    )


def at_edge(lane):
    return jnp.logical_or(lane < 4, lane >= 124)


def inside_kernel(
    x_far, act, weights, mixer, cg, cb, mg, mb,
    slope_far, hidden_far, block_far, pieces_far, edge_inner_far, edge_x_far,
    x, slope, hidden, block, pieces, edge_inner, edge_x, sems,
):
    far = Far(sems)
    load = far.start(x_far, x)
    eye = identity(LANES)
    lane, lane_c = lanes_of(MR), lanes_of(CR)
    gain, shift = splat(cg, MID), splat(cb, MID)
    gain_out, shift_out = splat(mg, CH), splat(mb, CH)
    packed, packed_x = jnp.zeros((MR, LANES), F32), jnp.zeros((CR, LANES), F32)
    load.wait()
    for pair in range(GROUPS // 2):
        two = slice(pair * 2 * LANES, (pair + 1) * 2 * LANES)
        product = dot(weights[...], act[:, two])
        for half in range(2):
            g = 2 * pair + half
            p = product[:, half * LANES : (half + 1) * LANES]
            inner = (
                p[MR : 2 * MR]
                + jnp.where(lane < 4, 0.0, pltpu.roll(p[0:MR], 4, 1))
                + jnp.where(lane >= 124, 0.0, pltpu.roll(p[2 * MR : 3 * MR], LANES - 4, 1))
            )
            packed = jnp.where(lane // 8 == g, pltpu.roll(inner, (8 * g - 124) % LANES, 1), packed)
            pre = inner * gain + shift
            at = slice(g * LANES, (g + 1) * LANES)
            slope[:, at] = smooth_slope(pre) * gain
            hidden[:, at] = smooth(pre).astype(BF)
        mixed = dot(mixer[...], hidden[:, two])
        for half in range(2):
            g = 2 * pair + half
            m = mixed[:, half * LANES : (half + 1) * LANES]
            own = x[g].astype(F32).reshape(CR, LANES)
            packed_x = jnp.where(lane_c // 8 == g, pltpu.roll(own, (8 * g - 124) % LANES, 1), packed_x)
            value = (own + m * gain_out + shift_out).astype(BF)
            block[g] = value.astype(F32).reshape(CH, H, LANES).astype(BF)
            turn_out(value, eye, pieces, g, 0)
            far.send(block.at[g], block_far.at[g])
            far.send(pieces.at[:, g], pieces_far.at[:, g, 2:5])
    edge_inner[...] = packed
    edge_x[...] = packed_x
    far.send(slope, slope_far)
    far.send(hidden, hidden_far)
    far.send(edge_inner, edge_inner_far)
    far.send(edge_x, edge_x_far)
    far.finish()


def split(value):
    high = value.astype(BF)
    return high, (value - high.astype(F32)).astype(BF)


def exact_dot(value, onehot):
    high, low = split(value)
    return dot(high, onehot) + dot(low, onehot)


def inner_kernel(
    d_far, arrived, slope_far, hidden_far, edge_inner_far, edge_x_far, from_left, from_right,
    weights_far, mixer_far, back_far, pieces_in, cg, cb, mg, mb,
    grad_inner_far, down, up, half_sum_far, pieces_far, edge_block_far, gmi, shifted, edge_rows, hidden_out, rim_out,
    d, slope, hidden, edge_inner, edge_x, weights, mixer, back, grad_inner, half_sum, ends, edge_block, buffer, sems,
):
    far = Far(sems)
    first = [far.start(weights_far.at[0:MR], weights.at[0:MR])]
    first.append(far.start(weights_far.at[2 * MR : 3 * MR], weights.at[MR : 2 * MR]))
    first += [far.start(edge_inner_far, edge_inner), far.start(edge_x_far, edge_x), far.start(mixer_far, mixer)]
    later = [far.start(d_far, d), far.start(slope_far, slope), far.start(back_far, back), far.start(hidden_far, hidden)]
    tails = [
        far.start(pieces_in.at[r, :, 2:5], ends.at[i]) for i, r in enumerate((0, ROWS - 1))
    ]
    lane, lane_c = lanes_of(MR), lanes_of(CR)
    gain, shift = splat(cg, MID), splat(cb, MID)
    gain_out, shift_out = splat(mg, CH), splat(mb, CH)
    rim = merge_edges(from_left[...].astype(F32), from_right[...].astype(F32)).astype(BF)
    rim_out[...] = rim
    for load in first:
        load.wait()
    outer = dot(weights[:, 0:CR], rim) + pltpu.roll(dot(weights[:, CR : 2 * CR], rim), 64, 1)
    outer = jnp.where(lane % 8 < 4, outer[MR : 2 * MR], outer[0:MR])
    pre = (edge_inner[...] + outer) * gain + shift
    slope_edge = smooth_slope(pre) * gain
    hidden_edge = smooth(pre).astype(BF)
    mixed = dot(mixer[...], hidden_edge)
    value = (edge_x[...] + mixed * gain_out + shift_out).astype(BF)
    edge_block[...] = value.astype(F32)
    far.send(edge_block, edge_block_far)
    hidden_edge = hidden_edge.astype(F32)
    turned = dot(identity(LANES), value, NT)
    for load in tails:
        load.wait()
    low = iota((COLS, H, LANES), 1) < 4
    for k in range(3):
        part = pltpu.roll(turned[0 : COLS * H, k * LANES : (k + 1) * LANES].reshape(COLS, H, LANES), 4, 1)
        ends[0, :, k] = jnp.where(low, part, ends[0, :, k].astype(F32)).astype(BF)
        ends[1, :, k] = jnp.where(low, ends[1, :, k].astype(F32), part).astype(BF)
    for i, r in enumerate((0, ROWS - 1)):
        far.send(ends.at[i], pieces_far.at[r, :, 2:5])

    for load in later:
        load.wait()
    packed = jnp.zeros((MR, LANES), F32)
    for pair in range(GROUPS // 2):
        two = slice(pair * 2 * LANES, (pair + 1) * 2 * LANES)
        for half in range(2):
            g = 2 * pair + half
            both = 0.5 * (d[g].astype(F32).reshape(CR, LANES) + turn_in(arrived, g, 0, buffer))
            half_sum[g] = both.reshape(CH, H, LANES)
            gmi[:, g * LANES : (g + 1) * LANES] = (both * gain_out).astype(BF)
        into = dot(back[...], gmi[:, two])
        for half in range(2):
            g = 2 * pair + half
            at = slice(g * LANES, (g + 1) * LANES)
            turn = (124 - 8 * g) % LANES
            here = jnp.where(at_edge(lane), pltpu.roll(slope_edge, turn, 1), slope[:, at])
            value = into[:, half * LANES : (half + 1) * LANES] * here
            grad_inner[g] = value.reshape(MID, H, LANES).astype(BF)
            shifted[0:MR, at] = jnp.where(lane < 124, pltpu.roll(value, LANES - 4, 1), 0.0).astype(BF)
            shifted[MR : 2 * MR, at] = value.astype(BF)
            shifted[2 * MR : 3 * MR, at] = jnp.where(lane >= 4, pltpu.roll(value, 4, 1), 0.0).astype(BF)
            packed = jnp.where(lane // 8 == g, pltpu.roll(value, (8 * g - 124) % LANES, 1), packed)
            here = jnp.where(at_edge(lane), pltpu.roll(hidden_edge, turn, 1), hidden[:, at].astype(F32))
            hidden_out[:, at] = here.astype(BF)
    far.send(grad_inner, grad_inner_far)
    far.send(half_sum, half_sum_far)
    send_rows(grad_inner, down, up, MID)
    packed = packed + pltpu.roll(packed, 64, 1)
    edge_rows[0:MR] = jnp.where(lane % 8 >= 4, packed, 0.0).astype(BF)
    edge_rows[MR : 2 * MR] = jnp.zeros((MR, LANES), BF)
    edge_rows[2 * MR : 3 * MR] = jnp.where(lane % 8 < 4, packed, 0.0).astype(BF)
    far.finish()


def sums_kernel(
    act_far, gmi, shifted, edge_rows, hidden, rim, pieces_in, pieces_far, act, sums_out, wide, mixwide, sems
):
    far = Far(sems)
    loads = [far.start(act_far.at[k * CR : (k + 1) * CR], act.at[k * CR : (k + 1) * CR]) for k in range(2)]
    lane_c = lanes_of(CR)
    rim_value = rim[...].astype(F32)
    rim_own = jnp.where(lane_c < 64, rim_value, 0.0).astype(BF)
    rim_rest = jnp.where(lane_c >= 64, rim_value, 0.0).astype(BF)
    mixwide[...] = dot(hidden[...], gmi[...], NT)
    for k in range(2):
        rows = slice(k * CR, (k + 1) * CR)
        loads[k].wait()
        wide[:, rows] = dot(shifted[...], act[rows], NT) + dot(edge_rows[...], (rim_own, rim_rest)[k], NT)

    h, col = iota((H, CR), 0), iota((H, CR), 1)
    same = jnp.where(col % 8 == h, 1.0, 0.0)[None]
    other = jnp.where(col % 8 == (h + 4) % 8, 1.0, 0.0)[None]
    low_half = col < CR // 2
    across = jnp.where(jnp.where(low_half, col, col - CR // 2) % 4 == jnp.where(low_half, h, h - 4), 1.0, 0.0)[None]
    col, lane_s = iota((CR, LANES), 0), iota((CR, LANES), 1)

    def gather(keep, channel, side):
        return jnp.where(jnp.logical_and(keep, channel + 64 * side == lane_s), 1.0, 0.0).astype(BF)

    blocks = []
    sums = []
    for b in range(3):
        block = wide[b * MR : (b + 1) * MR]
        own = block[:, 0:CR].reshape(MID, H, CR)
        rest = block[:, CR : 2 * CR].reshape(MID, H, CR)
        sums.append([jnp.sum(own * same, axis=1), jnp.sum(own * other, axis=1), jnp.sum(rest * across, axis=1)])
    mixed = jnp.sum(mixwide[...].reshape(MID, H, CR) * same, axis=1)
    always = col >= 0
    own_low = col % 8 < 4
    rest_low = col < CR // 2
    rest_channel = jnp.where(rest_low, col, col - CR // 2) // 4
    for index in range(10):
        side = index % 2
        if index == 9:
            value = exact_dot(mixed, gather(always, col // 8, side))
        else:
            a, b = index // 3, index % 3
            if a == 1:
                value = exact_dot(sums[b][0], gather(always, col // 8, side))
            else:
                low = a == 0
                keep_own = own_low if low else jnp.logical_not(own_low)
                keep_rest = rest_low if low else jnp.logical_not(rest_low)
                value = exact_dot(sums[b][1], gather(keep_own, col // 8, side))
                value += exact_dot(sums[b][2], gather(keep_rest, rest_channel, side))
        blocks.append(value)
    for p in range(5):
        value = blocks[2 * p] + blocks[2 * p + 1]
        high = value.astype(BF).astype(F32)
        low = value - high
        for k in range(3):
            r = 3 * p + k
            rows = slice(k * H, (k + 1) * H)
            sums_out[r, :, 0] = jnp.broadcast_to(high[rows][None], (COLS, H, LANES)).astype(BF)
            sums_out[r, :, 1] = jnp.broadcast_to(low[rows][None], (COLS, H, LANES)).astype(BF)
    sums_out[ROWS - 1] = jnp.zeros((COLS, 2, H, LANES), BF)
    far.send(sums_out, pieces_far.at[:, :, 0:2])
    far.finish()


def spread_kernel(grad_inner_far, above, below, weights_far, main, edge, rhs, grad_inner, weights, sems):
    far = Far(sems)
    loads = [far.start(grad_inner_far, grad_inner), far.start(weights_far, weights)]
    for load in loads:
        load.wait()
    lane = lanes_of(CR)
    packed = jnp.zeros((CR, LANES), F32)
    for pair in range(GROUPS // 2):
        for half in range(2):
            g = 2 * pair + half
            at = slice(half * LANES, (half + 1) * LANES)
            rhs[0:MR, at] = grad_inner[g].astype(F32).reshape(MR, LANES).astype(BF)
            rhs[MR : MR + MR // 2, at] = above[g].astype(F32).reshape(MR // 2, LANES).astype(BF)
            rhs[MR + MR // 2 : 2 * MR, at] = below[g].astype(F32).reshape(MR // 2, LANES).astype(BF)
        product = dot(weights[...], rhs[...])
        for half in range(2):
            g = 2 * pair + half
            p = product[:, half * LANES : (half + 1) * LANES]
            left, mid, right = p[0:CR], p[CR : 2 * CR], p[2 * CR : 3 * CR]
            main[:, g * LANES : (g + 1) * LANES] = (
                mid
                + jnp.where(lane < 124, pltpu.roll(left, LANES - 4, 1), 0.0)
                + jnp.where(lane >= 4, pltpu.roll(right, 4, 1), 0.0)
            )
            out = jnp.where(lane >= 124, right, left)
            packed = jnp.where(lane // 8 == g, pltpu.roll(out, (8 * g - 124) % LANES, 1), packed)
    edge[...] = packed[0 : CR // 2] + pltpu.roll(packed[CR // 2 : CR], 64, 1)


def input_kernel(x_far, half_far, main, from_left, from_right, out_far, x, half_sum, grad_input, sems):
    far = Far(sems)
    loads = [(far.start(x_far.at[g], x.at[g]), far.start(half_far.at[g], half_sum.at[g])) for g in range(GROUPS)]
    lane = lanes_of(CR)
    rim = merge_edges(from_left[...], from_right[...])
    rim = jnp.concatenate([rim, pltpu.roll(rim, 64, 1)], axis=0)
    for g in range(GROUPS):
        for load in loads[g]:
            load.wait()
        q = pltpu.roll(rim, (124 - 8 * g) % LANES, 1)
        total = main[:, g * LANES : (g + 1) * LANES]
        total = total + jnp.where(jnp.logical_or(lane < 4, lane >= 124), q, 0.0)
        slope = smooth_slope(x[g].astype(F32).reshape(CR, LANES))
        value = half_sum[g].reshape(CR, LANES) + total * slope
        grad_input[g] = value.reshape(CH, H, LANES).astype(BF)
        far.send(grad_input.at[g], out_far.at[g])
    far.finish()


def total_kernel(arrived, out):
    total = jnp.zeros((H, LANES), F32)
    for g in range(COLS):
        part = arrived[:, g, 0:2].astype(F32)
        total += jnp.sum(part[:, 0] + part[:, 1], axis=0)
    out[...] = jnp.broadcast_to((total * (1.0 / (ROWS * H * COLS)))[None], (ROWS, H, LANES))


def symmetric_kernel(block_far, edge_far, arrived_far, out_far, edge, block, arrived, out, buffer, sems):
    far = Far(sems)
    loads = [
        (far.start(block_far.at[g], block.at[g]), far.start(arrived_far.at[:, g, 2:5], arrived.at[:, g]))
        for g in range(GROUPS)
    ]
    far.start(edge_far, edge).wait()
    lane = lanes_of(CR)
    for g in range(GROUPS):
        for load in loads[g]:
            load.wait()
        own = jnp.where(
            at_edge(lane), pltpu.roll(edge[...], (124 - 8 * g) % LANES, 1), block[g].astype(F32).reshape(CR, LANES)
        )
        value = 0.5 * (own + turn_in(arrived, g, 0, buffer))
        out[g] = value.reshape(CH, H, LANES).astype(BF)
        far.send(out.at[g], out_far.at[g])
    far.finish()


def unpack_kernel(tiles, conv, mix):
    for p in range(5):
        value = tiles[3 * p : 3 * p + 3].reshape(3 * H, LANES)
        conv[2 * p] = value[:, 0:CH]
        if p < 4:
            conv[2 * p + 1] = value[:, 64 : 64 + CH]
        else:
            mix[...] = value[:, 64 : 64 + CH]


def both_ways(first, second, axis):
    count = lax.axis_size(axis)
    onward = [(i, (i + 1) % count) for i in range(count)]
    back = [(t, s) for s, t in onward]
    return lax.ppermute(first, axis, onward), lax.ppermute(second, axis, back)


def local(pair_map, cotangent, conv_weight, conv_gain, conv_bias, mix_weight, mix_gain, mix_bias):
    tile = (GROUPS, CH, H, LANES)
    cut = (ROWS, COLS, 3, H, LANES)
    everyone = ("row", "col")
    vmem = pltpu.VMEM
    down, up = call(
        rows_kernel, [((GROUPS, CH // 2, H, LANES), BF)] * 2, (pair_map,), "rows",
        far=(0,), scratch=[vmem(tile, BF)], copies=GROUPS,
    )
    above, below = both_ways(down, up, "row")
    (d_pieces,) = call(
        mirror_kernel, [(cut, BF)], (cotangent,), "turn_d",
        far_out=(0,), scratch=[vmem(cut, BF)], copies=GROUPS,
    )
    d_arrived = lax.all_to_all(d_pieces.reshape(ROWS * COLS, 3, H, LANES), everyone, 0, 0, tiled=True)
    d_arrived = d_arrived.reshape(cut)

    taps = jnp.transpose(conv_weight, (2, 3, 0, 1)).reshape(9, MID, CH)
    wf, wb, mf, mbk, wf_far, mf_far = call(
        weights_kernel,
        [((3 * MR, 2 * CR), BF), ((3 * CR, 2 * MR), BF), ((CR, MR), BF), ((MR, CR), BF)]
        + [((3 * MR, 2 * CR), BF), ((CR, MR), BF)],
        (taps, mix_weight.T), "weights", far_out=(1, 3, 4, 5),
        scratch=[vmem((3 * CR, 2 * MR), BF), vmem((MR, CR), BF)], copies=4,
    )
    act, edge, act_far = call(
        act_kernel,
        [((2 * CR, POS), BF), ((CR, LANES), BF), ((2 * CR, POS), BF)],
        (pair_map, above, below), "act", far=(0,), far_out=(2,),
        scratch=[vmem(tile, BF)], copies=GROUPS + 1,
    )
    from_left, from_right = both_ways(edge, edge, "col")
    five = (ROWS, COLS, 5, H, LANES)
    slope, hidden, block, pieces, edge_inner, edge_x = call(
        inside_kernel,
        [((MR, POS), F32), ((MR, POS), BF), (tile, BF), (five, BF), ((MR, LANES), F32), ((CR, LANES), F32)],
        (pair_map, act, wf, mf, conv_gain, conv_bias, mix_gain, mix_bias),
        "inside", smem=(4, 5, 6, 7), far=(0,), far_out=(0, 1, 2, 3, 4, 5),
        scratch=[
            vmem(tile, BF), vmem((MR, POS), F32), vmem((MR, POS), BF), vmem(tile, BF), vmem(cut, BF),
            vmem((MR, LANES), F32), vmem((CR, LANES), F32),
        ],
        copies=2 * GROUPS + 5,
    )
    grad_inner, g_down, g_up, half_sum, pieces, edge_block, gmi, shifted, edge_rows, hidden, rim = call(
        inner_kernel,
        [
            ((GROUPS, MID, H, LANES), BF),
            ((GROUPS, MID // 2, H, LANES), BF),
            ((GROUPS, MID // 2, H, LANES), BF),
            (tile, F32),
            (five, BF),
            ((CR, LANES), F32),
            ((CR, POS), BF),
            ((3 * MR, POS), BF),
            ((3 * MR, LANES), BF),
            ((MR, POS), BF),
            ((CR, LANES), BF),
        ],
        (
            cotangent, d_arrived, slope, hidden, edge_inner, edge_x, from_left, from_right,
            wf_far, mf_far, mbk, pieces, conv_gain, conv_bias, mix_gain, mix_bias,
        ),
        "inner", smem=(12, 13, 14, 15), far=(0, 2, 3, 4, 5, 8, 9, 10, 11), far_out=(0, 3, 4, 5), alias={11: 4},
        scratch=[
            vmem(tile, BF), vmem((MR, POS), F32), vmem((MR, POS), BF), vmem((MR, LANES), F32), vmem((CR, LANES), F32),
            vmem((2 * MR, 2 * CR), BF), vmem((CR, MR), BF), vmem((MR, CR), BF),
            vmem((GROUPS, MID, H, LANES), BF), vmem(tile, F32), vmem((2, COLS, 3, H, LANES), BF),
            vmem((CR, LANES), F32), vmem((3, ROWS, H, LANES), F32),
        ],
        copies=16,
    )
    g_above, g_below = both_ways(g_down, g_up, "row")
    (pieces,) = call(
        sums_kernel, [(five, BF)], (act_far, gmi, shifted, edge_rows, hidden, rim, pieces), "sums",
        far=(0, 6), far_out=(0,), alias={6: 0},
        scratch=[
            vmem((2 * CR, POS), BF), vmem((ROWS, COLS, 2, H, LANES), BF),
            vmem((3 * MR, 2 * CR), F32), vmem((MR, CR), F32),
        ],
        copies=3,
    )
    pieces, g_above, g_below = lax.optimization_barrier((pieces, g_above, g_below))
    arrived = lax.all_to_all(pieces.reshape(ROWS * COLS, 5, H, LANES), everyone, 0, 0, tiled=True)
    arrived = arrived.reshape(five)
    (sums,) = call(
        total_kernel, [((ROWS, H, LANES), F32)], (arrived,), "total", flops=500_000_000
    )
    spread_sums = lax.all_to_all(sums, "row", 0, 0, tiled=True)
    main, g_edge = call(
        spread_kernel,
        [((CR, POS), F32), ((CR // 2, LANES), F32)],
        (grad_inner, g_above, g_below, wb),
        "spread", far=(0, 3), copies=2,
        scratch=[vmem((2 * MR, 2 * LANES), BF), vmem((GROUPS, MID, H, LANES), BF), vmem((3 * CR, 2 * MR), BF)],
    )
    g_left, g_right = both_ways(g_edge, g_edge, "col")
    g_left, g_right, _ = lax.optimization_barrier((g_left, g_right, sums))
    (grad_input,) = call(
        input_kernel, [(tile, BF)], (pair_map, half_sum, main, g_left, g_right), "grad_input",
        far=(0, 1), far_out=(0,), scratch=[vmem(tile, BF), vmem(tile, F32), vmem(tile, BF)], copies=3 * GROUPS,
    )
    (symmetric,) = call(
        symmetric_kernel, [(tile, BF)], (block, edge_block, arrived), "symmetric", far=(0, 1, 2), far_out=(0,),
        scratch=[
            vmem((CR, LANES), F32), vmem(tile, BF), vmem(cut, BF), vmem(tile, BF), vmem((3, ROWS, H, LANES), F32),
        ],
        copies=3 * GROUPS + 1,
    )
    conv, mix = call(
        unpack_kernel, [((9, MID, CH), F32), ((MID, CH), F32)], (spread_sums,), "unpack", flops=100_000_000
    )
    grad_conv = jnp.transpose(conv.reshape(3, 3, MID, CH), (2, 3, 0, 1))
    return symmetric, grad_input, grad_conv, mix.T


def solution(mesh):
    field = P(None, None, "row", "col")
    return jax.shard_map(
        local,
        mesh=mesh,
        in_specs=(field, field, P(), P(), P(), P(), P(), P()),
        out_specs=(field, field, P(), P()),
        check_vma=False,
    )
```

```python
import functools

import jax
import jax.numpy as jnp
from jax import lax
from jax.experimental import pallas as pl
from jax.experimental.pallas import tpu as pltpu
from jax.sharding import PartitionSpec as P

BF = jnp.bfloat16
F32 = jnp.float32
CH, MID, GROUPS, H, LANES, ROWS, COLS = 48, 24, 8, 8, 128, 16, 8
POS = GROUPS * LANES
CR, MR = CH * H, MID * H
TANH_SCALE = 0.7978845608028654
CUBIC = 0.044715
NN = (((1,), (0,)), ((), ()))
NT = (((1,), (1,)), ((), ()))
TN = (((0,), (0,)), ((), ()))


def smooth(v):
    t = jnp.tanh(TANH_SCALE * (v + CUBIC * (v * v * v)))
    return 0.5 * v * (1.0 + t)


def smooth_slope(v):
    s = v * v
    t = jnp.tanh(TANH_SCALE * (v + CUBIC * (v * s)))
    return 0.5 * (1.0 + t) + (0.5 * v) * (1.0 - t * t) * (TANH_SCALE * (1.0 + (3.0 * CUBIC) * s))


def dot(a, b, dims=NN):
    return lax.dot_general(a, b, dims, preferred_element_type=F32)


def iota(shape, dim):
    return lax.broadcasted_iota(jnp.int32, shape, dim)


def identity(n):
    return jnp.where(iota((n, n), 0) == iota((n, n), 1), 1.0, 0.0).astype(BF)


def lanes_of(rows):
    return iota((rows, LANES), 1)


class Far:
    def __init__(self, sems):
        self.sems, self.used, self.open = sems, 0, []

    def start(self, source, target):
        copy = pltpu.make_async_copy(source, target, self.sems.at[self.used])
        self.used += 1
        copy.start()
        return copy

    def send(self, source, target):
        self.open.append(self.start(source, target))

    def finish(self):
        for copy in self.open:
            copy.wait()


def call(kernel, outs, args, name, smem=(), far=(), far_out=(), flops=4_000_000_000, scratch=(), copies=0, limit=16, alias=None):
    specs = [
        pl.BlockSpec(memory_space=pltpu.SMEM if i in smem else pltpu.HBM if i in far else pltpu.VMEM)
        for i in range(len(args))
    ]
    scratch = list(scratch)
    if copies:
        scratch.append(pltpu.SemaphoreType.DMA((copies,)))
    return pl.pallas_call(
        kernel,
        name=name,
        out_shape=[
            pltpu.HBM(s, t) if i in far_out else jax.ShapeDtypeStruct(s, t)
            for i, (s, t) in enumerate(outs)
        ],
        in_specs=specs,
        out_specs=[
            pl.BlockSpec(memory_space=pltpu.HBM if i in far_out else pltpu.VMEM)
            for i in range(len(outs))
        ],
        scratch_shapes=scratch,
        input_output_aliases=alias or {},
        compiler_params=pltpu.CompilerParams(vmem_limit_bytes=limit * 1024 * 1024),
        cost_estimate=pl.CostEstimate(flops=flops, bytes_accessed=1_000_000, transcendentals=0),
    )(
        *(
            pltpu.with_memory_space_constraint(v, pltpu.HBM) if i in far else v
            for i, v in enumerate(args)
        )
    )


def splat(values, count):
    return jnp.concatenate([jnp.full((H, LANES), values[o], F32) for o in range(count)], axis=0)


def pack_rows(field, count):
    pairs = field.reshape(count // 2, 2, H, LANES)
    even, odd = pairs[:, 0], pairs[:, 1]
    low = iota(even.shape, 1) < 4
    last = jnp.where(low, pltpu.roll(even, 4, 1), odd)
    first = jnp.where(low, even, pltpu.roll(odd, 4, 1))
    return last, first


def send_rows(source, down, up, count):
    at_end = (lax.axis_index("row") == ROWS - 1).astype(jnp.int32)
    at_start = (lax.axis_index("row") == 0).astype(jnp.int32)
    for g in range(GROUPS):
        before = g - at_end
        last, _ = pack_rows(source[jnp.maximum(before, 0)].astype(F32), count)
        down[g] = jnp.where(before >= 0, last, 0.0).astype(BF)
        after = g + at_start
        _, first = pack_rows(source[jnp.minimum(after, GROUPS - 1)].astype(F32), count)
        up[g] = jnp.where(after < GROUPS, first, 0.0).astype(BF)


def rows_kernel(x, down, up, held, sems):
    far = Far(sems)
    loads = [far.start(x.at[g], held.at[g]) for g in range(GROUPS)]
    for load in loads:
        load.wait()
    send_rows(held, down, up, CH)


def swap_blocks(parts):
    lane = iota(parts[0].shape, 1)
    parts = list(parts)
    for k in range(4):
        m = 1 << k
        high = (lane // (8 * m)) % 2 == 1
        for i in range(ROWS):
            if i & m:
                continue
            a, b = parts[i], parts[i | m]
            parts[i] = jnp.where(high, pltpu.roll(b, 8 * m, 1), a)
            parts[i | m] = jnp.where(high, b, pltpu.roll(a, LANES - 8 * m, 1))
    return parts


def turn(tiles):
    return tiles.reshape(LANES, LANES).T.reshape(ROWS, H, LANES)


def swap_in(pieces, g, buffer):
    parts = swap_blocks([pieces[r, g : g + 2].reshape(6 * H, LANES) for r in range(ROWS)])
    for i in range(ROWS):
        value = parts[i].reshape(2, 3, H, LANES)
        for n in range(2):
            for k in range(3):
                buffer[n, k * ROWS + i] = value[n, k]


def swap_out(block, pieces, g):
    parts = swap_blocks(
        [
            jnp.concatenate([block[g + n, k * ROWS + i] for n in range(2) for k in range(3)], axis=0)
            for i in range(ROWS)
        ]
    )
    for r in range(ROWS):
        pieces[r, g : g + 2] = parts[r].reshape(2, 3, H, LANES)


def mirror_kernel(d, pieces, turned, sems):
    far = Far(sems)
    for g in range(GROUPS):
        for k in range(3):
            turned[:, g, k] = turn(d[g, k * ROWS : (k + 1) * ROWS])
        far.send(turned.at[:, g], pieces.at[:, g])
    far.finish()


def spread_channels(n, own, width):
    col = iota((n, width), 1)
    half = (width - own) // 2
    rim = jnp.where(col < own + half, col - own, col - own - half) // 4
    return jnp.where(jnp.where(col < own, col // 8, rim) == iota((n, width), 0), 1.0, 0.0).astype(BF)


def row_distance(own, width):
    col, h = iota((H, width), 1), iota((H, width), 0)
    half = (width - own) // 2
    rim = jnp.where(col < own + half, (col - own) % 4 - 4, (col - own - half) % 4 + 8)
    return jnp.where(col < own, col % 8, rim) - h


def weights_kernel(w, mix, a_out, mf_out, a_far, mf_far, mb_far, mb_out, sems):
    far = Far(sems)
    sf, st = spread_channels(CH, CR, 2 * CR), spread_channels(MID, MR, MR)
    pf, pt = row_distance(CR, 2 * CR), row_distance(MR, MR)
    masks = [jnp.where(pf == 4 * (a - 1), 1.0, 0.0)[None] for a in range(3)]
    for b in range(3):
        total = jnp.zeros((MID, H, 2 * CR), F32)
        for a in range(3):
            total += dot(w[3 * a + b], sf)[:, None, :] * masks[a]
        a_out[b * MR : (b + 1) * MR] = total.reshape(MR, 2 * CR).astype(BF)
    far.send(a_out, a_far)
    mask = jnp.where(pf[:, :CR] == 0, 1.0, 0.0)
    mb_out[...] = (dot(mix[...], sf[:, :CR])[:, None, :] * mask[None]).reshape(MR, CR).astype(BF)
    far.send(mb_out, mb_far)
    mask = jnp.where(pt == 0, 1.0, 0.0)
    mf_out[...] = (dot(mix[...], st, TN)[:, None, :] * mask[None]).reshape(CR, MR).astype(BF)
    far.send(mf_out, mf_far)
    far.finish()


def back_weights(w, out):
    st, pt = spread_channels(MID, MR, 2 * MR), row_distance(MR, 2 * MR)
    masks = [jnp.where(pt == -4 * (a - 1), 1.0, 0.0)[None] for a in range(3)]
    for b in range(3):
        total = jnp.zeros((CH, H, 2 * MR), F32)
        for a in range(3):
            total += dot(w[3 * a + b], st, TN)[:, None, :] * masks[a]
        out[b * CR : (b + 1) * CR] = total.reshape(CR, 2 * MR).astype(BF)


def act_kernel(x, above, below, act, edge, act_far, sems):
    far = Far(sems)
    lane = lanes_of(CR)
    packed = jnp.zeros((CR, LANES), F32)
    for g in range(GROUPS):
        own = smooth(x[g].astype(F32).reshape(CR, LANES))
        high = smooth(above[g].astype(F32).reshape(CR // 2, LANES))
        low = smooth(below[g].astype(F32).reshape(CR // 2, LANES))
        rim = jnp.concatenate([high, low], axis=0)
        at = slice(g * LANES, (g + 1) * LANES)
        act[0:CR, at] = own.astype(BF)
        act[CR : 2 * CR, at] = rim.astype(BF)
        far.send(act.at[:, at], act_far.at[:, at])
        packed = jnp.where(lane // 8 == g, pltpu.roll(own, (8 * g - 124) % LANES, 1), packed)
        packed = jnp.where(lane // 8 == 8 + g, pltpu.roll(rim, (8 * g - 60) % LANES, 1), packed)
    edge[...] = packed.astype(BF)
    far.finish()


def merge_edges(from_left, from_right):
    lane = lanes_of(from_left.shape[0])
    col = lax.axis_index("col")
    has_left = jnp.where(col > 0, 1.0, 0.0)
    has_right = jnp.where(col < COLS - 1, 1.0, 0.0)
    return jnp.where(
        lane % 8 < 4,
        pltpu.roll(from_right, LANES - 4, 1) * has_right,
        pltpu.roll(from_left, 4, 1) * has_left,
    )


def at_edge(lane):
    return jnp.logical_or(lane < 4, lane >= 124)


def inside_kernel(
    x, act, weights, mixer, cg, cb, mg, mb,
    slope_far, hidden_far, block_far, pieces_far, edge_inner_far, edge_x_far,
    slope, hidden, block, pieces, edge_inner, edge_x, sems,
):
    far = Far(sems)
    lane, lane_c = lanes_of(MR), lanes_of(CR)
    gain, shift = splat(cg, MID), splat(cb, MID)
    gain_out, shift_out = splat(mg, CH), splat(mb, CH)
    packed, packed_x = jnp.zeros((MR, LANES), F32), jnp.zeros((CR, LANES), F32)
    for pair in range(GROUPS // 2):
        two = slice(pair * 2 * LANES, (pair + 1) * 2 * LANES)
        product = dot(weights[...], act[:, two])
        for half in range(2):
            g = 2 * pair + half
            p = product[:, half * LANES : (half + 1) * LANES]
            inner = (
                p[MR : 2 * MR]
                + jnp.where(lane < 4, 0.0, pltpu.roll(p[0:MR], 4, 1))
                + jnp.where(lane >= 124, 0.0, pltpu.roll(p[2 * MR : 3 * MR], LANES - 4, 1))
            )
            packed = jnp.where(lane // 8 == g, pltpu.roll(inner, (8 * g - 124) % LANES, 1), packed)
            pre = inner * gain + shift
            at = slice(g * LANES, (g + 1) * LANES)
            slope[:, at] = smooth_slope(pre) * gain
            hidden[:, at] = smooth(pre).astype(BF)
        far.send(slope.at[:, two], slope_far.at[:, two])
        far.send(hidden.at[:, two], hidden_far.at[:, two])
        mixed = dot(mixer[...], hidden[:, two])
        for half in range(2):
            g = 2 * pair + half
            m = mixed[:, half * LANES : (half + 1) * LANES]
            own = x[g].astype(F32).reshape(CR, LANES)
            packed_x = jnp.where(lane_c // 8 == g, pltpu.roll(own, (8 * g - 124) % LANES, 1), packed_x)
            value = (own + m * gain_out + shift_out).astype(BF)
            block[g] = value.astype(F32).reshape(CH, H, LANES).astype(BF)
        g = 2 * pair
        far.send(block.at[g : g + 2], block_far.at[g : g + 2])
        swap_out(block, pieces, g)
        far.send(pieces.at[:, g : g + 2], pieces_far.at[:, g : g + 2, 2:5])
    edge_inner[...] = packed
    edge_x[...] = packed_x
    far.send(edge_inner, edge_inner_far)
    far.send(edge_x, edge_x_far)
    far.finish()


def split(value):
    high = value.astype(BF)
    return high, (value - high.astype(F32)).astype(BF)


def exact_dot(value, onehot):
    high, low = split(value)
    return dot(high, onehot) + dot(low, onehot)


def inner_kernel(
    d_far, arrived, slope_far, hidden_far, edge_inner_far, edge_x_far, from_left, from_right,
    weights_far, mixer_far, back_far, pieces_in, cg, cb, mg, mb,
    grad_inner_far, down, up, half_sum_far, pieces_far, edge_block_far, gmi, shifted, edge_rows, hidden_out, rim_out,
    d, slope, hidden, edge_inner, edge_x, weights, mixer, back, grad_inner, half_sum, ends, edge_block, buffer, sems,
):
    far = Far(sems)
    first = [far.start(weights_far.at[0:MR], weights.at[0:MR])]
    first.append(far.start(weights_far.at[2 * MR : 3 * MR], weights.at[MR : 2 * MR]))
    first += [far.start(edge_inner_far, edge_inner), far.start(edge_x_far, edge_x), far.start(mixer_far, mixer)]
    later = [far.start(d_far, d), far.start(slope_far, slope), far.start(back_far, back), far.start(hidden_far, hidden)]
    tails = [
        far.start(pieces_in.at[r, :, 2:5], ends.at[i]) for i, r in enumerate((0, ROWS - 1))
    ]
    lane, lane_c = lanes_of(MR), lanes_of(CR)
    gain, shift = splat(cg, MID), splat(cb, MID)
    gain_out, shift_out = splat(mg, CH), splat(mb, CH)
    rim = merge_edges(from_left[...].astype(F32), from_right[...].astype(F32)).astype(BF)
    rim_out[...] = rim
    for load in first:
        load.wait()
    outer = dot(weights[:, 0:CR], rim) + pltpu.roll(dot(weights[:, CR : 2 * CR], rim), 64, 1)
    outer = jnp.where(lane % 8 < 4, outer[MR : 2 * MR], outer[0:MR])
    pre = (edge_inner[...] + outer) * gain + shift
    slope_edge = smooth_slope(pre) * gain
    hidden_edge = smooth(pre).astype(BF)
    mixed = dot(mixer[...], hidden_edge)
    value = (edge_x[...] + mixed * gain_out + shift_out).astype(BF)
    edge_block[...] = value.astype(F32)
    far.send(edge_block, edge_block_far)
    hidden_edge = hidden_edge.astype(F32)
    parts = value.astype(F32).reshape(3, ROWS, H, LANES)
    parts = swap_blocks([parts[:, i].reshape(3 * H, LANES) for i in range(ROWS)])
    for load in tails:
        load.wait()
    low = iota((3, H, LANES), 2) % 8 < 4
    for g in range(GROUPS):
        lower = pltpu.roll(parts[g], LANES - 4, 1).reshape(3, H, LANES)
        upper = pltpu.roll(parts[g], 4, 1).reshape(3, H, LANES)
        ends[0, g] = jnp.where(low, lower, ends[0, g].astype(F32)).astype(BF)
        ends[1, g] = jnp.where(low, ends[1, g].astype(F32), upper).astype(BF)
    for i, r in enumerate((0, ROWS - 1)):
        far.send(ends.at[i], pieces_far.at[r, :, 2:5])

    for load in later:
        load.wait()
    packed = jnp.zeros((MR, LANES), F32)
    for pair in range(GROUPS // 2):
        two = slice(pair * 2 * LANES, (pair + 1) * 2 * LANES)
        swap_in(arrived, 2 * pair, buffer)
        for half in range(2):
            g = 2 * pair + half
            both = 0.5 * (d[g].astype(F32) + buffer[half].astype(F32)).reshape(CR, LANES)
            half_sum[g] = both.reshape(CH, H, LANES)
            gmi[:, g * LANES : (g + 1) * LANES] = (both * gain_out).astype(BF)
        into = dot(back[...], gmi[:, two])
        for half in range(2):
            g = 2 * pair + half
            at = slice(g * LANES, (g + 1) * LANES)
            turn = (124 - 8 * g) % LANES
            here = jnp.where(at_edge(lane), pltpu.roll(slope_edge, turn, 1), slope[:, at])
            value = into[:, half * LANES : (half + 1) * LANES] * here
            grad_inner[g] = value.reshape(MID, H, LANES).astype(BF)
            shifted[0:MR, at] = jnp.where(lane < 124, pltpu.roll(value, LANES - 4, 1), 0.0).astype(BF)
            shifted[MR : 2 * MR, at] = value.astype(BF)
            shifted[2 * MR : 3 * MR, at] = jnp.where(lane >= 4, pltpu.roll(value, 4, 1), 0.0).astype(BF)
            packed = jnp.where(lane // 8 == g, pltpu.roll(value, (8 * g - 124) % LANES, 1), packed)
            here = jnp.where(at_edge(lane), pltpu.roll(hidden_edge, turn, 1), hidden[:, at].astype(F32))
            hidden_out[:, at] = here.astype(BF)
    far.send(grad_inner, grad_inner_far)
    far.send(half_sum, half_sum_far)
    send_rows(grad_inner, down, up, MID)
    packed = packed + pltpu.roll(packed, 64, 1)
    edge_rows[0:MR] = jnp.where(lane % 8 >= 4, packed, 0.0).astype(BF)
    edge_rows[MR : 2 * MR] = jnp.zeros((MR, LANES), BF)
    edge_rows[2 * MR : 3 * MR] = jnp.where(lane % 8 < 4, packed, 0.0).astype(BF)
    far.finish()


def sums_kernel(
    act_far, gmi, shifted, edge_rows, hidden, rim, pieces_in, pieces_far, act, sums_out, wide, mixwide, sems
):
    far = Far(sems)
    loads = [far.start(act_far.at[k * CR : (k + 1) * CR], act.at[k * CR : (k + 1) * CR]) for k in range(2)]
    lane_c = lanes_of(CR)
    rim_value = rim[...].astype(F32)
    rim_own = jnp.where(lane_c < 64, rim_value, 0.0).astype(BF)
    rim_rest = jnp.where(lane_c >= 64, rim_value, 0.0).astype(BF)
    mixwide[...] = dot(hidden[...], gmi[...], NT)
    for k in range(2):
        rows = slice(k * CR, (k + 1) * CR)
        loads[k].wait()
        wide[:, rows] = dot(shifted[...], act[rows], NT) + dot(edge_rows[...], (rim_own, rim_rest)[k], NT)

    h, col = iota((H, CR), 0), iota((H, CR), 1)
    same = jnp.where(col % 8 == h, 1.0, 0.0)[None]
    other = jnp.where(col % 8 == (h + 4) % 8, 1.0, 0.0)[None]
    low_half = col < CR // 2
    across = jnp.where(jnp.where(low_half, col, col - CR // 2) % 4 == jnp.where(low_half, h, h - 4), 1.0, 0.0)[None]
    col, lane_s = iota((CR, LANES), 0), iota((CR, LANES), 1)

    def gather(keep, channel, side):
        return jnp.where(jnp.logical_and(keep, channel + 64 * side == lane_s), 1.0, 0.0).astype(BF)

    blocks = []
    sums = []
    for b in range(3):
        block = wide[b * MR : (b + 1) * MR]
        own = block[:, 0:CR].reshape(MID, H, CR)
        rest = block[:, CR : 2 * CR].reshape(MID, H, CR)
        sums.append([jnp.sum(own * same, axis=1), jnp.sum(own * other, axis=1), jnp.sum(rest * across, axis=1)])
    mixed = jnp.sum(mixwide[...].reshape(MID, H, CR) * same, axis=1)
    always = col >= 0
    own_low = col % 8 < 4
    rest_low = col < CR // 2
    rest_channel = jnp.where(rest_low, col, col - CR // 2) // 4
    for index in range(10):
        side = index % 2
        if index == 9:
            value = exact_dot(mixed, gather(always, col // 8, side))
        else:
            a, b = index // 3, index % 3
            if a == 1:
                value = exact_dot(sums[b][0], gather(always, col // 8, side))
            else:
                low = a == 0
                keep_own = own_low if low else jnp.logical_not(own_low)
                keep_rest = rest_low if low else jnp.logical_not(rest_low)
                value = exact_dot(sums[b][1], gather(keep_own, col // 8, side))
                value += exact_dot(sums[b][2], gather(keep_rest, rest_channel, side))
        blocks.append(value)
    for p in range(5):
        value = blocks[2 * p] + blocks[2 * p + 1]
        high = value.astype(BF).astype(F32)
        low = value - high
        for k in range(3):
            r = 3 * p + k
            rows = slice(k * H, (k + 1) * H)
            sums_out[r, :, 0] = jnp.broadcast_to(high[rows][None], (COLS, H, LANES)).astype(BF)
            sums_out[r, :, 1] = jnp.broadcast_to(low[rows][None], (COLS, H, LANES)).astype(BF)
    sums_out[ROWS - 1] = jnp.zeros((COLS, 2, H, LANES), BF)
    far.send(sums_out, pieces_far.at[:, :, 0:2])
    far.finish()


def spread_kernel(
    grad_inner_far, above, below, w, half_far, x_far, block_far, edge_block_far,
    edge, out_far, edge_value_far, edge_slope_far, block_out_far,
    weights, rhs, grad_inner, half_sum, x, block, edge_block, out, edge_value, edge_slope, sems,
):
    far = Far(sems)
    first = far.start(grad_inner_far, grad_inner)
    loads = [far.start(half_far, half_sum), far.start(x_far, x)]
    last = [far.start(block_far, block), far.start(edge_block_far, edge_block)]
    back_weights(w, weights)
    first.wait()
    lane = lanes_of(CR)
    packed, packed_value, packed_slope = (jnp.zeros((CR, LANES), F32) for _ in range(3))
    for load in loads:
        load.wait()
    for pair in range(GROUPS // 2):
        for half in range(2):
            g = 2 * pair + half
            at = slice(half * LANES, (half + 1) * LANES)
            rhs[0:MR, at] = grad_inner[g].astype(F32).reshape(MR, LANES).astype(BF)
            rhs[MR : MR + MR // 2, at] = above[g].astype(F32).reshape(MR // 2, LANES).astype(BF)
            rhs[MR + MR // 2 : 2 * MR, at] = below[g].astype(F32).reshape(MR // 2, LANES).astype(BF)
        product = dot(weights[...], rhs[...])
        for half in range(2):
            g = 2 * pair + half
            p = product[:, half * LANES : (half + 1) * LANES]
            left, mid, right = p[0:CR], p[CR : 2 * CR], p[2 * CR : 3 * CR]
            total = (
                mid
                + jnp.where(lane < 124, pltpu.roll(left, LANES - 4, 1), 0.0)
                + jnp.where(lane >= 4, pltpu.roll(right, 4, 1), 0.0)
            )
            slope = smooth_slope(x[g].astype(F32).reshape(CR, LANES))
            value = half_sum[g].reshape(CR, LANES) + total * slope
            out[g] = value.reshape(CH, H, LANES).astype(BF)
            far.send(out.at[g], out_far.at[g])
            here = lane // 8 == g
            turn_by = (8 * g - 124) % LANES
            packed = jnp.where(here, pltpu.roll(jnp.where(lane >= 124, right, left), turn_by, 1), packed)
            packed_value = jnp.where(here, pltpu.roll(value, turn_by, 1), packed_value)
            packed_slope = jnp.where(here, pltpu.roll(slope, turn_by, 1), packed_slope)
    edge[...] = packed[0 : CR // 2] + pltpu.roll(packed[CR // 2 : CR], 64, 1)
    edge_value[...] = packed_value
    edge_slope[...] = packed_slope
    far.send(edge_value, edge_value_far)
    far.send(edge_slope, edge_slope_far)
    for load in last:
        load.wait()
    for g in range(GROUPS):
        moved = pltpu.roll(edge_block[...], (124 - 8 * g) % LANES, 1)
        value = jnp.where(at_edge(lane), moved, block[g].astype(F32).reshape(CR, LANES))
        block[g] = value.reshape(CH, H, LANES).astype(BF)
        far.send(block.at[g], block_out_far.at[g])
    far.finish()


def input_kernel(value_far, edge_value_far, edge_slope_far, from_left, from_right, out_far, value, out, edge_value, edge_slope, sems):
    far = Far(sems)
    first = [far.start(edge_value_far, edge_value), far.start(edge_slope_far, edge_slope)]
    loads = [far.start(value_far.at[g], value.at[g]) for g in range(GROUPS)]
    lane = lanes_of(CR)
    rim = merge_edges(from_left[...], from_right[...])
    rim = jnp.concatenate([rim, pltpu.roll(rim, 64, 1)], axis=0)
    for load in first:
        load.wait()
    rim = edge_value[...] + rim * edge_slope[...]
    for g in range(GROUPS):
        loads[g].wait()
        moved = pltpu.roll(rim, (124 - 8 * g) % LANES, 1)
        total = jnp.where(at_edge(lane), moved, value[g].astype(F32).reshape(CR, LANES))
        out[g] = total.reshape(CH, H, LANES).astype(BF)
        far.send(out.at[g], out_far.at[g])
    far.finish()


def total_kernel(arrived, out):
    total = jnp.zeros((H, LANES), F32)
    for g in range(COLS):
        part = arrived[:, g, 0:2].astype(F32)
        total += jnp.sum(part[:, 0] + part[:, 1], axis=0)
    out[...] = jnp.broadcast_to((total * (1.0 / (ROWS * H * COLS)))[None], (ROWS, H, LANES))


def symmetric_kernel(block_far, arrived_far, out_far, block, arrived, out, sems):
    far = Far(sems)
    loads = [
        (far.start(block_far.at[g], block.at[g]), far.start(arrived_far.at[:, g, 2:5], arrived.at[:, g]))
        for g in range(GROUPS)
    ]
    for g in range(GROUPS):
        for load in loads[g]:
            load.wait()
        for k in range(3):
            at = slice(k * ROWS, (k + 1) * ROWS)
            value = 0.5 * (block[g, at].astype(F32) + turn(arrived[:, g, k]).astype(F32))
            out[g, at] = value.astype(BF)
        far.send(out.at[g], out_far.at[g])
    far.finish()


def unpack_kernel(tiles, conv, mix):
    for p in range(5):
        value = tiles[3 * p : 3 * p + 3].reshape(3 * H, LANES)
        conv[2 * p] = value[:, 0:CH]
        if p < 4:
            conv[2 * p + 1] = value[:, 64 : 64 + CH]
        else:
            mix[...] = value[:, 64 : 64 + CH]


def both_ways(first, second, axis):
    count = lax.axis_size(axis)
    onward = [(i, (i + 1) % count) for i in range(count)]
    back = [(t, s) for s, t in onward]
    return lax.ppermute(first, axis, onward), lax.ppermute(second, axis, back)


def local(pair_map, cotangent, conv_weight, conv_gain, conv_bias, mix_weight, mix_gain, mix_bias):
    tile = (GROUPS, CH, H, LANES)
    cut = (ROWS, COLS, 3, H, LANES)
    everyone = ("row", "col")
    vmem = pltpu.VMEM
    down, up = call(
        rows_kernel, [((GROUPS, CH // 2, H, LANES), BF)] * 2, (pair_map,), "rows",
        far=(0,), scratch=[vmem(tile, BF)], copies=GROUPS,
    )
    above, below = both_ways(down, up, "row")
    (d_pieces,) = call(
        mirror_kernel, [(cut, BF)], (cotangent,), "turn_d",
        far_out=(0,), scratch=[vmem(cut, BF)], copies=GROUPS,
    )
    d_arrived = lax.all_to_all(d_pieces.reshape(ROWS * COLS, 3, H, LANES), everyone, 0, 0, tiled=True)
    d_arrived = d_arrived.reshape(cut)

    taps = jnp.transpose(conv_weight, (2, 3, 0, 1)).reshape(9, MID, CH)
    wf, mf, wf_far, mf_far, mbk = call(
        weights_kernel,
        [((3 * MR, 2 * CR), BF), ((CR, MR), BF)] * 2 + [((MR, CR), BF)],
        (taps, mix_weight.T), "weights", far_out=(2, 3, 4), scratch=[vmem((MR, CR), BF)], copies=3,
    )
    act, edge, act_far = call(
        act_kernel,
        [((2 * CR, POS), BF), ((CR, LANES), BF), ((2 * CR, POS), BF)],
        (pair_map, above, below), "act", far_out=(2,), copies=GROUPS,
    )
    from_left, from_right = both_ways(edge, edge, "col")
    five = (ROWS, COLS, 5, H, LANES)
    slope, hidden, block, pieces, edge_inner, edge_x = call(
        inside_kernel,
        [((MR, POS), F32), ((MR, POS), BF), (tile, BF), (five, BF), ((MR, LANES), F32), ((CR, LANES), F32)],
        (pair_map, act, wf, mf, conv_gain, conv_bias, mix_gain, mix_bias),
        "inside", smem=(4, 5, 6, 7), far_out=(0, 1, 2, 3, 4, 5),
        scratch=[
            vmem((MR, POS), F32), vmem((MR, POS), BF), vmem(tile, BF), vmem(cut, BF),
            vmem((MR, LANES), F32), vmem((CR, LANES), F32),
        ],
        copies=2 * GROUPS + 2,
    )
    grad_inner, g_down, g_up, half_sum, pieces, edge_block, gmi, shifted, edge_rows, hidden, rim = call(
        inner_kernel,
        [
            ((GROUPS, MID, H, LANES), BF),
            ((GROUPS, MID // 2, H, LANES), BF),
            ((GROUPS, MID // 2, H, LANES), BF),
            (tile, F32),
            (five, BF),
            ((CR, LANES), F32),
            ((CR, POS), BF),
            ((3 * MR, POS), BF),
            ((3 * MR, LANES), BF),
            ((MR, POS), BF),
            ((CR, LANES), BF),
        ],
        (
            cotangent, d_arrived, slope, hidden, edge_inner, edge_x, from_left, from_right,
            wf_far, mf_far, mbk, pieces, conv_gain, conv_bias, mix_gain, mix_bias,
        ),
        "inner", smem=(12, 13, 14, 15), far=(0, 2, 3, 4, 5, 8, 9, 10, 11), far_out=(0, 3, 4, 5), alias={11: 4},
        scratch=[
            vmem(tile, BF), vmem((MR, POS), F32), vmem((MR, POS), BF), vmem((MR, LANES), F32), vmem((CR, LANES), F32),
            vmem((2 * MR, 2 * CR), BF), vmem((CR, MR), BF), vmem((MR, CR), BF),
            vmem((GROUPS, MID, H, LANES), BF), vmem(tile, F32), vmem((2, COLS, 3, H, LANES), BF),
            vmem((CR, LANES), F32), vmem((2, CH, H, LANES), BF),
        ],
        copies=16,
    )
    g_above, g_below = both_ways(g_down, g_up, "row")
    (pieces,) = call(
        sums_kernel, [(five, BF)], (act_far, gmi, shifted, edge_rows, hidden, rim, pieces), "sums",
        far=(0, 6), far_out=(0,), alias={6: 0},
        scratch=[
            vmem((2 * CR, POS), BF), vmem((ROWS, COLS, 2, H, LANES), BF),
            vmem((3 * MR, 2 * CR), F32), vmem((MR, CR), F32),
        ],
        copies=3,
    )
    pieces, g_above, g_below = lax.optimization_barrier((pieces, g_above, g_below))
    arrived = lax.all_to_all(pieces.reshape(ROWS * COLS, 5, H, LANES), everyone, 0, 0, tiled=True)
    arrived = arrived.reshape(five)
    (sums,) = call(
        total_kernel, [((ROWS, H, LANES), F32)], (arrived,), "total", flops=500_000_000
    )
    spread_sums = lax.all_to_all(sums, "row", 0, 0, tiled=True)
    taps, _ = lax.optimization_barrier((taps, pieces))
    g_edge, inputs, edge_value, edge_slope, block = call(
        spread_kernel,
        [((CR // 2, LANES), F32), (tile, BF), ((CR, LANES), F32), ((CR, LANES), F32), (tile, BF)],
        (grad_inner, g_above, g_below, taps, half_sum, pair_map, block, edge_block),
        "spread", far=(0, 4, 5, 6, 7), far_out=(1, 2, 3, 4), copies=2 * GROUPS + 7,
        scratch=[
            vmem((3 * CR, 2 * MR), BF), vmem((2 * MR, 2 * LANES), BF), vmem((GROUPS, MID, H, LANES), BF),
            vmem(tile, F32), vmem(tile, BF), vmem(tile, BF), vmem((CR, LANES), F32), vmem(tile, BF),
            vmem((CR, LANES), F32), vmem((CR, LANES), F32),
        ],
    )
    g_left, g_right = both_ways(g_edge, g_edge, "col")
    g_left, g_right, block, _ = lax.optimization_barrier((g_left, g_right, block, sums))
    (grad_input,) = call(
        input_kernel, [(tile, BF)], (inputs, edge_value, edge_slope, g_left, g_right), "grad_input",
        far=(0, 1, 2), far_out=(0,), copies=2 * GROUPS + 2,
        scratch=[vmem(tile, BF), vmem(tile, BF), vmem((CR, LANES), F32), vmem((CR, LANES), F32)],
    )
    (symmetric,) = call(
        symmetric_kernel, [(tile, BF)], (block, arrived), "symmetric", far=(0, 1), far_out=(0,),
        scratch=[vmem(tile, BF), vmem(cut, BF), vmem(tile, BF)], copies=3 * GROUPS,
    )
    conv, mix = call(
        unpack_kernel, [((9, MID, CH), F32), ((MID, CH), F32)], (spread_sums,), "unpack", flops=100_000_000
    )
    grad_conv = jnp.transpose(conv.reshape(3, 3, MID, CH), (2, 3, 0, 1))
    return symmetric, grad_input, grad_conv, mix.T


def solution(mesh):
    field = P(None, None, "row", "col")
    return jax.shard_map(
        local,
        mesh=mesh,
        in_specs=(field, field, P(), P(), P(), P(), P(), P()),
        out_specs=(field, field, P(), P()),
        check_vma=False,
    )
```

```python
import functools

import jax
import jax.numpy as jnp
from jax import lax
from jax.experimental import pallas as pl
from jax.experimental.pallas import tpu as pltpu
from jax.sharding import PartitionSpec as P

BF = jnp.bfloat16
F32 = jnp.float32
CH, MID, GROUPS, H, LANES, ROWS, COLS = 48, 24, 8, 8, 128, 16, 8
POS = GROUPS * LANES
CR, MR = CH * H, MID * H
TANH_SCALE = 0.7978845608028654
CUBIC = 0.044715
NN = (((1,), (0,)), ((), ()))
NT = (((1,), (1,)), ((), ()))
TN = (((0,), (0,)), ((), ()))


def smooth(v):
    t = jnp.tanh(TANH_SCALE * (v + CUBIC * (v * v * v)))
    return 0.5 * v * (1.0 + t)


def smooth_slope(v):
    s = v * v
    t = jnp.tanh(TANH_SCALE * (v + CUBIC * (v * s)))
    return 0.5 * (1.0 + t) + (0.5 * v) * (1.0 - t * t) * (TANH_SCALE * (1.0 + (3.0 * CUBIC) * s))


def dot(a, b, dims=NN):
    return lax.dot_general(a, b, dims, preferred_element_type=F32)


def iota(shape, dim):
    return lax.broadcasted_iota(jnp.int32, shape, dim)


def identity(n):
    return jnp.where(iota((n, n), 0) == iota((n, n), 1), 1.0, 0.0).astype(BF)


def lanes_of(rows):
    return iota((rows, LANES), 1)


class Far:
    def __init__(self, sems):
        self.sems, self.used, self.open = sems, 0, []

    def start(self, source, target):
        copy = pltpu.make_async_copy(source, target, self.sems.at[self.used])
        self.used += 1
        copy.start()
        return copy

    def send(self, source, target):
        self.open.append(self.start(source, target))

    def finish(self):
        for copy in self.open:
            copy.wait()


def call(kernel, outs, args, name, smem=(), far=(), far_out=(), flops=4_000_000_000, scratch=(), copies=0, limit=16, alias=None):
    specs = [
        pl.BlockSpec(memory_space=pltpu.SMEM if i in smem else pltpu.HBM if i in far else pltpu.VMEM)
        for i in range(len(args))
    ]
    scratch = list(scratch)
    if copies:
        scratch.append(pltpu.SemaphoreType.DMA((copies,)))
    return pl.pallas_call(
        kernel,
        name=name,
        out_shape=[
            pltpu.HBM(s, t) if i in far_out else jax.ShapeDtypeStruct(s, t)
            for i, (s, t) in enumerate(outs)
        ],
        in_specs=specs,
        out_specs=[
            pl.BlockSpec(memory_space=pltpu.HBM if i in far_out else pltpu.VMEM)
            for i in range(len(outs))
        ],
        scratch_shapes=scratch,
        input_output_aliases=alias or {},
        compiler_params=pltpu.CompilerParams(vmem_limit_bytes=limit * 1024 * 1024),
        cost_estimate=pl.CostEstimate(flops=flops, bytes_accessed=1_000_000, transcendentals=0),
    )(
        *(
            pltpu.with_memory_space_constraint(v, pltpu.HBM) if i in far else v
            for i, v in enumerate(args)
        )
    )


def splat(values, count):
    return jnp.concatenate([jnp.full((H, LANES), values[o], F32) for o in range(count)], axis=0)


def pack_rows(field, count):
    pairs = field.reshape(count // 2, 2, H, LANES)
    even, odd = pairs[:, 0], pairs[:, 1]
    low = iota(even.shape, 1) < 4
    last = jnp.where(low, pltpu.roll(even, 4, 1), odd)
    first = jnp.where(low, even, pltpu.roll(odd, 4, 1))
    return last, first


def send_rows(source, down, up, count):
    at_end = (lax.axis_index("row") == ROWS - 1).astype(jnp.int32)
    at_start = (lax.axis_index("row") == 0).astype(jnp.int32)
    for g in range(GROUPS):
        before = g - at_end
        last, _ = pack_rows(source[jnp.maximum(before, 0)].astype(F32), count)
        down[g] = jnp.where(before >= 0, last, 0.0).astype(BF)
        after = g + at_start
        _, first = pack_rows(source[jnp.minimum(after, GROUPS - 1)].astype(F32), count)
        up[g] = jnp.where(after < GROUPS, first, 0.0).astype(BF)


def swap_blocks(parts):
    lane = iota(parts[0].shape, 1)
    parts = list(parts)
    for k in range(4):
        m = 1 << k
        high = (lane // (8 * m)) % 2 == 1
        for i in range(ROWS):
            if i & m:
                continue
            a, b = parts[i], parts[i | m]
            parts[i] = jnp.where(high, pltpu.roll(b, 8 * m, 1), a)
            parts[i | m] = jnp.where(high, b, pltpu.roll(a, LANES - 8 * m, 1))
    return parts


def turn(tiles):
    return tiles.reshape(LANES, LANES).T.reshape(ROWS, H, LANES)


def swap_in(pieces, g, buffer):
    parts = swap_blocks([pieces[r, g : g + 2].reshape(6 * H, LANES) for r in range(ROWS)])
    for i in range(ROWS):
        value = parts[i].reshape(2, 3, H, LANES)
        for n in range(2):
            for k in range(3):
                buffer[n, k * ROWS + i] = value[n, k]


def swap_out(block, pieces, g):
    parts = swap_blocks(
        [
            jnp.concatenate([block[g + n, k * ROWS + i] for n in range(2) for k in range(3)], axis=0)
            for i in range(ROWS)
        ]
    )
    for r in range(ROWS):
        pieces[r, g : g + 2] = parts[r].reshape(2, 3, H, LANES)


def first_kernel(x_far, d_far, down, up, pieces, x, d, turned, sems):
    far = Far(sems)
    loads = [far.start(x_far.at[g], x.at[g]) for g in range(GROUPS)]
    later = [far.start(d_far.at[g], d.at[g]) for g in range(GROUPS)]
    for load in loads:
        load.wait()
    send_rows(x, down, up, CH)
    for g in range(GROUPS):
        later[g].wait()
        for k in range(3):
            turned[:, g, k] = turn(d[g, k * ROWS : (k + 1) * ROWS])
        far.send(turned.at[:, g], pieces.at[:, g])
    far.finish()


def spread_channels(n, own, width):
    col = iota((n, width), 1)
    half = (width - own) // 2
    rim = jnp.where(col < own + half, col - own, col - own - half) // 4
    return jnp.where(jnp.where(col < own, col // 8, rim) == iota((n, width), 0), 1.0, 0.0).astype(BF)


def row_distance(own, width):
    col, h = iota((H, width), 1), iota((H, width), 0)
    half = (width - own) // 2
    rim = jnp.where(col < own + half, (col - own) % 4 - 4, (col - own - half) % 4 + 8)
    return jnp.where(col < own, col % 8, rim) - h


def weights_kernel(w, mix, a_out, mf_out, a_far, mf_far, mb_far, mb_out, sems):
    far = Far(sems)
    sf, st = spread_channels(CH, CR, 2 * CR), spread_channels(MID, MR, MR)
    pf, pt = row_distance(CR, 2 * CR), row_distance(MR, MR)
    masks = [jnp.where(pf == 4 * (a - 1), 1.0, 0.0)[None] for a in range(3)]
    for b in range(3):
        total = jnp.zeros((MID, H, 2 * CR), F32)
        for a in range(3):
            total += dot(w[3 * a + b], sf)[:, None, :] * masks[a]
        a_out[b * MR : (b + 1) * MR] = total.reshape(MR, 2 * CR).astype(BF)
    far.send(a_out, a_far)
    mask = jnp.where(pf[:, :CR] == 0, 1.0, 0.0)
    mb_out[...] = (dot(mix[...], sf[:, :CR])[:, None, :] * mask[None]).reshape(MR, CR).astype(BF)
    far.send(mb_out, mb_far)
    mask = jnp.where(pt == 0, 1.0, 0.0)
    mf_out[...] = (dot(mix[...], st, TN)[:, None, :] * mask[None]).reshape(CR, MR).astype(BF)
    far.send(mf_out, mf_far)
    far.finish()


def back_weights(w, out):
    st, pt = spread_channels(MID, MR, 2 * MR), row_distance(MR, 2 * MR)
    masks = [jnp.where(pt == -4 * (a - 1), 1.0, 0.0)[None] for a in range(3)]
    for b in range(3):
        total = jnp.zeros((CH, H, 2 * MR), F32)
        for a in range(3):
            total += dot(w[3 * a + b], st, TN)[:, None, :] * masks[a]
        out[b * CR : (b + 1) * CR] = total.reshape(CR, 2 * MR).astype(BF)


def act_kernel(x, above, below, act, edge, act_far, sems):
    far = Far(sems)
    lane = lanes_of(CR)
    packed = jnp.zeros((CR, LANES), F32)
    for g in range(GROUPS):
        own = smooth(x[g].astype(F32).reshape(CR, LANES))
        high = smooth(above[g].astype(F32).reshape(CR // 2, LANES))
        low = smooth(below[g].astype(F32).reshape(CR // 2, LANES))
        rim = jnp.concatenate([high, low], axis=0)
        at = slice(g * LANES, (g + 1) * LANES)
        act[0:CR, at] = own.astype(BF)
        act[CR : 2 * CR, at] = rim.astype(BF)
        far.send(act.at[:, at], act_far.at[:, at])
        packed = jnp.where(lane // 8 == g, pltpu.roll(own, (8 * g - 124) % LANES, 1), packed)
        packed = jnp.where(lane // 8 == 8 + g, pltpu.roll(rim, (8 * g - 60) % LANES, 1), packed)
    edge[...] = packed.astype(BF)
    far.finish()


def merge_edges(from_left, from_right):
    lane = lanes_of(from_left.shape[0])
    col = lax.axis_index("col")
    has_left = jnp.where(col > 0, 1.0, 0.0)
    has_right = jnp.where(col < COLS - 1, 1.0, 0.0)
    return jnp.where(
        lane % 8 < 4,
        pltpu.roll(from_right, LANES - 4, 1) * has_right,
        pltpu.roll(from_left, 4, 1) * has_left,
    )


def at_edge(lane):
    return jnp.logical_or(lane < 4, lane >= 124)


def inside_kernel(
    x, act, weights, mixer, cg, cb, mg, mb,
    slope_far, hidden_far, block_far, pieces_far, edge_inner_far, edge_x_far,
    slope, hidden, block, pieces, edge_inner, edge_x, sems,
):
    far = Far(sems)
    lane, lane_c = lanes_of(MR), lanes_of(CR)
    gain, shift = splat(cg, MID), splat(cb, MID)
    gain_out, shift_out = splat(mg, CH), splat(mb, CH)
    packed, packed_x = jnp.zeros((MR, LANES), F32), jnp.zeros((CR, LANES), F32)
    for pair in range(GROUPS // 2):
        two = slice(pair * 2 * LANES, (pair + 1) * 2 * LANES)
        product = dot(weights[...], act[:, two])
        for half in range(2):
            g = 2 * pair + half
            p = product[:, half * LANES : (half + 1) * LANES]
            inner = (
                p[MR : 2 * MR]
                + jnp.where(lane < 4, 0.0, pltpu.roll(p[0:MR], 4, 1))
                + jnp.where(lane >= 124, 0.0, pltpu.roll(p[2 * MR : 3 * MR], LANES - 4, 1))
            )
            packed = jnp.where(lane // 8 == g, pltpu.roll(inner, (8 * g - 124) % LANES, 1), packed)
            pre = inner * gain + shift
            at = slice(g * LANES, (g + 1) * LANES)
            slope[:, at] = smooth_slope(pre) * gain
            hidden[:, at] = smooth(pre).astype(BF)
        far.send(slope.at[:, two], slope_far.at[:, two])
        far.send(hidden.at[:, two], hidden_far.at[:, two])
        mixed = dot(mixer[...], hidden[:, two])
        for half in range(2):
            g = 2 * pair + half
            m = mixed[:, half * LANES : (half + 1) * LANES]
            own = x[g].astype(F32).reshape(CR, LANES)
            packed_x = jnp.where(lane_c // 8 == g, pltpu.roll(own, (8 * g - 124) % LANES, 1), packed_x)
            value = (own + m * gain_out + shift_out).astype(BF)
            block[g] = value.astype(F32).reshape(CH, H, LANES).astype(BF)
        g = 2 * pair
        far.send(block.at[g : g + 2], block_far.at[g : g + 2])
        swap_out(block, pieces, g)
        far.send(pieces.at[:, g : g + 2], pieces_far.at[:, g : g + 2, 2:5])
    edge_inner[...] = packed
    edge_x[...] = packed_x
    far.send(edge_inner, edge_inner_far)
    far.send(edge_x, edge_x_far)
    far.finish()


def split(value):
    high = value.astype(BF)
    return high, (value - high.astype(F32)).astype(BF)


def exact_dot(value, onehot):
    high, low = split(value)
    return dot(high, onehot) + dot(low, onehot)


def inner_kernel(
    d_far, arrived, slope_far, hidden_far, edge_inner_far, edge_x_far, from_left, from_right,
    weights_far, mixer_far, back_far, pieces_in, cg, cb, mg, mb,
    grad_inner_far, down, up, half_sum_far, pieces_far, edge_block_far, gmi, shifted, edge_rows, hidden_out, rim_out,
    d, slope, hidden, edge_inner, edge_x, weights, mixer, back, grad_inner, half_sum, ends, edge_block, buffer, sems,
):
    far = Far(sems)
    loads = [far.start(d_far.at[2 * p : 2 * p + 2], d.at[2 * p : 2 * p + 2]) for p in range(GROUPS // 2)]
    first = [far.start(weights_far.at[0:MR], weights.at[0:MR])]
    first.append(far.start(weights_far.at[2 * MR : 3 * MR], weights.at[MR : 2 * MR]))
    first += [far.start(edge_inner_far, edge_inner), far.start(edge_x_far, edge_x), far.start(mixer_far, mixer)]
    tails = [
        far.start(pieces_in.at[r, :, 2:5], ends.at[i]) for i, r in enumerate((0, ROWS - 1))
    ]
    later = [far.start(back_far, back), far.start(slope_far, slope), far.start(hidden_far, hidden)]
    lane, lane_c = lanes_of(MR), lanes_of(CR)
    gain, shift = splat(cg, MID), splat(cb, MID)
    gain_out, shift_out = splat(mg, CH), splat(mb, CH)
    rim = merge_edges(from_left[...].astype(F32), from_right[...].astype(F32)).astype(BF)
    rim_out[...] = rim
    for pair in range(GROUPS // 2):
        loads[pair].wait()
        swap_in(arrived, 2 * pair, buffer)
        for half in range(2):
            g = 2 * pair + half
            both = 0.5 * (d[g].astype(F32) + buffer[half].astype(F32)).reshape(CR, LANES)
            half_sum[g] = both.reshape(CH, H, LANES)
            gmi[:, g * LANES : (g + 1) * LANES] = (both * gain_out).astype(BF)
        far.send(half_sum.at[2 * pair : 2 * pair + 2], half_sum_far.at[2 * pair : 2 * pair + 2])
    for load in first:
        load.wait()
    outer = dot(weights[:, 0:CR], rim) + pltpu.roll(dot(weights[:, CR : 2 * CR], rim), 64, 1)
    outer = jnp.where(lane % 8 < 4, outer[MR : 2 * MR], outer[0:MR])
    pre = (edge_inner[...] + outer) * gain + shift
    slope_edge = smooth_slope(pre) * gain
    hidden_edge = smooth(pre).astype(BF)
    mixed = dot(mixer[...], hidden_edge)
    value = (edge_x[...] + mixed * gain_out + shift_out).astype(BF)
    edge_block[...] = value.astype(F32)
    far.send(edge_block, edge_block_far)
    hidden_edge = hidden_edge.astype(F32)
    parts = value.astype(F32).reshape(3, ROWS, H, LANES)
    parts = swap_blocks([parts[:, i].reshape(3 * H, LANES) for i in range(ROWS)])
    for load in tails:
        load.wait()
    low = iota((3, H, LANES), 2) % 8 < 4
    for g in range(GROUPS):
        lower = pltpu.roll(parts[g], LANES - 4, 1).reshape(3, H, LANES)
        upper = pltpu.roll(parts[g], 4, 1).reshape(3, H, LANES)
        ends[0, g] = jnp.where(low, lower, ends[0, g].astype(F32)).astype(BF)
        ends[1, g] = jnp.where(low, ends[1, g].astype(F32), upper).astype(BF)
    for i, r in enumerate((0, ROWS - 1)):
        far.send(ends.at[i], pieces_far.at[r, :, 2:5])

    for load in later:
        load.wait()
    packed = jnp.zeros((MR, LANES), F32)
    for pair in range(GROUPS // 2):
        two = slice(pair * 2 * LANES, (pair + 1) * 2 * LANES)
        into = dot(back[...], gmi[:, two])
        for half in range(2):
            g = 2 * pair + half
            at = slice(g * LANES, (g + 1) * LANES)
            turn = (124 - 8 * g) % LANES
            here = jnp.where(at_edge(lane), pltpu.roll(slope_edge, turn, 1), slope[:, at])
            value = into[:, half * LANES : (half + 1) * LANES] * here
            grad_inner[g] = value.reshape(MID, H, LANES).astype(BF)
            shifted[0:MR, at] = jnp.where(lane < 124, pltpu.roll(value, LANES - 4, 1), 0.0).astype(BF)
            shifted[MR : 2 * MR, at] = value.astype(BF)
            shifted[2 * MR : 3 * MR, at] = jnp.where(lane >= 4, pltpu.roll(value, 4, 1), 0.0).astype(BF)
            packed = jnp.where(lane // 8 == g, pltpu.roll(value, (8 * g - 124) % LANES, 1), packed)
            here = jnp.where(at_edge(lane), pltpu.roll(hidden_edge, turn, 1), hidden[:, at].astype(F32))
            hidden_out[:, at] = here.astype(BF)
        far.send(grad_inner.at[2 * pair : 2 * pair + 2], grad_inner_far.at[2 * pair : 2 * pair + 2])
    send_rows(grad_inner, down, up, MID)
    packed = packed + pltpu.roll(packed, 64, 1)
    edge_rows[0:MR] = jnp.where(lane % 8 >= 4, packed, 0.0).astype(BF)
    edge_rows[MR : 2 * MR] = jnp.zeros((MR, LANES), BF)
    edge_rows[2 * MR : 3 * MR] = jnp.where(lane % 8 < 4, packed, 0.0).astype(BF)
    far.finish()


def sums_kernel(
    act_far, gmi, shifted, edge_rows, hidden, rim, pieces_in, pieces_far, act, sums_out, wide, mixwide, sems
):
    far = Far(sems)
    loads = [far.start(act_far.at[k * CR : (k + 1) * CR], act.at[k * CR : (k + 1) * CR]) for k in range(2)]
    sums_out[ROWS - 1] = jnp.zeros((COLS, 2, H, LANES), BF)
    far.send(sums_out.at[ROWS - 1], pieces_far.at[ROWS - 1, :, 0:2])
    lane_c = lanes_of(CR)
    rim_value = rim[...].astype(F32)
    rim_own = jnp.where(lane_c < 64, rim_value, 0.0).astype(BF)
    rim_rest = jnp.where(lane_c >= 64, rim_value, 0.0).astype(BF)
    mixwide[...] = dot(hidden[...], gmi[...], NT)
    for k in range(2):
        rows = slice(k * CR, (k + 1) * CR)
        loads[k].wait()
        wide[:, rows] = dot(shifted[...], act[rows], NT) + dot(edge_rows[...], (rim_own, rim_rest)[k], NT)

    h, col = iota((H, CR), 0), iota((H, CR), 1)
    same = jnp.where(col % 8 == h, 1.0, 0.0)[None]
    other = jnp.where(col % 8 == (h + 4) % 8, 1.0, 0.0)[None]
    low_half = col < CR // 2
    across = jnp.where(jnp.where(low_half, col, col - CR // 2) % 4 == jnp.where(low_half, h, h - 4), 1.0, 0.0)[None]
    col, lane_s = iota((CR, LANES), 0), iota((CR, LANES), 1)

    def gather(keep, channel, side):
        return jnp.where(jnp.logical_and(keep, channel + 64 * side == lane_s), 1.0, 0.0).astype(BF)

    blocks = []
    sums = []
    for b in range(3):
        block = wide[b * MR : (b + 1) * MR]
        own = block[:, 0:CR].reshape(MID, H, CR)
        rest = block[:, CR : 2 * CR].reshape(MID, H, CR)
        sums.append([jnp.sum(own * same, axis=1), jnp.sum(own * other, axis=1), jnp.sum(rest * across, axis=1)])
    mixed = jnp.sum(mixwide[...].reshape(MID, H, CR) * same, axis=1)
    always = col >= 0
    own_low = col % 8 < 4
    rest_low = col < CR // 2
    rest_channel = jnp.where(rest_low, col, col - CR // 2) // 4
    for index in range(10):
        side = index % 2
        if index == 9:
            value = exact_dot(mixed, gather(always, col // 8, side))
        else:
            a, b = index // 3, index % 3
            if a == 1:
                value = exact_dot(sums[b][0], gather(always, col // 8, side))
            else:
                low = a == 0
                keep_own = own_low if low else jnp.logical_not(own_low)
                keep_rest = rest_low if low else jnp.logical_not(rest_low)
                value = exact_dot(sums[b][1], gather(keep_own, col // 8, side))
                value += exact_dot(sums[b][2], gather(keep_rest, rest_channel, side))
        blocks.append(value)
    for p in range(5):
        value = blocks[2 * p] + blocks[2 * p + 1]
        high = value.astype(BF).astype(F32)
        low = value - high
        for k in range(3):
            r = 3 * p + k
            rows = slice(k * H, (k + 1) * H)
            sums_out[r, :, 0] = jnp.broadcast_to(high[rows][None], (COLS, H, LANES)).astype(BF)
            sums_out[r, :, 1] = jnp.broadcast_to(low[rows][None], (COLS, H, LANES)).astype(BF)
        far.send(sums_out.at[3 * p : 3 * p + 3], pieces_far.at[3 * p : 3 * p + 3, :, 0:2])
    far.finish()


def spread_kernel(
    grad_inner_far, above, below, w, half_far, x_far, block_far, edge_block_far,
    edge, out_far, edge_value_far, edge_slope_far, block_out_far,
    weights, rhs, grad_inner, half_sum, x, block, edge_block, out, edge_value, edge_slope, sems,
):
    far = Far(sems)
    first = far.start(grad_inner_far, grad_inner)
    loads = [far.start(half_far, half_sum), far.start(x_far, x)]
    last = [far.start(block_far, block), far.start(edge_block_far, edge_block)]
    back_weights(w, weights)
    first.wait()
    lane = lanes_of(CR)
    packed, packed_value, packed_slope = (jnp.zeros((CR, LANES), F32) for _ in range(3))
    for load in loads:
        load.wait()
    for pair in range(GROUPS // 2):
        for half in range(2):
            g = 2 * pair + half
            at = slice(half * LANES, (half + 1) * LANES)
            rhs[0:MR, at] = grad_inner[g].astype(F32).reshape(MR, LANES).astype(BF)
            rhs[MR : MR + MR // 2, at] = above[g].astype(F32).reshape(MR // 2, LANES).astype(BF)
            rhs[MR + MR // 2 : 2 * MR, at] = below[g].astype(F32).reshape(MR // 2, LANES).astype(BF)
        product = dot(weights[...], rhs[...])
        for half in range(2):
            g = 2 * pair + half
            p = product[:, half * LANES : (half + 1) * LANES]
            left, mid, right = p[0:CR], p[CR : 2 * CR], p[2 * CR : 3 * CR]
            total = (
                mid
                + jnp.where(lane < 124, pltpu.roll(left, LANES - 4, 1), 0.0)
                + jnp.where(lane >= 4, pltpu.roll(right, 4, 1), 0.0)
            )
            slope = smooth_slope(x[g].astype(F32).reshape(CR, LANES))
            value = half_sum[g].reshape(CR, LANES) + total * slope
            out[g] = value.reshape(CH, H, LANES).astype(BF)
            far.send(out.at[g], out_far.at[g])
            here = lane // 8 == g
            turn_by = (8 * g - 124) % LANES
            packed = jnp.where(here, pltpu.roll(jnp.where(lane >= 124, right, left), turn_by, 1), packed)
            packed_value = jnp.where(here, pltpu.roll(value, turn_by, 1), packed_value)
            packed_slope = jnp.where(here, pltpu.roll(slope, turn_by, 1), packed_slope)
    edge[...] = packed[0 : CR // 2] + pltpu.roll(packed[CR // 2 : CR], 64, 1)
    edge_value[...] = packed_value
    edge_slope[...] = packed_slope
    far.send(edge_value, edge_value_far)
    far.send(edge_slope, edge_slope_far)
    for load in last:
        load.wait()
    for g in range(GROUPS):
        moved = pltpu.roll(edge_block[...], (124 - 8 * g) % LANES, 1)
        value = jnp.where(at_edge(lane), moved, block[g].astype(F32).reshape(CR, LANES))
        block[g] = value.reshape(CH, H, LANES).astype(BF)
        far.send(block.at[g], block_out_far.at[g])
    far.finish()


def input_kernel(value_far, edge_value_far, edge_slope_far, from_left, from_right, out_far, value, out, edge_value, edge_slope, sems):
    far = Far(sems)
    first = [far.start(edge_value_far, edge_value), far.start(edge_slope_far, edge_slope)]
    loads = [far.start(value_far.at[g], value.at[g]) for g in range(GROUPS)]
    lane = lanes_of(CR)
    rim = merge_edges(from_left[...], from_right[...])
    rim = jnp.concatenate([rim, pltpu.roll(rim, 64, 1)], axis=0)
    for load in first:
        load.wait()
    rim = edge_value[...] + rim * edge_slope[...]
    for g in range(GROUPS):
        loads[g].wait()
        moved = pltpu.roll(rim, (124 - 8 * g) % LANES, 1)
        total = jnp.where(at_edge(lane), moved, value[g].astype(F32).reshape(CR, LANES))
        out[g] = total.reshape(CH, H, LANES).astype(BF)
        far.send(out.at[g], out_far.at[g])
    far.finish()


def total_kernel(arrived, out):
    total = jnp.zeros((H, LANES), F32)
    for g in range(COLS):
        part = arrived[:, g, 0:2].astype(F32)
        total += jnp.sum(part[:, 0] + part[:, 1], axis=0)
    out[...] = jnp.broadcast_to((total * (1.0 / (ROWS * H * COLS)))[None], (ROWS, H, LANES))


def symmetric_kernel(block_far, arrived_far, out_far, block, arrived, out, sems):
    far = Far(sems)
    loads = [
        (far.start(block_far.at[g], block.at[g]), far.start(arrived_far.at[:, g, 2:5], arrived.at[:, g]))
        for g in range(GROUPS)
    ]
    for g in range(GROUPS):
        for load in loads[g]:
            load.wait()
        for k in range(3):
            at = slice(k * ROWS, (k + 1) * ROWS)
            value = 0.5 * (block[g, at].astype(F32) + turn(arrived[:, g, k]).astype(F32))
            out[g, at] = value.astype(BF)
        far.send(out.at[g], out_far.at[g])
    far.finish()


def unpack_kernel(tiles, conv, mix):
    for p in range(5):
        value = tiles[3 * p : 3 * p + 3].reshape(3 * H, LANES)
        conv[2 * p] = value[:, 0:CH]
        if p < 4:
            conv[2 * p + 1] = value[:, 64 : 64 + CH]
        else:
            mix[...] = value[:, 64 : 64 + CH]


def both_ways(first, second, axis):
    count = lax.axis_size(axis)
    onward = [(i, (i + 1) % count) for i in range(count)]
    back = [(t, s) for s, t in onward]
    return lax.ppermute(first, axis, onward), lax.ppermute(second, axis, back)


def local(pair_map, cotangent, conv_weight, conv_gain, conv_bias, mix_weight, mix_gain, mix_bias):
    tile = (GROUPS, CH, H, LANES)
    cut = (ROWS, COLS, 3, H, LANES)
    everyone = ("row", "col")
    vmem = pltpu.VMEM
    down, up, d_pieces = call(
        first_kernel, [((GROUPS, CH // 2, H, LANES), BF)] * 2 + [(cut, BF)], (pair_map, cotangent), "first",
        far=(0, 1), far_out=(2,), scratch=[vmem(tile, BF), vmem(tile, BF), vmem(cut, BF)], copies=3 * GROUPS,
    )
    above, below = both_ways(down, up, "row")
    d_arrived = lax.all_to_all(d_pieces.reshape(ROWS * COLS, 3, H, LANES), everyone, 0, 0, tiled=True)
    d_arrived = d_arrived.reshape(cut)

    taps = jnp.transpose(conv_weight, (2, 3, 0, 1)).reshape(9, MID, CH)
    wf, mf, wf_far, mf_far, mbk = call(
        weights_kernel,
        [((3 * MR, 2 * CR), BF), ((CR, MR), BF)] * 2 + [((MR, CR), BF)],
        (taps, mix_weight.T), "weights", far_out=(2, 3, 4), scratch=[vmem((MR, CR), BF)], copies=3,
    )
    act, edge, act_far = call(
        act_kernel,
        [((2 * CR, POS), BF), ((CR, LANES), BF), ((2 * CR, POS), BF)],
        (pair_map, above, below), "act", far_out=(2,), copies=GROUPS,
    )
    from_left, from_right = both_ways(edge, edge, "col")
    five = (ROWS, COLS, 5, H, LANES)
    slope, hidden, block, pieces, edge_inner, edge_x = call(
        inside_kernel,
        [((MR, POS), F32), ((MR, POS), BF), (tile, BF), (five, BF), ((MR, LANES), F32), ((CR, LANES), F32)],
        (pair_map, act, wf, mf, conv_gain, conv_bias, mix_gain, mix_bias),
        "inside", smem=(4, 5, 6, 7), far_out=(0, 1, 2, 3, 4, 5),
        scratch=[
            vmem((MR, POS), F32), vmem((MR, POS), BF), vmem(tile, BF), vmem(cut, BF),
            vmem((MR, LANES), F32), vmem((CR, LANES), F32),
        ],
        copies=2 * GROUPS + 2,
    )
    grad_inner, g_down, g_up, half_sum, pieces, edge_block, gmi, shifted, edge_rows, hidden, rim = call(
        inner_kernel,
        [
            ((GROUPS, MID, H, LANES), BF),
            ((GROUPS, MID // 2, H, LANES), BF),
            ((GROUPS, MID // 2, H, LANES), BF),
            (tile, F32),
            (five, BF),
            ((CR, LANES), F32),
            ((CR, POS), BF),
            ((3 * MR, POS), BF),
            ((3 * MR, LANES), BF),
            ((MR, POS), BF),
            ((CR, LANES), BF),
        ],
        (
            cotangent, d_arrived, slope, hidden, edge_inner, edge_x, from_left, from_right,
            wf_far, mf_far, mbk, pieces, conv_gain, conv_bias, mix_gain, mix_bias,
        ),
        "inner", smem=(12, 13, 14, 15), far=(0, 2, 3, 4, 5, 8, 9, 10, 11), far_out=(0, 3, 4, 5), alias={11: 4},
        scratch=[
            vmem(tile, BF), vmem((MR, POS), F32), vmem((MR, POS), BF), vmem((MR, LANES), F32), vmem((CR, LANES), F32),
            vmem((2 * MR, 2 * CR), BF), vmem((CR, MR), BF), vmem((MR, CR), BF),
            vmem((GROUPS, MID, H, LANES), BF), vmem(tile, F32), vmem((2, COLS, 3, H, LANES), BF),
            vmem((CR, LANES), F32), vmem((2, CH, H, LANES), BF),
        ],
        copies=25,
    )
    g_above, g_below = both_ways(g_down, g_up, "row")
    (pieces,) = call(
        sums_kernel, [(five, BF)], (act_far, gmi, shifted, edge_rows, hidden, rim, pieces), "sums",
        far=(0, 6), far_out=(0,), alias={6: 0},
        scratch=[
            vmem((2 * CR, POS), BF), vmem((ROWS, COLS, 2, H, LANES), BF),
            vmem((3 * MR, 2 * CR), F32), vmem((MR, CR), F32),
        ],
        copies=8,
    )
    pieces, g_above, g_below = lax.optimization_barrier((pieces, g_above, g_below))
    arrived = lax.all_to_all(pieces.reshape(ROWS * COLS, 5, H, LANES), everyone, 0, 0, tiled=True)
    arrived = arrived.reshape(five)
    (sums,) = call(
        total_kernel, [((ROWS, H, LANES), F32)], (arrived,), "total", flops=500_000_000
    )
    spread_sums = lax.all_to_all(sums, "row", 0, 0, tiled=True)
    taps, _ = lax.optimization_barrier((taps, pieces))
    g_edge, inputs, edge_value, edge_slope, block = call(
        spread_kernel,
        [((CR // 2, LANES), F32), (tile, BF), ((CR, LANES), F32), ((CR, LANES), F32), (tile, BF)],
        (grad_inner, g_above, g_below, taps, half_sum, pair_map, block, edge_block),
        "spread", far=(0, 4, 5, 6, 7), far_out=(1, 2, 3, 4), copies=2 * GROUPS + 7,
        scratch=[
            vmem((3 * CR, 2 * MR), BF), vmem((2 * MR, 2 * LANES), BF), vmem((GROUPS, MID, H, LANES), BF),
            vmem(tile, F32), vmem(tile, BF), vmem(tile, BF), vmem((CR, LANES), F32), vmem(tile, BF),
            vmem((CR, LANES), F32), vmem((CR, LANES), F32),
        ],
    )
    g_left, g_right = both_ways(g_edge, g_edge, "col")
    g_left, g_right, block, _ = lax.optimization_barrier((g_left, g_right, block, sums))
    (grad_input,) = call(
        input_kernel, [(tile, BF)], (inputs, edge_value, edge_slope, g_left, g_right), "grad_input",
        far=(0, 1, 2), far_out=(0,), copies=2 * GROUPS + 2,
        scratch=[vmem(tile, BF), vmem(tile, BF), vmem((CR, LANES), F32), vmem((CR, LANES), F32)],
    )
    (symmetric,) = call(
        symmetric_kernel, [(tile, BF)], (block, arrived), "symmetric", far=(0, 1), far_out=(0,),
        scratch=[vmem(tile, BF), vmem(cut, BF), vmem(tile, BF)], copies=3 * GROUPS,
    )
    conv, mix = call(
        unpack_kernel, [((9, MID, CH), F32), ((MID, CH), F32)], (spread_sums,), "unpack", flops=100_000_000
    )
    grad_conv = jnp.transpose(conv.reshape(3, 3, MID, CH), (2, 3, 0, 1))
    return symmetric, grad_input, grad_conv, mix.T


def solution(mesh):
    field = P(None, None, "row", "col")
    return jax.shard_map(
        local,
        mesh=mesh,
        in_specs=(field, field, P(), P(), P(), P(), P(), P()),
        out_specs=(field, field, P(), P()),
        check_vma=False,
    )
```

```python
import functools

import jax
import jax.numpy as jnp
from jax import lax
from jax.experimental import pallas as pl
from jax.experimental.pallas import tpu as pltpu
from jax.sharding import PartitionSpec as P

BF = jnp.bfloat16
F32 = jnp.float32
CH, MID, GROUPS, H, LANES, ROWS, COLS = 48, 24, 8, 8, 128, 16, 8
POS = GROUPS * LANES
CR, MR = CH * H, MID * H
TANH_SCALE = 0.7978845608028654
CUBIC = 0.044715
NN = (((1,), (0,)), ((), ()))
NT = (((1,), (1,)), ((), ()))
TN = (((0,), (0,)), ((), ()))


def smooth(v):
    t = jnp.tanh(TANH_SCALE * (v + CUBIC * (v * v * v)))
    return 0.5 * v * (1.0 + t)


def smooth_slope(v):
    s = v * v
    t = jnp.tanh(TANH_SCALE * (v + CUBIC * (v * s)))
    return 0.5 * (1.0 + t) + (0.5 * v) * (1.0 - t * t) * (TANH_SCALE * (1.0 + (3.0 * CUBIC) * s))


def dot(a, b, dims=NN):
    return lax.dot_general(a, b, dims, preferred_element_type=F32)


def iota(shape, dim):
    return lax.broadcasted_iota(jnp.int32, shape, dim)


def identity(n):
    return jnp.where(iota((n, n), 0) == iota((n, n), 1), 1.0, 0.0).astype(BF)


def lanes_of(rows):
    return iota((rows, LANES), 1)


class Far:
    def __init__(self, sems):
        self.sems, self.used, self.open = sems, 0, []

    def start(self, source, target):
        copy = pltpu.make_async_copy(source, target, self.sems.at[self.used])
        self.used += 1
        copy.start()
        return copy

    def send(self, source, target):
        self.open.append(self.start(source, target))

    def finish(self):
        for copy in self.open:
            copy.wait()


def call(kernel, outs, args, name, smem=(), far=(), far_out=(), flops=4_000_000_000, scratch=(), copies=0, limit=16, alias=None):
    specs = [
        pl.BlockSpec(memory_space=pltpu.SMEM if i in smem else pltpu.HBM if i in far else pltpu.VMEM)
        for i in range(len(args))
    ]
    scratch = list(scratch)
    if copies:
        scratch.append(pltpu.SemaphoreType.DMA((copies,)))
    return pl.pallas_call(
        kernel,
        name=name,
        out_shape=[
            pltpu.HBM(s, t) if i in far_out else jax.ShapeDtypeStruct(s, t)
            for i, (s, t) in enumerate(outs)
        ],
        in_specs=specs,
        out_specs=[
            pl.BlockSpec(memory_space=pltpu.HBM if i in far_out else pltpu.VMEM)
            for i in range(len(outs))
        ],
        scratch_shapes=scratch,
        input_output_aliases=alias or {},
        compiler_params=pltpu.CompilerParams(vmem_limit_bytes=limit * 1024 * 1024),
        cost_estimate=pl.CostEstimate(flops=flops, bytes_accessed=1_000_000, transcendentals=0),
    )(
        *(
            pltpu.with_memory_space_constraint(v, pltpu.HBM) if i in far else v
            for i, v in enumerate(args)
        )
    )


def splat(values, count):
    return jnp.concatenate([jnp.full((H, LANES), values[o], F32) for o in range(count)], axis=0)


def pack_rows(field, count):
    pairs = field.reshape(count // 2, 2, H, LANES)
    even, odd = pairs[:, 0], pairs[:, 1]
    low = iota(even.shape, 1) < 4
    last = jnp.where(low, pltpu.roll(even, 4, 1), odd)
    first = jnp.where(low, even, pltpu.roll(odd, 4, 1))
    return last, first


def send_rows(source, down, up, count):
    at_end = (lax.axis_index("row") == ROWS - 1).astype(jnp.int32)
    at_start = (lax.axis_index("row") == 0).astype(jnp.int32)
    for g in range(GROUPS):
        before = g - at_end
        last, _ = pack_rows(source[jnp.maximum(before, 0)].astype(F32), count)
        down[g] = jnp.where(before >= 0, last, 0.0).astype(BF)
        after = g + at_start
        _, first = pack_rows(source[jnp.minimum(after, GROUPS - 1)].astype(F32), count)
        up[g] = jnp.where(after < GROUPS, first, 0.0).astype(BF)


def swap_blocks(parts):
    lane = iota(parts[0].shape, 1)
    parts = list(parts)
    for k in range(4):
        m = 1 << k
        high = (lane // (8 * m)) % 2 == 1
        for i in range(ROWS):
            if i & m:
                continue
            a, b = parts[i], parts[i | m]
            parts[i] = jnp.where(high, pltpu.roll(b, 8 * m, 1), a)
            parts[i | m] = jnp.where(high, b, pltpu.roll(a, LANES - 8 * m, 1))
    return parts


def turn(tiles):
    return tiles.reshape(LANES, LANES).T.reshape(ROWS, H, LANES)


def swap_in(pieces, g, buffer):
    parts = swap_blocks([pieces[r, g : g + 2].reshape(6 * H, LANES) for r in range(ROWS)])
    for i in range(ROWS):
        value = parts[i].reshape(2, 3, H, LANES)
        for n in range(2):
            for k in range(3):
                buffer[n, k * ROWS + i] = value[n, k]


def swap_out(block, pieces, g):
    parts = swap_blocks(
        [
            jnp.concatenate([block[g + n, k * ROWS + i] for n in range(2) for k in range(3)], axis=0)
            for i in range(ROWS)
        ]
    )
    for r in range(ROWS):
        pieces[r, g : g + 2] = parts[r].reshape(2, 3, H, LANES)


def first_kernel(x_far, d_far, down, up, pieces, x, d, turned, sems):
    far = Far(sems)
    loads = [far.start(x_far.at[g], x.at[g]) for g in range(GROUPS)]
    later = [far.start(d_far.at[g], d.at[g]) for g in range(GROUPS)]
    for load in loads:
        load.wait()
    send_rows(x, down, up, CH)
    for g in range(GROUPS):
        later[g].wait()
        for k in range(3):
            turned[:, g, k] = turn(d[g, k * ROWS : (k + 1) * ROWS])
        far.send(turned.at[:, g], pieces.at[:, g])
    far.finish()


def spread_channels(n, own, width):
    col = iota((n, width), 1)
    half = (width - own) // 2
    rim = jnp.where(col < own + half, col - own, col - own - half) // 4
    return jnp.where(jnp.where(col < own, col // 8, rim) == iota((n, width), 0), 1.0, 0.0).astype(BF)


def row_distance(own, width):
    col, h = iota((H, width), 1), iota((H, width), 0)
    half = (width - own) // 2
    rim = jnp.where(col < own + half, (col - own) % 4 - 4, (col - own - half) % 4 + 8)
    return jnp.where(col < own, col % 8, rim) - h


def weights_kernel(w, mix, a_out, mf_out, a_far, mf_far, mb_far, mb_out, sems):
    far = Far(sems)
    sf, st = spread_channels(CH, CR, 2 * CR), spread_channels(MID, MR, MR)
    pf, pt = row_distance(CR, 2 * CR), row_distance(MR, MR)
    masks = [jnp.where(pf == 4 * (a - 1), 1.0, 0.0)[None] for a in range(3)]
    for b in range(3):
        total = jnp.zeros((MID, H, 2 * CR), F32)
        for a in range(3):
            total += dot(w[3 * a + b], sf)[:, None, :] * masks[a]
        a_out[b * MR : (b + 1) * MR] = total.reshape(MR, 2 * CR).astype(BF)
    far.send(a_out, a_far)
    mask = jnp.where(pf[:, :CR] == 0, 1.0, 0.0)
    mb_out[...] = (dot(mix[...], sf[:, :CR])[:, None, :] * mask[None]).reshape(MR, CR).astype(BF)
    far.send(mb_out, mb_far)
    mask = jnp.where(pt == 0, 1.0, 0.0)
    mf_out[...] = (dot(mix[...], st, TN)[:, None, :] * mask[None]).reshape(CR, MR).astype(BF)
    far.send(mf_out, mf_far)
    far.finish()


def back_weights(w, out):
    st, pt = spread_channels(MID, MR, 2 * MR), row_distance(MR, 2 * MR)
    masks = [jnp.where(pt == -4 * (a - 1), 1.0, 0.0)[None] for a in range(3)]
    for b in range(3):
        total = jnp.zeros((CH, H, 2 * MR), F32)
        for a in range(3):
            total += dot(w[3 * a + b], st, TN)[:, None, :] * masks[a]
        out[b * CR : (b + 1) * CR] = total.reshape(CR, 2 * MR).astype(BF)


def act_kernel(x, above, below, act, edge, wide_far, wide, rows, sems):
    far = Far(sems)
    for p in range(4):
        wide[64 * p + CH : 64 * p + 64, :] = jnp.zeros((64 - CH, 4 * POS), BF)
    lane = lanes_of(CR)
    packed = jnp.zeros((CR, LANES), F32)
    for g in range(GROUPS):
        own = smooth(x[g].astype(F32).reshape(CR, LANES))
        high = smooth(above[g].astype(F32).reshape(CR // 2, LANES))
        low = smooth(below[g].astype(F32).reshape(CR // 2, LANES))
        rim = jnp.concatenate([high, low], axis=0)
        at = slice(g * LANES, (g + 1) * LANES)
        act[0:CR, at] = own.astype(BF)
        act[CR : 2 * CR, at] = rim.astype(BF)
        rows[0:CR] = own
        rows[CR : 2 * CR] = rim
        for m in range(4):
            to = slice((m * GROUPS + g) * LANES, (m * GROUPS + g + 1) * LANES)
            for p, (start, step) in enumerate(((CR, 4), (0, 8), (4, 8), (CR + CR // 2, 4))):
                wide[64 * p : 64 * p + CH, to] = rows[pl.ds(start + m, CH, stride=step), :].astype(BF)
        packed = jnp.where(lane // 8 == g, pltpu.roll(own, (8 * g - 124) % LANES, 1), packed)
        packed = jnp.where(lane // 8 == 8 + g, pltpu.roll(rim, (8 * g - 60) % LANES, 1), packed)
    edge[...] = packed.astype(BF)
    far.send(wide, wide_far)
    far.finish()


def merge_edges(from_left, from_right):
    lane = lanes_of(from_left.shape[0])
    col = lax.axis_index("col")
    has_left = jnp.where(col > 0, 1.0, 0.0)
    has_right = jnp.where(col < COLS - 1, 1.0, 0.0)
    return jnp.where(
        lane % 8 < 4,
        pltpu.roll(from_right, LANES - 4, 1) * has_right,
        pltpu.roll(from_left, 4, 1) * has_left,
    )


def at_edge(lane):
    return jnp.logical_or(lane < 4, lane >= 124)


def inside_kernel(
    x, act, weights, mixer, cg, cb, mg, mb,
    slope_far, hidden_far, block_far, pieces_far, edge_inner_far, edge_x_far,
    slope, hidden, block, pieces, edge_inner, edge_x, sems,
):
    far = Far(sems)
    lane, lane_c = lanes_of(MR), lanes_of(CR)
    gain, shift = splat(cg, MID), splat(cb, MID)
    gain_out, shift_out = splat(mg, CH), splat(mb, CH)
    packed, packed_x = jnp.zeros((MR, LANES), F32), jnp.zeros((CR, LANES), F32)
    for pair in range(GROUPS // 2):
        two = slice(pair * 2 * LANES, (pair + 1) * 2 * LANES)
        product = dot(weights[...], act[:, two])
        for half in range(2):
            g = 2 * pair + half
            p = product[:, half * LANES : (half + 1) * LANES]
            inner = (
                p[MR : 2 * MR]
                + jnp.where(lane < 4, 0.0, pltpu.roll(p[0:MR], 4, 1))
                + jnp.where(lane >= 124, 0.0, pltpu.roll(p[2 * MR : 3 * MR], LANES - 4, 1))
            )
            packed = jnp.where(lane // 8 == g, pltpu.roll(inner, (8 * g - 124) % LANES, 1), packed)
            pre = inner * gain + shift
            at = slice(g * LANES, (g + 1) * LANES)
            slope[:, at] = smooth_slope(pre) * gain
            hidden[:, at] = smooth(pre).astype(BF)
        far.send(slope.at[:, two], slope_far.at[:, two])
        far.send(hidden.at[:, two], hidden_far.at[:, two])
        mixed = dot(mixer[...], hidden[:, two])
        for half in range(2):
            g = 2 * pair + half
            m = mixed[:, half * LANES : (half + 1) * LANES]
            own = x[g].astype(F32).reshape(CR, LANES)
            packed_x = jnp.where(lane_c // 8 == g, pltpu.roll(own, (8 * g - 124) % LANES, 1), packed_x)
            value = (own + m * gain_out + shift_out).astype(BF)
            block[g] = value.astype(F32).reshape(CH, H, LANES).astype(BF)
        g = 2 * pair
        far.send(block.at[g : g + 2], block_far.at[g : g + 2])
        swap_out(block, pieces, g)
        far.send(pieces.at[:, g : g + 2], pieces_far.at[:, g : g + 2, 2:5])
    edge_inner[...] = packed
    edge_x[...] = packed_x
    far.send(edge_inner, edge_inner_far)
    far.send(edge_x, edge_x_far)
    far.finish()


def split(value):
    high = value.astype(BF)
    return high, (value - high.astype(F32)).astype(BF)


def exact_dot(value, onehot):
    high, low = split(value)
    return dot(high, onehot) + dot(low, onehot)


def inner_kernel(
    d_far, arrived, slope_far, hidden_far, edge_inner_far, edge_x_far, from_left, from_right,
    weights_far, mixer_far, back_far, pieces_in, cg, cb, mg, mb,
    grad_inner_far, down, up, half_sum_far, pieces_far, edge_block_far, gmi, taps_out, hidden_out, rim_wide,
    d, slope, hidden, edge_inner, edge_x, weights, mixer, back, grad_inner, half_sum, ends, edge_block, buffer, rows, sems,
):
    far = Far(sems)
    loads = [far.start(d_far.at[2 * p : 2 * p + 2], d.at[2 * p : 2 * p + 2]) for p in range(GROUPS // 2)]
    first = [far.start(weights_far.at[0:MR], weights.at[0:MR])]
    first.append(far.start(weights_far.at[2 * MR : 3 * MR], weights.at[MR : 2 * MR]))
    first += [far.start(edge_inner_far, edge_inner), far.start(edge_x_far, edge_x), far.start(mixer_far, mixer)]
    tails = [
        far.start(pieces_in.at[r, :, 2:5], ends.at[i]) for i, r in enumerate((0, ROWS - 1))
    ]
    later = [far.start(back_far, back), far.start(slope_far, slope), far.start(hidden_far, hidden)]
    lane, lane_c = lanes_of(MR), lanes_of(CR)
    gain, shift = splat(cg, MID), splat(cb, MID)
    gain_out, shift_out = splat(mg, CH), splat(mb, CH)
    rim = merge_edges(from_left[...].astype(F32), from_right[...].astype(F32))
    rows[...] = rim
    for m in range(4):
        to = slice(m * LANES, (m + 1) * LANES)
        for p, (start, step) in enumerate(((0, 4), (0, 8), (4, 8), (CR // 2, 4))):
            part = rows[pl.ds(start + m, CH, stride=step), :]
            if step == 4:
                part = pltpu.roll(part, 64, 1)
            rim_wide[64 * p : 64 * p + CH, to] = part.astype(BF)
    for p in range(4):
        rim_wide[64 * p + CH : 64 * p + 64, :] = jnp.zeros((64 - CH, 4 * LANES), BF)
    rim = rim.astype(BF)
    for pair in range(GROUPS // 2):
        loads[pair].wait()
        swap_in(arrived, 2 * pair, buffer)
        for half in range(2):
            g = 2 * pair + half
            both = 0.5 * (d[g].astype(F32) + buffer[half].astype(F32)).reshape(CR, LANES)
            half_sum[g] = both.reshape(CH, H, LANES)
            gmi[:, g * LANES : (g + 1) * LANES] = (both * gain_out).astype(BF)
        far.send(half_sum.at[2 * pair : 2 * pair + 2], half_sum_far.at[2 * pair : 2 * pair + 2])
    for load in first:
        load.wait()
    outer = dot(weights[:, 0:CR], rim) + pltpu.roll(dot(weights[:, CR : 2 * CR], rim), 64, 1)
    outer = jnp.where(lane % 8 < 4, outer[MR : 2 * MR], outer[0:MR])
    pre = (edge_inner[...] + outer) * gain + shift
    slope_edge = smooth_slope(pre) * gain
    hidden_edge = smooth(pre).astype(BF)
    mixed = dot(mixer[...], hidden_edge)
    value = (edge_x[...] + mixed * gain_out + shift_out).astype(BF)
    edge_block[...] = value.astype(F32)
    far.send(edge_block, edge_block_far)
    hidden_edge = hidden_edge.astype(F32)
    parts = value.astype(F32).reshape(3, ROWS, H, LANES)
    parts = swap_blocks([parts[:, i].reshape(3 * H, LANES) for i in range(ROWS)])
    for load in tails:
        load.wait()
    low = iota((3, H, LANES), 2) % 8 < 4
    for g in range(GROUPS):
        lower = pltpu.roll(parts[g], LANES - 4, 1).reshape(3, H, LANES)
        upper = pltpu.roll(parts[g], 4, 1).reshape(3, H, LANES)
        ends[0, g] = jnp.where(low, lower, ends[0, g].astype(F32)).astype(BF)
        ends[1, g] = jnp.where(low, ends[1, g].astype(F32), upper).astype(BF)
    for i, r in enumerate((0, ROWS - 1)):
        far.send(ends.at[i], pieces_far.at[r, :, 2:5])

    for load in later:
        load.wait()
    packed = jnp.zeros((MR, LANES), F32)
    for pair in range(GROUPS // 2):
        two = slice(pair * 2 * LANES, (pair + 1) * 2 * LANES)
        into = dot(back[...], gmi[:, two])
        for half in range(2):
            g = 2 * pair + half
            at = slice(g * LANES, (g + 1) * LANES)
            turn = (124 - 8 * g) % LANES
            here = jnp.where(at_edge(lane), pltpu.roll(slope_edge, turn, 1), slope[:, at])
            value = into[:, half * LANES : (half + 1) * LANES] * here
            grad_inner[g] = value.reshape(MID, H, LANES).astype(BF)
            rows[0:MR] = value
            for r in range(H):
                part = jnp.concatenate([rows[pl.ds(r, MID, stride=8), :], jnp.zeros((H, LANES), F32)], axis=0)
                lane_t = lanes_of(MID + H)
                three = (
                    jnp.where(lane_t < 124, pltpu.roll(part, LANES - 4, 1), 0.0),
                    part,
                    jnp.where(lane_t >= 4, pltpu.roll(part, 4, 1), 0.0),
                )
                to = slice((r % 4 * GROUPS + g) * LANES, (r % 4 * GROUPS + g + 1) * LANES)
                for b in range(3):
                    top = 32 * (3 * (r // 4) + b)
                    taps_out[top : top + 32, to] = three[b].astype(BF)
            packed = jnp.where(lane // 8 == g, pltpu.roll(value, (8 * g - 124) % LANES, 1), packed)
            here = jnp.where(at_edge(lane), pltpu.roll(hidden_edge, turn, 1), hidden[:, at].astype(F32))
            hidden_out[:, at] = here.astype(BF)
        far.send(grad_inner.at[2 * pair : 2 * pair + 2], grad_inner_far.at[2 * pair : 2 * pair + 2])
    send_rows(grad_inner, down, up, MID)
    rows[0:MR] = packed
    for r in range(H):
        part = jnp.concatenate([rows[pl.ds(r, MID, stride=8), :], jnp.zeros((H, LANES), F32)], axis=0)
        lane_t = lanes_of(MID + H)
        low = jnp.where(lane_t % 8 < 4, part, 0.0)
        three = (part - low, jnp.zeros_like(part), low)
        to = slice(4 * POS + r % 4 * LANES, 4 * POS + (r % 4 + 1) * LANES)
        for b in range(3):
            top = 32 * (3 * (r // 4) + b)
            taps_out[top : top + 32, to] = three[b].astype(BF)
    far.finish()


def sums_kernel(wide_far, gmi, taps, hidden, rim_wide, pieces_in, pieces_far, wide, sums_out, sems):
    far = Far(sems)
    load = far.start(wide_far, wide)
    sums_out[ROWS - 1] = jnp.zeros((COLS, 2, H, LANES), BF)
    far.send(sums_out.at[ROWS - 1], pieces_far.at[ROWS - 1, :, 0:2])
    mixwide = dot(hidden[...], gmi[...], NT)
    h, col = iota((H, CR), 0), iota((H, CR), 1)
    same = jnp.where(col % 8 == h, 1.0, 0.0)[None]
    mixed = jnp.sum(mixwide.reshape(MID, H, CR) * same, axis=1)
    col, lane_s = iota((CR, LANES), 0), iota((CR, LANES), 1)
    mixed = exact_dot(mixed, jnp.where(col // 8 + 64 == lane_s, 1.0, 0.0).astype(BF))
    total = dot(taps[:, 4 * POS :], rim_wide[...], NT)
    load.wait()
    total += dot(taps[:, 0 : 4 * POS], wide[...], NT)
    lane = lanes_of(MID)
    blocks, thirds = [], []
    for b in range(3):
        near, next_one = total[32 * b : 32 * b + MID], total[32 * (3 + b) : 32 * (3 + b) + MID]
        moved = pltpu.roll(next_one[:, 0:LANES], 64, 1)
        ahead = pltpu.roll(next_one[:, LANES : 2 * LANES], 64, 1)
        blocks.append(near[:, 0:LANES] + jnp.where(lane < 64, moved, ahead))
        thirds.append(jnp.where(lane < 64, near[:, LANES : 2 * LANES] + ahead, 0.0))
    blocks.append(thirds[0] + pltpu.roll(thirds[1], 64, 1))
    blocks.append(thirds[2] + mixed)
    for p in range(5):
        high = blocks[p].astype(BF).astype(F32)
        low = blocks[p] - high
        for k in range(3):
            r = 3 * p + k
            at = slice(k * H, (k + 1) * H)
            sums_out[r, :, 0] = jnp.broadcast_to(high[at][None], (COLS, H, LANES)).astype(BF)
            sums_out[r, :, 1] = jnp.broadcast_to(low[at][None], (COLS, H, LANES)).astype(BF)
        far.send(sums_out.at[3 * p : 3 * p + 3], pieces_far.at[3 * p : 3 * p + 3, :, 0:2])
    far.finish()


def spread_kernel(
    grad_inner_far, above, below, w, half_far, x_far, block_far, edge_block_far,
    edge, out_far, edge_value_far, edge_slope_far, block_out_far,
    weights, rhs, grad_inner, half_sum, x, block, edge_block, out, edge_value, edge_slope, sems,
):
    far = Far(sems)
    first = far.start(grad_inner_far, grad_inner)
    loads = [far.start(half_far, half_sum), far.start(x_far, x)]
    last = [far.start(block_far, block), far.start(edge_block_far, edge_block)]
    back_weights(w, weights)
    first.wait()
    lane = lanes_of(CR)
    packed, packed_value, packed_slope = (jnp.zeros((CR, LANES), F32) for _ in range(3))
    for load in loads:
        load.wait()
    for pair in range(GROUPS // 2):
        for half in range(2):
            g = 2 * pair + half
            at = slice(half * LANES, (half + 1) * LANES)
            rhs[0:MR, at] = grad_inner[g].astype(F32).reshape(MR, LANES).astype(BF)
            rhs[MR : MR + MR // 2, at] = above[g].astype(F32).reshape(MR // 2, LANES).astype(BF)
            rhs[MR + MR // 2 : 2 * MR, at] = below[g].astype(F32).reshape(MR // 2, LANES).astype(BF)
        product = dot(weights[...], rhs[...])
        for half in range(2):
            g = 2 * pair + half
            p = product[:, half * LANES : (half + 1) * LANES]
            left, mid, right = p[0:CR], p[CR : 2 * CR], p[2 * CR : 3 * CR]
            total = (
                mid
                + jnp.where(lane < 124, pltpu.roll(left, LANES - 4, 1), 0.0)
                + jnp.where(lane >= 4, pltpu.roll(right, 4, 1), 0.0)
            )
            slope = smooth_slope(x[g].astype(F32).reshape(CR, LANES))
            value = half_sum[g].reshape(CR, LANES) + total * slope
            out[g] = value.reshape(CH, H, LANES).astype(BF)
            far.send(out.at[g], out_far.at[g])
            here = lane // 8 == g
            turn_by = (8 * g - 124) % LANES
            packed = jnp.where(here, pltpu.roll(jnp.where(lane >= 124, right, left), turn_by, 1), packed)
            packed_value = jnp.where(here, pltpu.roll(value, turn_by, 1), packed_value)
            packed_slope = jnp.where(here, pltpu.roll(slope, turn_by, 1), packed_slope)
    edge[...] = packed[0 : CR // 2] + pltpu.roll(packed[CR // 2 : CR], 64, 1)
    edge_value[...] = packed_value
    edge_slope[...] = packed_slope
    far.send(edge_value, edge_value_far)
    far.send(edge_slope, edge_slope_far)
    for load in last:
        load.wait()
    for g in range(GROUPS):
        moved = pltpu.roll(edge_block[...], (124 - 8 * g) % LANES, 1)
        value = jnp.where(at_edge(lane), moved, block[g].astype(F32).reshape(CR, LANES))
        block[g] = value.reshape(CH, H, LANES).astype(BF)
        far.send(block.at[g], block_out_far.at[g])
    far.finish()


def total_kernel(arrived, out):
    total = jnp.zeros((H, LANES), F32)
    for g in range(COLS):
        part = arrived[:, g, 0:2].astype(F32)
        total += jnp.sum(part[:, 0] + part[:, 1], axis=0)
    out[...] = jnp.broadcast_to((total * (1.0 / (ROWS * H * COLS)))[None], (ROWS, H, LANES))


def last_kernel(
    block_far, arrived_far, value_far, edge_value_far, edge_slope_far, from_left, from_right, out_far, grad_far,
    block, arrived, out, value, grad, edge_value, edge_slope, sems,
):
    far = Far(sems)
    first = [far.start(edge_value_far, edge_value), far.start(edge_slope_far, edge_slope)]
    loads = [far.start(value_far.at[g], value.at[g]) for g in range(GROUPS)]
    later = [
        (far.start(block_far.at[g], block.at[g]), far.start(arrived_far.at[:, g, 2:5], arrived.at[:, g]))
        for g in range(GROUPS)
    ]
    lane = lanes_of(CR)
    rim = merge_edges(from_left[...], from_right[...])
    rim = jnp.concatenate([rim, pltpu.roll(rim, 64, 1)], axis=0)
    for load in first:
        load.wait()
    rim = edge_value[...] + rim * edge_slope[...]
    for g in range(GROUPS):
        loads[g].wait()
        moved = pltpu.roll(rim, (124 - 8 * g) % LANES, 1)
        total = jnp.where(at_edge(lane), moved, value[g].astype(F32).reshape(CR, LANES))
        grad[g] = total.reshape(CH, H, LANES).astype(BF)
        far.send(grad.at[g], grad_far.at[g])
    for g in range(GROUPS):
        for load in later[g]:
            load.wait()
        for k in range(3):
            at = slice(k * ROWS, (k + 1) * ROWS)
            both = 0.5 * (block[g, at].astype(F32) + turn(arrived[:, g, k]).astype(F32))
            out[g, at] = both.astype(BF)
        far.send(out.at[g], out_far.at[g])
    far.finish()


def unpack_kernel(tiles, conv, mix):
    order = ((0, 3), (1, 4), (2, 5), (6, 7), (8, None))
    for p, (left, right) in enumerate(order):
        value = tiles[3 * p : 3 * p + 3].reshape(3 * H, LANES)
        conv[left] = value[:, 0:CH]
        if right is None:
            mix[...] = value[:, 64 : 64 + CH]
        else:
            conv[right] = value[:, 64 : 64 + CH]


def both_ways(first, second, axis):
    count = lax.axis_size(axis)
    onward = [(i, (i + 1) % count) for i in range(count)]
    back = [(t, s) for s, t in onward]
    return lax.ppermute(first, axis, onward), lax.ppermute(second, axis, back)


def local(pair_map, cotangent, conv_weight, conv_gain, conv_bias, mix_weight, mix_gain, mix_bias):
    tile = (GROUPS, CH, H, LANES)
    cut = (ROWS, COLS, 3, H, LANES)
    everyone = ("row", "col")
    vmem = pltpu.VMEM
    down, up, d_pieces = call(
        first_kernel, [((GROUPS, CH // 2, H, LANES), BF)] * 2 + [(cut, BF)], (pair_map, cotangent), "first",
        far=(0, 1), far_out=(2,), scratch=[vmem(tile, BF), vmem(tile, BF), vmem(cut, BF)], copies=3 * GROUPS,
    )
    above, below = both_ways(down, up, "row")
    d_arrived = lax.all_to_all(d_pieces.reshape(ROWS * COLS, 3, H, LANES), everyone, 0, 0, tiled=True)
    d_arrived = d_arrived.reshape(cut)

    taps = jnp.transpose(conv_weight, (2, 3, 0, 1)).reshape(9, MID, CH)
    wf, mf, wf_far, mf_far, mbk = call(
        weights_kernel,
        [((3 * MR, 2 * CR), BF), ((CR, MR), BF)] * 2 + [((MR, CR), BF)],
        (taps, mix_weight.T), "weights", far_out=(2, 3, 4), scratch=[vmem((MR, CR), BF)], copies=3,
    )
    act, edge, wide = call(
        act_kernel,
        [((2 * CR, POS), BF), ((CR, LANES), BF), ((256, 4 * POS), BF)],
        (pair_map, above, below), "act", far_out=(2,), copies=1,
        scratch=[vmem((256, 4 * POS), BF), vmem((2 * CR, LANES), F32)],
    )
    from_left, from_right = both_ways(edge, edge, "col")
    five = (ROWS, COLS, 5, H, LANES)
    slope, hidden, block, pieces, edge_inner, edge_x = call(
        inside_kernel,
        [((MR, POS), F32), ((MR, POS), BF), (tile, BF), (five, BF), ((MR, LANES), F32), ((CR, LANES), F32)],
        (pair_map, act, wf, mf, conv_gain, conv_bias, mix_gain, mix_bias),
        "inside", smem=(4, 5, 6, 7), far_out=(0, 1, 2, 3, 4, 5),
        scratch=[
            vmem((MR, POS), F32), vmem((MR, POS), BF), vmem(tile, BF), vmem(cut, BF),
            vmem((MR, LANES), F32), vmem((CR, LANES), F32),
        ],
        copies=2 * GROUPS + 2,
    )
    grad_inner, g_down, g_up, half_sum, pieces, edge_block, gmi, tap_rows, hidden, rim_wide = call(
        inner_kernel,
        [
            ((GROUPS, MID, H, LANES), BF),
            ((GROUPS, MID // 2, H, LANES), BF),
            ((GROUPS, MID // 2, H, LANES), BF),
            (tile, F32),
            (five, BF),
            ((CR, LANES), F32),
            ((CR, POS), BF),
            ((192, 4 * POS + 4 * LANES), BF),
            ((MR, POS), BF),
            ((256, 4 * LANES), BF),
        ],
        (
            cotangent, d_arrived, slope, hidden, edge_inner, edge_x, from_left, from_right,
            wf_far, mf_far, mbk, pieces, conv_gain, conv_bias, mix_gain, mix_bias,
        ),
        "inner", smem=(12, 13, 14, 15), far=(0, 2, 3, 4, 5, 8, 9, 10, 11), far_out=(0, 3, 4, 5), alias={11: 4},
        scratch=[
            vmem(tile, BF), vmem((MR, POS), F32), vmem((MR, POS), BF), vmem((MR, LANES), F32), vmem((CR, LANES), F32),
            vmem((2 * MR, 2 * CR), BF), vmem((CR, MR), BF), vmem((MR, CR), BF),
            vmem((GROUPS, MID, H, LANES), BF), vmem(tile, F32), vmem((2, COLS, 3, H, LANES), BF),
            vmem((CR, LANES), F32), vmem((2, CH, H, LANES), BF), vmem((CR, LANES), F32),
        ],
        copies=25,
    )
    g_above, g_below = both_ways(g_down, g_up, "row")
    (pieces,) = call(
        sums_kernel, [(five, BF)], (wide, gmi, tap_rows, hidden, rim_wide, pieces), "sums",
        far=(0, 5), far_out=(0,), alias={5: 0},
        scratch=[vmem((256, 4 * POS), BF), vmem((ROWS, COLS, 2, H, LANES), BF)], copies=7,
    )
    pieces, g_above, g_below = lax.optimization_barrier((pieces, g_above, g_below))
    arrived = lax.all_to_all(pieces.reshape(ROWS * COLS, 5, H, LANES), everyone, 0, 0, tiled=True)
    arrived = arrived.reshape(five)
    (sums,) = call(
        total_kernel, [((ROWS, H, LANES), F32)], (arrived,), "total", flops=500_000_000
    )
    spread_sums = lax.all_to_all(sums, "row", 0, 0, tiled=True)
    taps, _ = lax.optimization_barrier((taps, pieces))
    g_edge, inputs, edge_value, edge_slope, block = call(
        spread_kernel,
        [((CR // 2, LANES), F32), (tile, BF), ((CR, LANES), F32), ((CR, LANES), F32), (tile, BF)],
        (grad_inner, g_above, g_below, taps, half_sum, pair_map, block, edge_block),
        "spread", far=(0, 4, 5, 6, 7), far_out=(1, 2, 3, 4), copies=2 * GROUPS + 7,
        scratch=[
            vmem((3 * CR, 2 * MR), BF), vmem((2 * MR, 2 * LANES), BF), vmem((GROUPS, MID, H, LANES), BF),
            vmem(tile, F32), vmem(tile, BF), vmem(tile, BF), vmem((CR, LANES), F32), vmem(tile, BF),
            vmem((CR, LANES), F32), vmem((CR, LANES), F32),
        ],
    )
    g_left, g_right = both_ways(g_edge, g_edge, "col")
    g_left, g_right, block, _ = lax.optimization_barrier((g_left, g_right, block, sums))
    symmetric, grad_input = call(
        last_kernel, [(tile, BF)] * 2, (block, arrived, inputs, edge_value, edge_slope, g_left, g_right), "last",
        far=(0, 1, 2, 3, 4), far_out=(0, 1), copies=5 * GROUPS + 2,
        scratch=[
            vmem(tile, BF), vmem(cut, BF), vmem(tile, BF), vmem(tile, BF), vmem(tile, BF),
            vmem((CR, LANES), F32), vmem((CR, LANES), F32),
        ],
    )
    conv, mix = call(
        unpack_kernel, [((9, MID, CH), F32), ((MID, CH), F32)], (spread_sums,), "unpack", flops=100_000_000
    )
    grad_conv = jnp.transpose(conv.reshape(3, 3, MID, CH), (2, 3, 0, 1))
    return symmetric, grad_input, grad_conv, mix.T


def solution(mesh):
    field = P(None, None, "row", "col")
    return jax.shard_map(
        local,
        mesh=mesh,
        in_specs=(field, field, P(), P(), P(), P(), P(), P()),
        out_specs=(field, field, P(), P()),
        check_vma=False,
    )
```

```python
import functools

import jax
import jax.numpy as jnp
from jax import lax
from jax.experimental import pallas as pl
from jax.experimental.pallas import tpu as pltpu
from jax.sharding import PartitionSpec as P

BF = jnp.bfloat16
F32 = jnp.float32
CH, MID, GROUPS, H, LANES, ROWS, COLS = 48, 24, 8, 8, 128, 16, 8
POS = GROUPS * LANES
CR, MR = CH * H, MID * H
TANH_SCALE = 0.7978845608028654
CUBIC = 0.044715
NN = (((1,), (0,)), ((), ()))
NT = (((1,), (1,)), ((), ()))
TN = (((0,), (0,)), ((), ()))


def smooth(v):
    t = jnp.tanh(TANH_SCALE * (v + CUBIC * (v * v * v)))
    return 0.5 * v * (1.0 + t)


def smooth_slope(v):
    s = v * v
    t = jnp.tanh(TANH_SCALE * (v + CUBIC * (v * s)))
    return 0.5 * (1.0 + t) + (0.5 * v) * (1.0 - t * t) * (TANH_SCALE * (1.0 + (3.0 * CUBIC) * s))


def smooth_both(v):
    s = v * v
    t = jnp.tanh(TANH_SCALE * (v + CUBIC * (v * s)))
    upper, half = 0.5 * (1.0 + t), 0.5 * v
    return half * (1.0 + t), upper + half * (1.0 - t * t) * (TANH_SCALE * (1.0 + (3.0 * CUBIC) * s))


def dot(a, b, dims=NN):
    return lax.dot_general(a, b, dims, preferred_element_type=F32)


def iota(shape, dim):
    return lax.broadcasted_iota(jnp.int32, shape, dim)


def identity(n):
    return jnp.where(iota((n, n), 0) == iota((n, n), 1), 1.0, 0.0).astype(BF)


def lanes_of(rows):
    return iota((rows, LANES), 1)


class Far:
    def __init__(self, sems):
        self.sems, self.used, self.open = sems, 0, []

    def start(self, source, target):
        copy = pltpu.make_async_copy(source, target, self.sems.at[self.used])
        self.used += 1
        copy.start()
        return copy

    def send(self, source, target):
        self.open.append(self.start(source, target))

    def finish(self):
        for copy in self.open:
            copy.wait()


def call(kernel, outs, args, name, smem=(), far=(), far_out=(), flops=4_000_000_000, scratch=(), copies=0, limit=16, alias=None):
    specs = [
        pl.BlockSpec(memory_space=pltpu.SMEM if i in smem else pltpu.HBM if i in far else pltpu.VMEM)
        for i in range(len(args))
    ]
    scratch = list(scratch)
    if copies:
        scratch.append(pltpu.SemaphoreType.DMA((copies,)))
    return pl.pallas_call(
        kernel,
        name=name,
        out_shape=[
            pltpu.HBM(s, t) if i in far_out else jax.ShapeDtypeStruct(s, t)
            for i, (s, t) in enumerate(outs)
        ],
        in_specs=specs,
        out_specs=[
            pl.BlockSpec(memory_space=pltpu.HBM if i in far_out else pltpu.VMEM)
            for i in range(len(outs))
        ],
        scratch_shapes=scratch,
        input_output_aliases=alias or {},
        compiler_params=pltpu.CompilerParams(vmem_limit_bytes=limit * 1024 * 1024),
        cost_estimate=pl.CostEstimate(flops=flops, bytes_accessed=1_000_000, transcendentals=0),
    )(
        *(
            pltpu.with_memory_space_constraint(v, pltpu.HBM) if i in far else v
            for i, v in enumerate(args)
        )
    )


def splat(values, count):
    return jnp.concatenate([jnp.full((H, LANES), values[o], F32) for o in range(count)], axis=0)


def pack_rows(field, count):
    pairs = field.reshape(count // 2, 2, H, LANES)
    even, odd = pairs[:, 0], pairs[:, 1]
    low = iota(even.shape, 1) < 4
    last = jnp.where(low, pltpu.roll(even, 4, 1), odd)
    first = jnp.where(low, even, pltpu.roll(odd, 4, 1))
    return last, first


def send_rows(source, down, up, count):
    at_end = (lax.axis_index("row") == ROWS - 1).astype(jnp.int32)
    at_start = (lax.axis_index("row") == 0).astype(jnp.int32)
    for g in range(GROUPS):
        before = g - at_end
        last, _ = pack_rows(source[jnp.maximum(before, 0)].astype(F32), count)
        down[g] = jnp.where(before >= 0, last, 0.0).astype(BF)
        after = g + at_start
        _, first = pack_rows(source[jnp.minimum(after, GROUPS - 1)].astype(F32), count)
        up[g] = jnp.where(after < GROUPS, first, 0.0).astype(BF)


def swap_blocks(parts):
    lane = iota(parts[0].shape, 1)
    parts = list(parts)
    for k in range(4):
        m = 1 << k
        high = (lane // (8 * m)) % 2 == 1
        for i in range(ROWS):
            if i & m:
                continue
            a, b = parts[i], parts[i | m]
            parts[i] = jnp.where(high, pltpu.roll(b, 8 * m, 1), a)
            parts[i | m] = jnp.where(high, b, pltpu.roll(a, LANES - 8 * m, 1))
    return parts


def turn(tiles):
    return tiles.reshape(LANES, LANES).T.reshape(ROWS, H, LANES)


def swap_in(pieces, g, buffer):
    parts = swap_blocks([pieces[r, g : g + 2].reshape(6 * H, LANES) for r in range(ROWS)])
    for i in range(ROWS):
        value = parts[i].reshape(2, 3, H, LANES)
        for n in range(2):
            for k in range(3):
                buffer[n, k * ROWS + i] = value[n, k]


def swap_out(block, pieces, g):
    parts = swap_blocks(
        [
            jnp.concatenate([block[g + n, k * ROWS + i] for n in range(2) for k in range(3)], axis=0)
            for i in range(ROWS)
        ]
    )
    for r in range(ROWS):
        pieces[r, g : g + 2] = parts[r].reshape(2, 3, H, LANES)


def first_kernel(x_far, d_far, down, up, pieces, x, d, turned, sems):
    far = Far(sems)
    loads = [far.start(d_far.at[g], d.at[g]) for g in range(GROUPS)]
    later = [far.start(x_far.at[g], x.at[g]) for g in range(GROUPS)]
    for g in range(GROUPS):
        loads[g].wait()
        for k in range(3):
            turned[:, g, k] = turn(d[g, k * ROWS : (k + 1) * ROWS])
        far.send(turned.at[:, g], pieces.at[:, g])
    for load in later:
        load.wait()
    send_rows(x, down, up, CH)
    far.finish()


def spread_channels(n, own, width):
    col = iota((n, width), 1)
    half = (width - own) // 2
    rim = jnp.where(col < own + half, col - own, col - own - half) // 4
    return jnp.where(jnp.where(col < own, col // 8, rim) == iota((n, width), 0), 1.0, 0.0).astype(BF)


def row_distance(own, width):
    col, h = iota((H, width), 1), iota((H, width), 0)
    half = (width - own) // 2
    rim = jnp.where(col < own + half, (col - own) % 4 - 4, (col - own - half) % 4 + 8)
    return jnp.where(col < own, col % 8, rim) - h


def weights_kernel(w, mix, a_out, mf_out, a_far, mf_far, mb_far, mb_out, sems):
    far = Far(sems)
    sf, st = spread_channels(CH, CR, 2 * CR), spread_channels(MID, MR, MR)
    pf, pt = row_distance(CR, 2 * CR), row_distance(MR, MR)
    masks = [jnp.where(pf == 4 * (a - 1), 1.0, 0.0)[None] for a in range(3)]
    col = iota((CH, CR), 1)
    above = jnp.where(col < CR // 2, sf[:, CR:].astype(F32), 0.0).astype(BF)
    below = jnp.where(col < CR // 2, 0.0, sf[:, CR:].astype(F32)).astype(BF)
    for b in range(3):
        total = jnp.zeros((MID, H, CR), F32)
        for a in range(3):
            total += dot(w[3 * a + b], sf[:, :CR])[:, None, :] * masks[a][:, :, :CR]
        rest = (dot(w[b], above) + dot(w[6 + b], below))[:, None, :] * (masks[0] + masks[2])[:, :, CR:]
        a_out[b * MR : (b + 1) * MR, 0:CR] = total.reshape(MR, CR).astype(BF)
        a_out[b * MR : (b + 1) * MR, CR : 2 * CR] = rest.reshape(MR, CR).astype(BF)
    far.send(a_out, a_far)
    mask = jnp.where(pf[:, :CR] == 0, 1.0, 0.0)
    mb_out[...] = (dot(mix[...], sf[:, :CR])[:, None, :] * mask[None]).reshape(MR, CR).astype(BF)
    far.send(mb_out, mb_far)
    mask = jnp.where(pt == 0, 1.0, 0.0)
    mf_out[...] = (dot(mix[...], st, TN)[:, None, :] * mask[None]).reshape(CR, MR).astype(BF)
    far.send(mf_out, mf_far)
    far.finish()


def back_weights(w, out):
    st, pt = spread_channels(MID, MR, 2 * MR), row_distance(MR, 2 * MR)
    masks = [jnp.where(pt == -4 * (a - 1), 1.0, 0.0)[None] for a in range(3)]
    for b in range(3):
        total = jnp.zeros((CH, H, 2 * MR), F32)
        for a in range(3):
            total += dot(w[3 * a + b], st, TN)[:, None, :] * masks[a]
        out[b * CR : (b + 1) * CR] = total.reshape(CR, 2 * MR).astype(BF)


def act_kernel(x, above, below, act, edge, wide_far, wide, rows, sems):
    far = Far(sems)
    for p in range(4):
        wide[64 * p + CH : 64 * p + 64, :] = jnp.zeros((64 - CH, 4 * POS), BF)
    lane = lanes_of(CR)
    packed = jnp.zeros((CR, LANES), F32)
    for g in range(GROUPS):
        own = smooth(x[g].astype(F32).reshape(CR, LANES))
        high = smooth(above[g].astype(F32).reshape(CR // 2, LANES))
        low = smooth(below[g].astype(F32).reshape(CR // 2, LANES))
        rim = jnp.concatenate([high, low], axis=0)
        at = slice(g * LANES, (g + 1) * LANES)
        act[0:CR, at] = own.astype(BF)
        act[CR : 2 * CR, at] = rim.astype(BF)
        rows[0:CR] = own
        rows[CR : 2 * CR] = rim
        for m in range(4):
            to = slice((m * GROUPS + g) * LANES, (m * GROUPS + g + 1) * LANES)
            for p, (start, step) in enumerate(((CR, 4), (0, 8), (4, 8), (CR + CR // 2, 4))):
                wide[64 * p : 64 * p + CH, to] = rows[pl.ds(start + m, CH, stride=step), :].astype(BF)
            far.send(wide.at[:, to], wide_far.at[:, to])
        packed = jnp.where(lane // 8 == g, pltpu.roll(own, (8 * g - 124) % LANES, 1), packed)
        packed = jnp.where(lane // 8 == 8 + g, pltpu.roll(rim, (8 * g - 60) % LANES, 1), packed)
    edge[...] = packed.astype(BF)
    far.finish()


def merge_edges(from_left, from_right):
    lane = lanes_of(from_left.shape[0])
    col = lax.axis_index("col")
    has_left = jnp.where(col > 0, 1.0, 0.0)
    has_right = jnp.where(col < COLS - 1, 1.0, 0.0)
    return jnp.where(
        lane % 8 < 4,
        pltpu.roll(from_right, LANES - 4, 1) * has_right,
        pltpu.roll(from_left, 4, 1) * has_left,
    )


def at_edge(lane):
    return jnp.logical_or(lane < 4, lane >= 124)


def inside_kernel(
    x, act, weights, mixer, cg, cb, mg, mb,
    slope_far, hidden_far, block_far, pieces_far, edge_inner_far, edge_x_far,
    slope, hidden, block, pieces, edge_inner, edge_x, sems,
):
    far = Far(sems)
    lane, lane_c = lanes_of(MR), lanes_of(CR)
    gain, shift = splat(cg, MID), splat(cb, MID)
    gain_out, shift_out = splat(mg, CH), splat(mb, CH)
    packed, packed_x = jnp.zeros((MR, LANES), F32), jnp.zeros((CR, LANES), F32)
    for pair in range(GROUPS // 2):
        two = slice(pair * 2 * LANES, (pair + 1) * 2 * LANES)
        product = dot(weights[...], act[:, two])
        for half in range(2):
            g = 2 * pair + half
            p = product[:, half * LANES : (half + 1) * LANES]
            inner = (
                p[MR : 2 * MR]
                + jnp.where(lane < 4, 0.0, pltpu.roll(p[0:MR], 4, 1))
                + jnp.where(lane >= 124, 0.0, pltpu.roll(p[2 * MR : 3 * MR], LANES - 4, 1))
            )
            packed = jnp.where(lane // 8 == g, pltpu.roll(inner, (8 * g - 124) % LANES, 1), packed)
            pre = inner * gain + shift
            at = slice(g * LANES, (g + 1) * LANES)
            smoothed, steep = smooth_both(pre)
            slope[:, at] = steep * gain
            hidden[:, at] = smoothed.astype(BF)
        far.send(slope.at[:, two], slope_far.at[:, two])
        far.send(hidden.at[:, two], hidden_far.at[:, two])
        mixed = dot(mixer[...], hidden[:, two])
        for half in range(2):
            g = 2 * pair + half
            m = mixed[:, half * LANES : (half + 1) * LANES]
            own = x[g].astype(F32).reshape(CR, LANES)
            packed_x = jnp.where(lane_c // 8 == g, pltpu.roll(own, (8 * g - 124) % LANES, 1), packed_x)
            value = (own + m * gain_out + shift_out).astype(BF)
            block[g] = value.astype(F32).reshape(CH, H, LANES).astype(BF)
        g = 2 * pair
        far.send(block.at[g : g + 2], block_far.at[g : g + 2])
        swap_out(block, pieces, g)
        far.send(pieces.at[:, g : g + 2], pieces_far.at[:, g : g + 2, 2:5])
    edge_inner[...] = packed
    edge_x[...] = packed_x
    far.send(edge_inner, edge_inner_far)
    far.send(edge_x, edge_x_far)
    far.finish()


def split(value):
    high = value.astype(BF)
    return high, (value - high.astype(F32)).astype(BF)


def exact_dot(value, onehot):
    high, low = split(value)
    return dot(high, onehot) + dot(low, onehot)


def inner_kernel(
    d_far, arrived, slope_far, hidden_far, edge_inner_far, edge_x_far, from_left, from_right,
    weights_far, mixer_far, back_far, pieces_in, cg, cb, mg, mb, wide_far,
    grad_inner_far, down, up, half_sum_far, pieces_far, edge_block_far, gmi, taps_out, hidden_out, rim_wide, wide,
    d, slope, hidden, edge_inner, edge_x, weights, mixer, back, grad_inner, half_sum, ends, edge_block, buffer, rows, sems,
):
    far = Far(sems)
    loads = [far.start(d_far.at[2 * p : 2 * p + 2], d.at[2 * p : 2 * p + 2]) for p in range(GROUPS // 2)]
    first = [far.start(weights_far.at[0:MR], weights.at[0:MR])]
    first.append(far.start(weights_far.at[2 * MR : 3 * MR], weights.at[MR : 2 * MR]))
    first += [far.start(edge_inner_far, edge_inner), far.start(edge_x_far, edge_x), far.start(mixer_far, mixer)]
    tails = [
        far.start(pieces_in.at[r, :, 2:5], ends.at[i]) for i, r in enumerate((0, ROWS - 1))
    ]
    later = [far.start(back_far, back), far.start(slope_far, slope), far.start(hidden_far, hidden)]
    far.send(wide_far, wide)
    lane, lane_c = lanes_of(MR), lanes_of(CR)
    gain, shift = splat(cg, MID), splat(cb, MID)
    gain_out, shift_out = splat(mg, CH), splat(mb, CH)
    rim = merge_edges(from_left[...].astype(F32), from_right[...].astype(F32))
    rows[...] = rim
    for m in range(4):
        to = slice(m * LANES, (m + 1) * LANES)
        for p, (start, step) in enumerate(((0, 4), (0, 8), (4, 8), (CR // 2, 4))):
            part = rows[pl.ds(start + m, CH, stride=step), :]
            if step == 4:
                part = pltpu.roll(part, 64, 1)
            rim_wide[64 * p : 64 * p + CH, to] = part.astype(BF)
    for p in range(4):
        rim_wide[64 * p + CH : 64 * p + 64, :] = jnp.zeros((64 - CH, 4 * LANES), BF)
    rim = rim.astype(BF)
    for pair in range(GROUPS // 2):
        loads[pair].wait()
        swap_in(arrived, 2 * pair, buffer)
        for half in range(2):
            g = 2 * pair + half
            both = 0.5 * (d[g].astype(F32) + buffer[half].astype(F32)).reshape(CR, LANES)
            half_sum[g] = both.reshape(CH, H, LANES)
            gmi[:, g * LANES : (g + 1) * LANES] = (both * gain_out).astype(BF)
        far.send(half_sum.at[2 * pair : 2 * pair + 2], half_sum_far.at[2 * pair : 2 * pair + 2])
    for load in first:
        load.wait()
    outer = dot(weights[:, 0:CR], rim) + pltpu.roll(dot(weights[:, CR : 2 * CR], rim), 64, 1)
    outer = jnp.where(lane % 8 < 4, outer[MR : 2 * MR], outer[0:MR])
    pre = (edge_inner[...] + outer) * gain + shift
    hidden_edge, slope_edge = smooth_both(pre)
    slope_edge = slope_edge * gain
    hidden_edge = hidden_edge.astype(BF)
    mixed = dot(mixer[...], hidden_edge)
    value = (edge_x[...] + mixed * gain_out + shift_out).astype(BF)
    edge_block[...] = value.astype(F32)
    far.send(edge_block, edge_block_far)
    hidden_edge = hidden_edge.astype(F32)
    parts = value.astype(F32).reshape(3, ROWS, H, LANES)
    parts = swap_blocks([parts[:, i].reshape(3 * H, LANES) for i in range(ROWS)])
    for load in tails:
        load.wait()
    low = iota((3, H, LANES), 2) % 8 < 4
    for g in range(GROUPS):
        lower = pltpu.roll(parts[g], LANES - 4, 1).reshape(3, H, LANES)
        upper = pltpu.roll(parts[g], 4, 1).reshape(3, H, LANES)
        ends[0, g] = jnp.where(low, lower, ends[0, g].astype(F32)).astype(BF)
        ends[1, g] = jnp.where(low, ends[1, g].astype(F32), upper).astype(BF)
    for i, r in enumerate((0, ROWS - 1)):
        far.send(ends.at[i], pieces_far.at[r, :, 2:5])

    for load in later:
        load.wait()
    packed = jnp.zeros((MR, LANES), F32)
    for pair in range(GROUPS // 2):
        two = slice(pair * 2 * LANES, (pair + 1) * 2 * LANES)
        into = dot(back[...], gmi[:, two])
        for half in range(2):
            g = 2 * pair + half
            at = slice(g * LANES, (g + 1) * LANES)
            turn = (124 - 8 * g) % LANES
            here = jnp.where(at_edge(lane), pltpu.roll(slope_edge, turn, 1), slope[:, at])
            value = into[:, half * LANES : (half + 1) * LANES] * here
            grad_inner[g] = value.reshape(MID, H, LANES).astype(BF)
            rows[0:MR] = value
            for r in range(H):
                part = jnp.concatenate([rows[pl.ds(r, MID, stride=8), :], jnp.zeros((H, LANES), F32)], axis=0)
                lane_t = lanes_of(MID + H)
                three = (
                    jnp.where(lane_t < 124, pltpu.roll(part, LANES - 4, 1), 0.0),
                    part,
                    jnp.where(lane_t >= 4, pltpu.roll(part, 4, 1), 0.0),
                )
                to = slice((r % 4 * GROUPS + g) * LANES, (r % 4 * GROUPS + g + 1) * LANES)
                for b in range(3):
                    top = 32 * (3 * (r // 4) + b)
                    taps_out[top : top + 32, to] = three[b].astype(BF)
            packed = jnp.where(lane // 8 == g, pltpu.roll(value, (8 * g - 124) % LANES, 1), packed)
            here = jnp.where(at_edge(lane), pltpu.roll(hidden_edge, turn, 1), hidden[:, at].astype(F32))
            hidden_out[:, at] = here.astype(BF)
        far.send(grad_inner.at[2 * pair : 2 * pair + 2], grad_inner_far.at[2 * pair : 2 * pair + 2])
    send_rows(grad_inner, down, up, MID)
    rows[0:MR] = packed
    for r in range(H):
        part = jnp.concatenate([rows[pl.ds(r, MID, stride=8), :], jnp.zeros((H, LANES), F32)], axis=0)
        lane_t = lanes_of(MID + H)
        low = jnp.where(lane_t % 8 < 4, part, 0.0)
        three = (part - low, jnp.zeros_like(part), low)
        to = slice(4 * POS + r % 4 * LANES, 4 * POS + (r % 4 + 1) * LANES)
        for b in range(3):
            top = 32 * (3 * (r // 4) + b)
            taps_out[top : top + 32, to] = three[b].astype(BF)
    far.finish()


def holder(t, yh, zh, xh):
    xl, yl, core, zl = t // 8, t // 4 % 2, t // 2 % 2, t % 2
    return (4 * xl + 2 * yh + yl) * 2 + core, 4 * zh + 2 * zl + xh


def holders(t):
    return [holder(t, *at) for at in near_groups()]


def near_groups():
    return [(yh, zh, xh) for yh in range(2) for zh in range(2) for xh in range(2)]


def sums_kernel(wide, gmi, taps, hidden, rim_wide, pieces_in, pieces_far, sums_out, sems):
    far = Far(sems)
    mixwide = dot(hidden[...], gmi[...], NT)
    h, col = iota((H, CR), 0), iota((H, CR), 1)
    same = jnp.where(col % 8 == h, 1.0, 0.0)[None]
    mixed = jnp.sum(mixwide.reshape(MID, H, CR) * same, axis=1)
    col, lane_s = iota((CR, LANES), 0), iota((CR, LANES), 1)
    mixed = exact_dot(mixed, jnp.where(col // 8 + 64 == lane_s, 1.0, 0.0).astype(BF))
    total = dot(taps[:, 4 * POS :], rim_wide[...], NT)
    total += dot(taps[:, 0 : 4 * POS], wide[...], NT)
    lane = lanes_of(MID)
    blocks, thirds = [], []
    for b in range(3):
        near, next_one = total[32 * b : 32 * b + MID], total[32 * (3 + b) : 32 * (3 + b) + MID]
        moved = pltpu.roll(next_one[:, 0:LANES], 64, 1)
        ahead = pltpu.roll(next_one[:, LANES : 2 * LANES], 64, 1)
        blocks.append(near[:, 0:LANES] + jnp.where(lane < 64, moved, ahead))
        thirds.append(jnp.where(lane < 64, near[:, LANES : 2 * LANES] + ahead, 0.0))
    blocks.append(thirds[0] + pltpu.roll(thirds[1], 64, 1))
    blocks.append(thirds[2] + mixed)
    blocks.append(jnp.zeros((MID, LANES), F32))
    for t in range(ROWS):
        part = blocks[t // 3][t % 3 * H : (t % 3 + 1) * H]
        high = part.astype(BF).astype(F32)
        both = jnp.concatenate([high[None], (part - high)[None]], axis=0).astype(BF)
        for r, c in holders(t):
            sums_out[r, c] = both
        if t % 2:
            for r in sorted({r for r, _ in holders(t)}):
                far.send(sums_out.at[r], pieces_far.at[r, :, 0:2])
    far.finish()


def spread_kernel(
    grad_inner_far, above, below, w, half_far, x_far, block_far, edge_block_far,
    edge, out_far, edge_value_far, edge_slope_far, block_out_far,
    weights, rhs, grad_inner, half_sum, x, block, edge_block, out, edge_value, edge_slope, sems,
):
    far = Far(sems)
    first = far.start(grad_inner_far, grad_inner)
    loads = [far.start(half_far, half_sum), far.start(x_far, x)]
    last = [far.start(block_far, block), far.start(edge_block_far, edge_block)]
    back_weights(w, weights)
    first.wait()
    lane = lanes_of(CR)
    packed, packed_value, packed_slope = (jnp.zeros((CR, LANES), F32) for _ in range(3))
    for load in loads:
        load.wait()
    for pair in range(GROUPS // 2):
        for half in range(2):
            g = 2 * pair + half
            at = slice(half * LANES, (half + 1) * LANES)
            rhs[0:MR, at] = grad_inner[g].astype(F32).reshape(MR, LANES).astype(BF)
            rhs[MR : MR + MR // 2, at] = above[g].astype(F32).reshape(MR // 2, LANES).astype(BF)
            rhs[MR + MR // 2 : 2 * MR, at] = below[g].astype(F32).reshape(MR // 2, LANES).astype(BF)
        product = dot(weights[...], rhs[...])
        for half in range(2):
            g = 2 * pair + half
            p = product[:, half * LANES : (half + 1) * LANES]
            left, mid, right = p[0:CR], p[CR : 2 * CR], p[2 * CR : 3 * CR]
            total = (
                mid
                + jnp.where(lane < 124, pltpu.roll(left, LANES - 4, 1), 0.0)
                + jnp.where(lane >= 4, pltpu.roll(right, 4, 1), 0.0)
            )
            slope = smooth_slope(x[g].astype(F32).reshape(CR, LANES))
            value = half_sum[g].reshape(CR, LANES) + total * slope
            out[g] = value.reshape(CH, H, LANES).astype(BF)
            far.send(out.at[g], out_far.at[g])
            here = lane // 8 == g
            turn_by = (8 * g - 124) % LANES
            packed = jnp.where(here, pltpu.roll(jnp.where(lane >= 124, right, left), turn_by, 1), packed)
            packed_value = jnp.where(here, pltpu.roll(value, turn_by, 1), packed_value)
            packed_slope = jnp.where(here, pltpu.roll(slope, turn_by, 1), packed_slope)
    edge[...] = packed[0 : CR // 2] + pltpu.roll(packed[CR // 2 : CR], 64, 1)
    edge_value[...] = packed_value
    edge_slope[...] = packed_slope
    far.send(edge_value, edge_value_far)
    far.send(edge_slope, edge_slope_far)
    for load in last:
        load.wait()
    for g in range(GROUPS):
        moved = pltpu.roll(edge_block[...], (124 - 8 * g) % LANES, 1)
        value = jnp.where(at_edge(lane), moved, block[g].astype(F32).reshape(CR, LANES))
        block[g] = value.reshape(CH, H, LANES).astype(BF)
        far.send(block.at[g], block_out_far.at[g])
    far.finish()


def total_kernel(arrived, out):
    total = jnp.zeros((H, LANES), F32)
    for g in range(COLS):
        part = arrived[:, g, 0:2].astype(F32)
        total += jnp.sum(part[:, 0] + part[:, 1], axis=0)
    out[...] = jnp.broadcast_to((total * (1.0 / (ROWS * H * COLS)))[None], (ROWS, H, LANES))


def last_kernel(
    block_far, arrived_far, value_far, edge_value_far, edge_slope_far, from_left, from_right, out_far, grad_far,
    block, arrived, out, value, grad, edge_value, edge_slope, sems,
):
    far = Far(sems)
    first = [far.start(edge_value_far, edge_value), far.start(edge_slope_far, edge_slope)]
    loads = [far.start(value_far.at[g], value.at[g]) for g in range(GROUPS)]
    later = [
        (far.start(block_far.at[g], block.at[g]), far.start(arrived_far.at[:, g, 2:5], arrived.at[:, g]))
        for g in range(GROUPS)
    ]
    lane = lanes_of(CR)
    rim = merge_edges(from_left[...], from_right[...])
    rim = jnp.concatenate([rim, pltpu.roll(rim, 64, 1)], axis=0)
    for load in first:
        load.wait()
    rim = edge_value[...] + rim * edge_slope[...]
    for g in range(GROUPS):
        loads[g].wait()
        moved = pltpu.roll(rim, (124 - 8 * g) % LANES, 1)
        total = jnp.where(at_edge(lane), moved, value[g].astype(F32).reshape(CR, LANES))
        grad[g] = total.reshape(CH, H, LANES).astype(BF)
        far.send(grad.at[g], grad_far.at[g])
    for g in range(GROUPS):
        for load in later[g]:
            load.wait()
        for k in range(3):
            at = slice(k * ROWS, (k + 1) * ROWS)
            both = 0.5 * (block[g, at].astype(F32) + turn(arrived[:, g, k]).astype(F32))
            out[g, at] = both.astype(BF)
        far.send(out.at[g], out_far.at[g])
    far.finish()


def unpack_kernel(tiles, conv, mix):
    order = ((0, 3), (1, 4), (2, 5), (6, 7), (8, None))
    for p, (left, right) in enumerate(order):
        value = tiles[3 * p : 3 * p + 3].reshape(3 * H, LANES)
        conv[left] = value[:, 0:CH]
        if right is None:
            mix[...] = value[:, 64 : 64 + CH]
        else:
            conv[right] = value[:, 64 : 64 + CH]


def both_ways(first, second, axis):
    count = lax.axis_size(axis)
    onward = [(i, (i + 1) % count) for i in range(count)]
    back = [(t, s) for s, t in onward]
    return lax.ppermute(first, axis, onward), lax.ppermute(second, axis, back)


def local(pair_map, cotangent, conv_weight, conv_gain, conv_bias, mix_weight, mix_gain, mix_bias):
    tile = (GROUPS, CH, H, LANES)
    cut = (ROWS, COLS, 3, H, LANES)
    everyone = ("row", "col")
    vmem = pltpu.VMEM
    down, up, d_pieces = call(
        first_kernel, [((GROUPS, CH // 2, H, LANES), BF)] * 2 + [(cut, BF)], (pair_map, cotangent), "first",
        far=(0, 1), far_out=(2,), scratch=[vmem(tile, BF), vmem(tile, BF), vmem(cut, BF)], copies=3 * GROUPS,
    )
    above, below = both_ways(down, up, "row")
    d_arrived = lax.all_to_all(d_pieces.reshape(ROWS * COLS, 3, H, LANES), everyone, 0, 0, tiled=True)
    d_arrived = d_arrived.reshape(cut)

    taps = jnp.transpose(conv_weight, (2, 3, 0, 1)).reshape(9, MID, CH)
    wf, mf, wf_far, mf_far, mbk = call(
        weights_kernel,
        [((3 * MR, 2 * CR), BF), ((CR, MR), BF)] * 2 + [((MR, CR), BF)],
        (taps, mix_weight.T), "weights", far_out=(2, 3, 4), scratch=[vmem((MR, CR), BF)], copies=3,
    )
    act, edge, wide = call(
        act_kernel,
        [((2 * CR, POS), BF), ((CR, LANES), BF), ((256, 4 * POS), BF)],
        (pair_map, above, below), "act", far_out=(2,), copies=4 * GROUPS,
        scratch=[vmem((256, 4 * POS), BF), vmem((2 * CR, LANES), F32)],
    )
    from_left, from_right = both_ways(edge, edge, "col")
    five = (ROWS, COLS, 5, H, LANES)
    slope, hidden, block, pieces, edge_inner, edge_x = call(
        inside_kernel,
        [((MR, POS), F32), ((MR, POS), BF), (tile, BF), (five, BF), ((MR, LANES), F32), ((CR, LANES), F32)],
        (pair_map, act, wf, mf, conv_gain, conv_bias, mix_gain, mix_bias),
        "inside", smem=(4, 5, 6, 7), far_out=(0, 1, 2, 3, 4, 5),
        scratch=[
            vmem((MR, POS), F32), vmem((MR, POS), BF), vmem(tile, BF), vmem(cut, BF),
            vmem((MR, LANES), F32), vmem((CR, LANES), F32),
        ],
        copies=2 * GROUPS + 2,
    )
    grad_inner, g_down, g_up, half_sum, pieces, edge_block, gmi, tap_rows, hidden, rim_wide, wide = call(
        inner_kernel,
        [
            ((GROUPS, MID, H, LANES), BF),
            ((GROUPS, MID // 2, H, LANES), BF),
            ((GROUPS, MID // 2, H, LANES), BF),
            (tile, F32),
            (five, BF),
            ((CR, LANES), F32),
            ((CR, POS), BF),
            ((192, 4 * POS + 4 * LANES), BF),
            ((MR, POS), BF),
            ((256, 4 * LANES), BF),
            ((256, 4 * POS), BF),
        ],
        (
            cotangent, d_arrived, slope, hidden, edge_inner, edge_x, from_left, from_right,
            wf_far, mf_far, mbk, pieces, conv_gain, conv_bias, mix_gain, mix_bias, wide,
        ),
        "inner", smem=(12, 13, 14, 15), far=(0, 2, 3, 4, 5, 8, 9, 10, 11, 16), far_out=(0, 3, 4, 5), alias={11: 4},
        scratch=[
            vmem(tile, BF), vmem((MR, POS), F32), vmem((MR, POS), BF), vmem((MR, LANES), F32), vmem((CR, LANES), F32),
            vmem((2 * MR, 2 * CR), BF), vmem((CR, MR), BF), vmem((MR, CR), BF),
            vmem((GROUPS, MID, H, LANES), BF), vmem(tile, F32), vmem((2, COLS, 3, H, LANES), BF),
            vmem((CR, LANES), F32), vmem((2, CH, H, LANES), BF), vmem((CR, LANES), F32),
        ],
        copies=26,
    )
    g_above, g_below = both_ways(g_down, g_up, "row")
    (pieces,) = call(
        sums_kernel, [(five, BF)], (wide, gmi, tap_rows, hidden, rim_wide, pieces), "sums",
        far=(5,), far_out=(0,), alias={5: 0}, scratch=[vmem((ROWS, COLS, 2, H, LANES), BF)], copies=ROWS,
    )
    pieces, g_above, g_below = lax.optimization_barrier((pieces, g_above, g_below))
    arrived = lax.all_to_all(pieces.reshape(ROWS * COLS, 5, H, LANES), everyone, 0, 0, tiled=True)
    arrived = arrived.reshape(five)
    (sums,) = call(
        total_kernel, [((ROWS, H, LANES), F32)], (arrived,), "total", flops=500_000_000
    )
    groups = [[r * COLS + c for r, c in (holder(t, *at) for t in range(ROWS))] for at in near_groups()]
    spread_sums = lax.all_to_all(sums, everyone, 0, 0, axis_index_groups=groups, tiled=True)
    taps, _ = lax.optimization_barrier((taps, pieces))
    g_edge, inputs, edge_value, edge_slope, block = call(
        spread_kernel,
        [((CR // 2, LANES), F32), (tile, BF), ((CR, LANES), F32), ((CR, LANES), F32), (tile, BF)],
        (grad_inner, g_above, g_below, taps, half_sum, pair_map, block, edge_block),
        "spread", far=(0, 4, 5, 6, 7), far_out=(1, 2, 3, 4), copies=2 * GROUPS + 7,
        scratch=[
            vmem((3 * CR, 2 * MR), BF), vmem((2 * MR, 2 * LANES), BF), vmem((GROUPS, MID, H, LANES), BF),
            vmem(tile, F32), vmem(tile, BF), vmem(tile, BF), vmem((CR, LANES), F32), vmem(tile, BF),
            vmem((CR, LANES), F32), vmem((CR, LANES), F32),
        ],
    )
    g_left, g_right = both_ways(g_edge, g_edge, "col")
    g_left, g_right, block, _ = lax.optimization_barrier((g_left, g_right, block, sums))
    symmetric, grad_input = call(
        last_kernel, [(tile, BF)] * 2, (block, arrived, inputs, edge_value, edge_slope, g_left, g_right), "last",
        far=(0, 1, 2, 3, 4), far_out=(0, 1), copies=5 * GROUPS + 2,
        scratch=[
            vmem(tile, BF), vmem(cut, BF), vmem(tile, BF), vmem(tile, BF), vmem(tile, BF),
            vmem((CR, LANES), F32), vmem((CR, LANES), F32),
        ],
    )
    conv, mix = call(
        unpack_kernel, [((9, MID, CH), F32), ((MID, CH), F32)], (spread_sums,), "unpack", flops=100_000_000
    )
    grad_conv = jnp.transpose(conv.reshape(3, 3, MID, CH), (2, 3, 0, 1))
    return symmetric, grad_input, grad_conv, mix.T


def solution(mesh):
    field = P(None, None, "row", "col")
    return jax.shard_map(
        local,
        mesh=mesh,
        in_specs=(field, field, P(), P(), P(), P(), P(), P()),
        out_specs=(field, field, P(), P()),
        check_vma=False,
    )
```

```python
import functools

import jax
import jax.numpy as jnp
from jax import lax
from jax.experimental import pallas as pl
from jax.experimental.pallas import tpu as pltpu
from jax.sharding import PartitionSpec as P

BF = jnp.bfloat16
F32 = jnp.float32
CH, MID, GROUPS, H, LANES, ROWS, COLS = 48, 24, 8, 8, 128, 16, 8
POS = GROUPS * LANES
CR, MR = CH * H, MID * H
TANH_SCALE = 0.7978845608028654
CUBIC = 0.044715
NN = (((1,), (0,)), ((), ()))
NT = (((1,), (1,)), ((), ()))
TN = (((0,), (0,)), ((), ()))


def smooth(v):
    t = jnp.tanh(TANH_SCALE * (v + CUBIC * (v * v * v)))
    return 0.5 * v * (1.0 + t)


def smooth_slope(v):
    s = v * v
    t = jnp.tanh(TANH_SCALE * (v + CUBIC * (v * s)))
    return 0.5 * (1.0 + t) + (0.5 * v) * (1.0 - t * t) * (TANH_SCALE * (1.0 + (3.0 * CUBIC) * s))


def smooth_both(v):
    s = v * v
    t = jnp.tanh(TANH_SCALE * (v + CUBIC * (v * s)))
    upper, half = 0.5 * (1.0 + t), 0.5 * v
    return half * (1.0 + t), upper + half * (1.0 - t * t) * (TANH_SCALE * (1.0 + (3.0 * CUBIC) * s))


def dot(a, b, dims=NN):
    return lax.dot_general(a, b, dims, preferred_element_type=F32)


def iota(shape, dim):
    return lax.broadcasted_iota(jnp.int32, shape, dim)


def identity(n):
    return jnp.where(iota((n, n), 0) == iota((n, n), 1), 1.0, 0.0).astype(BF)


def lanes_of(rows):
    return iota((rows, LANES), 1)


class Far:
    def __init__(self, sems):
        self.sems, self.used, self.open = sems, 0, []

    def start(self, source, target):
        copy = pltpu.make_async_copy(source, target, self.sems.at[self.used])
        self.used += 1
        copy.start()
        return copy

    def send(self, source, target):
        self.open.append(self.start(source, target))

    def finish(self):
        for copy in self.open:
            copy.wait()


def call(kernel, outs, args, name, smem=(), far=(), far_out=(), flops=4_000_000_000, scratch=(), copies=0, limit=16, alias=None):
    specs = [
        pl.BlockSpec(memory_space=pltpu.SMEM if i in smem else pltpu.HBM if i in far else pltpu.VMEM)
        for i in range(len(args))
    ]
    scratch = list(scratch)
    if copies:
        scratch.append(pltpu.SemaphoreType.DMA((copies,)))
    return pl.pallas_call(
        kernel,
        name=name,
        out_shape=[
            pltpu.HBM(s, t) if i in far_out else jax.ShapeDtypeStruct(s, t)
            for i, (s, t) in enumerate(outs)
        ],
        in_specs=specs,
        out_specs=[
            pl.BlockSpec(memory_space=pltpu.HBM if i in far_out else pltpu.VMEM)
            for i in range(len(outs))
        ],
        scratch_shapes=scratch,
        input_output_aliases=alias or {},
        compiler_params=pltpu.CompilerParams(vmem_limit_bytes=limit * 1024 * 1024),
        cost_estimate=pl.CostEstimate(flops=flops, bytes_accessed=1_000_000, transcendentals=0),
    )(
        *(
            pltpu.with_memory_space_constraint(v, pltpu.HBM) if i in far else v
            for i, v in enumerate(args)
        )
    )


def splat(values, count):
    return jnp.concatenate([jnp.full((H, LANES), values[o], F32) for o in range(count)], axis=0)


def pack_rows(field, count):
    pairs = field.reshape(count // 2, 2, H, LANES)
    even, odd = pairs[:, 0], pairs[:, 1]
    low = iota(even.shape, 1) < 4
    last = jnp.where(low, pltpu.roll(even, 4, 1), odd)
    first = jnp.where(low, even, pltpu.roll(odd, 4, 1))
    return last, first


def send_rows(source, down, up, count):
    at_end = (lax.axis_index("row") == ROWS - 1).astype(jnp.int32)
    at_start = (lax.axis_index("row") == 0).astype(jnp.int32)
    for g in range(GROUPS):
        before = g - at_end
        last, _ = pack_rows(source[jnp.maximum(before, 0)].astype(F32), count)
        down[g] = jnp.where(before >= 0, last, 0.0).astype(BF)
        after = g + at_start
        _, first = pack_rows(source[jnp.minimum(after, GROUPS - 1)].astype(F32), count)
        up[g] = jnp.where(after < GROUPS, first, 0.0).astype(BF)


def swap_blocks(parts):
    lane = iota(parts[0].shape, 1)
    parts = list(parts)
    for k in range(4):
        m = 1 << k
        high = (lane // (8 * m)) % 2 == 1
        for i in range(ROWS):
            if i & m:
                continue
            a, b = parts[i], parts[i | m]
            parts[i] = jnp.where(high, pltpu.roll(b, 8 * m, 1), a)
            parts[i | m] = jnp.where(high, b, pltpu.roll(a, LANES - 8 * m, 1))
    return parts


def turn(tiles):
    return tiles.reshape(LANES, LANES).T.reshape(ROWS, H, LANES)


def swap_in(pieces, g, buffer):
    parts = swap_blocks([pieces[r, g : g + 2].reshape(6 * H, LANES) for r in range(ROWS)])
    for i in range(ROWS):
        value = parts[i].reshape(2, 3, H, LANES)
        for n in range(2):
            for k in range(3):
                buffer[n, k * ROWS + i] = value[n, k]


def swap_out(block, pieces, g):
    parts = swap_blocks(
        [
            jnp.concatenate([block[g + n, k * ROWS + i] for n in range(2) for k in range(3)], axis=0)
            for i in range(ROWS)
        ]
    )
    for r in range(ROWS):
        pieces[r, g : g + 2] = parts[r].reshape(2, 3, H, LANES)


def first_kernel(x_far, d_far, down, up, pieces, x, d, turned, sems):
    far = Far(sems)
    loads = [far.start(d_far.at[g], d.at[g]) for g in range(GROUPS)]
    later = [far.start(x_far.at[g], x.at[g]) for g in range(GROUPS)]
    for g in range(GROUPS):
        loads[g].wait()
        for k in range(3):
            turned[:, g, k] = turn(d[g, k * ROWS : (k + 1) * ROWS])
        far.send(turned.at[:, g], pieces.at[:, g])
    for load in later:
        load.wait()
    send_rows(x, down, up, CH)
    far.finish()


def spread_channels(n, own, width):
    col = iota((n, width), 1)
    half = (width - own) // 2
    rim = jnp.where(col < own + half, col - own, col - own - half) // 4
    return jnp.where(jnp.where(col < own, col // 8, rim) == iota((n, width), 0), 1.0, 0.0).astype(BF)


def row_distance(own, width):
    col, h = iota((H, width), 1), iota((H, width), 0)
    half = (width - own) // 2
    rim = jnp.where(col < own + half, (col - own) % 4 - 4, (col - own - half) % 4 + 8)
    return jnp.where(col < own, col % 8, rim) - h


def weights_kernel(w, mix, a_out, mf_out, a_far, mf_far, mb_far, mb_out, sems):
    far = Far(sems)
    sf, st = spread_channels(CH, CR, 2 * CR), spread_channels(MID, MR, MR)
    pf, pt = row_distance(CR, 2 * CR), row_distance(MR, MR)
    masks = [jnp.where(pf == 4 * (a - 1), 1.0, 0.0)[None] for a in range(3)]
    col = iota((CH, CR), 1)
    above = jnp.where(col < CR // 2, sf[:, CR:].astype(F32), 0.0).astype(BF)
    below = jnp.where(col < CR // 2, 0.0, sf[:, CR:].astype(F32)).astype(BF)
    for b in range(3):
        total = jnp.zeros((MID, H, CR), F32)
        for a in range(3):
            total += dot(w[3 * a + b], sf[:, :CR])[:, None, :] * masks[a][:, :, :CR]
        rest = (dot(w[b], above) + dot(w[6 + b], below))[:, None, :] * (masks[0] + masks[2])[:, :, CR:]
        a_out[b * MR : (b + 1) * MR, 0:CR] = total.reshape(MR, CR).astype(BF)
        a_out[b * MR : (b + 1) * MR, CR : 2 * CR] = rest.reshape(MR, CR).astype(BF)
    far.send(a_out, a_far)
    mask = jnp.where(pf[:, :CR] == 0, 1.0, 0.0)
    mb_out[...] = (dot(mix[...], sf[:, :CR])[:, None, :] * mask[None]).reshape(MR, CR).astype(BF)
    far.send(mb_out, mb_far)
    mask = jnp.where(pt == 0, 1.0, 0.0)
    mf_out[...] = (dot(mix[...], st, TN)[:, None, :] * mask[None]).reshape(CR, MR).astype(BF)
    far.send(mf_out, mf_far)
    far.finish()


def back_weights(w, out):
    st, pt = spread_channels(MID, MR, 2 * MR), row_distance(MR, 2 * MR)
    masks = [jnp.where(pt == -4 * (a - 1), 1.0, 0.0)[None] for a in range(3)]
    for b in range(3):
        total = jnp.zeros((CH, H, 2 * MR), F32)
        for a in range(3):
            total += dot(w[3 * a + b], st, TN)[:, None, :] * masks[a]
        out[b * CR : (b + 1) * CR] = total.reshape(CR, 2 * MR).astype(BF)


def act_kernel(x, above, below, act, edge, wide_far, wide, rows, sems):
    far = Far(sems)
    for p in range(4):
        wide[64 * p + CH : 64 * p + 64, :] = jnp.zeros((64 - CH, 4 * POS), BF)
    lane = lanes_of(CR)
    packed = jnp.zeros((CR, LANES), F32)
    for g in range(GROUPS):
        own = smooth(x[g].astype(F32).reshape(CR, LANES))
        high = smooth(above[g].astype(F32).reshape(CR // 2, LANES))
        low = smooth(below[g].astype(F32).reshape(CR // 2, LANES))
        rim = jnp.concatenate([high, low], axis=0)
        at = slice(g * LANES, (g + 1) * LANES)
        act[0:CR, at] = own.astype(BF)
        act[CR : 2 * CR, at] = rim.astype(BF)
        rows[0:CR] = own
        rows[CR : 2 * CR] = rim
        for m in range(4):
            to = slice((m * GROUPS + g) * LANES, (m * GROUPS + g + 1) * LANES)
            for p, (start, step) in enumerate(((CR, 4), (0, 8), (4, 8), (CR + CR // 2, 4))):
                wide[64 * p : 64 * p + CH, to] = rows[pl.ds(start + m, CH, stride=step), :].astype(BF)
            far.send(wide.at[:, to], wide_far.at[:, to])
        packed = jnp.where(lane // 8 == g, pltpu.roll(own, (8 * g - 124) % LANES, 1), packed)
        packed = jnp.where(lane // 8 == 8 + g, pltpu.roll(rim, (8 * g - 60) % LANES, 1), packed)
    edge[...] = packed.astype(BF)
    far.finish()


def merge_edges(from_left, from_right):
    lane = lanes_of(from_left.shape[0])
    col = lax.axis_index("col")
    has_left = jnp.where(col > 0, 1.0, 0.0)
    has_right = jnp.where(col < COLS - 1, 1.0, 0.0)
    return jnp.where(
        lane % 8 < 4,
        pltpu.roll(from_right, LANES - 4, 1) * has_right,
        pltpu.roll(from_left, 4, 1) * has_left,
    )


def at_edge(lane):
    return jnp.logical_or(lane < 4, lane >= 124)


def inside_kernel(
    x, act, weights, mixer, cg, cb, mg, mb,
    slope_far, hidden_far, block_far, pieces_far, edge_inner_far, edge_x_far,
    slope, hidden, block, pieces, edge_inner, edge_x, sems,
):
    far = Far(sems)
    lane, lane_c = lanes_of(MR), lanes_of(CR)
    gain, shift = splat(cg, MID), splat(cb, MID)
    gain_out, shift_out = splat(mg, CH), splat(mb, CH)
    packed, packed_x = jnp.zeros((MR, LANES), F32), jnp.zeros((CR, LANES), F32)
    for pair in range(GROUPS // 2):
        two = slice(pair * 2 * LANES, (pair + 1) * 2 * LANES)
        product = dot(weights[...], act[:, two])
        for half in range(2):
            g = 2 * pair + half
            p = product[:, half * LANES : (half + 1) * LANES]
            inner = (
                p[MR : 2 * MR]
                + jnp.where(lane < 4, 0.0, pltpu.roll(p[0:MR], 4, 1))
                + jnp.where(lane >= 124, 0.0, pltpu.roll(p[2 * MR : 3 * MR], LANES - 4, 1))
            )
            packed = jnp.where(lane // 8 == g, pltpu.roll(inner, (8 * g - 124) % LANES, 1), packed)
            pre = inner * gain + shift
            at = slice(g * LANES, (g + 1) * LANES)
            smoothed, steep = smooth_both(pre)
            slope[:, at] = steep * gain
            hidden[:, at] = smoothed.astype(BF)
        far.send(slope.at[:, two], slope_far.at[:, two])
        far.send(hidden.at[:, two], hidden_far.at[:, two])
        mixed = dot(mixer[...], hidden[:, two])
        for half in range(2):
            g = 2 * pair + half
            m = mixed[:, half * LANES : (half + 1) * LANES]
            own = x[g].astype(F32).reshape(CR, LANES)
            packed_x = jnp.where(lane_c // 8 == g, pltpu.roll(own, (8 * g - 124) % LANES, 1), packed_x)
            value = (own + m * gain_out + shift_out).astype(BF)
            block[g] = value.astype(F32).reshape(CH, H, LANES).astype(BF)
        g = 2 * pair
        far.send(block.at[g : g + 2], block_far.at[g : g + 2])
        swap_out(block, pieces, g)
        far.send(pieces.at[:, g : g + 2], pieces_far.at[:, g : g + 2, 2:5])
    edge_inner[...] = packed
    edge_x[...] = packed_x
    far.send(edge_inner, edge_inner_far)
    far.send(edge_x, edge_x_far)
    far.finish()


def split(value):
    high = value.astype(BF)
    return high, (value - high.astype(F32)).astype(BF)


def exact_dot(value, onehot):
    high, low = split(value)
    return dot(high, onehot) + dot(low, onehot)


def inner_kernel(
    d_far, arrived, slope_far, hidden_far, edge_inner_far, edge_x_far, from_left, from_right,
    weights_far, mixer_far, back_far, pieces_in, cg, cb, mg, mb, wide_far,
    grad_inner_far, down, up, half_sum_far, pieces_far, edge_block_far, gmi, taps_out, hidden_out, rim_wide, wide,
    d, slope, hidden, edge_inner, edge_x, weights, mixer, back, grad_inner, half_sum, ends, edge_block, buffer, rows, sems,
):
    far = Far(sems)
    loads = [far.start(d_far.at[2 * p : 2 * p + 2], d.at[2 * p : 2 * p + 2]) for p in range(GROUPS // 2)]
    first = [far.start(weights_far.at[0:MR], weights.at[0:MR])]
    first.append(far.start(weights_far.at[2 * MR : 3 * MR], weights.at[MR : 2 * MR]))
    first += [far.start(edge_inner_far, edge_inner), far.start(edge_x_far, edge_x), far.start(mixer_far, mixer)]
    tails = [
        far.start(pieces_in.at[r, :, 2:5], ends.at[i]) for i, r in enumerate((0, ROWS - 1))
    ]
    later = [far.start(back_far, back), far.start(slope_far, slope), far.start(hidden_far, hidden)]
    far.send(wide_far, wide)
    lane, lane_c = lanes_of(MR), lanes_of(CR)
    gain, shift = splat(cg, MID), splat(cb, MID)
    gain_out, shift_out = splat(mg, CH), splat(mb, CH)
    rim = merge_edges(from_left[...].astype(F32), from_right[...].astype(F32))
    rows[...] = rim
    for m in range(4):
        to = slice(m * LANES, (m + 1) * LANES)
        for p, (start, step) in enumerate(((0, 4), (0, 8), (4, 8), (CR // 2, 4))):
            part = rows[pl.ds(start + m, CH, stride=step), :]
            if step == 4:
                part = pltpu.roll(part, 64, 1)
            rim_wide[64 * p : 64 * p + CH, to] = part.astype(BF)
    for p in range(4):
        rim_wide[64 * p + CH : 64 * p + 64, :] = jnp.zeros((64 - CH, 4 * LANES), BF)
    rim = rim.astype(BF)
    for pair in range(GROUPS // 2):
        loads[pair].wait()
        swap_in(arrived, 2 * pair, buffer)
        for half in range(2):
            g = 2 * pair + half
            both = 0.5 * (d[g].astype(F32) + buffer[half].astype(F32)).reshape(CR, LANES)
            half_sum[g] = both.reshape(CH, H, LANES)
            gmi[:, g * LANES : (g + 1) * LANES] = (both * gain_out).astype(BF)
        far.send(half_sum.at[2 * pair : 2 * pair + 2], half_sum_far.at[2 * pair : 2 * pair + 2])
    for load in first:
        load.wait()
    outer = dot(weights[:, 0:CR], rim) + pltpu.roll(dot(weights[:, CR : 2 * CR], rim), 64, 1)
    outer = jnp.where(lane % 8 < 4, outer[MR : 2 * MR], outer[0:MR])
    pre = (edge_inner[...] + outer) * gain + shift
    hidden_edge, slope_edge = smooth_both(pre)
    slope_edge = slope_edge * gain
    hidden_edge = hidden_edge.astype(BF)
    mixed = dot(mixer[...], hidden_edge)
    value = (edge_x[...] + mixed * gain_out + shift_out).astype(BF)
    edge_block[...] = value.astype(F32)
    far.send(edge_block, edge_block_far)
    hidden_edge = hidden_edge.astype(F32)
    parts = value.astype(F32).reshape(3, ROWS, H, LANES)
    parts = swap_blocks([parts[:, i].reshape(3 * H, LANES) for i in range(ROWS)])
    for load in tails:
        load.wait()
    low = iota((3, H, LANES), 2) % 8 < 4
    for g in range(GROUPS):
        lower = pltpu.roll(parts[g], LANES - 4, 1).reshape(3, H, LANES)
        upper = pltpu.roll(parts[g], 4, 1).reshape(3, H, LANES)
        ends[0, g] = jnp.where(low, lower, ends[0, g].astype(F32)).astype(BF)
        ends[1, g] = jnp.where(low, ends[1, g].astype(F32), upper).astype(BF)
    for i, r in enumerate((0, ROWS - 1)):
        far.send(ends.at[i], pieces_far.at[r, :, 2:5])

    for load in later:
        load.wait()
    packed = jnp.zeros((MR, LANES), F32)
    for pair in range(GROUPS // 2):
        two = slice(pair * 2 * LANES, (pair + 1) * 2 * LANES)
        into = dot(back[...], gmi[:, two])
        for half in range(2):
            g = 2 * pair + half
            at = slice(g * LANES, (g + 1) * LANES)
            turn = (124 - 8 * g) % LANES
            here = jnp.where(at_edge(lane), pltpu.roll(slope_edge, turn, 1), slope[:, at])
            value = into[:, half * LANES : (half + 1) * LANES] * here
            grad_inner[g] = value.reshape(MID, H, LANES).astype(BF)
            rows[0:MR] = value
            for r in range(H):
                part = jnp.concatenate([rows[pl.ds(r, MID, stride=8), :], jnp.zeros((H, LANES), F32)], axis=0)
                lane_t = lanes_of(MID + H)
                three = (
                    jnp.where(lane_t < 124, pltpu.roll(part, LANES - 4, 1), 0.0),
                    part,
                    jnp.where(lane_t >= 4, pltpu.roll(part, 4, 1), 0.0),
                )
                to = slice((r % 4 * GROUPS + g) * LANES, (r % 4 * GROUPS + g + 1) * LANES)
                for b in range(3):
                    top = 32 * (3 * (r // 4) + b)
                    taps_out[top : top + 32, to] = three[b].astype(BF)
            packed = jnp.where(lane // 8 == g, pltpu.roll(value, (8 * g - 124) % LANES, 1), packed)
            here = jnp.where(at_edge(lane), pltpu.roll(hidden_edge, turn, 1), hidden[:, at].astype(F32))
            hidden_out[:, at] = here.astype(BF)
        far.send(grad_inner.at[2 * pair : 2 * pair + 2], grad_inner_far.at[2 * pair : 2 * pair + 2])
    send_rows(grad_inner, down, up, MID)
    rows[0:MR] = packed
    for r in range(H):
        part = jnp.concatenate([rows[pl.ds(r, MID, stride=8), :], jnp.zeros((H, LANES), F32)], axis=0)
        lane_t = lanes_of(MID + H)
        low = jnp.where(lane_t % 8 < 4, part, 0.0)
        three = (part - low, jnp.zeros_like(part), low)
        to = slice(4 * POS + r % 4 * LANES, 4 * POS + (r % 4 + 1) * LANES)
        for b in range(3):
            top = 32 * (3 * (r // 4) + b)
            taps_out[top : top + 32, to] = three[b].astype(BF)
    far.finish()


def holder(t, yh, zh, xh):
    xl, yl, core, zl = t // 8, t // 4 % 2, t // 2 % 2, t % 2
    return (4 * xl + 2 * yh + yl) * 2 + core, 4 * zh + 2 * zl + xh


def holders(t):
    return [holder(t, *at) for at in near_groups()]


def near_groups():
    return [(yh, zh, xh) for yh in range(2) for zh in range(2) for xh in range(2)]


def sums_kernel(wide, gmi, taps, hidden, rim_wide, pieces_in, pieces_far, sums_out, sems):
    far = Far(sems)
    mixwide = dot(hidden[...], gmi[...], NT)
    h, col = iota((H, CR), 0), iota((H, CR), 1)
    same = jnp.where(col % 8 == h, 1.0, 0.0)[None]
    mixed = jnp.sum(mixwide.reshape(MID, H, CR) * same, axis=1)
    col, lane_s = iota((CR, LANES), 0), iota((CR, LANES), 1)
    mixed = exact_dot(mixed, jnp.where(col // 8 + 64 == lane_s, 1.0, 0.0).astype(BF))
    total = dot(taps[:, 4 * POS :], rim_wide[...], NT)
    total += dot(taps[:, 0 : 4 * POS], wide[...], NT)
    lane = lanes_of(MID)
    blocks, thirds = [], []
    for b in range(3):
        near, next_one = total[32 * b : 32 * b + MID], total[32 * (3 + b) : 32 * (3 + b) + MID]
        moved = pltpu.roll(next_one[:, 0:LANES], 64, 1)
        ahead = pltpu.roll(next_one[:, LANES : 2 * LANES], 64, 1)
        blocks.append(near[:, 0:LANES] + jnp.where(lane < 64, moved, ahead))
        thirds.append(jnp.where(lane < 64, near[:, LANES : 2 * LANES] + ahead, 0.0))
    blocks.append(thirds[0] + pltpu.roll(thirds[1], 64, 1))
    blocks.append(thirds[2] + mixed)
    blocks.append(jnp.zeros((MID, LANES), F32))
    for t in range(ROWS):
        part = blocks[t // 3][t % 3 * H : (t % 3 + 1) * H]
        high = part.astype(BF).astype(F32)
        both = jnp.concatenate([high[None], (part - high)[None]], axis=0).astype(BF)
        for r, c in holders(t):
            sums_out[r, c] = both
        if t % 2:
            for r in sorted({r for r, _ in holders(t)}):
                far.send(sums_out.at[r], pieces_far.at[r, :, 0:2])
    far.finish()


def spread_kernel(
    grad_inner_far, above, below, w, half_far, x_far, block_far, edge_block_far,
    edge, out_far, edge_value_far, edge_slope_far, block_out_far,
    weights, rhs, grad_inner, half_sum, x, block, edge_block, out, edge_value, edge_slope, sems,
):
    far = Far(sems)
    first = far.start(grad_inner_far, grad_inner)
    loads = [far.start(half_far, half_sum), far.start(x_far, x)]
    last = [far.start(block_far, block), far.start(edge_block_far, edge_block)]
    back_weights(w, weights)
    first.wait()
    lane = lanes_of(CR)
    packed, packed_value, packed_slope = (jnp.zeros((CR, LANES), F32) for _ in range(3))
    for load in loads:
        load.wait()
    for pair in range(GROUPS // 2):
        for half in range(2):
            g = 2 * pair + half
            at = slice(half * LANES, (half + 1) * LANES)
            rhs[0:MR, at] = grad_inner[g].astype(F32).reshape(MR, LANES).astype(BF)
            rhs[MR : MR + MR // 2, at] = above[g].astype(F32).reshape(MR // 2, LANES).astype(BF)
            rhs[MR + MR // 2 : 2 * MR, at] = below[g].astype(F32).reshape(MR // 2, LANES).astype(BF)
        product = dot(weights[...], rhs[...])
        for half in range(2):
            g = 2 * pair + half
            p = product[:, half * LANES : (half + 1) * LANES]
            left, mid, right = p[0:CR], p[CR : 2 * CR], p[2 * CR : 3 * CR]
            total = (
                mid
                + jnp.where(lane < 124, pltpu.roll(left, LANES - 4, 1), 0.0)
                + jnp.where(lane >= 4, pltpu.roll(right, 4, 1), 0.0)
            )
            slope = smooth_slope(x[g].astype(F32).reshape(CR, LANES))
            value = half_sum[g].reshape(CR, LANES) + total * slope
            out[g] = value.reshape(CH, H, LANES).astype(BF)
            far.send(out.at[g], out_far.at[g])
            here = lane // 8 == g
            turn_by = (8 * g - 124) % LANES
            packed = jnp.where(here, pltpu.roll(jnp.where(lane >= 124, right, left), turn_by, 1), packed)
            packed_value = jnp.where(here, pltpu.roll(value, turn_by, 1), packed_value)
            packed_slope = jnp.where(here, pltpu.roll(slope, turn_by, 1), packed_slope)
    edge[...] = packed[0 : CR // 2] + pltpu.roll(packed[CR // 2 : CR], 64, 1)
    edge_value[...] = packed_value
    edge_slope[...] = packed_slope
    far.send(edge_value, edge_value_far)
    far.send(edge_slope, edge_slope_far)
    for load in last:
        load.wait()
    for g in range(GROUPS):
        moved = pltpu.roll(edge_block[...], (124 - 8 * g) % LANES, 1)
        value = jnp.where(at_edge(lane), moved, block[g].astype(F32).reshape(CR, LANES))
        block[g] = value.reshape(CH, H, LANES).astype(BF)
        far.send(block.at[g], block_out_far.at[g])
    far.finish()


def total_kernel(arrived, out):
    total = jnp.zeros((H, LANES), F32)
    for g in range(COLS):
        part = arrived[:, g, 0:2].astype(F32)
        total += jnp.sum(part[:, 0] + part[:, 1], axis=0)
    out[...] = jnp.broadcast_to((total * (1.0 / (ROWS * H * COLS)))[None], (ROWS, H, LANES))


def last_kernel(
    block_far, arrived_far, value_far, edge_value_far, edge_slope_far, from_left, from_right, out_far, grad_far,
    block, arrived, out, value, grad, edge_value, edge_slope, sems,
):
    far = Far(sems)
    first = [far.start(edge_value_far, edge_value), far.start(edge_slope_far, edge_slope)]
    loads = [far.start(value_far.at[g], value.at[g]) for g in range(GROUPS)]
    later = [
        (far.start(block_far.at[g], block.at[g]), far.start(arrived_far.at[:, g, 2:5], arrived.at[:, g]))
        for g in range(GROUPS)
    ]
    lane = lanes_of(CR)
    rim = merge_edges(from_left[...], from_right[...])
    rim = jnp.concatenate([rim, pltpu.roll(rim, 64, 1)], axis=0)
    for load in first:
        load.wait()
    rim = edge_value[...] + rim * edge_slope[...]
    for g in range(GROUPS):
        loads[g].wait()
        moved = pltpu.roll(rim, (124 - 8 * g) % LANES, 1)
        total = jnp.where(at_edge(lane), moved, value[g].astype(F32).reshape(CR, LANES))
        grad[g] = total.reshape(CH, H, LANES).astype(BF)
        far.send(grad.at[g], grad_far.at[g])
    for g in range(GROUPS):
        for load in later[g]:
            load.wait()
        for k in range(3):
            at = slice(k * ROWS, (k + 1) * ROWS)
            both = 0.5 * (block[g, at].astype(F32) + turn(arrived[:, g, k]).astype(F32))
            out[g, at] = both.astype(BF)
        far.send(out.at[g], out_far.at[g])
    far.finish()


def unpack_kernel(tiles, conv, mix):
    order = ((0, 3), (1, 4), (2, 5), (6, 7), (8, None))
    for p, (left, right) in enumerate(order):
        value = tiles[3 * p : 3 * p + 3].reshape(3 * H, LANES)
        conv[left] = value[:, 0:CH]
        if right is None:
            mix[...] = value[:, 64 : 64 + CH]
        else:
            conv[right] = value[:, 64 : 64 + CH]


def both_ways(first, second, axis, around):
    count = lax.axis_size(axis)
    onward = [(i, (i + 1) % count) for i in range(count if around else count - 1)]
    back = [(t, s) for s, t in onward]
    return lax.ppermute(first, axis, onward), lax.ppermute(second, axis, back)


def local(pair_map, cotangent, conv_weight, conv_gain, conv_bias, mix_weight, mix_gain, mix_bias):
    tile = (GROUPS, CH, H, LANES)
    cut = (ROWS, COLS, 3, H, LANES)
    everyone = ("row", "col")
    vmem = pltpu.VMEM
    down, up, d_pieces = call(
        first_kernel, [((GROUPS, CH // 2, H, LANES), BF)] * 2 + [(cut, BF)], (pair_map, cotangent), "first",
        far=(0, 1), far_out=(2,), scratch=[vmem(tile, BF), vmem(tile, BF), vmem(cut, BF)], copies=3 * GROUPS,
    )
    above, below = both_ways(down, up, "row", True)
    d_arrived = lax.all_to_all(d_pieces.reshape(ROWS * COLS, 3, H, LANES), everyone, 0, 0, tiled=True)
    d_arrived = d_arrived.reshape(cut)

    taps = jnp.transpose(conv_weight, (2, 3, 0, 1)).reshape(9, MID, CH)
    wf, mf, wf_far, mf_far, mbk = call(
        weights_kernel,
        [((3 * MR, 2 * CR), BF), ((CR, MR), BF)] * 2 + [((MR, CR), BF)],
        (taps, mix_weight.T), "weights", far_out=(2, 3, 4), scratch=[vmem((MR, CR), BF)], copies=3,
    )
    act, edge, wide = call(
        act_kernel,
        [((2 * CR, POS), BF), ((CR, LANES), BF), ((256, 4 * POS), BF)],
        (pair_map, above, below), "act", far_out=(2,), copies=4 * GROUPS,
        scratch=[vmem((256, 4 * POS), BF), vmem((2 * CR, LANES), F32)],
    )
    from_left, from_right = both_ways(edge, edge, "col", False)
    five = (ROWS, COLS, 5, H, LANES)
    slope, hidden, block, pieces, edge_inner, edge_x = call(
        inside_kernel,
        [((MR, POS), F32), ((MR, POS), BF), (tile, BF), (five, BF), ((MR, LANES), F32), ((CR, LANES), F32)],
        (pair_map, act, wf, mf, conv_gain, conv_bias, mix_gain, mix_bias),
        "inside", smem=(4, 5, 6, 7), far_out=(0, 1, 2, 3, 4, 5),
        scratch=[
            vmem((MR, POS), F32), vmem((MR, POS), BF), vmem(tile, BF), vmem(cut, BF),
            vmem((MR, LANES), F32), vmem((CR, LANES), F32),
        ],
        copies=2 * GROUPS + 2,
    )
    grad_inner, g_down, g_up, half_sum, pieces, edge_block, gmi, tap_rows, hidden, rim_wide, wide = call(
        inner_kernel,
        [
            ((GROUPS, MID, H, LANES), BF),
            ((GROUPS, MID // 2, H, LANES), BF),
            ((GROUPS, MID // 2, H, LANES), BF),
            (tile, F32),
            (five, BF),
            ((CR, LANES), F32),
            ((CR, POS), BF),
            ((192, 4 * POS + 4 * LANES), BF),
            ((MR, POS), BF),
            ((256, 4 * LANES), BF),
            ((256, 4 * POS), BF),
        ],
        (
            cotangent, d_arrived, slope, hidden, edge_inner, edge_x, from_left, from_right,
            wf_far, mf_far, mbk, pieces, conv_gain, conv_bias, mix_gain, mix_bias, wide,
        ),
        "inner", smem=(12, 13, 14, 15), far=(0, 2, 3, 4, 5, 8, 9, 10, 11, 16), far_out=(0, 3, 4, 5), alias={11: 4},
        scratch=[
            vmem(tile, BF), vmem((MR, POS), F32), vmem((MR, POS), BF), vmem((MR, LANES), F32), vmem((CR, LANES), F32),
            vmem((2 * MR, 2 * CR), BF), vmem((CR, MR), BF), vmem((MR, CR), BF),
            vmem((GROUPS, MID, H, LANES), BF), vmem(tile, F32), vmem((2, COLS, 3, H, LANES), BF),
            vmem((CR, LANES), F32), vmem((2, CH, H, LANES), BF), vmem((CR, LANES), F32),
        ],
        copies=26,
    )
    g_above, g_below = both_ways(g_down, g_up, "row", True)
    (pieces,) = call(
        sums_kernel, [(five, BF)], (wide, gmi, tap_rows, hidden, rim_wide, pieces), "sums",
        far=(5,), far_out=(0,), alias={5: 0}, scratch=[vmem((ROWS, COLS, 2, H, LANES), BF)], copies=ROWS,
    )
    pieces, g_above, g_below = lax.optimization_barrier((pieces, g_above, g_below))
    arrived = lax.all_to_all(pieces.reshape(ROWS * COLS, 5, H, LANES), everyone, 0, 0, tiled=True)
    arrived = arrived.reshape(five)
    (sums,) = call(
        total_kernel, [((ROWS, H, LANES), F32)], (arrived,), "total", flops=500_000_000
    )
    groups = [[r * COLS + c for r, c in (holder(t, *at) for t in range(ROWS))] for at in near_groups()]
    spread_sums = lax.all_to_all(sums, everyone, 0, 0, axis_index_groups=groups, tiled=True)
    taps, _ = lax.optimization_barrier((taps, pieces))
    g_edge, inputs, edge_value, edge_slope, block = call(
        spread_kernel,
        [((CR // 2, LANES), F32), (tile, BF), ((CR, LANES), F32), ((CR, LANES), F32), (tile, BF)],
        (grad_inner, g_above, g_below, taps, half_sum, pair_map, block, edge_block),
        "spread", far=(0, 4, 5, 6, 7), far_out=(1, 2, 3, 4), copies=2 * GROUPS + 7,
        scratch=[
            vmem((3 * CR, 2 * MR), BF), vmem((2 * MR, 2 * LANES), BF), vmem((GROUPS, MID, H, LANES), BF),
            vmem(tile, F32), vmem(tile, BF), vmem(tile, BF), vmem((CR, LANES), F32), vmem(tile, BF),
            vmem((CR, LANES), F32), vmem((CR, LANES), F32),
        ],
    )
    g_left, g_right = both_ways(g_edge, g_edge, "col", False)
    g_left, g_right, block, _ = lax.optimization_barrier((g_left, g_right, block, sums))
    symmetric, grad_input = call(
        last_kernel, [(tile, BF)] * 2, (block, arrived, inputs, edge_value, edge_slope, g_left, g_right), "last",
        far=(0, 1, 2, 3, 4), far_out=(0, 1), copies=5 * GROUPS + 2,
        scratch=[
            vmem(tile, BF), vmem(cut, BF), vmem(tile, BF), vmem(tile, BF), vmem(tile, BF),
            vmem((CR, LANES), F32), vmem((CR, LANES), F32),
        ],
    )
    conv, mix = call(
        unpack_kernel, [((9, MID, CH), F32), ((MID, CH), F32)], (spread_sums,), "unpack", flops=100_000_000
    )
    grad_conv = jnp.transpose(conv.reshape(3, 3, MID, CH), (2, 3, 0, 1))
    return symmetric, grad_input, grad_conv, mix.T


def solution(mesh):
    field = P(None, None, "row", "col")
    return jax.shard_map(
        local,
        mesh=mesh,
        in_specs=(field, field, P(), P(), P(), P(), P(), P()),
        out_specs=(field, field, P(), P()),
        check_vma=False,
    )
```

```python
import functools

import jax
import jax.numpy as jnp
from jax import lax
from jax.experimental import pallas as pl
from jax.experimental.pallas import tpu as pltpu
from jax.sharding import PartitionSpec as P

BF = jnp.bfloat16
F32 = jnp.float32
CH, MID, GROUPS, H, LANES, ROWS, COLS = 48, 24, 8, 8, 128, 16, 8
POS = GROUPS * LANES
CR, MR = CH * H, MID * H
TANH_SCALE = 0.7978845608028654
CUBIC = 0.044715
NN = (((1,), (0,)), ((), ()))
NT = (((1,), (1,)), ((), ()))
TN = (((0,), (0,)), ((), ()))


def smooth(v):
    t = jnp.tanh(TANH_SCALE * (v + CUBIC * (v * v * v)))
    return 0.5 * v * (1.0 + t)


def smooth_slope(v):
    s = v * v
    t = jnp.tanh(TANH_SCALE * (v + CUBIC * (v * s)))
    return 0.5 * (1.0 + t) + (0.5 * v) * (1.0 - t * t) * (TANH_SCALE * (1.0 + (3.0 * CUBIC) * s))


def smooth_both(v):
    s = v * v
    t = jnp.tanh(TANH_SCALE * (v + CUBIC * (v * s)))
    upper, half = 0.5 * (1.0 + t), 0.5 * v
    return half * (1.0 + t), upper + half * (1.0 - t * t) * (TANH_SCALE * (1.0 + (3.0 * CUBIC) * s))


def dot(a, b, dims=NN):
    return lax.dot_general(a, b, dims, preferred_element_type=F32)


def iota(shape, dim):
    return lax.broadcasted_iota(jnp.int32, shape, dim)


def identity(n):
    return jnp.where(iota((n, n), 0) == iota((n, n), 1), 1.0, 0.0).astype(BF)


def lanes_of(rows):
    return iota((rows, LANES), 1)


class Far:
    def __init__(self, sems):
        self.sems, self.used, self.open = sems, 0, []

    def start(self, source, target):
        copy = pltpu.make_async_copy(source, target, self.sems.at[self.used])
        self.used += 1
        copy.start()
        return copy

    def send(self, source, target):
        self.open.append(self.start(source, target))

    def finish(self):
        for copy in self.open:
            copy.wait()


def call(kernel, outs, args, name, smem=(), far=(), far_out=(), flops=4_000_000_000, scratch=(), copies=0, limit=16, alias=None):
    specs = [
        pl.BlockSpec(memory_space=pltpu.SMEM if i in smem else pltpu.HBM if i in far else pltpu.VMEM)
        for i in range(len(args))
    ]
    scratch = list(scratch)
    if copies:
        scratch.append(pltpu.SemaphoreType.DMA((copies,)))
    return pl.pallas_call(
        kernel,
        name=name,
        out_shape=[
            pltpu.HBM(s, t) if i in far_out else jax.ShapeDtypeStruct(s, t)
            for i, (s, t) in enumerate(outs)
        ],
        in_specs=specs,
        out_specs=[
            pl.BlockSpec(memory_space=pltpu.HBM if i in far_out else pltpu.VMEM)
            for i in range(len(outs))
        ],
        scratch_shapes=scratch,
        input_output_aliases=alias or {},
        compiler_params=pltpu.CompilerParams(vmem_limit_bytes=limit * 1024 * 1024),
        cost_estimate=pl.CostEstimate(flops=flops, bytes_accessed=1_000_000, transcendentals=0),
    )(
        *(
            pltpu.with_memory_space_constraint(v, pltpu.HBM) if i in far else v
            for i, v in enumerate(args)
        )
    )


def splat(values, count):
    return jnp.concatenate([jnp.full((H, LANES), values[o], F32) for o in range(count)], axis=0)


def pack_rows(field, count):
    pairs = field.reshape(count // 2, 2, H, LANES)
    even, odd = pairs[:, 0], pairs[:, 1]
    low = iota(even.shape, 1) < 4
    last = jnp.where(low, pltpu.roll(even, 4, 1), odd)
    first = jnp.where(low, even, pltpu.roll(odd, 4, 1))
    return last, first


def send_rows(source, down, up, count):
    at_end = (lax.axis_index("row") == ROWS - 1).astype(jnp.int32)
    at_start = (lax.axis_index("row") == 0).astype(jnp.int32)
    for g in range(GROUPS):
        before = g - at_end
        last, _ = pack_rows(source[jnp.maximum(before, 0)].astype(F32), count)
        down[g] = jnp.where(before >= 0, last, 0.0).astype(BF)
        after = g + at_start
        _, first = pack_rows(source[jnp.minimum(after, GROUPS - 1)].astype(F32), count)
        up[g] = jnp.where(after < GROUPS, first, 0.0).astype(BF)


def swap_blocks(parts):
    lane = iota(parts[0].shape, 1)
    parts = list(parts)
    for k in range(4):
        m = 1 << k
        high = (lane // (8 * m)) % 2 == 1
        for i in range(ROWS):
            if i & m:
                continue
            a, b = parts[i], parts[i | m]
            parts[i] = jnp.where(high, pltpu.roll(b, 8 * m, 1), a)
            parts[i | m] = jnp.where(high, b, pltpu.roll(a, LANES - 8 * m, 1))
    return parts


def turn(tiles):
    return tiles.reshape(LANES, LANES).T.reshape(ROWS, H, LANES)


def swap_in(pieces, g, buffer):
    parts = swap_blocks([pieces[r, g : g + 2].reshape(6 * H, LANES) for r in range(ROWS)])
    for i in range(ROWS):
        value = parts[i].reshape(2, 3, H, LANES)
        for n in range(2):
            for k in range(3):
                buffer[n, k * ROWS + i] = value[n, k]


def swap_out(block, pieces, g):
    parts = swap_blocks(
        [
            jnp.concatenate([block[g + n, k * ROWS + i] for n in range(2) for k in range(3)], axis=0)
            for i in range(ROWS)
        ]
    )
    for r in range(ROWS):
        pieces[r, g : g + 2] = parts[r].reshape(2, 3, H, LANES)


def first_kernel(x_far, d_far, down, up, pieces, x, d, turned, sems):
    far = Far(sems)
    loads = [far.start(d_far.at[g], d.at[g]) for g in range(GROUPS)]
    later = [far.start(x_far.at[g], x.at[g]) for g in range(GROUPS)]
    for g in range(GROUPS):
        loads[g].wait()
        for k in range(3):
            turned[:, g, k] = turn(d[g, k * ROWS : (k + 1) * ROWS])
        far.send(turned.at[:, g], pieces.at[:, g])
    for load in later:
        load.wait()
    send_rows(x, down, up, CH)
    far.finish()


def spread_channels(n, own, width):
    col = iota((n, width), 1)
    half = (width - own) // 2
    rim = jnp.where(col < own + half, col - own, col - own - half) // 4
    return jnp.where(jnp.where(col < own, col // 8, rim) == iota((n, width), 0), 1.0, 0.0).astype(BF)


def row_distance(own, width):
    col, h = iota((H, width), 1), iota((H, width), 0)
    half = (width - own) // 2
    rim = jnp.where(col < own + half, (col - own) % 4 - 4, (col - own - half) % 4 + 8)
    return jnp.where(col < own, col % 8, rim) - h


def weights_kernel(w, mix, a_out, mf_out, a_far, mf_far, mb_far, mb_out, sems):
    far = Far(sems)
    sf, st = spread_channels(CH, CR, 2 * CR), spread_channels(MID, MR, MR)
    pf, pt = row_distance(CR, 2 * CR), row_distance(MR, MR)
    masks = [jnp.where(pf == 4 * (a - 1), 1.0, 0.0)[None] for a in range(3)]
    col = iota((CH, CR), 1)
    above = jnp.where(col < CR // 2, sf[:, CR:].astype(F32), 0.0).astype(BF)
    below = jnp.where(col < CR // 2, 0.0, sf[:, CR:].astype(F32)).astype(BF)
    for b in range(3):
        total = jnp.zeros((MID, H, CR), F32)
        for a in range(3):
            total += dot(w[3 * a + b], sf[:, :CR])[:, None, :] * masks[a][:, :, :CR]
        rest = (dot(w[b], above) + dot(w[6 + b], below))[:, None, :] * (masks[0] + masks[2])[:, :, CR:]
        a_out[b * MR : (b + 1) * MR, 0:CR] = total.reshape(MR, CR).astype(BF)
        a_out[b * MR : (b + 1) * MR, CR : 2 * CR] = rest.reshape(MR, CR).astype(BF)
    far.send(a_out, a_far)
    mask = jnp.where(pf[:, :CR] == 0, 1.0, 0.0)
    mb_out[...] = (dot(mix[...], sf[:, :CR])[:, None, :] * mask[None]).reshape(MR, CR).astype(BF)
    far.send(mb_out, mb_far)
    mask = jnp.where(pt == 0, 1.0, 0.0)
    mf_out[...] = (dot(mix[...], st, TN)[:, None, :] * mask[None]).reshape(CR, MR).astype(BF)
    far.send(mf_out, mf_far)
    far.finish()


def back_weights(w, out):
    st, pt = spread_channels(MID, MR, 2 * MR), row_distance(MR, 2 * MR)
    masks = [jnp.where(pt == -4 * (a - 1), 1.0, 0.0)[None] for a in range(3)]
    for b in range(3):
        total = jnp.zeros((CH, H, 2 * MR), F32)
        for a in range(3):
            total += dot(w[3 * a + b], st, TN)[:, None, :] * masks[a]
        out[b * CR : (b + 1) * CR] = total.reshape(CR, 2 * MR).astype(BF)


def act_kernel(x, above, below, act, edge, wide_far, wide, rows, sems):
    far = Far(sems)
    for p in range(4):
        wide[64 * p + CH : 64 * p + 64, :] = jnp.zeros((64 - CH, 4 * POS), BF)
    lane = lanes_of(CR)
    packed = jnp.zeros((CR, LANES), F32)
    for g in range(GROUPS):
        own = smooth(x[g].astype(F32).reshape(CR, LANES))
        high = smooth(above[g].astype(F32).reshape(CR // 2, LANES))
        low = smooth(below[g].astype(F32).reshape(CR // 2, LANES))
        rim = jnp.concatenate([high, low], axis=0)
        at = slice(g * LANES, (g + 1) * LANES)
        act[0:CR, at] = own.astype(BF)
        act[CR : 2 * CR, at] = rim.astype(BF)
        rows[0:CR] = own
        rows[CR : 2 * CR] = rim
        for m in range(4):
            to = slice((m * GROUPS + g) * LANES, (m * GROUPS + g + 1) * LANES)
            for p, (start, step) in enumerate(((CR, 4), (0, 8), (4, 8), (CR + CR // 2, 4))):
                wide[64 * p : 64 * p + CH, to] = rows[pl.ds(start + m, CH, stride=step), :].astype(BF)
            far.send(wide.at[:, to], wide_far.at[:, to])
        packed = jnp.where(lane // 8 == g, pltpu.roll(own, (8 * g - 124) % LANES, 1), packed)
        packed = jnp.where(lane // 8 == 8 + g, pltpu.roll(rim, (8 * g - 60) % LANES, 1), packed)
    edge[...] = packed.astype(BF)
    far.finish()


def merge_edges(first, second):
    lane = lanes_of(first.shape[0])
    col = lax.axis_index("col")
    even = col % 2 == 0
    right, left = jnp.where(even, first, second), jnp.where(even, second, first)
    has_left = jnp.where(col > 0, 1.0, 0.0)
    has_right = jnp.where(col < COLS - 1, 1.0, 0.0)
    return jnp.where(
        lane % 8 < 4,
        pltpu.roll(right, LANES - 4, 1) * has_right,
        pltpu.roll(left, 4, 1) * has_left,
    )


def at_edge(lane):
    return jnp.logical_or(lane < 4, lane >= 124)


def inside_kernel(
    x, act, weights, mixer, cg, cb, mg, mb,
    slope_far, hidden_far, block_far, pieces_far, edge_inner_far, edge_x_far,
    slope, hidden, block, pieces, edge_inner, edge_x, sems,
):
    far = Far(sems)
    lane, lane_c = lanes_of(MR), lanes_of(CR)
    gain, shift = splat(cg, MID), splat(cb, MID)
    gain_out, shift_out = splat(mg, CH), splat(mb, CH)
    packed, packed_x = jnp.zeros((MR, LANES), F32), jnp.zeros((CR, LANES), F32)
    for pair in range(GROUPS // 2):
        two = slice(pair * 2 * LANES, (pair + 1) * 2 * LANES)
        product = dot(weights[...], act[:, two])
        for half in range(2):
            g = 2 * pair + half
            p = product[:, half * LANES : (half + 1) * LANES]
            inner = (
                p[MR : 2 * MR]
                + jnp.where(lane < 4, 0.0, pltpu.roll(p[0:MR], 4, 1))
                + jnp.where(lane >= 124, 0.0, pltpu.roll(p[2 * MR : 3 * MR], LANES - 4, 1))
            )
            packed = jnp.where(lane // 8 == g, pltpu.roll(inner, (8 * g - 124) % LANES, 1), packed)
            pre = inner * gain + shift
            at = slice(g * LANES, (g + 1) * LANES)
            smoothed, steep = smooth_both(pre)
            slope[:, at] = steep * gain
            hidden[:, at] = smoothed.astype(BF)
        far.send(slope.at[:, two], slope_far.at[:, two])
        far.send(hidden.at[:, two], hidden_far.at[:, two])
        mixed = dot(mixer[...], hidden[:, two])
        for half in range(2):
            g = 2 * pair + half
            m = mixed[:, half * LANES : (half + 1) * LANES]
            own = x[g].astype(F32).reshape(CR, LANES)
            packed_x = jnp.where(lane_c // 8 == g, pltpu.roll(own, (8 * g - 124) % LANES, 1), packed_x)
            value = (own + m * gain_out + shift_out).astype(BF)
            block[g] = value.astype(F32).reshape(CH, H, LANES).astype(BF)
        g = 2 * pair
        far.send(block.at[g : g + 2], block_far.at[g : g + 2])
        swap_out(block, pieces, g)
        far.send(pieces.at[:, g : g + 2], pieces_far.at[:, g : g + 2, 2:5])
    edge_inner[...] = packed
    edge_x[...] = packed_x
    far.send(edge_inner, edge_inner_far)
    far.send(edge_x, edge_x_far)
    far.finish()


def split(value):
    high = value.astype(BF)
    return high, (value - high.astype(F32)).astype(BF)


def exact_dot(value, onehot):
    high, low = split(value)
    return dot(high, onehot) + dot(low, onehot)


def inner_kernel(
    d_far, arrived, slope_far, hidden_far, edge_inner_far, edge_x_far, edges_a, edges_b,
    weights_far, mixer_far, back_far, pieces_in, cg, cb, mg, mb, wide_far,
    grad_inner_far, down, up, half_sum_far, pieces_far, edge_block_far, gmi, taps_out, hidden_out, rim_wide, wide,
    d, slope, hidden, edge_inner, edge_x, weights, mixer, back, grad_inner, half_sum, ends, edge_block, buffer, rows, sems,
):
    far = Far(sems)
    loads = [far.start(d_far.at[2 * p : 2 * p + 2], d.at[2 * p : 2 * p + 2]) for p in range(GROUPS // 2)]
    first = [far.start(weights_far.at[0:MR], weights.at[0:MR])]
    first.append(far.start(weights_far.at[2 * MR : 3 * MR], weights.at[MR : 2 * MR]))
    first += [far.start(edge_inner_far, edge_inner), far.start(edge_x_far, edge_x), far.start(mixer_far, mixer)]
    tails = [
        far.start(pieces_in.at[r, :, 2:5], ends.at[i]) for i, r in enumerate((0, ROWS - 1))
    ]
    later = [far.start(back_far, back), far.start(slope_far, slope), far.start(hidden_far, hidden)]
    far.send(wide_far, wide)
    lane, lane_c = lanes_of(MR), lanes_of(CR)
    gain, shift = splat(cg, MID), splat(cb, MID)
    gain_out, shift_out = splat(mg, CH), splat(mb, CH)
    rim = merge_edges(edges_a[...].astype(F32), edges_b[...].astype(F32))
    rows[...] = rim
    for m in range(4):
        to = slice(m * LANES, (m + 1) * LANES)
        for p, (start, step) in enumerate(((0, 4), (0, 8), (4, 8), (CR // 2, 4))):
            part = rows[pl.ds(start + m, CH, stride=step), :]
            if step == 4:
                part = pltpu.roll(part, 64, 1)
            rim_wide[64 * p : 64 * p + CH, to] = part.astype(BF)
    for p in range(4):
        rim_wide[64 * p + CH : 64 * p + 64, :] = jnp.zeros((64 - CH, 4 * LANES), BF)
    rim = rim.astype(BF)
    for pair in range(GROUPS // 2):
        loads[pair].wait()
        swap_in(arrived, 2 * pair, buffer)
        for half in range(2):
            g = 2 * pair + half
            both = 0.5 * (d[g].astype(F32) + buffer[half].astype(F32)).reshape(CR, LANES)
            half_sum[g] = both.reshape(CH, H, LANES)
            gmi[:, g * LANES : (g + 1) * LANES] = (both * gain_out).astype(BF)
        far.send(half_sum.at[2 * pair : 2 * pair + 2], half_sum_far.at[2 * pair : 2 * pair + 2])
    for load in first:
        load.wait()
    outer = dot(weights[:, 0:CR], rim) + pltpu.roll(dot(weights[:, CR : 2 * CR], rim), 64, 1)
    outer = jnp.where(lane % 8 < 4, outer[MR : 2 * MR], outer[0:MR])
    pre = (edge_inner[...] + outer) * gain + shift
    hidden_edge, slope_edge = smooth_both(pre)
    slope_edge = slope_edge * gain
    hidden_edge = hidden_edge.astype(BF)
    mixed = dot(mixer[...], hidden_edge)
    value = (edge_x[...] + mixed * gain_out + shift_out).astype(BF)
    edge_block[...] = value.astype(F32)
    far.send(edge_block, edge_block_far)
    hidden_edge = hidden_edge.astype(F32)
    parts = value.astype(F32).reshape(3, ROWS, H, LANES)
    parts = swap_blocks([parts[:, i].reshape(3 * H, LANES) for i in range(ROWS)])
    for load in tails:
        load.wait()
    low = iota((3, H, LANES), 2) % 8 < 4
    for g in range(GROUPS):
        lower = pltpu.roll(parts[g], LANES - 4, 1).reshape(3, H, LANES)
        upper = pltpu.roll(parts[g], 4, 1).reshape(3, H, LANES)
        ends[0, g] = jnp.where(low, lower, ends[0, g].astype(F32)).astype(BF)
        ends[1, g] = jnp.where(low, ends[1, g].astype(F32), upper).astype(BF)
    for i, r in enumerate((0, ROWS - 1)):
        far.send(ends.at[i], pieces_far.at[r, :, 2:5])

    for load in later:
        load.wait()
    packed = jnp.zeros((MR, LANES), F32)
    for pair in range(GROUPS // 2):
        two = slice(pair * 2 * LANES, (pair + 1) * 2 * LANES)
        into = dot(back[...], gmi[:, two])
        for half in range(2):
            g = 2 * pair + half
            at = slice(g * LANES, (g + 1) * LANES)
            turn = (124 - 8 * g) % LANES
            here = jnp.where(at_edge(lane), pltpu.roll(slope_edge, turn, 1), slope[:, at])
            value = into[:, half * LANES : (half + 1) * LANES] * here
            grad_inner[g] = value.reshape(MID, H, LANES).astype(BF)
            rows[0:MR] = value
            for r in range(H):
                part = jnp.concatenate([rows[pl.ds(r, MID, stride=8), :], jnp.zeros((H, LANES), F32)], axis=0)
                lane_t = lanes_of(MID + H)
                three = (
                    jnp.where(lane_t < 124, pltpu.roll(part, LANES - 4, 1), 0.0),
                    part,
                    jnp.where(lane_t >= 4, pltpu.roll(part, 4, 1), 0.0),
                )
                to = slice((r % 4 * GROUPS + g) * LANES, (r % 4 * GROUPS + g + 1) * LANES)
                for b in range(3):
                    top = 32 * (3 * (r // 4) + b)
                    taps_out[top : top + 32, to] = three[b].astype(BF)
            packed = jnp.where(lane // 8 == g, pltpu.roll(value, (8 * g - 124) % LANES, 1), packed)
            here = jnp.where(at_edge(lane), pltpu.roll(hidden_edge, turn, 1), hidden[:, at].astype(F32))
            hidden_out[:, at] = here.astype(BF)
        far.send(grad_inner.at[2 * pair : 2 * pair + 2], grad_inner_far.at[2 * pair : 2 * pair + 2])
    send_rows(grad_inner, down, up, MID)
    rows[0:MR] = packed
    for r in range(H):
        part = jnp.concatenate([rows[pl.ds(r, MID, stride=8), :], jnp.zeros((H, LANES), F32)], axis=0)
        lane_t = lanes_of(MID + H)
        low = jnp.where(lane_t % 8 < 4, part, 0.0)
        three = (part - low, jnp.zeros_like(part), low)
        to = slice(4 * POS + r % 4 * LANES, 4 * POS + (r % 4 + 1) * LANES)
        for b in range(3):
            top = 32 * (3 * (r // 4) + b)
            taps_out[top : top + 32, to] = three[b].astype(BF)
    far.finish()


def holder(t, yh, zh, xh):
    xl, yl, core, zl = t // 8, t // 4 % 2, t // 2 % 2, t % 2
    return (4 * xl + 2 * yh + yl) * 2 + core, 4 * zh + 2 * zl + xh


def holders(t):
    return [holder(t, *at) for at in near_groups()]


def near_groups():
    return [(yh, zh, xh) for yh in range(2) for zh in range(2) for xh in range(2)]


def sums_kernel(wide, gmi, taps, hidden, rim_wide, pieces_in, pieces_far, sums_out, sems):
    far = Far(sems)
    mixwide = dot(hidden[...], gmi[...], NT)
    h, col = iota((H, CR), 0), iota((H, CR), 1)
    same = jnp.where(col % 8 == h, 1.0, 0.0)[None]
    mixed = jnp.sum(mixwide.reshape(MID, H, CR) * same, axis=1)
    col, lane_s = iota((CR, LANES), 0), iota((CR, LANES), 1)
    mixed = exact_dot(mixed, jnp.where(col // 8 + 64 == lane_s, 1.0, 0.0).astype(BF))
    total = dot(taps[:, 4 * POS :], rim_wide[...], NT)
    total += dot(taps[:, 0 : 4 * POS], wide[...], NT)
    lane = lanes_of(MID)
    blocks, thirds = [], []
    for b in range(3):
        near, next_one = total[32 * b : 32 * b + MID], total[32 * (3 + b) : 32 * (3 + b) + MID]
        moved = pltpu.roll(next_one[:, 0:LANES], 64, 1)
        ahead = pltpu.roll(next_one[:, LANES : 2 * LANES], 64, 1)
        blocks.append(near[:, 0:LANES] + jnp.where(lane < 64, moved, ahead))
        thirds.append(jnp.where(lane < 64, near[:, LANES : 2 * LANES] + ahead, 0.0))
    blocks.append(thirds[0] + pltpu.roll(thirds[1], 64, 1))
    blocks.append(thirds[2] + mixed)
    blocks.append(jnp.zeros((MID, LANES), F32))
    for t in range(ROWS):
        part = blocks[t // 3][t % 3 * H : (t % 3 + 1) * H]
        high = part.astype(BF).astype(F32)
        both = jnp.concatenate([high[None], (part - high)[None]], axis=0).astype(BF)
        for r, c in holders(t):
            sums_out[r, c] = both
        if t % 2:
            for r in sorted({r for r, _ in holders(t)}):
                far.send(sums_out.at[r], pieces_far.at[r, :, 0:2])
    far.finish()


def spread_kernel(
    grad_inner_far, above, below, w, half_far, x_far, block_far, edge_block_far,
    edge, out_far, edge_value_far, edge_slope_far, block_out_far,
    weights, rhs, grad_inner, half_sum, x, block, edge_block, out, edge_value, edge_slope, sems,
):
    far = Far(sems)
    first = far.start(grad_inner_far, grad_inner)
    loads = [far.start(half_far, half_sum), far.start(x_far, x)]
    last = [far.start(block_far, block), far.start(edge_block_far, edge_block)]
    back_weights(w, weights)
    first.wait()
    lane = lanes_of(CR)
    packed, packed_value, packed_slope = (jnp.zeros((CR, LANES), F32) for _ in range(3))
    for load in loads:
        load.wait()
    for pair in range(GROUPS // 2):
        for half in range(2):
            g = 2 * pair + half
            at = slice(half * LANES, (half + 1) * LANES)
            rhs[0:MR, at] = grad_inner[g].astype(F32).reshape(MR, LANES).astype(BF)
            rhs[MR : MR + MR // 2, at] = above[g].astype(F32).reshape(MR // 2, LANES).astype(BF)
            rhs[MR + MR // 2 : 2 * MR, at] = below[g].astype(F32).reshape(MR // 2, LANES).astype(BF)
        product = dot(weights[...], rhs[...])
        for half in range(2):
            g = 2 * pair + half
            p = product[:, half * LANES : (half + 1) * LANES]
            left, mid, right = p[0:CR], p[CR : 2 * CR], p[2 * CR : 3 * CR]
            total = (
                mid
                + jnp.where(lane < 124, pltpu.roll(left, LANES - 4, 1), 0.0)
                + jnp.where(lane >= 4, pltpu.roll(right, 4, 1), 0.0)
            )
            slope = smooth_slope(x[g].astype(F32).reshape(CR, LANES))
            value = half_sum[g].reshape(CR, LANES) + total * slope
            out[g] = value.reshape(CH, H, LANES).astype(BF)
            far.send(out.at[g], out_far.at[g])
            here = lane // 8 == g
            turn_by = (8 * g - 124) % LANES
            packed = jnp.where(here, pltpu.roll(jnp.where(lane >= 124, right, left), turn_by, 1), packed)
            packed_value = jnp.where(here, pltpu.roll(value, turn_by, 1), packed_value)
            packed_slope = jnp.where(here, pltpu.roll(slope, turn_by, 1), packed_slope)
    edge[...] = packed[0 : CR // 2] + pltpu.roll(packed[CR // 2 : CR], 64, 1)
    edge_value[...] = packed_value
    edge_slope[...] = packed_slope
    far.send(edge_value, edge_value_far)
    far.send(edge_slope, edge_slope_far)
    for load in last:
        load.wait()
    for g in range(GROUPS):
        moved = pltpu.roll(edge_block[...], (124 - 8 * g) % LANES, 1)
        value = jnp.where(at_edge(lane), moved, block[g].astype(F32).reshape(CR, LANES))
        block[g] = value.reshape(CH, H, LANES).astype(BF)
        far.send(block.at[g], block_out_far.at[g])
    far.finish()


def total_kernel(arrived, out):
    total = jnp.zeros((H, LANES), F32)
    for g in range(COLS):
        part = arrived[:, g, 0:2].astype(F32)
        total += jnp.sum(part[:, 0] + part[:, 1], axis=0)
    out[...] = jnp.broadcast_to((total * (1.0 / (ROWS * H * COLS)))[None], (ROWS, H, LANES))


def last_kernel(
    block_far, arrived_far, value_far, edge_value_far, edge_slope_far, edges_a, edges_b, out_far, grad_far,
    block, arrived, out, value, grad, edge_value, edge_slope, sems,
):
    far = Far(sems)
    first = [far.start(edge_value_far, edge_value), far.start(edge_slope_far, edge_slope)]
    loads = [far.start(value_far.at[g], value.at[g]) for g in range(GROUPS)]
    later = [
        (far.start(block_far.at[g], block.at[g]), far.start(arrived_far.at[:, g, 2:5], arrived.at[:, g]))
        for g in range(GROUPS)
    ]
    lane = lanes_of(CR)
    rim = merge_edges(edges_a[...], edges_b[...])
    rim = jnp.concatenate([rim, pltpu.roll(rim, 64, 1)], axis=0)
    for load in first:
        load.wait()
    rim = edge_value[...] + rim * edge_slope[...]
    for g in range(GROUPS):
        loads[g].wait()
        moved = pltpu.roll(rim, (124 - 8 * g) % LANES, 1)
        total = jnp.where(at_edge(lane), moved, value[g].astype(F32).reshape(CR, LANES))
        grad[g] = total.reshape(CH, H, LANES).astype(BF)
        far.send(grad.at[g], grad_far.at[g])
    for g in range(GROUPS):
        for load in later[g]:
            load.wait()
        for k in range(3):
            at = slice(k * ROWS, (k + 1) * ROWS)
            both = 0.5 * (block[g, at].astype(F32) + turn(arrived[:, g, k]).astype(F32))
            out[g, at] = both.astype(BF)
        far.send(out.at[g], out_far.at[g])
    far.finish()


def unpack_kernel(tiles, conv, mix):
    order = ((0, 3), (1, 4), (2, 5), (6, 7), (8, None))
    for p, (left, right) in enumerate(order):
        value = tiles[3 * p : 3 * p + 3].reshape(3 * H, LANES)
        conv[left] = value[:, 0:CH]
        if right is None:
            mix[...] = value[:, 64 : 64 + CH]
        else:
            conv[right] = value[:, 64 : 64 + CH]


def both_ways(first, second, axis):
    count = lax.axis_size(axis)
    onward = [(i, (i + 1) % count) for i in range(count)]
    back = [(t, s) for s, t in onward]
    return lax.ppermute(first, axis, onward), lax.ppermute(second, axis, back)


def swap_cols(edge):
    count = lax.axis_size("col")
    first = [(i, i ^ 1) for i in range(count)]
    second = [(i, min(max(((i + 1) ^ 1) - 1, 0), count - 1)) for i in range(count)]
    return lax.ppermute(edge, "col", first), lax.ppermute(edge, "col", second)


def local(pair_map, cotangent, conv_weight, conv_gain, conv_bias, mix_weight, mix_gain, mix_bias):
    tile = (GROUPS, CH, H, LANES)
    cut = (ROWS, COLS, 3, H, LANES)
    everyone = ("row", "col")
    vmem = pltpu.VMEM
    down, up, d_pieces = call(
        first_kernel, [((GROUPS, CH // 2, H, LANES), BF)] * 2 + [(cut, BF)], (pair_map, cotangent), "first",
        far=(0, 1), far_out=(2,), scratch=[vmem(tile, BF), vmem(tile, BF), vmem(cut, BF)], copies=3 * GROUPS,
    )
    above, below = both_ways(down, up, "row")
    d_arrived = lax.all_to_all(d_pieces.reshape(ROWS * COLS, 3, H, LANES), everyone, 0, 0, tiled=True)
    d_arrived = d_arrived.reshape(cut)

    taps = jnp.transpose(conv_weight, (2, 3, 0, 1)).reshape(9, MID, CH)
    wf, mf, wf_far, mf_far, mbk = call(
        weights_kernel,
        [((3 * MR, 2 * CR), BF), ((CR, MR), BF)] * 2 + [((MR, CR), BF)],
        (taps, mix_weight.T), "weights", far_out=(2, 3, 4), scratch=[vmem((MR, CR), BF)], copies=3,
    )
    act, edge, wide = call(
        act_kernel,
        [((2 * CR, POS), BF), ((CR, LANES), BF), ((256, 4 * POS), BF)],
        (pair_map, above, below), "act", far_out=(2,), copies=4 * GROUPS,
        scratch=[vmem((256, 4 * POS), BF), vmem((2 * CR, LANES), F32)],
    )
    edges_a, edges_b = swap_cols(edge)
    five = (ROWS, COLS, 5, H, LANES)
    slope, hidden, block, pieces, edge_inner, edge_x = call(
        inside_kernel,
        [((MR, POS), F32), ((MR, POS), BF), (tile, BF), (five, BF), ((MR, LANES), F32), ((CR, LANES), F32)],
        (pair_map, act, wf, mf, conv_gain, conv_bias, mix_gain, mix_bias),
        "inside", smem=(4, 5, 6, 7), far_out=(0, 1, 2, 3, 4, 5),
        scratch=[
            vmem((MR, POS), F32), vmem((MR, POS), BF), vmem(tile, BF), vmem(cut, BF),
            vmem((MR, LANES), F32), vmem((CR, LANES), F32),
        ],
        copies=2 * GROUPS + 2,
    )
    grad_inner, g_down, g_up, half_sum, pieces, edge_block, gmi, tap_rows, hidden, rim_wide, wide = call(
        inner_kernel,
        [
            ((GROUPS, MID, H, LANES), BF),
            ((GROUPS, MID // 2, H, LANES), BF),
            ((GROUPS, MID // 2, H, LANES), BF),
            (tile, F32),
            (five, BF),
            ((CR, LANES), F32),
            ((CR, POS), BF),
            ((192, 4 * POS + 4 * LANES), BF),
            ((MR, POS), BF),
            ((256, 4 * LANES), BF),
            ((256, 4 * POS), BF),
        ],
        (
            cotangent, d_arrived, slope, hidden, edge_inner, edge_x, edges_a, edges_b,
            wf_far, mf_far, mbk, pieces, conv_gain, conv_bias, mix_gain, mix_bias, wide,
        ),
        "inner", smem=(12, 13, 14, 15), far=(0, 2, 3, 4, 5, 8, 9, 10, 11, 16), far_out=(0, 3, 4, 5), alias={11: 4},
        scratch=[
            vmem(tile, BF), vmem((MR, POS), F32), vmem((MR, POS), BF), vmem((MR, LANES), F32), vmem((CR, LANES), F32),
            vmem((2 * MR, 2 * CR), BF), vmem((CR, MR), BF), vmem((MR, CR), BF),
            vmem((GROUPS, MID, H, LANES), BF), vmem(tile, F32), vmem((2, COLS, 3, H, LANES), BF),
            vmem((CR, LANES), F32), vmem((2, CH, H, LANES), BF), vmem((CR, LANES), F32),
        ],
        copies=26,
    )
    g_above, g_below = both_ways(g_down, g_up, "row")
    (pieces,) = call(
        sums_kernel, [(five, BF)], (wide, gmi, tap_rows, hidden, rim_wide, pieces), "sums",
        far=(5,), far_out=(0,), alias={5: 0}, scratch=[vmem((ROWS, COLS, 2, H, LANES), BF)], copies=ROWS,
    )
    pieces, g_above, g_below = lax.optimization_barrier((pieces, g_above, g_below))
    arrived = lax.all_to_all(pieces.reshape(ROWS * COLS, 5, H, LANES), everyone, 0, 0, tiled=True)
    arrived = arrived.reshape(five)
    (sums,) = call(
        total_kernel, [((ROWS, H, LANES), F32)], (arrived,), "total", flops=500_000_000
    )
    groups = [[r * COLS + c for r, c in (holder(t, *at) for t in range(ROWS))] for at in near_groups()]
    spread_sums = lax.all_to_all(sums, everyone, 0, 0, axis_index_groups=groups, tiled=True)
    taps, _ = lax.optimization_barrier((taps, pieces))
    g_edge, inputs, edge_value, edge_slope, block = call(
        spread_kernel,
        [((CR // 2, LANES), F32), (tile, BF), ((CR, LANES), F32), ((CR, LANES), F32), (tile, BF)],
        (grad_inner, g_above, g_below, taps, half_sum, pair_map, block, edge_block),
        "spread", far=(0, 4, 5, 6, 7), far_out=(1, 2, 3, 4), copies=2 * GROUPS + 7,
        scratch=[
            vmem((3 * CR, 2 * MR), BF), vmem((2 * MR, 2 * LANES), BF), vmem((GROUPS, MID, H, LANES), BF),
            vmem(tile, F32), vmem(tile, BF), vmem(tile, BF), vmem((CR, LANES), F32), vmem(tile, BF),
            vmem((CR, LANES), F32), vmem((CR, LANES), F32),
        ],
    )
    g_left, g_right = swap_cols(g_edge)
    g_left, g_right, block, _ = lax.optimization_barrier((g_left, g_right, block, sums))
    symmetric, grad_input = call(
        last_kernel, [(tile, BF)] * 2, (block, arrived, inputs, edge_value, edge_slope, g_left, g_right), "last",
        far=(0, 1, 2, 3, 4), far_out=(0, 1), copies=5 * GROUPS + 2,
        scratch=[
            vmem(tile, BF), vmem(cut, BF), vmem(tile, BF), vmem(tile, BF), vmem(tile, BF),
            vmem((CR, LANES), F32), vmem((CR, LANES), F32),
        ],
    )
    conv, mix = call(
        unpack_kernel, [((9, MID, CH), F32), ((MID, CH), F32)], (spread_sums,), "unpack", flops=100_000_000
    )
    grad_conv = jnp.transpose(conv.reshape(3, 3, MID, CH), (2, 3, 0, 1))
    return symmetric, grad_input, grad_conv, mix.T


def solution(mesh):
    field = P(None, None, "row", "col")
    return jax.shard_map(
        local,
        mesh=mesh,
        in_specs=(field, field, P(), P(), P(), P(), P(), P()),
        out_specs=(field, field, P(), P()),
        check_vma=False,
    )
```

```python
import functools

import jax
import jax.numpy as jnp
from jax import lax
from jax.experimental import pallas as pl
from jax.experimental.pallas import tpu as pltpu
from jax.sharding import PartitionSpec as P

BF = jnp.bfloat16
F32 = jnp.float32
CH, MID, GROUPS, H, LANES, ROWS, COLS = 48, 24, 8, 8, 128, 16, 8
POS = GROUPS * LANES
CR, MR = CH * H, MID * H
TANH_SCALE = 0.7978845608028654
CUBIC = 0.044715
NN = (((1,), (0,)), ((), ()))
NT = (((1,), (1,)), ((), ()))
TN = (((0,), (0,)), ((), ()))


def smooth(v):
    t = jnp.tanh(TANH_SCALE * (v + CUBIC * (v * v * v)))
    return 0.5 * v * (1.0 + t)


def smooth_slope(v):
    s = v * v
    t = jnp.tanh(TANH_SCALE * (v + CUBIC * (v * s)))
    return 0.5 * (1.0 + t) + (0.5 * v) * (1.0 - t * t) * (TANH_SCALE * (1.0 + (3.0 * CUBIC) * s))


def smooth_both(v):
    s = v * v
    t = jnp.tanh(TANH_SCALE * (v + CUBIC * (v * s)))
    upper, half = 0.5 * (1.0 + t), 0.5 * v
    return half * (1.0 + t), upper + half * (1.0 - t * t) * (TANH_SCALE * (1.0 + (3.0 * CUBIC) * s))


def dot(a, b, dims=NN):
    return lax.dot_general(a, b, dims, preferred_element_type=F32)


def iota(shape, dim):
    return lax.broadcasted_iota(jnp.int32, shape, dim)


def identity(n):
    return jnp.where(iota((n, n), 0) == iota((n, n), 1), 1.0, 0.0).astype(BF)


def lanes_of(rows):
    return iota((rows, LANES), 1)


class Far:
    def __init__(self, sems):
        self.sems, self.used, self.open = sems, 0, []

    def start(self, source, target):
        copy = pltpu.make_async_copy(source, target, self.sems.at[self.used])
        self.used += 1
        copy.start()
        return copy

    def send(self, source, target):
        self.open.append(self.start(source, target))

    def finish(self):
        for copy in self.open:
            copy.wait()


def call(kernel, outs, args, name, smem=(), far=(), far_out=(), flops=4_000_000_000, scratch=(), copies=0, limit=16, alias=None):
    specs = [
        pl.BlockSpec(memory_space=pltpu.SMEM if i in smem else pltpu.HBM if i in far else pltpu.VMEM)
        for i in range(len(args))
    ]
    scratch = list(scratch)
    if copies:
        scratch.append(pltpu.SemaphoreType.DMA((copies,)))
    return pl.pallas_call(
        kernel,
        name=name,
        out_shape=[
            pltpu.HBM(s, t) if i in far_out else jax.ShapeDtypeStruct(s, t)
            for i, (s, t) in enumerate(outs)
        ],
        in_specs=specs,
        out_specs=[
            pl.BlockSpec(memory_space=pltpu.HBM if i in far_out else pltpu.VMEM)
            for i in range(len(outs))
        ],
        scratch_shapes=scratch,
        input_output_aliases=alias or {},
        compiler_params=pltpu.CompilerParams(vmem_limit_bytes=limit * 1024 * 1024),
        cost_estimate=pl.CostEstimate(flops=flops, bytes_accessed=1_000_000, transcendentals=0),
    )(
        *(
            pltpu.with_memory_space_constraint(v, pltpu.HBM) if i in far else v
            for i, v in enumerate(args)
        )
    )


def splat(values, count):
    return jnp.concatenate([jnp.full((H, LANES), values[o], F32) for o in range(count)], axis=0)


def pack_rows(field, count):
    pairs = field.reshape(count // 2, 2, H, LANES)
    even, odd = pairs[:, 0], pairs[:, 1]
    low = iota(even.shape, 1) < 4
    last = jnp.where(low, pltpu.roll(even, 4, 1), odd)
    first = jnp.where(low, even, pltpu.roll(odd, 4, 1))
    return last, first


def send_rows(source, down, up, count):
    at_end = (lax.axis_index("row") == ROWS - 1).astype(jnp.int32)
    at_start = (lax.axis_index("row") == 0).astype(jnp.int32)
    for g in range(GROUPS):
        before = g - at_end
        last, _ = pack_rows(source[jnp.maximum(before, 0)].astype(F32), count)
        down[g] = jnp.where(before >= 0, last, 0.0).astype(BF)
        after = g + at_start
        _, first = pack_rows(source[jnp.minimum(after, GROUPS - 1)].astype(F32), count)
        up[g] = jnp.where(after < GROUPS, first, 0.0).astype(BF)


def swap_blocks(parts):
    lane = iota(parts[0].shape, 1)
    parts = list(parts)
    for k in range(4):
        m = 1 << k
        high = (lane // (8 * m)) % 2 == 1
        for i in range(ROWS):
            if i & m:
                continue
            a, b = parts[i], parts[i | m]
            parts[i] = jnp.where(high, pltpu.roll(b, 8 * m, 1), a)
            parts[i | m] = jnp.where(high, b, pltpu.roll(a, LANES - 8 * m, 1))
    return parts


def turn(tiles):
    return tiles.reshape(LANES, LANES).T.reshape(ROWS, H, LANES)


def swap_in(pieces, g, buffer):
    parts = swap_blocks([pieces[r, g : g + 2].reshape(6 * H, LANES) for r in range(ROWS)])
    for i in range(ROWS):
        value = parts[i].reshape(2, 3, H, LANES)
        for n in range(2):
            for k in range(3):
                buffer[n, k * ROWS + i] = value[n, k]


def swap_out(block, pieces, g):
    parts = swap_blocks(
        [
            jnp.concatenate([block[g + n, k * ROWS + i] for n in range(2) for k in range(3)], axis=0)
            for i in range(ROWS)
        ]
    )
    for r in range(ROWS):
        pieces[r, g : g + 2] = parts[r].reshape(2, 3, H, LANES)


def first_kernel(x_far, d_far, down, up, pieces, x, d, turned, sems):
    far = Far(sems)
    loads = [far.start(d_far.at[g], d.at[g]) for g in range(GROUPS)]
    later = [far.start(x_far.at[g], x.at[g]) for g in range(GROUPS)]
    for g in range(GROUPS):
        loads[g].wait()
        for k in range(3):
            turned[:, g, k] = turn(d[g, k * ROWS : (k + 1) * ROWS])
        far.send(turned.at[:, g], pieces.at[:, g])
    for load in later:
        load.wait()
    send_rows(x, down, up, CH)
    far.finish()


def spread_channels(n, own, width):
    col = iota((n, width), 1)
    half = (width - own) // 2
    rim = jnp.where(col < own + half, col - own, col - own - half) // 4
    return jnp.where(jnp.where(col < own, col // 8, rim) == iota((n, width), 0), 1.0, 0.0).astype(BF)


def row_distance(own, width):
    col, h = iota((H, width), 1), iota((H, width), 0)
    half = (width - own) // 2
    rim = jnp.where(col < own + half, (col - own) % 4 - 4, (col - own - half) % 4 + 8)
    return jnp.where(col < own, col % 8, rim) - h


def weights_kernel(w, mix, a_out, mf_out, a_far, mf_far, mb_far, mb_out, sems):
    far = Far(sems)
    sf, st = spread_channels(CH, CR, 2 * CR), spread_channels(MID, MR, MR)
    pf, pt = row_distance(CR, 2 * CR), row_distance(MR, MR)
    masks = [jnp.where(pf == 4 * (a - 1), 1.0, 0.0)[None] for a in range(3)]
    col = iota((CH, CR), 1)
    above = jnp.where(col < CR // 2, sf[:, CR:].astype(F32), 0.0).astype(BF)
    below = jnp.where(col < CR // 2, 0.0, sf[:, CR:].astype(F32)).astype(BF)
    for b in range(3):
        total = jnp.zeros((MID, H, CR), F32)
        for a in range(3):
            total += dot(w[3 * a + b], sf[:, :CR])[:, None, :] * masks[a][:, :, :CR]
        rest = (dot(w[b], above) + dot(w[6 + b], below))[:, None, :] * (masks[0] + masks[2])[:, :, CR:]
        a_out[b * MR : (b + 1) * MR, 0:CR] = total.reshape(MR, CR).astype(BF)
        a_out[b * MR : (b + 1) * MR, CR : 2 * CR] = rest.reshape(MR, CR).astype(BF)
    far.send(a_out, a_far)
    mask = jnp.where(pf[:, :CR] == 0, 1.0, 0.0)
    mb_out[...] = (dot(mix[...], sf[:, :CR])[:, None, :] * mask[None]).reshape(MR, CR).astype(BF)
    far.send(mb_out, mb_far)
    mask = jnp.where(pt == 0, 1.0, 0.0)
    mf_out[...] = (dot(mix[...], st, TN)[:, None, :] * mask[None]).reshape(CR, MR).astype(BF)
    far.send(mf_out, mf_far)
    far.finish()


def back_weights(w, out):
    st, pt = spread_channels(MID, MR, 2 * MR), row_distance(MR, 2 * MR)
    masks = [jnp.where(pt == -4 * (a - 1), 1.0, 0.0)[None] for a in range(3)]
    for b in range(3):
        total = jnp.zeros((CH, H, 2 * MR), F32)
        for a in range(3):
            total += dot(w[3 * a + b], st, TN)[:, None, :] * masks[a]
        out[b * CR : (b + 1) * CR] = total.reshape(CR, 2 * MR).astype(BF)


def act_kernel(x, above, below, act, edge, wide_far, wide, rows, sems):
    far = Far(sems)
    for p in range(4):
        wide[64 * p + CH : 64 * p + 64, :] = jnp.zeros((64 - CH, 4 * POS), BF)
    lane = lanes_of(CR)
    packed = jnp.zeros((CR, LANES), F32)
    for g in range(GROUPS):
        own = smooth(x[g].astype(F32).reshape(CR, LANES))
        high = smooth(above[g].astype(F32).reshape(CR // 2, LANES))
        low = smooth(below[g].astype(F32).reshape(CR // 2, LANES))
        rim = jnp.concatenate([high, low], axis=0)
        at = slice(g * LANES, (g + 1) * LANES)
        act[0:CR, at] = own.astype(BF)
        act[CR : 2 * CR, at] = rim.astype(BF)
        rows[0:CR] = own
        rows[CR : 2 * CR] = rim
        for m in range(4):
            to = slice((m * GROUPS + g) * LANES, (m * GROUPS + g + 1) * LANES)
            for p, (start, step) in enumerate(((CR, 4), (0, 8), (4, 8), (CR + CR // 2, 4))):
                wide[64 * p : 64 * p + CH, to] = rows[pl.ds(start + m, CH, stride=step), :].astype(BF)
            far.send(wide.at[:, to], wide_far.at[:, to])
        packed = jnp.where(lane // 8 == g, pltpu.roll(own, (8 * g - 124) % LANES, 1), packed)
        packed = jnp.where(lane // 8 == 8 + g, pltpu.roll(rim, (8 * g - 60) % LANES, 1), packed)
    edge[...] = packed.astype(BF)
    far.finish()


def merge_edges(from_left, from_right):
    lane = lanes_of(from_left.shape[0])
    col = lax.axis_index("col")
    has_left = jnp.where(col > 0, 1.0, 0.0)
    has_right = jnp.where(col < COLS - 1, 1.0, 0.0)
    return jnp.where(
        lane % 8 < 4,
        pltpu.roll(from_right, LANES - 4, 1) * has_right,
        pltpu.roll(from_left, 4, 1) * has_left,
    )


def at_edge(lane):
    return jnp.logical_or(lane < 4, lane >= 124)


def inside_kernel(
    x, act, weights, mixer, cg, cb, mg, mb,
    slope_far, hidden_far, block_far, pieces_far, edge_inner_far, edge_x_far,
    slope, hidden, block, pieces, edge_inner, edge_x, sems,
):
    far = Far(sems)
    lane, lane_c = lanes_of(MR), lanes_of(CR)
    gain, shift = splat(cg, MID), splat(cb, MID)
    gain_out, shift_out = splat(mg, CH), splat(mb, CH)
    packed, packed_x = jnp.zeros((MR, LANES), F32), jnp.zeros((CR, LANES), F32)
    for pair in range(GROUPS // 2):
        two = slice(pair * 2 * LANES, (pair + 1) * 2 * LANES)
        product = dot(weights[...], act[:, two])
        for half in range(2):
            g = 2 * pair + half
            p = product[:, half * LANES : (half + 1) * LANES]
            inner = (
                p[MR : 2 * MR]
                + jnp.where(lane < 4, 0.0, pltpu.roll(p[0:MR], 4, 1))
                + jnp.where(lane >= 124, 0.0, pltpu.roll(p[2 * MR : 3 * MR], LANES - 4, 1))
            )
            packed = jnp.where(lane // 8 == g, pltpu.roll(inner, (8 * g - 124) % LANES, 1), packed)
            pre = inner * gain + shift
            at = slice(g * LANES, (g + 1) * LANES)
            smoothed, steep = smooth_both(pre)
            slope[:, at] = steep * gain
            hidden[:, at] = smoothed.astype(BF)
        far.send(slope.at[:, two], slope_far.at[:, two])
        far.send(hidden.at[:, two], hidden_far.at[:, two])
        mixed = dot(mixer[...], hidden[:, two])
        for half in range(2):
            g = 2 * pair + half
            m = mixed[:, half * LANES : (half + 1) * LANES]
            own = x[g].astype(F32).reshape(CR, LANES)
            packed_x = jnp.where(lane_c // 8 == g, pltpu.roll(own, (8 * g - 124) % LANES, 1), packed_x)
            value = (own + m * gain_out + shift_out).astype(BF)
            block[g] = value.astype(F32).reshape(CH, H, LANES).astype(BF)
        g = 2 * pair
        far.send(block.at[g : g + 2], block_far.at[g : g + 2])
        swap_out(block, pieces, g)
        far.send(pieces.at[:, g : g + 2], pieces_far.at[:, g : g + 2, 2:5])
    edge_inner[...] = packed
    edge_x[...] = packed_x
    far.send(edge_inner, edge_inner_far)
    far.send(edge_x, edge_x_far)
    far.finish()


def split(value):
    high = value.astype(BF)
    return high, (value - high.astype(F32)).astype(BF)


def exact_dot(value, onehot):
    high, low = split(value)
    return dot(high, onehot) + dot(low, onehot)


def inner_kernel(
    d_far, arrived, slope_far, edge_inner_far, from_left, from_right, weights_far, back_far, cg, cb, mg, wide_far,
    grad_inner_far, down, up, half_sum_far, gmi, taps_out, rim_wide, wide, hidden_edge,
    d, slope, edge_inner, weights, back, grad_inner, half_sum, buffer, rows, sems,
):
    far = Far(sems)
    loads = [far.start(d_far.at[2 * p : 2 * p + 2], d.at[2 * p : 2 * p + 2]) for p in range(GROUPS // 2)]
    first = [far.start(weights_far.at[0:MR], weights.at[0:MR])]
    first.append(far.start(weights_far.at[2 * MR : 3 * MR], weights.at[MR : 2 * MR]))
    first.append(far.start(edge_inner_far, edge_inner))
    later = [far.start(back_far, back), far.start(slope_far, slope)]
    far.send(wide_far, wide)
    lane, lane_c = lanes_of(MR), lanes_of(CR)
    gain, shift = splat(cg, MID), splat(cb, MID)
    gain_out = splat(mg, CH)
    rim = merge_edges(from_left[...].astype(F32), from_right[...].astype(F32))
    rows[...] = rim
    for m in range(4):
        to = slice(m * LANES, (m + 1) * LANES)
        for p, (start, step) in enumerate(((0, 4), (0, 8), (4, 8), (CR // 2, 4))):
            part = rows[pl.ds(start + m, CH, stride=step), :]
            if step == 4:
                part = pltpu.roll(part, 64, 1)
            rim_wide[64 * p : 64 * p + CH, to] = part.astype(BF)
    for p in range(4):
        rim_wide[64 * p + CH : 64 * p + 64, :] = jnp.zeros((64 - CH, 4 * LANES), BF)
    rim = rim.astype(BF)
    for pair in range(GROUPS // 2):
        loads[pair].wait()
        swap_in(arrived, 2 * pair, buffer)
        for half in range(2):
            g = 2 * pair + half
            both = 0.5 * (d[g].astype(F32) + buffer[half].astype(F32)).reshape(CR, LANES)
            half_sum[g] = both.reshape(CH, H, LANES)
            gmi[:, g * LANES : (g + 1) * LANES] = (both * gain_out).astype(BF)
        far.send(half_sum.at[2 * pair : 2 * pair + 2], half_sum_far.at[2 * pair : 2 * pair + 2])
    for load in first:
        load.wait()
    outer = dot(weights[:, 0:CR], rim) + pltpu.roll(dot(weights[:, CR : 2 * CR], rim), 64, 1)
    outer = jnp.where(lane % 8 < 4, outer[MR : 2 * MR], outer[0:MR])
    pre = (edge_inner[...] + outer) * gain + shift
    hidden_edge[...], slope_edge = smooth_both(pre)
    slope_edge = slope_edge * gain

    for load in later:
        load.wait()
    packed = jnp.zeros((MR, LANES), F32)
    for pair in range(GROUPS // 2):
        two = slice(pair * 2 * LANES, (pair + 1) * 2 * LANES)
        into = dot(back[...], gmi[:, two])
        for half in range(2):
            g = 2 * pair + half
            at = slice(g * LANES, (g + 1) * LANES)
            turn = (124 - 8 * g) % LANES
            here = jnp.where(at_edge(lane), pltpu.roll(slope_edge, turn, 1), slope[:, at])
            value = into[:, half * LANES : (half + 1) * LANES] * here
            grad_inner[g] = value.reshape(MID, H, LANES).astype(BF)
            rows[0:MR] = value
            for r in range(H):
                part = jnp.concatenate([rows[pl.ds(r, MID, stride=8), :], jnp.zeros((H, LANES), F32)], axis=0)
                lane_t = lanes_of(MID + H)
                three = (
                    jnp.where(lane_t < 124, pltpu.roll(part, LANES - 4, 1), 0.0),
                    part,
                    jnp.where(lane_t >= 4, pltpu.roll(part, 4, 1), 0.0),
                )
                to = slice((r % 4 * GROUPS + g) * LANES, (r % 4 * GROUPS + g + 1) * LANES)
                for b in range(3):
                    top = 32 * (3 * (r // 4) + b)
                    taps_out[top : top + 32, to] = three[b].astype(BF)
            packed = jnp.where(lane // 8 == g, pltpu.roll(value, (8 * g - 124) % LANES, 1), packed)
        far.send(grad_inner.at[2 * pair : 2 * pair + 2], grad_inner_far.at[2 * pair : 2 * pair + 2])
    send_rows(grad_inner, down, up, MID)
    rows[0:MR] = packed
    for r in range(H):
        part = jnp.concatenate([rows[pl.ds(r, MID, stride=8), :], jnp.zeros((H, LANES), F32)], axis=0)
        lane_t = lanes_of(MID + H)
        low = jnp.where(lane_t % 8 < 4, part, 0.0)
        three = (part - low, jnp.zeros_like(part), low)
        to = slice(4 * POS + r % 4 * LANES, 4 * POS + (r % 4 + 1) * LANES)
        for b in range(3):
            top = 32 * (3 * (r // 4) + b)
            taps_out[top : top + 32, to] = three[b].astype(BF)
    far.finish()


def holder(t, yh, zh, xh):
    xl, yl, core, zl = t // 8, t // 4 % 2, t // 2 % 2, t % 2
    return (4 * xl + 2 * yh + yl) * 2 + core, 4 * zh + 2 * zl + xh


def holders(t):
    return [holder(t, *at) for at in near_groups()]


def near_groups():
    return [(yh, zh, xh) for yh in range(2) for zh in range(2) for xh in range(2)]


def sums_kernel(
    wide, gmi, taps, rim_wide, hidden_edge, hidden_far, edge_x_far, mixer_far, mg, mb, pieces_in,
    pieces_far, edge_block_far,
    hidden, edge_x, mixer, ends, edge_block, sums_out, sems,
):
    far = Far(sems)
    loads = [far.start(mixer_far, mixer), far.start(edge_x_far, edge_x)]
    tails = [
        far.start(pieces_in.at[r, :, 2:5], ends.at[i]) for i, r in enumerate((0, ROWS - 1))
    ]
    late = far.start(hidden_far, hidden)
    total = dot(taps[:, 4 * POS :], rim_wide[...], NT)
    total += dot(taps[:, 0 : 4 * POS], wide[...], NT)
    for load in loads:
        load.wait()
    value = edge_x[...] + dot(mixer[...], hidden_edge[...].astype(BF)) * splat(mg, CH) + splat(mb, CH)
    value = value.astype(BF).astype(F32)
    edge_block[...] = value
    far.send(edge_block, edge_block_far)
    parts = value.reshape(3, ROWS, H, LANES)
    parts = swap_blocks([parts[:, i].reshape(3 * H, LANES) for i in range(ROWS)])
    for load in tails:
        load.wait()
    low = iota((3, H, LANES), 2) % 8 < 4
    for g in range(GROUPS):
        lower = pltpu.roll(parts[g], LANES - 4, 1).reshape(3, H, LANES)
        upper = pltpu.roll(parts[g], 4, 1).reshape(3, H, LANES)
        ends[0, g] = jnp.where(low, lower, ends[0, g].astype(F32)).astype(BF)
        ends[1, g] = jnp.where(low, ends[1, g].astype(F32), upper).astype(BF)
    for i, r in enumerate((0, ROWS - 1)):
        far.send(ends.at[i], pieces_far.at[r, :, 2:5])
    late.wait()
    lane = lanes_of(MR)
    for g in range(GROUPS):
        at = slice(g * LANES, (g + 1) * LANES)
        moved = pltpu.roll(hidden_edge[...], (124 - 8 * g) % LANES, 1)
        hidden[:, at] = jnp.where(at_edge(lane), moved, hidden[:, at].astype(F32)).astype(BF)
    mixwide = dot(hidden[...], gmi[...], NT)
    h, col = iota((H, CR), 0), iota((H, CR), 1)
    same = jnp.where(col % 8 == h, 1.0, 0.0)[None]
    mixed = jnp.sum(mixwide.reshape(MID, H, CR) * same, axis=1)
    col, lane_s = iota((CR, LANES), 0), iota((CR, LANES), 1)
    mixed = exact_dot(mixed, jnp.where(col // 8 + 64 == lane_s, 1.0, 0.0).astype(BF))
    lane = lanes_of(MID)
    blocks, thirds = [], []
    for b in range(3):
        near, next_one = total[32 * b : 32 * b + MID], total[32 * (3 + b) : 32 * (3 + b) + MID]
        moved = pltpu.roll(next_one[:, 0:LANES], 64, 1)
        ahead = pltpu.roll(next_one[:, LANES : 2 * LANES], 64, 1)
        blocks.append(near[:, 0:LANES] + jnp.where(lane < 64, moved, ahead))
        thirds.append(jnp.where(lane < 64, near[:, LANES : 2 * LANES] + ahead, 0.0))
    blocks.append(thirds[0] + pltpu.roll(thirds[1], 64, 1))
    blocks.append(thirds[2] + mixed)
    blocks.append(jnp.zeros((MID, LANES), F32))
    for t in range(ROWS):
        part = blocks[t // 3][t % 3 * H : (t % 3 + 1) * H]
        high = part.astype(BF).astype(F32)
        both = jnp.concatenate([high[None], (part - high)[None]], axis=0).astype(BF)
        for r, c in holders(t):
            sums_out[r, c] = both
        if t % 2:
            for r in sorted({r for r, _ in holders(t)}):
                far.send(sums_out.at[r], pieces_far.at[r, :, 0:2])
    far.finish()


def spread_kernel(
    grad_inner_far, above, below, w, half_far, x_far, block_far, edge_block_far,
    edge, out_far, edge_value_far, edge_slope_far, block_out_far,
    weights, rhs, grad_inner, half_sum, x, block, edge_block, out, edge_value, edge_slope, sems,
):
    far = Far(sems)
    first = far.start(grad_inner_far, grad_inner)
    loads = [far.start(half_far, half_sum), far.start(x_far, x)]
    last = [far.start(block_far, block), far.start(edge_block_far, edge_block)]
    back_weights(w, weights)
    first.wait()
    lane = lanes_of(CR)
    packed, packed_value, packed_slope = (jnp.zeros((CR, LANES), F32) for _ in range(3))
    for load in loads:
        load.wait()
    for pair in range(GROUPS // 2):
        for half in range(2):
            g = 2 * pair + half
            at = slice(half * LANES, (half + 1) * LANES)
            rhs[0:MR, at] = grad_inner[g].astype(F32).reshape(MR, LANES).astype(BF)
            rhs[MR : MR + MR // 2, at] = above[g].astype(F32).reshape(MR // 2, LANES).astype(BF)
            rhs[MR + MR // 2 : 2 * MR, at] = below[g].astype(F32).reshape(MR // 2, LANES).astype(BF)
        product = dot(weights[...], rhs[...])
        for half in range(2):
            g = 2 * pair + half
            p = product[:, half * LANES : (half + 1) * LANES]
            left, mid, right = p[0:CR], p[CR : 2 * CR], p[2 * CR : 3 * CR]
            total = (
                mid
                + jnp.where(lane < 124, pltpu.roll(left, LANES - 4, 1), 0.0)
                + jnp.where(lane >= 4, pltpu.roll(right, 4, 1), 0.0)
            )
            slope = smooth_slope(x[g].astype(F32).reshape(CR, LANES))
            value = half_sum[g].reshape(CR, LANES) + total * slope
            out[g] = value.reshape(CH, H, LANES).astype(BF)
            far.send(out.at[g], out_far.at[g])
            here = lane // 8 == g
            turn_by = (8 * g - 124) % LANES
            packed = jnp.where(here, pltpu.roll(jnp.where(lane >= 124, right, left), turn_by, 1), packed)
            packed_value = jnp.where(here, pltpu.roll(value, turn_by, 1), packed_value)
            packed_slope = jnp.where(here, pltpu.roll(slope, turn_by, 1), packed_slope)
    edge[...] = packed[0 : CR // 2] + pltpu.roll(packed[CR // 2 : CR], 64, 1)
    edge_value[...] = packed_value
    edge_slope[...] = packed_slope
    far.send(edge_value, edge_value_far)
    far.send(edge_slope, edge_slope_far)
    for load in last:
        load.wait()
    for g in range(GROUPS):
        moved = pltpu.roll(edge_block[...], (124 - 8 * g) % LANES, 1)
        value = jnp.where(at_edge(lane), moved, block[g].astype(F32).reshape(CR, LANES))
        block[g] = value.reshape(CH, H, LANES).astype(BF)
        far.send(block.at[g], block_out_far.at[g])
    far.finish()


def total_kernel(arrived, out):
    total = jnp.zeros((H, LANES), F32)
    for g in range(COLS):
        part = arrived[:, g, 0:2].astype(F32)
        total += jnp.sum(part[:, 0] + part[:, 1], axis=0)
    out[...] = jnp.broadcast_to((total * (1.0 / (ROWS * H * COLS)))[None], (ROWS, H, LANES))


def last_kernel(
    block_far, arrived_far, value_far, edge_value_far, edge_slope_far, from_left, from_right, out_far, grad_far,
    block, arrived, out, value, grad, edge_value, edge_slope, sems,
):
    far = Far(sems)
    first = [far.start(edge_value_far, edge_value), far.start(edge_slope_far, edge_slope)]
    loads = [far.start(value_far.at[g], value.at[g]) for g in range(GROUPS)]
    later = [
        (far.start(block_far.at[g], block.at[g]), far.start(arrived_far.at[:, g, 2:5], arrived.at[:, g]))
        for g in range(GROUPS)
    ]
    lane = lanes_of(CR)
    rim = merge_edges(from_left[...], from_right[...])
    rim = jnp.concatenate([rim, pltpu.roll(rim, 64, 1)], axis=0)
    for load in first:
        load.wait()
    rim = edge_value[...] + rim * edge_slope[...]
    for g in range(GROUPS):
        loads[g].wait()
        moved = pltpu.roll(rim, (124 - 8 * g) % LANES, 1)
        total = jnp.where(at_edge(lane), moved, value[g].astype(F32).reshape(CR, LANES))
        grad[g] = total.reshape(CH, H, LANES).astype(BF)
        far.send(grad.at[g], grad_far.at[g])
    for g in range(GROUPS):
        for load in later[g]:
            load.wait()
        for k in range(3):
            at = slice(k * ROWS, (k + 1) * ROWS)
            both = 0.5 * (block[g, at].astype(F32) + turn(arrived[:, g, k]).astype(F32))
            out[g, at] = both.astype(BF)
        far.send(out.at[g], out_far.at[g])
    far.finish()


def unpack_kernel(tiles, conv, mix):
    order = ((0, 3), (1, 4), (2, 5), (6, 7), (8, None))
    for p, (left, right) in enumerate(order):
        value = tiles[3 * p : 3 * p + 3].reshape(3 * H, LANES)
        conv[left] = value[:, 0:CH]
        if right is None:
            mix[...] = value[:, 64 : 64 + CH]
        else:
            conv[right] = value[:, 64 : 64 + CH]


def both_ways(first, second, axis):
    count = lax.axis_size(axis)
    onward = [(i, (i + 1) % count) for i in range(count)]
    back = [(t, s) for s, t in onward]
    return lax.ppermute(first, axis, onward), lax.ppermute(second, axis, back)


def local(pair_map, cotangent, conv_weight, conv_gain, conv_bias, mix_weight, mix_gain, mix_bias):
    tile = (GROUPS, CH, H, LANES)
    cut = (ROWS, COLS, 3, H, LANES)
    everyone = ("row", "col")
    vmem = pltpu.VMEM
    down, up, d_pieces = call(
        first_kernel, [((GROUPS, CH // 2, H, LANES), BF)] * 2 + [(cut, BF)], (pair_map, cotangent), "first",
        far=(0, 1), far_out=(2,), scratch=[vmem(tile, BF), vmem(tile, BF), vmem(cut, BF)], copies=3 * GROUPS,
    )
    above, below = both_ways(down, up, "row")
    d_arrived = lax.all_to_all(d_pieces.reshape(ROWS * COLS, 3, H, LANES), everyone, 0, 0, tiled=True)
    d_arrived = d_arrived.reshape(cut)

    taps = jnp.transpose(conv_weight, (2, 3, 0, 1)).reshape(9, MID, CH)
    wf, mf, wf_far, mf_far, mbk = call(
        weights_kernel,
        [((3 * MR, 2 * CR), BF), ((CR, MR), BF)] * 2 + [((MR, CR), BF)],
        (taps, mix_weight.T), "weights", far_out=(2, 3, 4), scratch=[vmem((MR, CR), BF)], copies=3,
    )
    act, edge, wide = call(
        act_kernel,
        [((2 * CR, POS), BF), ((CR, LANES), BF), ((256, 4 * POS), BF)],
        (pair_map, above, below), "act", far_out=(2,), copies=4 * GROUPS,
        scratch=[vmem((256, 4 * POS), BF), vmem((2 * CR, LANES), F32)],
    )
    five = (ROWS, COLS, 5, H, LANES)
    slope, hidden, block, pieces, edge_inner, edge_x = call(
        inside_kernel,
        [((MR, POS), F32), ((MR, POS), BF), (tile, BF), (five, BF), ((MR, LANES), F32), ((CR, LANES), F32)],
        (pair_map, act, wf, mf, conv_gain, conv_bias, mix_gain, mix_bias),
        "inside", smem=(4, 5, 6, 7), far_out=(0, 1, 2, 3, 4, 5),
        scratch=[
            vmem((MR, POS), F32), vmem((MR, POS), BF), vmem(tile, BF), vmem(cut, BF),
            vmem((MR, LANES), F32), vmem((CR, LANES), F32),
        ],
        copies=2 * GROUPS + 2,
    )
    edge, edge_inner = lax.optimization_barrier((edge, edge_inner))
    from_left, from_right = both_ways(edge, edge, "col")
    grad_inner, g_down, g_up, half_sum, gmi, tap_rows, rim_wide, wide, hidden_edge = call(
        inner_kernel,
        [
            ((GROUPS, MID, H, LANES), BF),
            ((GROUPS, MID // 2, H, LANES), BF),
            ((GROUPS, MID // 2, H, LANES), BF),
            (tile, F32),
            ((CR, POS), BF),
            ((192, 4 * POS + 4 * LANES), BF),
            ((256, 4 * LANES), BF),
            ((256, 4 * POS), BF),
            ((MR, LANES), F32),
        ],
        (
            cotangent, d_arrived, slope, edge_inner, from_left, from_right, wf_far, mbk,
            conv_gain, conv_bias, mix_gain, wide,
        ),
        "inner", smem=(8, 9, 10), far=(0, 2, 3, 6, 7, 11), far_out=(0, 3),
        scratch=[
            vmem(tile, BF), vmem((MR, POS), F32), vmem((MR, LANES), F32),
            vmem((2 * MR, 2 * CR), BF), vmem((MR, CR), BF),
            vmem((GROUPS, MID, H, LANES), BF), vmem(tile, F32),
            vmem((2, CH, H, LANES), BF), vmem((CR, LANES), F32),
        ],
        copies=18,
    )
    g_above, g_below = both_ways(g_down, g_up, "row")
    pieces, edge_block = call(
        sums_kernel, [(five, BF), ((CR, LANES), F32)],
        (wide, gmi, tap_rows, rim_wide, hidden_edge, hidden, edge_x, mf_far, mix_gain, mix_bias, pieces), "sums",
        smem=(8, 9), far=(5, 6, 7, 10), far_out=(0, 1), alias={10: 0},
        scratch=[
            vmem((MR, POS), BF), vmem((CR, LANES), F32), vmem((CR, MR), BF), vmem((2, COLS, 3, H, LANES), BF),
            vmem((CR, LANES), F32), vmem((ROWS, COLS, 2, H, LANES), BF),
        ],
        copies=ROWS + 8,
    )
    pieces, g_above, g_below = lax.optimization_barrier((pieces, g_above, g_below))
    arrived = lax.all_to_all(pieces.reshape(ROWS * COLS, 5, H, LANES), everyone, 0, 0, tiled=True)
    arrived = arrived.reshape(five)
    (sums,) = call(
        total_kernel, [((ROWS, H, LANES), F32)], (arrived,), "total", flops=500_000_000
    )
    groups = [[r * COLS + c for r, c in (holder(t, *at) for t in range(ROWS))] for at in near_groups()]
    spread_sums = lax.all_to_all(sums, everyone, 0, 0, axis_index_groups=groups, tiled=True)
    taps, _ = lax.optimization_barrier((taps, pieces))
    g_edge, inputs, edge_value, edge_slope, block = call(
        spread_kernel,
        [((CR // 2, LANES), F32), (tile, BF), ((CR, LANES), F32), ((CR, LANES), F32), (tile, BF)],
        (grad_inner, g_above, g_below, taps, half_sum, pair_map, block, edge_block),
        "spread", far=(0, 4, 5, 6, 7), far_out=(1, 2, 3, 4), copies=2 * GROUPS + 7,
        scratch=[
            vmem((3 * CR, 2 * MR), BF), vmem((2 * MR, 2 * LANES), BF), vmem((GROUPS, MID, H, LANES), BF),
            vmem(tile, F32), vmem(tile, BF), vmem(tile, BF), vmem((CR, LANES), F32), vmem(tile, BF),
            vmem((CR, LANES), F32), vmem((CR, LANES), F32),
        ],
    )
    g_left, g_right = both_ways(g_edge, g_edge, "col")
    g_left, g_right, block, _ = lax.optimization_barrier((g_left, g_right, block, sums))
    symmetric, grad_input = call(
        last_kernel, [(tile, BF)] * 2, (block, arrived, inputs, edge_value, edge_slope, g_left, g_right), "last",
        far=(0, 1, 2, 3, 4), far_out=(0, 1), copies=5 * GROUPS + 2,
        scratch=[
            vmem(tile, BF), vmem(cut, BF), vmem(tile, BF), vmem(tile, BF), vmem(tile, BF),
            vmem((CR, LANES), F32), vmem((CR, LANES), F32),
        ],
    )
    conv, mix = call(
        unpack_kernel, [((9, MID, CH), F32), ((MID, CH), F32)], (spread_sums,), "unpack", flops=100_000_000
    )
    grad_conv = jnp.transpose(conv.reshape(3, 3, MID, CH), (2, 3, 0, 1))
    return symmetric, grad_input, grad_conv, mix.T


def solution(mesh):
    field = P(None, None, "row", "col")
    return jax.shard_map(
        local,
        mesh=mesh,
        in_specs=(field, field, P(), P(), P(), P(), P(), P()),
        out_specs=(field, field, P(), P()),
        check_vma=False,
    )
```

```python
import functools

import jax
import jax.numpy as jnp
from jax import lax
from jax.experimental import pallas as pl
from jax.experimental.pallas import tpu as pltpu
from jax.sharding import PartitionSpec as P

BF = jnp.bfloat16
F32 = jnp.float32
CH, MID, GROUPS, H, LANES, ROWS, COLS = 48, 24, 8, 8, 128, 16, 8
POS = GROUPS * LANES
CR, MR = CH * H, MID * H
TANH_SCALE = 0.7978845608028654
CUBIC = 0.044715
NN = (((1,), (0,)), ((), ()))
NT = (((1,), (1,)), ((), ()))
TN = (((0,), (0,)), ((), ()))


def smooth(v):
    t = jnp.tanh(TANH_SCALE * (v + CUBIC * (v * v * v)))
    return 0.5 * v * (1.0 + t)


def smooth_slope(v):
    s = v * v
    t = jnp.tanh(TANH_SCALE * (v + CUBIC * (v * s)))
    return 0.5 * (1.0 + t) + (0.5 * v) * (1.0 - t * t) * (TANH_SCALE * (1.0 + (3.0 * CUBIC) * s))


def smooth_both(v):
    s = v * v
    t = jnp.tanh(TANH_SCALE * (v + CUBIC * (v * s)))
    upper, half = 0.5 * (1.0 + t), 0.5 * v
    return half * (1.0 + t), upper + half * (1.0 - t * t) * (TANH_SCALE * (1.0 + (3.0 * CUBIC) * s))


def dot(a, b, dims=NN):
    return lax.dot_general(a, b, dims, preferred_element_type=F32)


def iota(shape, dim):
    return lax.broadcasted_iota(jnp.int32, shape, dim)


def identity(n):
    return jnp.where(iota((n, n), 0) == iota((n, n), 1), 1.0, 0.0).astype(BF)


def lanes_of(rows):
    return iota((rows, LANES), 1)


class Far:
    def __init__(self, sems):
        self.sems, self.used, self.open = sems, 0, []

    def start(self, source, target):
        copy = pltpu.make_async_copy(source, target, self.sems.at[self.used])
        self.used += 1
        copy.start()
        return copy

    def send(self, source, target):
        self.open.append(self.start(source, target))

    def finish(self):
        for copy in self.open:
            copy.wait()


def call(kernel, outs, args, name, smem=(), far=(), far_out=(), flops=4_000_000_000, scratch=(), copies=0, limit=16, alias=None):
    specs = [
        pl.BlockSpec(memory_space=pltpu.SMEM if i in smem else pltpu.HBM if i in far else pltpu.VMEM)
        for i in range(len(args))
    ]
    scratch = list(scratch)
    if copies:
        scratch.append(pltpu.SemaphoreType.DMA((copies,)))
    return pl.pallas_call(
        kernel,
        name=name,
        out_shape=[
            pltpu.HBM(s, t) if i in far_out else jax.ShapeDtypeStruct(s, t)
            for i, (s, t) in enumerate(outs)
        ],
        in_specs=specs,
        out_specs=[
            pl.BlockSpec(memory_space=pltpu.HBM if i in far_out else pltpu.VMEM)
            for i in range(len(outs))
        ],
        scratch_shapes=scratch,
        input_output_aliases=alias or {},
        compiler_params=pltpu.CompilerParams(vmem_limit_bytes=limit * 1024 * 1024),
        cost_estimate=pl.CostEstimate(flops=flops, bytes_accessed=1_000_000, transcendentals=0),
    )(
        *(
            pltpu.with_memory_space_constraint(v, pltpu.HBM) if i in far else v
            for i, v in enumerate(args)
        )
    )


def splat(values, count):
    return jnp.concatenate([jnp.full((H, LANES), values[o], F32) for o in range(count)], axis=0)


def pack_rows(field, count):
    pairs = field.reshape(count // 2, 2, H, LANES)
    even, odd = pairs[:, 0], pairs[:, 1]
    low = iota(even.shape, 1) < 4
    last = jnp.where(low, pltpu.roll(even, 4, 1), odd)
    first = jnp.where(low, even, pltpu.roll(odd, 4, 1))
    return last, first


def send_rows(source, down, up, count):
    at_end = (lax.axis_index("row") == ROWS - 1).astype(jnp.int32)
    at_start = (lax.axis_index("row") == 0).astype(jnp.int32)
    for g in range(GROUPS):
        before = g - at_end
        last, _ = pack_rows(source[jnp.maximum(before, 0)].astype(F32), count)
        down[g] = jnp.where(before >= 0, last, 0.0).astype(BF)
        after = g + at_start
        _, first = pack_rows(source[jnp.minimum(after, GROUPS - 1)].astype(F32), count)
        up[g] = jnp.where(after < GROUPS, first, 0.0).astype(BF)


def swap_blocks(parts):
    lane = iota(parts[0].shape, 1)
    parts = list(parts)
    for k in range(4):
        m = 1 << k
        high = (lane // (8 * m)) % 2 == 1
        for i in range(ROWS):
            if i & m:
                continue
            a, b = parts[i], parts[i | m]
            parts[i] = jnp.where(high, pltpu.roll(b, 8 * m, 1), a)
            parts[i | m] = jnp.where(high, b, pltpu.roll(a, LANES - 8 * m, 1))
    return parts


def turn(tiles):
    return tiles.reshape(LANES, LANES).T.reshape(ROWS, H, LANES)


def swap_in(pieces, g, buffer):
    parts = swap_blocks([pieces[r, g : g + 2].reshape(6 * H, LANES) for r in range(ROWS)])
    for i in range(ROWS):
        value = parts[i].reshape(2, 3, H, LANES)
        for n in range(2):
            for k in range(3):
                buffer[n, k * ROWS + i] = value[n, k]


def swap_out(block, pieces, g):
    parts = swap_blocks(
        [
            jnp.concatenate([block[g + n, k * ROWS + i] for n in range(2) for k in range(3)], axis=0)
            for i in range(ROWS)
        ]
    )
    for r in range(ROWS):
        pieces[r, g : g + 2] = parts[r].reshape(2, 3, H, LANES)


def first_kernel(x_far, d_far, down, up, pieces, x, d, turned, sems):
    far = Far(sems)
    loads = [far.start(d_far.at[g], d.at[g]) for g in range(GROUPS)]
    later = [far.start(x_far.at[g], x.at[g]) for g in range(GROUPS)]
    for g in range(GROUPS):
        loads[g].wait()
        for k in range(3):
            turned[:, g, k] = turn(d[g, k * ROWS : (k + 1) * ROWS])
        far.send(turned.at[:, g], pieces.at[:, g])
    for load in later:
        load.wait()
    send_rows(x, down, up, CH)
    far.finish()


def spread_channels(n, own, width):
    col = iota((n, width), 1)
    half = (width - own) // 2
    rim = jnp.where(col < own + half, col - own, col - own - half) // 4
    return jnp.where(jnp.where(col < own, col // 8, rim) == iota((n, width), 0), 1.0, 0.0).astype(BF)


def row_distance(own, width):
    col, h = iota((H, width), 1), iota((H, width), 0)
    half = (width - own) // 2
    rim = jnp.where(col < own + half, (col - own) % 4 - 4, (col - own - half) % 4 + 8)
    return jnp.where(col < own, col % 8, rim) - h


def weights_kernel(w, mix, a_out, mf_out, a_far, mf_far, mb_far, mb_out, sems):
    far = Far(sems)
    sf, st = spread_channels(CH, CR, 2 * CR), spread_channels(MID, MR, MR)
    pf, pt = row_distance(CR, 2 * CR), row_distance(MR, MR)
    masks = [jnp.where(pf == 4 * (a - 1), 1.0, 0.0)[None] for a in range(3)]
    col = iota((CH, CR), 1)
    above = jnp.where(col < CR // 2, sf[:, CR:].astype(F32), 0.0).astype(BF)
    below = jnp.where(col < CR // 2, 0.0, sf[:, CR:].astype(F32)).astype(BF)
    for b in range(3):
        total = jnp.zeros((MID, H, CR), F32)
        for a in range(3):
            total += dot(w[3 * a + b], sf[:, :CR])[:, None, :] * masks[a][:, :, :CR]
        rest = (dot(w[b], above) + dot(w[6 + b], below))[:, None, :] * (masks[0] + masks[2])[:, :, CR:]
        a_out[b * MR : (b + 1) * MR, 0:CR] = total.reshape(MR, CR).astype(BF)
        a_out[b * MR : (b + 1) * MR, CR : 2 * CR] = rest.reshape(MR, CR).astype(BF)
    far.send(a_out, a_far)
    mask = jnp.where(pf[:, :CR] == 0, 1.0, 0.0)
    mb_out[...] = (dot(mix[...], sf[:, :CR])[:, None, :] * mask[None]).reshape(MR, CR).astype(BF)
    far.send(mb_out, mb_far)
    mask = jnp.where(pt == 0, 1.0, 0.0)
    mf_out[...] = (dot(mix[...], st, TN)[:, None, :] * mask[None]).reshape(CR, MR).astype(BF)
    far.send(mf_out, mf_far)
    far.finish()


def back_weights(w, out):
    st, pt = spread_channels(MID, MR, 2 * MR), row_distance(MR, 2 * MR)
    masks = [jnp.where(pt == -4 * (a - 1), 1.0, 0.0)[None] for a in range(3)]
    for b in range(3):
        total = jnp.zeros((CH, H, 2 * MR), F32)
        for a in range(3):
            total += dot(w[3 * a + b], st, TN)[:, None, :] * masks[a]
        out[b * CR : (b + 1) * CR] = total.reshape(CR, 2 * MR).astype(BF)


def act_kernel(x, above, below, act, edge, wide_far, wide, rows, sems):
    far = Far(sems)
    for p in range(4):
        wide[64 * p + CH : 64 * p + 64, :] = jnp.zeros((64 - CH, 4 * POS), BF)
    lane = lanes_of(CR)
    packed = jnp.zeros((CR, LANES), F32)
    for g in range(GROUPS):
        own = smooth(x[g].astype(F32).reshape(CR, LANES))
        high = smooth(above[g].astype(F32).reshape(CR // 2, LANES))
        low = smooth(below[g].astype(F32).reshape(CR // 2, LANES))
        rim = jnp.concatenate([high, low], axis=0)
        at = slice(g * LANES, (g + 1) * LANES)
        act[0:CR, at] = own.astype(BF)
        act[CR : 2 * CR, at] = rim.astype(BF)
        rows[0:CR] = own
        rows[CR : 2 * CR] = rim
        for m in range(4):
            to = slice((m * GROUPS + g) * LANES, (m * GROUPS + g + 1) * LANES)
            for p, (start, step) in enumerate(((CR, 4), (0, 8), (4, 8), (CR + CR // 2, 4))):
                wide[64 * p : 64 * p + CH, to] = rows[pl.ds(start + m, CH, stride=step), :].astype(BF)
            far.send(wide.at[:, to], wide_far.at[:, to])
        packed = jnp.where(lane // 8 == g, pltpu.roll(own, (8 * g - 124) % LANES, 1), packed)
        packed = jnp.where(lane // 8 == 8 + g, pltpu.roll(rim, (8 * g - 60) % LANES, 1), packed)
    edge[...] = packed.astype(BF)
    far.finish()


def merge_edges(first, second):
    lane = lanes_of(first.shape[0])
    col = lax.axis_index("col")
    odd = col % 2 == 1
    right, left = jnp.where(odd, first, second), jnp.where(odd, second, first)
    has_left = jnp.where(col > 0, 1.0, 0.0)
    has_right = jnp.where(col < COLS - 1, 1.0, 0.0)
    return jnp.where(
        lane % 8 < 4,
        pltpu.roll(right, LANES - 4, 1) * has_right,
        pltpu.roll(left, 4, 1) * has_left,
    )


def at_edge(lane):
    return jnp.logical_or(lane < 4, lane >= 124)


def inside_kernel(
    x, act, weights, mixer, cg, cb, mg, mb,
    slope_far, hidden_far, block_far, pieces_far, edge_inner_far, edge_x_far,
    slope, hidden, block, pieces, edge_inner, edge_x, sems,
):
    far = Far(sems)
    lane, lane_c = lanes_of(MR), lanes_of(CR)
    gain, shift = splat(cg, MID), splat(cb, MID)
    gain_out, shift_out = splat(mg, CH), splat(mb, CH)
    packed, packed_x = jnp.zeros((MR, LANES), F32), jnp.zeros((CR, LANES), F32)
    for pair in range(GROUPS // 2):
        two = slice(pair * 2 * LANES, (pair + 1) * 2 * LANES)
        product = dot(weights[...], act[:, two])
        for half in range(2):
            g = 2 * pair + half
            p = product[:, half * LANES : (half + 1) * LANES]
            inner = (
                p[MR : 2 * MR]
                + jnp.where(lane < 4, 0.0, pltpu.roll(p[0:MR], 4, 1))
                + jnp.where(lane >= 124, 0.0, pltpu.roll(p[2 * MR : 3 * MR], LANES - 4, 1))
            )
            packed = jnp.where(lane // 8 == g, pltpu.roll(inner, (8 * g - 124) % LANES, 1), packed)
            pre = inner * gain + shift
            at = slice(g * LANES, (g + 1) * LANES)
            smoothed, steep = smooth_both(pre)
            slope[:, at] = steep * gain
            hidden[:, at] = smoothed.astype(BF)
        far.send(slope.at[:, two], slope_far.at[:, two])
        far.send(hidden.at[:, two], hidden_far.at[:, two])
        mixed = dot(mixer[...], hidden[:, two])
        for half in range(2):
            g = 2 * pair + half
            m = mixed[:, half * LANES : (half + 1) * LANES]
            own = x[g].astype(F32).reshape(CR, LANES)
            packed_x = jnp.where(lane_c // 8 == g, pltpu.roll(own, (8 * g - 124) % LANES, 1), packed_x)
            value = (own + m * gain_out + shift_out).astype(BF)
            block[g] = value.astype(F32).reshape(CH, H, LANES).astype(BF)
        g = 2 * pair
        far.send(block.at[g : g + 2], block_far.at[g : g + 2])
        swap_out(block, pieces, g)
        far.send(pieces.at[:, g : g + 2], pieces_far.at[:, g : g + 2, 2:5])
    edge_inner[...] = packed
    edge_x[...] = packed_x
    far.send(edge_inner, edge_inner_far)
    far.send(edge_x, edge_x_far)
    far.finish()


def split(value):
    high = value.astype(BF)
    return high, (value - high.astype(F32)).astype(BF)


def exact_dot(value, onehot):
    high, low = split(value)
    return dot(high, onehot) + dot(low, onehot)


def inner_kernel(
    d_far, arrived, slope_far, hidden_far, edge_inner_far, edge_x_far, edges_a, edges_b,
    weights_far, mixer_far, back_far, pieces_in, cg, cb, mg, mb, wide_far,
    grad_inner_far, down, up, half_sum_far, pieces_far, edge_block_far, gmi, taps_out, hidden_out, rim_wide, wide,
    d, slope, hidden, edge_inner, edge_x, weights, mixer, back, grad_inner, half_sum, ends, edge_block, buffer, rows, sems,
):
    far = Far(sems)
    loads = [far.start(d_far.at[2 * p : 2 * p + 2], d.at[2 * p : 2 * p + 2]) for p in range(GROUPS // 2)]
    first = [far.start(weights_far.at[0:MR], weights.at[0:MR])]
    first.append(far.start(weights_far.at[2 * MR : 3 * MR], weights.at[MR : 2 * MR]))
    first += [far.start(edge_inner_far, edge_inner), far.start(edge_x_far, edge_x), far.start(mixer_far, mixer)]
    tails = [
        far.start(pieces_in.at[r, :, 2:5], ends.at[i]) for i, r in enumerate((0, ROWS - 1))
    ]
    later = [far.start(back_far, back), far.start(slope_far, slope), far.start(hidden_far, hidden)]
    far.send(wide_far, wide)
    lane, lane_c = lanes_of(MR), lanes_of(CR)
    gain, shift = splat(cg, MID), splat(cb, MID)
    gain_out, shift_out = splat(mg, CH), splat(mb, CH)
    rim = merge_edges(edges_a[...].astype(F32), edges_b[...].astype(F32))
    rows[...] = rim
    for m in range(4):
        to = slice(m * LANES, (m + 1) * LANES)
        for p, (start, step) in enumerate(((0, 4), (0, 8), (4, 8), (CR // 2, 4))):
            part = rows[pl.ds(start + m, CH, stride=step), :]
            if step == 4:
                part = pltpu.roll(part, 64, 1)
            rim_wide[64 * p : 64 * p + CH, to] = part.astype(BF)
    for p in range(4):
        rim_wide[64 * p + CH : 64 * p + 64, :] = jnp.zeros((64 - CH, 4 * LANES), BF)
    rim = rim.astype(BF)
    for pair in range(GROUPS // 2):
        loads[pair].wait()
        swap_in(arrived, 2 * pair, buffer)
        for half in range(2):
            g = 2 * pair + half
            both = 0.5 * (d[g].astype(F32) + buffer[half].astype(F32)).reshape(CR, LANES)
            half_sum[g] = both.reshape(CH, H, LANES)
            gmi[:, g * LANES : (g + 1) * LANES] = (both * gain_out).astype(BF)
        far.send(half_sum.at[2 * pair : 2 * pair + 2], half_sum_far.at[2 * pair : 2 * pair + 2])
    for load in first:
        load.wait()
    outer = dot(weights[:, 0:CR], rim) + pltpu.roll(dot(weights[:, CR : 2 * CR], rim), 64, 1)
    outer = jnp.where(lane % 8 < 4, outer[MR : 2 * MR], outer[0:MR])
    pre = (edge_inner[...] + outer) * gain + shift
    hidden_edge, slope_edge = smooth_both(pre)
    slope_edge = slope_edge * gain
    hidden_edge = hidden_edge.astype(BF)
    mixed = dot(mixer[...], hidden_edge)
    value = (edge_x[...] + mixed * gain_out + shift_out).astype(BF)
    edge_block[...] = value.astype(F32)
    far.send(edge_block, edge_block_far)
    hidden_edge = hidden_edge.astype(F32)
    parts = value.astype(F32).reshape(3, ROWS, H, LANES)
    parts = swap_blocks([parts[:, i].reshape(3 * H, LANES) for i in range(ROWS)])
    for load in tails:
        load.wait()
    low = iota((3, H, LANES), 2) % 8 < 4
    for g in range(GROUPS):
        lower = pltpu.roll(parts[g], LANES - 4, 1).reshape(3, H, LANES)
        upper = pltpu.roll(parts[g], 4, 1).reshape(3, H, LANES)
        ends[0, g] = jnp.where(low, lower, ends[0, g].astype(F32)).astype(BF)
        ends[1, g] = jnp.where(low, ends[1, g].astype(F32), upper).astype(BF)
    for i, r in enumerate((0, ROWS - 1)):
        far.send(ends.at[i], pieces_far.at[r, :, 2:5])

    for load in later:
        load.wait()
    packed = jnp.zeros((MR, LANES), F32)
    for pair in range(GROUPS // 2):
        two = slice(pair * 2 * LANES, (pair + 1) * 2 * LANES)
        into = dot(back[...], gmi[:, two])
        for half in range(2):
            g = 2 * pair + half
            at = slice(g * LANES, (g + 1) * LANES)
            turn = (124 - 8 * g) % LANES
            here = jnp.where(at_edge(lane), pltpu.roll(slope_edge, turn, 1), slope[:, at])
            value = into[:, half * LANES : (half + 1) * LANES] * here
            grad_inner[g] = value.reshape(MID, H, LANES).astype(BF)
            rows[0:MR] = value
            for r in range(H):
                part = jnp.concatenate([rows[pl.ds(r, MID, stride=8), :], jnp.zeros((H, LANES), F32)], axis=0)
                lane_t = lanes_of(MID + H)
                three = (
                    jnp.where(lane_t < 124, pltpu.roll(part, LANES - 4, 1), 0.0),
                    part,
                    jnp.where(lane_t >= 4, pltpu.roll(part, 4, 1), 0.0),
                )
                to = slice((r % 4 * GROUPS + g) * LANES, (r % 4 * GROUPS + g + 1) * LANES)
                for b in range(3):
                    top = 32 * (3 * (r // 4) + b)
                    taps_out[top : top + 32, to] = three[b].astype(BF)
            packed = jnp.where(lane // 8 == g, pltpu.roll(value, (8 * g - 124) % LANES, 1), packed)
            here = jnp.where(at_edge(lane), pltpu.roll(hidden_edge, turn, 1), hidden[:, at].astype(F32))
            hidden_out[:, at] = here.astype(BF)
        far.send(grad_inner.at[2 * pair : 2 * pair + 2], grad_inner_far.at[2 * pair : 2 * pair + 2])
    send_rows(grad_inner, down, up, MID)
    rows[0:MR] = packed
    for r in range(H):
        part = jnp.concatenate([rows[pl.ds(r, MID, stride=8), :], jnp.zeros((H, LANES), F32)], axis=0)
        lane_t = lanes_of(MID + H)
        low = jnp.where(lane_t % 8 < 4, part, 0.0)
        three = (part - low, jnp.zeros_like(part), low)
        to = slice(4 * POS + r % 4 * LANES, 4 * POS + (r % 4 + 1) * LANES)
        for b in range(3):
            top = 32 * (3 * (r // 4) + b)
            taps_out[top : top + 32, to] = three[b].astype(BF)
    far.finish()


def holder(t, yh, zh, xh):
    xl, yl, core, zl = t // 8, t // 4 % 2, t // 2 % 2, t % 2
    return (4 * xl + 2 * yh + yl) * 2 + core, 4 * zh + 2 * zl + xh


def holders(t):
    return [holder(t, *at) for at in near_groups()]


def near_groups():
    return [(yh, zh, xh) for yh in range(2) for zh in range(2) for xh in range(2)]


def sums_kernel(wide, gmi, taps, hidden, rim_wide, pieces_in, pieces_far, sums_out, sems):
    far = Far(sems)
    mixwide = dot(hidden[...], gmi[...], NT)
    h, col = iota((H, CR), 0), iota((H, CR), 1)
    same = jnp.where(col % 8 == h, 1.0, 0.0)[None]
    mixed = jnp.sum(mixwide.reshape(MID, H, CR) * same, axis=1)
    col, lane_s = iota((CR, LANES), 0), iota((CR, LANES), 1)
    mixed = exact_dot(mixed, jnp.where(col // 8 + 64 == lane_s, 1.0, 0.0).astype(BF))
    total = dot(taps[:, 4 * POS :], rim_wide[...], NT)
    total += dot(taps[:, 0 : 4 * POS], wide[...], NT)
    lane = lanes_of(MID)
    blocks, thirds = [], []
    for b in range(3):
        near, next_one = total[32 * b : 32 * b + MID], total[32 * (3 + b) : 32 * (3 + b) + MID]
        moved = pltpu.roll(next_one[:, 0:LANES], 64, 1)
        ahead = pltpu.roll(next_one[:, LANES : 2 * LANES], 64, 1)
        blocks.append(near[:, 0:LANES] + jnp.where(lane < 64, moved, ahead))
        thirds.append(jnp.where(lane < 64, near[:, LANES : 2 * LANES] + ahead, 0.0))
    blocks.append(thirds[0] + pltpu.roll(thirds[1], 64, 1))
    blocks.append(thirds[2] + mixed)
    blocks.append(jnp.zeros((MID, LANES), F32))
    for t in range(ROWS):
        part = blocks[t // 3][t % 3 * H : (t % 3 + 1) * H]
        high = part.astype(BF).astype(F32)
        both = jnp.concatenate([high[None], (part - high)[None]], axis=0).astype(BF)
        for r, c in holders(t):
            sums_out[r, c] = both
        if t % 2:
            for r in sorted({r for r, _ in holders(t)}):
                far.send(sums_out.at[r], pieces_far.at[r, :, 0:2])
    far.finish()


def spread_kernel(
    grad_inner_far, above, below, w, half_far, x_far, block_far, edge_block_far,
    edge, out_far, edge_value_far, edge_slope_far, block_out_far,
    weights, rhs, grad_inner, half_sum, x, block, edge_block, out, edge_value, edge_slope, sems,
):
    far = Far(sems)
    first = far.start(grad_inner_far, grad_inner)
    loads = [far.start(half_far, half_sum), far.start(x_far, x)]
    last = [far.start(block_far, block), far.start(edge_block_far, edge_block)]
    back_weights(w, weights)
    first.wait()
    lane = lanes_of(CR)
    packed, packed_value, packed_slope = (jnp.zeros((CR, LANES), F32) for _ in range(3))
    for load in loads:
        load.wait()
    for pair in range(GROUPS // 2):
        for half in range(2):
            g = 2 * pair + half
            at = slice(half * LANES, (half + 1) * LANES)
            rhs[0:MR, at] = grad_inner[g].astype(F32).reshape(MR, LANES).astype(BF)
            rhs[MR : MR + MR // 2, at] = above[g].astype(F32).reshape(MR // 2, LANES).astype(BF)
            rhs[MR + MR // 2 : 2 * MR, at] = below[g].astype(F32).reshape(MR // 2, LANES).astype(BF)
        product = dot(weights[...], rhs[...])
        for half in range(2):
            g = 2 * pair + half
            p = product[:, half * LANES : (half + 1) * LANES]
            left, mid, right = p[0:CR], p[CR : 2 * CR], p[2 * CR : 3 * CR]
            total = (
                mid
                + jnp.where(lane < 124, pltpu.roll(left, LANES - 4, 1), 0.0)
                + jnp.where(lane >= 4, pltpu.roll(right, 4, 1), 0.0)
            )
            slope = smooth_slope(x[g].astype(F32).reshape(CR, LANES))
            value = half_sum[g].reshape(CR, LANES) + total * slope
            out[g] = value.reshape(CH, H, LANES).astype(BF)
            far.send(out.at[g], out_far.at[g])
            here = lane // 8 == g
            turn_by = (8 * g - 124) % LANES
            packed = jnp.where(here, pltpu.roll(jnp.where(lane >= 124, right, left), turn_by, 1), packed)
            packed_value = jnp.where(here, pltpu.roll(value, turn_by, 1), packed_value)
            packed_slope = jnp.where(here, pltpu.roll(slope, turn_by, 1), packed_slope)
    edge[...] = packed[0 : CR // 2] + pltpu.roll(packed[CR // 2 : CR], 64, 1)
    edge_value[...] = packed_value
    edge_slope[...] = packed_slope
    far.send(edge_value, edge_value_far)
    far.send(edge_slope, edge_slope_far)
    for load in last:
        load.wait()
    for g in range(GROUPS):
        moved = pltpu.roll(edge_block[...], (124 - 8 * g) % LANES, 1)
        value = jnp.where(at_edge(lane), moved, block[g].astype(F32).reshape(CR, LANES))
        block[g] = value.reshape(CH, H, LANES).astype(BF)
        far.send(block.at[g], block_out_far.at[g])
    far.finish()


def total_kernel(arrived, out):
    total = jnp.zeros((H, LANES), F32)
    for g in range(COLS):
        part = arrived[:, g, 0:2].astype(F32)
        total += jnp.sum(part[:, 0] + part[:, 1], axis=0)
    out[...] = jnp.broadcast_to((total * (1.0 / (ROWS * H * COLS)))[None], (ROWS, H, LANES))


def last_kernel(
    block_far, arrived_far, value_far, edge_value_far, edge_slope_far, edges_a, edges_b, out_far, grad_far,
    block, arrived, out, value, grad, edge_value, edge_slope, sems,
):
    far = Far(sems)
    first = [far.start(edge_value_far, edge_value), far.start(edge_slope_far, edge_slope)]
    loads = [far.start(value_far.at[g], value.at[g]) for g in range(GROUPS)]
    later = [
        (far.start(block_far.at[g], block.at[g]), far.start(arrived_far.at[:, g, 2:5], arrived.at[:, g]))
        for g in range(GROUPS)
    ]
    lane = lanes_of(CR)
    rim = merge_edges(edges_a[...], edges_b[...])
    rim = jnp.concatenate([rim, pltpu.roll(rim, 64, 1)], axis=0)
    for load in first:
        load.wait()
    rim = edge_value[...] + rim * edge_slope[...]
    for g in range(GROUPS):
        loads[g].wait()
        moved = pltpu.roll(rim, (124 - 8 * g) % LANES, 1)
        total = jnp.where(at_edge(lane), moved, value[g].astype(F32).reshape(CR, LANES))
        grad[g] = total.reshape(CH, H, LANES).astype(BF)
        far.send(grad.at[g], grad_far.at[g])
    for g in range(GROUPS):
        for load in later[g]:
            load.wait()
        for k in range(3):
            at = slice(k * ROWS, (k + 1) * ROWS)
            both = 0.5 * (block[g, at].astype(F32) + turn(arrived[:, g, k]).astype(F32))
            out[g, at] = both.astype(BF)
        far.send(out.at[g], out_far.at[g])
    far.finish()


def unpack_kernel(tiles, conv, mix):
    order = ((0, 3), (1, 4), (2, 5), (6, 7), (8, None))
    for p, (left, right) in enumerate(order):
        value = tiles[3 * p : 3 * p + 3].reshape(3 * H, LANES)
        conv[left] = value[:, 0:CH]
        if right is None:
            mix[...] = value[:, 64 : 64 + CH]
        else:
            conv[right] = value[:, 64 : 64 + CH]


def both_ways(first, second, axis):
    count = lax.axis_size(axis)
    onward = [(i, (i + 1) % count) for i in range(count)]
    back = [(t, s) for s, t in onward]
    return lax.ppermute(first, axis, onward), lax.ppermute(second, axis, back)


def swap_cols(edge):
    count = lax.axis_size("col")
    first = [(i, i ^ 1) for i in range(count)]
    second = [(i, min(max(((i + 1) ^ 1) - 1, 0), count - 1)) for i in range(count)]
    return lax.ppermute(edge, "col", second), lax.ppermute(edge, "col", first)


def local(pair_map, cotangent, conv_weight, conv_gain, conv_bias, mix_weight, mix_gain, mix_bias):
    tile = (GROUPS, CH, H, LANES)
    cut = (ROWS, COLS, 3, H, LANES)
    everyone = ("row", "col")
    vmem = pltpu.VMEM
    down, up, d_pieces = call(
        first_kernel, [((GROUPS, CH // 2, H, LANES), BF)] * 2 + [(cut, BF)], (pair_map, cotangent), "first",
        far=(0, 1), far_out=(2,), scratch=[vmem(tile, BF), vmem(tile, BF), vmem(cut, BF)], copies=3 * GROUPS,
    )
    above, below = both_ways(down, up, "row")
    d_arrived = lax.all_to_all(d_pieces.reshape(ROWS * COLS, 3, H, LANES), everyone, 0, 0, tiled=True)
    d_arrived = d_arrived.reshape(cut)

    taps = jnp.transpose(conv_weight, (2, 3, 0, 1)).reshape(9, MID, CH)
    wf, mf, wf_far, mf_far, mbk = call(
        weights_kernel,
        [((3 * MR, 2 * CR), BF), ((CR, MR), BF)] * 2 + [((MR, CR), BF)],
        (taps, mix_weight.T), "weights", far_out=(2, 3, 4), scratch=[vmem((MR, CR), BF)], copies=3,
    )
    act, edge, wide = call(
        act_kernel,
        [((2 * CR, POS), BF), ((CR, LANES), BF), ((256, 4 * POS), BF)],
        (pair_map, above, below), "act", far_out=(2,), copies=4 * GROUPS,
        scratch=[vmem((256, 4 * POS), BF), vmem((2 * CR, LANES), F32)],
    )
    edges_a, edges_b = swap_cols(edge)
    five = (ROWS, COLS, 5, H, LANES)
    slope, hidden, block, pieces, edge_inner, edge_x = call(
        inside_kernel,
        [((MR, POS), F32), ((MR, POS), BF), (tile, BF), (five, BF), ((MR, LANES), F32), ((CR, LANES), F32)],
        (pair_map, act, wf, mf, conv_gain, conv_bias, mix_gain, mix_bias),
        "inside", smem=(4, 5, 6, 7), far_out=(0, 1, 2, 3, 4, 5),
        scratch=[
            vmem((MR, POS), F32), vmem((MR, POS), BF), vmem(tile, BF), vmem(cut, BF),
            vmem((MR, LANES), F32), vmem((CR, LANES), F32),
        ],
        copies=2 * GROUPS + 2,
    )
    grad_inner, g_down, g_up, half_sum, pieces, edge_block, gmi, tap_rows, hidden, rim_wide, wide = call(
        inner_kernel,
        [
            ((GROUPS, MID, H, LANES), BF),
            ((GROUPS, MID // 2, H, LANES), BF),
            ((GROUPS, MID // 2, H, LANES), BF),
            (tile, F32),
            (five, BF),
            ((CR, LANES), F32),
            ((CR, POS), BF),
            ((192, 4 * POS + 4 * LANES), BF),
            ((MR, POS), BF),
            ((256, 4 * LANES), BF),
            ((256, 4 * POS), BF),
        ],
        (
            cotangent, d_arrived, slope, hidden, edge_inner, edge_x, edges_a, edges_b,
            wf_far, mf_far, mbk, pieces, conv_gain, conv_bias, mix_gain, mix_bias, wide,
        ),
        "inner", smem=(12, 13, 14, 15), far=(0, 2, 3, 4, 5, 8, 9, 10, 11, 16), far_out=(0, 3, 4, 5), alias={11: 4},
        scratch=[
            vmem(tile, BF), vmem((MR, POS), F32), vmem((MR, POS), BF), vmem((MR, LANES), F32), vmem((CR, LANES), F32),
            vmem((2 * MR, 2 * CR), BF), vmem((CR, MR), BF), vmem((MR, CR), BF),
            vmem((GROUPS, MID, H, LANES), BF), vmem(tile, F32), vmem((2, COLS, 3, H, LANES), BF),
            vmem((CR, LANES), F32), vmem((2, CH, H, LANES), BF), vmem((CR, LANES), F32),
        ],
        copies=26,
    )
    g_above, g_below = both_ways(g_down, g_up, "row")
    (pieces,) = call(
        sums_kernel, [(five, BF)], (wide, gmi, tap_rows, hidden, rim_wide, pieces), "sums",
        far=(5,), far_out=(0,), alias={5: 0}, scratch=[vmem((ROWS, COLS, 2, H, LANES), BF)], copies=ROWS,
    )
    pieces, g_above, g_below = lax.optimization_barrier((pieces, g_above, g_below))
    arrived = lax.all_to_all(pieces.reshape(ROWS * COLS, 5, H, LANES), everyone, 0, 0, tiled=True)
    arrived = arrived.reshape(five)
    (sums,) = call(
        total_kernel, [((ROWS, H, LANES), F32)], (arrived,), "total", flops=500_000_000
    )
    groups = [[r * COLS + c for r, c in (holder(t, *at) for t in range(ROWS))] for at in near_groups()]
    spread_sums = lax.all_to_all(sums, everyone, 0, 0, axis_index_groups=groups, tiled=True)
    taps, _ = lax.optimization_barrier((taps, pieces))
    g_edge, inputs, edge_value, edge_slope, block = call(
        spread_kernel,
        [((CR // 2, LANES), F32), (tile, BF), ((CR, LANES), F32), ((CR, LANES), F32), (tile, BF)],
        (grad_inner, g_above, g_below, taps, half_sum, pair_map, block, edge_block),
        "spread", far=(0, 4, 5, 6, 7), far_out=(1, 2, 3, 4), copies=2 * GROUPS + 7,
        scratch=[
            vmem((3 * CR, 2 * MR), BF), vmem((2 * MR, 2 * LANES), BF), vmem((GROUPS, MID, H, LANES), BF),
            vmem(tile, F32), vmem(tile, BF), vmem(tile, BF), vmem((CR, LANES), F32), vmem(tile, BF),
            vmem((CR, LANES), F32), vmem((CR, LANES), F32),
        ],
    )
    g_left, g_right = swap_cols(g_edge)
    g_left, g_right, block, _ = lax.optimization_barrier((g_left, g_right, block, sums))
    symmetric, grad_input = call(
        last_kernel, [(tile, BF)] * 2, (block, arrived, inputs, edge_value, edge_slope, g_left, g_right), "last",
        far=(0, 1, 2, 3, 4), far_out=(0, 1), copies=5 * GROUPS + 2,
        scratch=[
            vmem(tile, BF), vmem(cut, BF), vmem(tile, BF), vmem(tile, BF), vmem(tile, BF),
            vmem((CR, LANES), F32), vmem((CR, LANES), F32),
        ],
    )
    conv, mix = call(
        unpack_kernel, [((9, MID, CH), F32), ((MID, CH), F32)], (spread_sums,), "unpack", flops=100_000_000
    )
    grad_conv = jnp.transpose(conv.reshape(3, 3, MID, CH), (2, 3, 0, 1))
    return symmetric, grad_input, grad_conv, mix.T


def solution(mesh):
    field = P(None, None, "row", "col")
    return jax.shard_map(
        local,
        mesh=mesh,
        in_specs=(field, field, P(), P(), P(), P(), P(), P()),
        out_specs=(field, field, P(), P()),
        check_vma=False,
    )
```

```python
import functools

import jax
import jax.numpy as jnp
from jax import lax
from jax.experimental import pallas as pl
from jax.experimental.pallas import tpu as pltpu
from jax.sharding import PartitionSpec as P

BF = jnp.bfloat16
F32 = jnp.float32
CH, MID, GROUPS, H, LANES, ROWS, COLS = 48, 24, 8, 8, 128, 16, 8
POS = GROUPS * LANES
CR, MR = CH * H, MID * H
TANH_SCALE = 0.7978845608028654
CUBIC = 0.044715
NN = (((1,), (0,)), ((), ()))
NT = (((1,), (1,)), ((), ()))
TN = (((0,), (0,)), ((), ()))


def smooth(v):
    t = jnp.tanh(TANH_SCALE * (v + CUBIC * (v * v * v)))
    return 0.5 * v * (1.0 + t)


def smooth_slope(v):
    s = v * v
    t = jnp.tanh(TANH_SCALE * (v + CUBIC * (v * s)))
    return 0.5 * (1.0 + t) + (0.5 * v) * (1.0 - t * t) * (TANH_SCALE * (1.0 + (3.0 * CUBIC) * s))


def smooth_both(v):
    s = v * v
    t = jnp.tanh(TANH_SCALE * (v + CUBIC * (v * s)))
    upper, half = 0.5 * (1.0 + t), 0.5 * v
    return half * (1.0 + t), upper + half * (1.0 - t * t) * (TANH_SCALE * (1.0 + (3.0 * CUBIC) * s))


def dot(a, b, dims=NN):
    return lax.dot_general(a, b, dims, preferred_element_type=F32)


def iota(shape, dim):
    return lax.broadcasted_iota(jnp.int32, shape, dim)


def identity(n):
    return jnp.where(iota((n, n), 0) == iota((n, n), 1), 1.0, 0.0).astype(BF)


def lanes_of(rows):
    return iota((rows, LANES), 1)


class Far:
    def __init__(self, sems):
        self.sems, self.used, self.open = sems, 0, []

    def start(self, source, target):
        copy = pltpu.make_async_copy(source, target, self.sems.at[self.used])
        self.used += 1
        copy.start()
        return copy

    def send(self, source, target):
        self.open.append(self.start(source, target))

    def finish(self):
        for copy in self.open:
            copy.wait()


def call(kernel, outs, args, name, smem=(), far=(), far_out=(), flops=4_000_000_000, scratch=(), copies=0, limit=16, alias=None):
    specs = [
        pl.BlockSpec(memory_space=pltpu.SMEM if i in smem else pltpu.HBM if i in far else pltpu.VMEM)
        for i in range(len(args))
    ]
    scratch = list(scratch)
    if copies:
        scratch.append(pltpu.SemaphoreType.DMA((copies,)))
    return pl.pallas_call(
        kernel,
        name=name,
        out_shape=[
            pltpu.HBM(s, t) if i in far_out else jax.ShapeDtypeStruct(s, t)
            for i, (s, t) in enumerate(outs)
        ],
        in_specs=specs,
        out_specs=[
            pl.BlockSpec(memory_space=pltpu.HBM if i in far_out else pltpu.VMEM)
            for i in range(len(outs))
        ],
        scratch_shapes=scratch,
        input_output_aliases=alias or {},
        compiler_params=pltpu.CompilerParams(vmem_limit_bytes=limit * 1024 * 1024),
        cost_estimate=pl.CostEstimate(flops=flops, bytes_accessed=1_000_000, transcendentals=0),
    )(
        *(
            pltpu.with_memory_space_constraint(v, pltpu.HBM) if i in far else v
            for i, v in enumerate(args)
        )
    )


def splat(values, count):
    return jnp.concatenate([jnp.full((H, LANES), values[o], F32) for o in range(count)], axis=0)


def pack_rows(field, count):
    pairs = field.reshape(count // 2, 2, H, LANES)
    even, odd = pairs[:, 0], pairs[:, 1]
    low = iota(even.shape, 1) < 4
    last = jnp.where(low, pltpu.roll(even, 4, 1), odd)
    first = jnp.where(low, even, pltpu.roll(odd, 4, 1))
    return last, first


def send_rows(source, down, up, count):
    at_end = (lax.axis_index("row") == ROWS - 1).astype(jnp.int32)
    at_start = (lax.axis_index("row") == 0).astype(jnp.int32)
    for g in range(GROUPS):
        before = g - at_end
        last, _ = pack_rows(source[jnp.maximum(before, 0)].astype(F32), count)
        down[g] = jnp.where(before >= 0, last, 0.0).astype(BF)
        after = g + at_start
        _, first = pack_rows(source[jnp.minimum(after, GROUPS - 1)].astype(F32), count)
        up[g] = jnp.where(after < GROUPS, first, 0.0).astype(BF)


def swap_blocks(parts):
    lane = iota(parts[0].shape, 1)
    parts = list(parts)
    for k in range(4):
        m = 1 << k
        high = (lane // (8 * m)) % 2 == 1
        for i in range(ROWS):
            if i & m:
                continue
            a, b = parts[i], parts[i | m]
            parts[i] = jnp.where(high, pltpu.roll(b, 8 * m, 1), a)
            parts[i | m] = jnp.where(high, b, pltpu.roll(a, LANES - 8 * m, 1))
    return parts


def turn(tiles):
    return tiles.reshape(LANES, LANES).T.reshape(ROWS, H, LANES)


def swap_in(pieces, g, buffer):
    parts = swap_blocks([pieces[r, g : g + 2].reshape(6 * H, LANES) for r in range(ROWS)])
    for i in range(ROWS):
        value = parts[i].reshape(2, 3, H, LANES)
        for n in range(2):
            for k in range(3):
                buffer[n, k * ROWS + i] = value[n, k]


def swap_out(block, pieces, g):
    parts = swap_blocks(
        [
            jnp.concatenate([block[g + n, k * ROWS + i] for n in range(2) for k in range(3)], axis=0)
            for i in range(ROWS)
        ]
    )
    for r in range(ROWS):
        pieces[r, g : g + 2] = parts[r].reshape(2, 3, H, LANES)


def first_kernel(x_far, d_far, down, up, pieces, x, d, turned, sems):
    far = Far(sems)
    loads = [far.start(d_far.at[g], d.at[g]) for g in range(GROUPS)]
    later = [far.start(x_far.at[g], x.at[g]) for g in range(GROUPS)]
    for g in range(GROUPS):
        loads[g].wait()
        for k in range(3):
            turned[:, g, k] = turn(d[g, k * ROWS : (k + 1) * ROWS])
        far.send(turned.at[:, g], pieces.at[:, g])
    for load in later:
        load.wait()
    send_rows(x, down, up, CH)
    far.finish()


def spread_channels(n, own, width):
    col = iota((n, width), 1)
    half = (width - own) // 2
    rim = jnp.where(col < own + half, col - own, col - own - half) // 4
    return jnp.where(jnp.where(col < own, col // 8, rim) == iota((n, width), 0), 1.0, 0.0).astype(BF)


def row_distance(own, width):
    col, h = iota((H, width), 1), iota((H, width), 0)
    half = (width - own) // 2
    rim = jnp.where(col < own + half, (col - own) % 4 - 4, (col - own - half) % 4 + 8)
    return jnp.where(col < own, col % 8, rim) - h


def weights_kernel(w, mix, a_out, mf_out, a_far, mf_far, mb_far, mb_out, sems):
    far = Far(sems)
    sf, st = spread_channels(CH, CR, 2 * CR), spread_channels(MID, MR, MR)
    pf, pt = row_distance(CR, 2 * CR), row_distance(MR, MR)
    masks = [jnp.where(pf == 4 * (a - 1), 1.0, 0.0)[None] for a in range(3)]
    col = iota((CH, CR), 1)
    above = jnp.where(col < CR // 2, sf[:, CR:].astype(F32), 0.0).astype(BF)
    below = jnp.where(col < CR // 2, 0.0, sf[:, CR:].astype(F32)).astype(BF)
    for b in range(3):
        total = jnp.zeros((MID, H, CR), F32)
        for a in range(3):
            total += dot(w[3 * a + b], sf[:, :CR])[:, None, :] * masks[a][:, :, :CR]
        rest = (dot(w[b], above) + dot(w[6 + b], below))[:, None, :] * (masks[0] + masks[2])[:, :, CR:]
        a_out[b * MR : (b + 1) * MR, 0:CR] = total.reshape(MR, CR).astype(BF)
        a_out[b * MR : (b + 1) * MR, CR : 2 * CR] = rest.reshape(MR, CR).astype(BF)
    far.send(a_out, a_far)
    mask = jnp.where(pf[:, :CR] == 0, 1.0, 0.0)
    mb_out[...] = (dot(mix[...], sf[:, :CR])[:, None, :] * mask[None]).reshape(MR, CR).astype(BF)
    far.send(mb_out, mb_far)
    mask = jnp.where(pt == 0, 1.0, 0.0)
    mf_out[...] = (dot(mix[...], st, TN)[:, None, :] * mask[None]).reshape(CR, MR).astype(BF)
    far.send(mf_out, mf_far)
    far.finish()


def back_weights(w, out):
    st, pt = spread_channels(MID, MR, 2 * MR), row_distance(MR, 2 * MR)
    masks = [jnp.where(pt == -4 * (a - 1), 1.0, 0.0)[None] for a in range(3)]
    for b in range(3):
        total = jnp.zeros((CH, H, 2 * MR), F32)
        for a in range(3):
            total += dot(w[3 * a + b], st, TN)[:, None, :] * masks[a]
        out[b * CR : (b + 1) * CR] = total.reshape(CR, 2 * MR).astype(BF)


def act_kernel(x, above, below, act, edge, wide_far, wide, rows, sems):
    far = Far(sems)
    for p in range(4):
        wide[64 * p + CH : 64 * p + 64, :] = jnp.zeros((64 - CH, 4 * POS), BF)
    lane = lanes_of(CR)
    packed = jnp.zeros((CR, LANES), F32)
    for g in range(GROUPS):
        own = smooth(x[g].astype(F32).reshape(CR, LANES))
        high = smooth(above[g].astype(F32).reshape(CR // 2, LANES))
        low = smooth(below[g].astype(F32).reshape(CR // 2, LANES))
        rim = jnp.concatenate([high, low], axis=0)
        at = slice(g * LANES, (g + 1) * LANES)
        act[0:CR, at] = own.astype(BF)
        act[CR : 2 * CR, at] = rim.astype(BF)
        rows[0:CR] = own
        rows[CR : 2 * CR] = rim
        for m in range(4):
            to = slice((m * GROUPS + g) * LANES, (m * GROUPS + g + 1) * LANES)
            for p, (start, step) in enumerate(((CR, 4), (0, 8), (4, 8), (CR + CR // 2, 4))):
                wide[64 * p : 64 * p + CH, to] = rows[pl.ds(start + m, CH, stride=step), :].astype(BF)
            far.send(wide.at[:, to], wide_far.at[:, to])
        packed = jnp.where(lane // 8 == g, pltpu.roll(own, (8 * g - 124) % LANES, 1), packed)
        packed = jnp.where(lane // 8 == 8 + g, pltpu.roll(rim, (8 * g - 60) % LANES, 1), packed)
    edge[...] = packed.astype(BF)
    far.finish()


def merge_edges(from_left, from_right):
    lane = lanes_of(from_left.shape[0])
    col = lax.axis_index("col")
    has_left = jnp.where(col > 0, 1.0, 0.0)
    has_right = jnp.where(col < COLS - 1, 1.0, 0.0)
    return jnp.where(
        lane % 8 < 4,
        pltpu.roll(from_right, LANES - 4, 1) * has_right,
        pltpu.roll(from_left, 4, 1) * has_left,
    )


def at_edge(lane):
    return jnp.logical_or(lane < 4, lane >= 124)


def inside_kernel(
    x, act, weights, mixer, cg, cb, mg, mb,
    slope_far, hidden_far, block_far, pieces_far, edge_inner_far, edge_x_far,
    slope, hidden, block, pieces, edge_inner, edge_x, sems,
):
    far = Far(sems)
    lane, lane_c = lanes_of(MR), lanes_of(CR)
    gain, shift = splat(cg, MID), splat(cb, MID)
    gain_out, shift_out = splat(mg, CH), splat(mb, CH)
    packed, packed_x = jnp.zeros((MR, LANES), F32), jnp.zeros((CR, LANES), F32)
    for pair in range(GROUPS // 2):
        two = slice(pair * 2 * LANES, (pair + 1) * 2 * LANES)
        product = dot(weights[...], act[:, two])
        for half in range(2):
            g = 2 * pair + half
            p = product[:, half * LANES : (half + 1) * LANES]
            inner = (
                p[MR : 2 * MR]
                + jnp.where(lane < 4, 0.0, pltpu.roll(p[0:MR], 4, 1))
                + jnp.where(lane >= 124, 0.0, pltpu.roll(p[2 * MR : 3 * MR], LANES - 4, 1))
            )
            packed = jnp.where(lane // 8 == g, pltpu.roll(inner, (8 * g - 124) % LANES, 1), packed)
            pre = inner * gain + shift
            at = slice(g * LANES, (g + 1) * LANES)
            smoothed, steep = smooth_both(pre)
            slope[:, at] = steep * gain
            hidden[:, at] = smoothed.astype(BF)
        far.send(slope.at[:, two], slope_far.at[:, two])
        far.send(hidden.at[:, two], hidden_far.at[:, two])
        mixed = dot(mixer[...], hidden[:, two])
        for half in range(2):
            g = 2 * pair + half
            m = mixed[:, half * LANES : (half + 1) * LANES]
            own = x[g].astype(F32).reshape(CR, LANES)
            packed_x = jnp.where(lane_c // 8 == g, pltpu.roll(own, (8 * g - 124) % LANES, 1), packed_x)
            value = (own + m * gain_out + shift_out).astype(BF)
            block[g] = value.astype(F32).reshape(CH, H, LANES).astype(BF)
        g = 2 * pair
        far.send(block.at[g : g + 2], block_far.at[g : g + 2])
        swap_out(block, pieces, g)
        far.send(pieces.at[:, g : g + 2], pieces_far.at[:, g : g + 2, 2:5])
    edge_inner[...] = packed
    edge_x[...] = packed_x
    far.send(edge_inner, edge_inner_far)
    far.send(edge_x, edge_x_far)
    far.finish()


def split(value):
    high = value.astype(BF)
    return high, (value - high.astype(F32)).astype(BF)


def exact_dot(value, onehot):
    high, low = split(value)
    return dot(high, onehot) + dot(low, onehot)


def inner_kernel(
    d_far, arrived, slope_far, hidden_far, edge_inner_far, edge_x_far, from_left, from_right,
    weights_far, mixer_far, back_far, pieces_in, cg, cb, mg, mb, wide_far,
    grad_inner_far, down, up, half_sum_far, pieces_far, edge_block_far, gmi, taps_out, hidden_out, rim_wide, wide,
    d, slope, hidden, edge_inner, edge_x, weights, mixer, back, grad_inner, half_sum, ends, edge_block, buffer, rows, sems,
):
    far = Far(sems)
    loads = [far.start(d_far.at[2 * p : 2 * p + 2], d.at[2 * p : 2 * p + 2]) for p in range(GROUPS // 2)]
    first = [far.start(weights_far.at[0:MR], weights.at[0:MR])]
    first.append(far.start(weights_far.at[2 * MR : 3 * MR], weights.at[MR : 2 * MR]))
    first += [far.start(edge_inner_far, edge_inner), far.start(edge_x_far, edge_x), far.start(mixer_far, mixer)]
    tails = [
        far.start(pieces_in.at[r, :, 2:5], ends.at[i]) for i, r in enumerate((0, ROWS - 1))
    ]
    later = [far.start(back_far, back), far.start(slope_far, slope), far.start(hidden_far, hidden)]
    far.send(wide_far, wide)
    lane, lane_c = lanes_of(MR), lanes_of(CR)
    gain, shift = splat(cg, MID), splat(cb, MID)
    gain_out, shift_out = splat(mg, CH), splat(mb, CH)
    rim = merge_edges(from_left[...].astype(F32), from_right[...].astype(F32))
    rows[...] = rim
    for m in range(4):
        to = slice(m * LANES, (m + 1) * LANES)
        for p, (start, step) in enumerate(((0, 4), (0, 8), (4, 8), (CR // 2, 4))):
            part = rows[pl.ds(start + m, CH, stride=step), :]
            if step == 4:
                part = pltpu.roll(part, 64, 1)
            rim_wide[64 * p : 64 * p + CH, to] = part.astype(BF)
    for p in range(4):
        rim_wide[64 * p + CH : 64 * p + 64, :] = jnp.zeros((64 - CH, 4 * LANES), BF)
    rim = rim.astype(BF)
    for pair in range(GROUPS // 2):
        loads[pair].wait()
        swap_in(arrived, 2 * pair, buffer)
        for half in range(2):
            g = 2 * pair + half
            both = 0.5 * (d[g].astype(F32) + buffer[half].astype(F32)).reshape(CR, LANES)
            half_sum[g] = both.reshape(CH, H, LANES)
            gmi[:, g * LANES : (g + 1) * LANES] = (both * gain_out).astype(BF)
        far.send(half_sum.at[2 * pair : 2 * pair + 2], half_sum_far.at[2 * pair : 2 * pair + 2])
    for load in first:
        load.wait()
    outer = dot(weights[:, 0:CR], rim) + pltpu.roll(dot(weights[:, CR : 2 * CR], rim), 64, 1)
    outer = jnp.where(lane % 8 < 4, outer[MR : 2 * MR], outer[0:MR])
    pre = (edge_inner[...] + outer) * gain + shift
    hidden_edge, slope_edge = smooth_both(pre)
    slope_edge = slope_edge * gain
    hidden_edge = hidden_edge.astype(BF)
    mixed = dot(mixer[...], hidden_edge)
    value = (edge_x[...] + mixed * gain_out + shift_out).astype(BF)
    edge_block[...] = value.astype(F32)
    far.send(edge_block, edge_block_far)
    hidden_edge = hidden_edge.astype(F32)
    parts = value.astype(F32).reshape(3, ROWS, H, LANES)
    parts = swap_blocks([parts[:, i].reshape(3 * H, LANES) for i in range(ROWS)])
    for load in tails:
        load.wait()
    low = iota((3, H, LANES), 2) % 8 < 4
    for g in range(GROUPS):
        lower = pltpu.roll(parts[g], LANES - 4, 1).reshape(3, H, LANES)
        upper = pltpu.roll(parts[g], 4, 1).reshape(3, H, LANES)
        ends[0, g] = jnp.where(low, lower, ends[0, g].astype(F32)).astype(BF)
        ends[1, g] = jnp.where(low, ends[1, g].astype(F32), upper).astype(BF)
    for i, r in enumerate((0, ROWS - 1)):
        far.send(ends.at[i], pieces_far.at[r, :, 2:5])

    for load in later:
        load.wait()
    packed = jnp.zeros((MR, LANES), F32)
    for pair in range(GROUPS // 2):
        two = slice(pair * 2 * LANES, (pair + 1) * 2 * LANES)
        into = dot(back[...], gmi[:, two])
        for half in range(2):
            g = 2 * pair + half
            at = slice(g * LANES, (g + 1) * LANES)
            turn = (124 - 8 * g) % LANES
            here = jnp.where(at_edge(lane), pltpu.roll(slope_edge, turn, 1), slope[:, at])
            value = into[:, half * LANES : (half + 1) * LANES] * here
            grad_inner[g] = value.reshape(MID, H, LANES).astype(BF)
            rows[0:MR] = value
            for r in range(H):
                part = jnp.concatenate([rows[pl.ds(r, MID, stride=8), :], jnp.zeros((H, LANES), F32)], axis=0)
                lane_t = lanes_of(MID + H)
                three = (
                    jnp.where(lane_t < 124, pltpu.roll(part, LANES - 4, 1), 0.0),
                    part,
                    jnp.where(lane_t >= 4, pltpu.roll(part, 4, 1), 0.0),
                )
                to = slice((r % 4 * GROUPS + g) * LANES, (r % 4 * GROUPS + g + 1) * LANES)
                for b in range(3):
                    top = 32 * (3 * (r // 4) + b)
                    taps_out[top : top + 32, to] = three[b].astype(BF)
            packed = jnp.where(lane // 8 == g, pltpu.roll(value, (8 * g - 124) % LANES, 1), packed)
            here = jnp.where(at_edge(lane), pltpu.roll(hidden_edge, turn, 1), hidden[:, at].astype(F32))
            hidden_out[:, at] = here.astype(BF)
        far.send(grad_inner.at[2 * pair : 2 * pair + 2], grad_inner_far.at[2 * pair : 2 * pair + 2])
    send_rows(grad_inner, down, up, MID)
    rows[0:MR] = packed
    for r in range(H):
        part = jnp.concatenate([rows[pl.ds(r, MID, stride=8), :], jnp.zeros((H, LANES), F32)], axis=0)
        lane_t = lanes_of(MID + H)
        low = jnp.where(lane_t % 8 < 4, part, 0.0)
        three = (part - low, jnp.zeros_like(part), low)
        to = slice(4 * POS + r % 4 * LANES, 4 * POS + (r % 4 + 1) * LANES)
        for b in range(3):
            top = 32 * (3 * (r // 4) + b)
            taps_out[top : top + 32, to] = three[b].astype(BF)
    far.finish()


def holder(t, yh, zh, xh):
    xl, yl, core, zl = t // 8, t // 4 % 2, t // 2 % 2, t % 2
    return (4 * xl + 2 * yh + yl) * 2 + core, 4 * zh + 2 * zl + xh


def holders(t):
    return [holder(t, *at) for at in near_groups()]


def near_groups():
    return [(yh, zh, xh) for yh in range(2) for zh in range(2) for xh in range(2)]


def sums_kernel(wide, gmi, taps, hidden, rim_wide, pieces_in, pieces_far, sums_out, sems):
    far = Far(sems)
    mixwide = dot(hidden[...], gmi[...], NT)
    h, col = iota((H, CR), 0), iota((H, CR), 1)
    same = jnp.where(col % 8 == h, 1.0, 0.0)[None]
    mixed = jnp.sum(mixwide.reshape(MID, H, CR) * same, axis=1)
    col, lane_s = iota((CR, LANES), 0), iota((CR, LANES), 1)
    mixed = exact_dot(mixed, jnp.where(col // 8 + 64 == lane_s, 1.0, 0.0).astype(BF))
    total = dot(taps[:, 4 * POS :], rim_wide[...], NT)
    total += dot(taps[:, 0 : 4 * POS], wide[...], NT)
    lane = lanes_of(MID)
    blocks, thirds = [], []
    for b in range(3):
        near, next_one = total[32 * b : 32 * b + MID], total[32 * (3 + b) : 32 * (3 + b) + MID]
        moved = pltpu.roll(next_one[:, 0:LANES], 64, 1)
        ahead = pltpu.roll(next_one[:, LANES : 2 * LANES], 64, 1)
        blocks.append(near[:, 0:LANES] + jnp.where(lane < 64, moved, ahead))
        thirds.append(jnp.where(lane < 64, near[:, LANES : 2 * LANES] + ahead, 0.0))
    blocks.append(thirds[0] + pltpu.roll(thirds[1], 64, 1))
    blocks.append(thirds[2] + mixed)
    blocks.append(jnp.zeros((MID, LANES), F32))
    for t in range(ROWS):
        part = blocks[t // 3][t % 3 * H : (t % 3 + 1) * H]
        high = part.astype(BF).astype(F32)
        both = jnp.concatenate([high[None], (part - high)[None]], axis=0).astype(BF)
        for r, c in holders(t):
            sums_out[r, c] = both
        if t % 2:
            for r in sorted({r for r, _ in holders(t)}):
                far.send(sums_out.at[r], pieces_far.at[r, :, 0:2])
    far.finish()


def spread_kernel(
    grad_inner_far, above, below, w, half_far, x_far, block_far, edge_block_far,
    edge, out_far, edge_value_far, edge_slope_far, block_out_far,
    weights, rhs, grad_inner, half_sum, x, block, edge_block, out, edge_value, edge_slope, sems,
):
    far = Far(sems)
    first = far.start(grad_inner_far, grad_inner)
    loads = [far.start(half_far, half_sum), far.start(x_far, x)]
    last = [far.start(block_far, block), far.start(edge_block_far, edge_block)]
    back_weights(w, weights)
    first.wait()
    lane = lanes_of(CR)
    packed, packed_value, packed_slope = (jnp.zeros((CR, LANES), F32) for _ in range(3))
    for load in loads:
        load.wait()
    for pair in range(GROUPS // 2):
        for half in range(2):
            g = 2 * pair + half
            at = slice(half * LANES, (half + 1) * LANES)
            rhs[0:MR, at] = grad_inner[g].astype(F32).reshape(MR, LANES).astype(BF)
            rhs[MR : MR + MR // 2, at] = above[g].astype(F32).reshape(MR // 2, LANES).astype(BF)
            rhs[MR + MR // 2 : 2 * MR, at] = below[g].astype(F32).reshape(MR // 2, LANES).astype(BF)
        product = dot(weights[...], rhs[...])
        for half in range(2):
            g = 2 * pair + half
            p = product[:, half * LANES : (half + 1) * LANES]
            left, mid, right = p[0:CR], p[CR : 2 * CR], p[2 * CR : 3 * CR]
            total = (
                mid
                + jnp.where(lane < 124, pltpu.roll(left, LANES - 4, 1), 0.0)
                + jnp.where(lane >= 4, pltpu.roll(right, 4, 1), 0.0)
            )
            slope = smooth_slope(x[g].astype(F32).reshape(CR, LANES))
            value = half_sum[g].reshape(CR, LANES) + total * slope
            out[g] = value.reshape(CH, H, LANES).astype(BF)
            far.send(out.at[g], out_far.at[g])
            here = lane // 8 == g
            turn_by = (8 * g - 124) % LANES
            packed = jnp.where(here, pltpu.roll(jnp.where(lane >= 124, right, left), turn_by, 1), packed)
            packed_value = jnp.where(here, pltpu.roll(value, turn_by, 1), packed_value)
            packed_slope = jnp.where(here, pltpu.roll(slope, turn_by, 1), packed_slope)
    edge[...] = packed[0 : CR // 2] + pltpu.roll(packed[CR // 2 : CR], 64, 1)
    edge_value[...] = packed_value
    edge_slope[...] = packed_slope
    far.send(edge_value, edge_value_far)
    far.send(edge_slope, edge_slope_far)
    for load in last:
        load.wait()
    for g in range(GROUPS):
        moved = pltpu.roll(edge_block[...], (124 - 8 * g) % LANES, 1)
        value = jnp.where(at_edge(lane), moved, block[g].astype(F32).reshape(CR, LANES))
        block[g] = value.reshape(CH, H, LANES).astype(BF)
        far.send(block.at[g], block_out_far.at[g])
    far.finish()


def total_kernel(arrived, out):
    total = jnp.zeros((H, LANES), F32)
    for g in range(COLS):
        part = arrived[:, g, 0:2].astype(F32)
        total += jnp.sum(part[:, 0] + part[:, 1], axis=0)
    out[...] = jnp.broadcast_to((total * (1.0 / (ROWS * H * COLS)))[None], (ROWS, H, LANES))


def last_kernel(
    block_far, arrived_far, value_far, edge_value_far, edge_slope_far, from_left, from_right, out_far, grad_far,
    block, arrived, out, value, grad, edge_value, edge_slope, sems,
):
    far = Far(sems)
    first = [far.start(edge_value_far, edge_value), far.start(edge_slope_far, edge_slope)]
    loads = [far.start(value_far.at[g], value.at[g]) for g in range(GROUPS)]
    later = [
        (far.start(block_far.at[g], block.at[g]), far.start(arrived_far.at[:, g, 2:5], arrived.at[:, g]))
        for g in range(GROUPS)
    ]
    lane = lanes_of(CR)
    rim = merge_edges(from_left[...], from_right[...])
    rim = jnp.concatenate([rim, pltpu.roll(rim, 64, 1)], axis=0)
    for load in first:
        load.wait()
    rim = edge_value[...] + rim * edge_slope[...]
    for g in range(GROUPS):
        loads[g].wait()
        moved = pltpu.roll(rim, (124 - 8 * g) % LANES, 1)
        total = jnp.where(at_edge(lane), moved, value[g].astype(F32).reshape(CR, LANES))
        grad[g] = total.reshape(CH, H, LANES).astype(BF)
        far.send(grad.at[g], grad_far.at[g])
    for g in range(GROUPS):
        for load in later[g]:
            load.wait()
        for k in range(3):
            at = slice(k * ROWS, (k + 1) * ROWS)
            both = 0.5 * (block[g, at].astype(F32) + turn(arrived[:, g, k]).astype(F32))
            out[g, at] = both.astype(BF)
        far.send(out.at[g], out_far.at[g])
    far.finish()


def unpack_kernel(tiles, conv, mix):
    order = ((0, 3), (1, 4), (2, 5), (6, 7), (8, None))
    for p, (left, right) in enumerate(order):
        value = tiles[3 * p : 3 * p + 3].reshape(3 * H, LANES)
        conv[left] = value[:, 0:CH]
        if right is None:
            mix[...] = value[:, 64 : 64 + CH]
        else:
            conv[right] = value[:, 64 : 64 + CH]


def both_ways(first, second, axis):
    count = lax.axis_size(axis)
    onward = [(i, (i + 1) % count) for i in range(count)]
    back = [(t, s) for s, t in onward]
    return lax.ppermute(first, axis, onward), lax.ppermute(second, axis, back)


def around_cols(edge):
    onward = []
    for r in range(ROWS):
        onward += [(r * COLS + c, r * COLS + c + 1) for c in range(COLS - 1)]
        onward.append((r * COLS + COLS - 1, (r ^ (ROWS // 2)) * COLS))
    back = [(t, s) for s, t in onward]
    return lax.ppermute(edge, ("row", "col"), onward), lax.ppermute(edge, ("row", "col"), back)


def local(pair_map, cotangent, conv_weight, conv_gain, conv_bias, mix_weight, mix_gain, mix_bias):
    tile = (GROUPS, CH, H, LANES)
    cut = (ROWS, COLS, 3, H, LANES)
    everyone = ("row", "col")
    vmem = pltpu.VMEM
    down, up, d_pieces = call(
        first_kernel, [((GROUPS, CH // 2, H, LANES), BF)] * 2 + [(cut, BF)], (pair_map, cotangent), "first",
        far=(0, 1), far_out=(2,), scratch=[vmem(tile, BF), vmem(tile, BF), vmem(cut, BF)], copies=3 * GROUPS,
    )
    above, below = both_ways(down, up, "row")
    d_arrived = lax.all_to_all(d_pieces.reshape(ROWS * COLS, 3, H, LANES), everyone, 0, 0, tiled=True)
    d_arrived = d_arrived.reshape(cut)

    taps = jnp.transpose(conv_weight, (2, 3, 0, 1)).reshape(9, MID, CH)
    wf, mf, wf_far, mf_far, mbk = call(
        weights_kernel,
        [((3 * MR, 2 * CR), BF), ((CR, MR), BF)] * 2 + [((MR, CR), BF)],
        (taps, mix_weight.T), "weights", far_out=(2, 3, 4), scratch=[vmem((MR, CR), BF)], copies=3,
    )
    act, edge, wide = call(
        act_kernel,
        [((2 * CR, POS), BF), ((CR, LANES), BF), ((256, 4 * POS), BF)],
        (pair_map, above, below), "act", far_out=(2,), copies=4 * GROUPS,
        scratch=[vmem((256, 4 * POS), BF), vmem((2 * CR, LANES), F32)],
    )
    from_left, from_right = around_cols(edge)
    five = (ROWS, COLS, 5, H, LANES)
    slope, hidden, block, pieces, edge_inner, edge_x = call(
        inside_kernel,
        [((MR, POS), F32), ((MR, POS), BF), (tile, BF), (five, BF), ((MR, LANES), F32), ((CR, LANES), F32)],
        (pair_map, act, wf, mf, conv_gain, conv_bias, mix_gain, mix_bias),
        "inside", smem=(4, 5, 6, 7), far_out=(0, 1, 2, 3, 4, 5),
        scratch=[
            vmem((MR, POS), F32), vmem((MR, POS), BF), vmem(tile, BF), vmem(cut, BF),
            vmem((MR, LANES), F32), vmem((CR, LANES), F32),
        ],
        copies=2 * GROUPS + 2,
    )
    grad_inner, g_down, g_up, half_sum, pieces, edge_block, gmi, tap_rows, hidden, rim_wide, wide = call(
        inner_kernel,
        [
            ((GROUPS, MID, H, LANES), BF),
            ((GROUPS, MID // 2, H, LANES), BF),
            ((GROUPS, MID // 2, H, LANES), BF),
            (tile, F32),
            (five, BF),
            ((CR, LANES), F32),
            ((CR, POS), BF),
            ((192, 4 * POS + 4 * LANES), BF),
            ((MR, POS), BF),
            ((256, 4 * LANES), BF),
            ((256, 4 * POS), BF),
        ],
        (
            cotangent, d_arrived, slope, hidden, edge_inner, edge_x, from_left, from_right,
            wf_far, mf_far, mbk, pieces, conv_gain, conv_bias, mix_gain, mix_bias, wide,
        ),
        "inner", smem=(12, 13, 14, 15), far=(0, 2, 3, 4, 5, 8, 9, 10, 11, 16), far_out=(0, 3, 4, 5), alias={11: 4},
        scratch=[
            vmem(tile, BF), vmem((MR, POS), F32), vmem((MR, POS), BF), vmem((MR, LANES), F32), vmem((CR, LANES), F32),
            vmem((2 * MR, 2 * CR), BF), vmem((CR, MR), BF), vmem((MR, CR), BF),
            vmem((GROUPS, MID, H, LANES), BF), vmem(tile, F32), vmem((2, COLS, 3, H, LANES), BF),
            vmem((CR, LANES), F32), vmem((2, CH, H, LANES), BF), vmem((CR, LANES), F32),
        ],
        copies=26,
    )
    g_above, g_below = both_ways(g_down, g_up, "row")
    (pieces,) = call(
        sums_kernel, [(five, BF)], (wide, gmi, tap_rows, hidden, rim_wide, pieces), "sums",
        far=(5,), far_out=(0,), alias={5: 0}, scratch=[vmem((ROWS, COLS, 2, H, LANES), BF)], copies=ROWS,
    )
    pieces, g_above, g_below = lax.optimization_barrier((pieces, g_above, g_below))
    arrived = lax.all_to_all(pieces.reshape(ROWS * COLS, 5, H, LANES), everyone, 0, 0, tiled=True)
    arrived = arrived.reshape(five)
    (sums,) = call(
        total_kernel, [((ROWS, H, LANES), F32)], (arrived,), "total", flops=500_000_000
    )
    groups = [[r * COLS + c for r, c in (holder(t, *at) for t in range(ROWS))] for at in near_groups()]
    spread_sums = lax.all_to_all(sums, everyone, 0, 0, axis_index_groups=groups, tiled=True)
    taps, _ = lax.optimization_barrier((taps, pieces))
    g_edge, inputs, edge_value, edge_slope, block = call(
        spread_kernel,
        [((CR // 2, LANES), F32), (tile, BF), ((CR, LANES), F32), ((CR, LANES), F32), (tile, BF)],
        (grad_inner, g_above, g_below, taps, half_sum, pair_map, block, edge_block),
        "spread", far=(0, 4, 5, 6, 7), far_out=(1, 2, 3, 4), copies=2 * GROUPS + 7,
        scratch=[
            vmem((3 * CR, 2 * MR), BF), vmem((2 * MR, 2 * LANES), BF), vmem((GROUPS, MID, H, LANES), BF),
            vmem(tile, F32), vmem(tile, BF), vmem(tile, BF), vmem((CR, LANES), F32), vmem(tile, BF),
            vmem((CR, LANES), F32), vmem((CR, LANES), F32),
        ],
    )
    g_left, g_right = around_cols(g_edge)
    g_left, g_right, block, _ = lax.optimization_barrier((g_left, g_right, block, sums))
    symmetric, grad_input = call(
        last_kernel, [(tile, BF)] * 2, (block, arrived, inputs, edge_value, edge_slope, g_left, g_right), "last",
        far=(0, 1, 2, 3, 4), far_out=(0, 1), copies=5 * GROUPS + 2,
        scratch=[
            vmem(tile, BF), vmem(cut, BF), vmem(tile, BF), vmem(tile, BF), vmem(tile, BF),
            vmem((CR, LANES), F32), vmem((CR, LANES), F32),
        ],
    )
    conv, mix = call(
        unpack_kernel, [((9, MID, CH), F32), ((MID, CH), F32)], (spread_sums,), "unpack", flops=100_000_000
    )
    grad_conv = jnp.transpose(conv.reshape(3, 3, MID, CH), (2, 3, 0, 1))
    return symmetric, grad_input, grad_conv, mix.T


def solution(mesh):
    field = P(None, None, "row", "col")
    return jax.shard_map(
        local,
        mesh=mesh,
        in_specs=(field, field, P(), P(), P(), P(), P(), P()),
        out_specs=(field, field, P(), P()),
        check_vma=False,
    )
```
